32 devices in a mesh: section: 2 (over core), wide: 16 (over z, y, x).
Axes of the slice: x: 2, y: 2, z: 4, core: 2. Of those that a mesh axis runs over, the one named last changes fastest.
Arguments:
- patches: bfloat16 [64, 196, 768], P('wide'), may hold values from -6 to 6
- out_cotangent: bfloat16 [64, 196, 768], P('wide'), may hold values from -6 to 6
- attn_gain: float32 [2, 768], P('section'), may hold values from 0.1 to 1.9
- qkv_weight: bfloat16 [2, 768, 2304], P('section'), may hold values from -0.21875 to 0.21875
- proj_weight: bfloat16 [2, 768, 768], P('section'), may hold values from -1.25 to 1.25
- ffn_gain: float32 [2, 768], P('section'), may hold values from 0.1 to 1.9
- mlp_in: bfloat16 [768, 3072], replicated, may hold values from -0.21875 to 0.21875
- mlp_out: bfloat16 [3072, 768], replicated, may hold values from -0.109375 to 0.109375
- router_weight: bfloat16 [768, 16], replicated, may hold values from -0.21875 to 0.21875
- expert_in: bfloat16 [16, 768, 3072], P('wide'), may hold values from -0.21875 to 0.21875
- expert_out: bfloat16 [16, 3072, 768], P('wide'), may hold values from -0.109375 to 0.109375
- expert_ids: int32 [64, 196, 2], P('wide'), may hold values from 0 to 15, all different within a row
- priority: int32 [32, 392], P('wide'), may hold values from 0 to 391, each once within a row
Outputs:
- activations: bfloat16 [2, 64, 196, 768], P('section', 'wide')
- input_grads: float32 [2, 64, 196, 768], P('section', 'wide')
- attn_gain_grad: float32 [2, 768], P('section')
- qkv_grad: float32 [2, 768, 2304], P('section')
- proj_grad: float32 [2, 768, 768], P('section')
- ffn_gain_grad: float32 [2, 768], P('section')
- mlp_in_grad: float32 [768, 3072], replicated
- mlp_out_grad: float32 [3072, 768], replicated
- router_grad: float32 [768, 16], replicated
- expert_in_grad: float32 [16, 768, 3072], P('wide')
- expert_out_grad: float32 [16, 3072, 768], P('wide')
The draws below stay inside these ranges and needn't reach their ends.
Inputs may be any that keep to these rules, and one draw needn't show every extreme that they name: `expert_ids`: each patch names two different experts. `priority`: row g ranks the 392 patches of image group g, images g * 2 to (g + 1) * 2 - 1 taken image-major; every rank once.
All inputs are finite; a program needn't handle non-finite values.
Results may differ from the reference program's by a relative error of at most 0.02.
Values may be sent and summed in bfloat16 or wider, within the bound.
No kernel may reach another device: no remote copies, remote signals or barrier semaphores. Data moves between devices by JAX's collectives and lax.ppermute only.
A program may use at most 320 MiB of HBM per device.

```python
import jax
import jax.numpy as jnp
from jax import lax

D = 768
H = 12
FF = 3072
SEQ = 196
IMG_MB = 2
TOK_MB = 392
EXPERTS = 16
CAP = 24
GROUPS = 32
IMAGES = 64


def shard_levels(rng, extent, shards, least, high):
    def one(position, shards_of):
        steps = jax.random.uniform(jax.random.fold_in(jax.random.fold_in(rng, 6), position), (shards_of,), jnp.float32, least / len(shards), high / len(shards))
        return jnp.repeat(jnp.exp(steps), extent[position] // shards_of).reshape((-1,) + (1,) * (len(extent) - position - 1))

    gain = one(*shards[0])
    for cut in shards[1:]:
        gain = gain * one(*cut)
    return gain


def distinct(own_key, rows, amount, top, lift):
    order = jax.random.permutation(jax.random.fold_in(own_key, 1), amount)
    favour = order
    for power in range(3):
        favour = favour * favour // amount
    favour = favour * lift // amount
    lots = jax.random.randint(jax.random.fold_in(own_key, 2), (rows, amount), 0, 4096) + favour
    fixed_rows = jax.random.permutation(jax.random.fold_in(own_key, 3), rows)[jnp.arange(amount) % rows]
    lots = jnp.where(jnp.arange(rows)[:, None] == fixed_rows[None, :], 1 << 14, lots)
    merit = lots * amount + jnp.arange(amount)
    return lax.top_k(merit.astype(jnp.int32), top)[1].astype(jnp.int32)


def scatter_about(stream_key, dims, width, limit, cuts=(), kind=jnp.bfloat16):
    level = shard_levels(stream_key, dims, cuts, -0.22, 0.18) if cuts else 1.0
    drawn = jax.random.normal(stream_key, dims, jnp.float32) * width * level
    return jnp.minimum(jnp.maximum(drawn, -limit), limit).astype(kind)


def setup_inputs(seed: int = 0) -> dict:
    keys = jax.random.split(jax.random.key(seed), 14)
    return {
        "patches": scatter_about(keys[0], (IMAGES, SEQ, D), 1.0, 6.0, ((0, 16),)),
        "out_cotangent": scatter_about(keys[1], (IMAGES, SEQ, D), 1.0, 6.0, ((0, 16),)),
        "attn_gain": jnp.clip(1.0 + 0.18 * jax.random.normal(keys[2], (2, D), jnp.float32), 0.1, 1.9),
        "qkv_weight": scatter_about(keys[3], (2, D, 3 * D), D ** -0.5, 0.21875, ((0, 2),)),
        "proj_weight": scatter_about(keys[4], (2, D, D), (D // 32) ** -0.5, 1.25, ((0, 2),)),
        "ffn_gain": jnp.clip(1.0 + 0.18 * jax.random.normal(keys[5], (2, D), jnp.float32), 0.1, 1.9),
        "mlp_in": scatter_about(keys[6], (D, FF), D ** -0.5, 0.21875),
        "mlp_out": scatter_about(keys[7], (FF, D), FF ** -0.5, 0.109375),
        "router_weight": scatter_about(keys[8], (D, EXPERTS), D ** -0.5, 0.21875),
        "expert_in": scatter_about(keys[9], (EXPERTS, D, FF), D ** -0.5, 0.21875, ((0, 16),)),
        "expert_out": scatter_about(keys[10], (EXPERTS, FF, D), FF ** -0.5, 0.109375, ((0, 16),)),
        "expert_ids": distinct(keys[11], IMAGES * SEQ, EXPERTS, 2, 1024).reshape((IMAGES, SEQ, 2)),
        "priority": jax.vmap(lambda own: jax.random.permutation(own, TOK_MB))(jax.random.split(keys[12], GROUPS)).reshape((GROUPS, TOK_MB)).astype(jnp.int32),
    }


@jax.custom_vjp
def low(v):
    return lax.optimization_barrier(v.astype(jnp.bfloat16)).astype(jnp.float32)

@jax.custom_vjp
def low_back(v):
    return v

def low_keep(v):
    return (low(v), None)

def low_pass(kept, grad):
    return (grad,)

def back_keep(v):
    return (v, None)

def back_low(kept, grad):
    return (low(grad),)
low.defvjp(low_keep, low_pass)
low_back.defvjp(back_keep, back_low)
norm_epsilon = 1e-06
highest = lax.Precision.HIGHEST

def layer_norm(stream, gain_vec):
    mean_value = lax.optimization_barrier(jnp.mean(stream, axis=-1, keepdims=True))
    centered = stream - mean_value
    variance = lax.optimization_barrier(jnp.mean(centered * centered, axis=-1, keepdims=True))
    return centered * lax.rsqrt(variance + norm_epsilon) * gain_vec

def attention_block(stream, gain_vec, qkv_matrix, proj_matrix):
    images, length, model_width = stream.shape
    head_size = model_width // H
    normed = low(layer_norm(stream, gain_vec))
    packed = jnp.einsum('bsd,de->bse', normed, qkv_matrix, precision=highest)
    packed = low(low_back(packed)).reshape(images, length, 3, H, head_size)
    queries = packed[:, :, 0]
    key_rows = packed[:, :, 1]
    value_rows = packed[:, :, 2]
    raw_scores = jnp.einsum('bqhd,bkhd->bhqk', queries, key_rows, precision=highest)
    scores = low_back(raw_scores) * head_size ** (-0.5)
    weights_low = low(jax.nn.softmax(scores, axis=-1))
    mixture = jnp.einsum('bhqk,bkhd->bqhd', weights_low, value_rows, precision=highest)
    mixture = low(low_back(mixture)).reshape(images, length, model_width)
    attended = low_back(jnp.einsum('bsd,de->bse', mixture, proj_matrix, precision=highest))
    return stream + attended

def slot_plan(choice_ids, rank_row):
    token_count = rank_row.shape[0]
    token_range = jnp.arange(token_count, dtype=jnp.int32)
    sorted_order = jnp.zeros((token_count,), jnp.int32).at[rank_row].set(token_range)
    sorted_ids = choice_ids[sorted_order]
    flat_ids = jnp.transpose(sorted_ids).reshape(2 * token_count)
    one_hot = (flat_ids[:, None] == jnp.arange(EXPERTS, dtype=jnp.int32)[None, :]).astype(jnp.int32)
    running = jnp.cumsum(one_hot, axis=0).astype(jnp.int32)
    place_flat = (lax.optimization_barrier(jnp.sum(running * one_hot, axis=1)) - 1).astype(jnp.int32)
    slot_place = jnp.transpose(place_flat.reshape(2, token_count)[:, rank_row])
    kept_mask = slot_place < CAP
    slot_index = (choice_ids * CAP + jnp.minimum(slot_place, CAP - 1)).astype(jnp.int32)
    target = jnp.where(kept_mask, slot_index, EXPERTS * CAP).reshape(2 * token_count)
    token_pair = jnp.broadcast_to(token_range[:, None], (token_count, 2)).reshape(2 * token_count)
    slot_token = jnp.full((EXPERTS * CAP,), -1, jnp.int32).at[target].set(token_pair, mode='drop')
    return (kept_mask, slot_index, slot_token)

def expert_block(flat_stream, gain_vec, router_matrix, expert_first, expert_second, choice_ids, rank_row):
    token_count, model_width = flat_stream.shape
    normed = low(layer_norm(flat_stream, gain_vec))
    logits = low_back(jnp.dot(normed, router_matrix, precision=highest))
    one_hot = (choice_ids[:, :, None] == jnp.arange(EXPERTS, dtype=jnp.int32)[None, None, :]).astype(jnp.float32)
    chosen = jnp.einsum('rje,re->rj', one_hot, logits, precision=highest)
    gate_values = jax.nn.softmax(chosen, axis=-1)
    kept_mask, slot_index, slot_token = slot_plan(choice_ids, rank_row)
    slot_valid = slot_token >= 0
    source_token = jnp.maximum(slot_token, 0)
    slot_rows = jnp.where(slot_valid[:, None], normed[source_token], 0.0)
    slot_rows = low_back(slot_rows).reshape(EXPERTS, CAP, model_width)
    hidden = low_back(jnp.einsum('ecd,edf->ecf', slot_rows, expert_first, precision=highest))
    active = low(jax.nn.gelu(hidden))
    result = jnp.einsum('ecf,efd->ecd', active, expert_second, precision=highest)
    result = low(low_back(result)).reshape(EXPERTS * CAP, model_width)
    weighting = gate_values * kept_mask.astype(jnp.float32)
    picked = result[slot_index]
    return flat_stream + lax.optimization_barrier(jnp.sum(weighting[:, :, None] * picked, axis=1))

def two_blocks(params, patch_block, probe_block, id_block, rank_row):
    gain_attn, qkv_all, proj_all, gain_ffn, first_matrix, second_matrix, router_matrix, expert_first, expert_second = params
    stream = attention_block(patch_block, gain_attn[0], qkv_all[0], proj_all[0])
    normed = low(layer_norm(stream, gain_ffn[0]))
    hidden = low_back(jnp.einsum('bsd,df->bsf', normed, first_matrix, precision=highest))
    active = low(jax.nn.gelu(hidden))
    first_out = stream + low_back(jnp.einsum('bsf,fd->bsd', active, second_matrix, precision=highest))
    handed = low(low_back(first_out + probe_block))
    stream_two = attention_block(handed, gain_attn[1], qkv_all[1], proj_all[1])
    flat_stream = stream_two.reshape(TOK_MB, D)
    second_out = expert_block(flat_stream, gain_ffn[1], router_matrix, expert_first, expert_second, id_block, rank_row)
    return (first_out, second_out.reshape(IMG_MB, SEQ, D))

def add_up(left_part, right_part):
    return left_part + right_part

def reference(patches, out_cotangent, attn_gain, qkv_weight, proj_weight, ffn_gain, mlp_in, mlp_out, router_weight, expert_in, expert_out, expert_ids, priority):
    params = tuple((item_array.astype(jnp.float32) for item_array in (attn_gain, qkv_weight, proj_weight, ffn_gain, mlp_in, mlp_out, router_weight, expert_in, expert_out)))
    patch_groups = patches.astype(jnp.float32).reshape(GROUPS, IMG_MB, SEQ, D)
    cotangent_groups = out_cotangent.astype(jnp.float32).reshape(GROUPS, IMG_MB, SEQ, D)
    id_groups = expert_ids.reshape(GROUPS, TOK_MB, 2)

    def step_group(totals, group_items):
        patch_block, cotangent_block, id_block, rank_row = group_items
        probe_block = jnp.zeros_like(patch_block)

        def forward(param_set, input_block, probe_input):
            return two_blocks(param_set, input_block, probe_input, id_block, rank_row)
        outputs, pullback = jax.vjp(forward, params, patch_block, probe_block)
        grad_params, grad_inputs, grad_probe = pullback((jnp.zeros_like(outputs[0]), cotangent_block))
        totals = jax.tree.map(add_up, totals, grad_params)
        return (totals, (outputs[0], outputs[1], grad_inputs, grad_probe))
    zero_totals = jax.tree.map(jnp.zeros_like, params)
    totals, stacked = lax.scan(step_group, zero_totals, (patch_groups, cotangent_groups, id_groups, priority))
    first_all = stacked[0].reshape(IMAGES, SEQ, D).astype(jnp.bfloat16)
    second_all = stacked[1].reshape(IMAGES, SEQ, D).astype(jnp.bfloat16)
    activations = jnp.stack([first_all, second_all])
    input_grads = jnp.stack([stacked[2].reshape(IMAGES, SEQ, D), stacked[3].reshape(IMAGES, SEQ, D)])
    return (activations, input_grads, totals[0], totals[1], totals[2], totals[3], totals[4], totals[5], totals[6], totals[7], totals[8])
```

```python
import jax
import jax.numpy as jnp
from jax import lax
from jax.sharding import PartitionSpec as P

H = 12
norm_epsilon = 1e-06
bf16 = jnp.bfloat16
f32 = jnp.float32


def dot(left, right, dims):
    return lax.dot_general(left, right, (dims, ((), ())), preferred_element_type=f32)


def nn(left, right):
    return dot(left, right, ((1,), (0,)))


def nt(left, right):
    return dot(left, right, ((1,), (1,)))


def tn(left, right):
    return dot(left, right, ((0,), (0,)))


def norm_stats(stream):
    mean_value = jnp.mean(stream, axis=-1, keepdims=True)
    centered = stream - mean_value
    variance = jnp.mean(centered * centered, axis=-1, keepdims=True)
    scale = lax.rsqrt(variance + norm_epsilon)
    return (centered * scale, scale)


def norm_back(unit, scale, gain_vec, upstream):
    weighted = upstream * gain_vec
    first = jnp.mean(weighted, axis=-1, keepdims=True)
    second = jnp.mean(weighted * unit, axis=-1, keepdims=True)
    return (scale * (weighted - first - unit * second), jnp.sum(upstream * unit, axis=0))


def gelu_back(hidden, upstream):
    gelu_value, pullback = jax.vjp(jax.nn.gelu, hidden)
    return pullback(upstream)[0]


def attention_forward(stream, gain_vec, qkv_matrix, proj_matrix, images):
    rows, model_width = stream.shape
    length = rows // images
    head_size = model_width // H
    unit, scale = norm_stats(stream)
    normed = (unit * gain_vec).astype(bf16)
    packed = nn(normed, qkv_matrix).astype(bf16).reshape(images, length, 3, H, head_size)
    queries, keys, values = packed[:, :, 0], packed[:, :, 1], packed[:, :, 2]
    scores = jnp.einsum("bqhd,bkhd->bhqk", queries, keys, preferred_element_type=f32)
    weights = jax.nn.softmax(scores * head_size ** (-0.5), axis=-1)
    mixture = jnp.einsum("bhqk,bkhd->bqhd", weights.astype(bf16), values, preferred_element_type=f32)
    mixture = mixture.astype(bf16).reshape(rows, model_width)
    return (
        stream + nn(mixture, proj_matrix),
        (unit, scale, normed, queries, keys, values, weights, mixture),
    )


def attention_backward(kept, gain_vec, qkv_matrix, proj_matrix, upstream):
    unit, scale, normed, queries, keys, values, weights, mixture = kept
    images, length, heads, head_size = queries.shape
    rows, model_width = upstream.shape
    upstream_low = upstream.astype(bf16)
    grad_proj = tn(mixture, upstream_low)
    grad_mixture = nt(upstream_low, proj_matrix).astype(bf16).reshape(queries.shape)
    grad_weights = jnp.einsum("bqhd,bkhd->bhqk", grad_mixture, values, preferred_element_type=f32)
    grad_values = jnp.einsum(
        "bhqk,bqhd->bkhd", weights.astype(bf16), grad_mixture, preferred_element_type=f32
    )
    inner = jnp.sum(grad_weights * weights, axis=-1, keepdims=True)
    grad_raw = (weights * (grad_weights - inner) * head_size ** (-0.5)).astype(bf16)
    grad_queries = jnp.einsum("bhqk,bkhd->bqhd", grad_raw, keys, preferred_element_type=f32)
    grad_keys = jnp.einsum("bhqk,bqhd->bkhd", grad_raw, queries, preferred_element_type=f32)
    grad_packed = jnp.stack([grad_queries, grad_keys, grad_values], axis=2).astype(bf16)
    grad_packed = grad_packed.reshape(rows, 3 * model_width)
    grad_qkv = tn(normed, grad_packed)
    grad_stream, grad_gain = norm_back(unit, scale, gain_vec, nt(grad_packed, qkv_matrix))
    return (upstream + grad_stream, grad_gain, grad_qkv, grad_proj)


def slot_plan(ids, rank, capacity, slots):
    before = rank[None, :] < rank[:, None]
    first, second = ids[:, 0], ids[:, 1]

    def count(mask):
        return jnp.sum(mask.astype(jnp.int32), axis=1)

    place_first = count((first[:, None] == first[None, :]) & before)
    place_second = count(
        ((second[:, None] == second[None, :]) & before)
        | (second[:, None] == first[None, :])
    )
    both = count((second[:, None] == second[None, :]) & before & (second[:, None] == first[None, :]))
    place_second = place_second + both
    slot_first = jnp.where(place_first < capacity, first * capacity + place_first, -1)
    slot_second = jnp.where(place_second < capacity, second * capacity + place_second, -1)
    return (slot_first, slot_second)


def body(
    patches,
    out_cotangent,
    attn_gain,
    qkv_weight,
    proj_weight,
    ffn_gain,
    mlp_in,
    mlp_out,
    router_weight,
    expert_in,
    expert_out,
    expert_ids,
    priority,
):
    expert_count = lax.axis_size("wide")
    sections = lax.axis_size("section")
    section = lax.axis_index("section")
    is_first = section == 0
    images = patches.shape[0] // sections
    length, model_width = patches.shape[1:]
    hidden_width = mlp_in.shape[1]
    rows = images * length
    capacity = max(2, rows // expert_count)
    slots = expert_count * capacity
    slot_shape = (expert_count, capacity, model_width)

    def mine(whole, count):
        return lax.dynamic_slice_in_dim(whole, section * count, count)

    def swap(value):
        return lax.ppermute(value, "section", [(0, 1), (1, 0)])

    def both(own):
        other = swap(own)
        return (jnp.where(is_first, own, other), jnp.where(is_first, other, own))

    def across(value):
        moved = lax.all_to_all(
            value.reshape(slot_shape), "wide", split_axis=0, concat_axis=0, tiled=True
        )
        return moved.reshape(slots, model_width)

    qkv_one, qkv_two = both(qkv_weight[0])
    proj_one, proj_two = both(proj_weight[0])
    gain_attn_one, gain_attn_two = both(attn_gain[0])
    gain_ffn_one, gain_ffn_two = both(ffn_gain[0])

    ids = mine(expert_ids, images).reshape(rows, 2)
    rank = mine(priority, 1)[0]
    slot_first, slot_second = slot_plan(ids, rank, capacity, slots)
    slot_range = jnp.arange(slots, dtype=jnp.int32)
    pick_first = slot_first[:, None] == slot_range[None, :]
    pick_second = slot_second[:, None] == slot_range[None, :]
    pick_any = (pick_first | pick_second).astype(bf16)
    kept = jnp.stack([slot_first >= 0, slot_second >= 0], axis=1).astype(f32)
    cotangent = mine(out_cotangent, images).reshape(rows, model_width)
    arrived_cotangent = across(tn(pick_any, cotangent).astype(bf16))

    stream_zero = mine(patches, images).reshape(rows, model_width).astype(f32)
    mixed_one, kept_one = attention_forward(stream_zero, gain_attn_one, qkv_one, proj_one, images)
    unit_one, scale_one = norm_stats(mixed_one)
    normed_one = (unit_one * gain_ffn_one).astype(bf16)
    hidden_one = nn(normed_one, mlp_in)
    active_one = jax.nn.gelu(hidden_one).astype(bf16)
    first_low = (mixed_one + nn(active_one, mlp_out)).astype(bf16)

    stream_two = first_low.astype(f32)
    mixed_two, kept_two = attention_forward(stream_two, gain_attn_two, qkv_two, proj_two, images)
    unit_two, scale_two = norm_stats(mixed_two)
    normed_two = (unit_two * gain_ffn_two).astype(bf16)
    logits = nn(normed_two, router_weight)
    one_hot = (ids[:, :, None] == jnp.arange(expert_count, dtype=jnp.int32)[None, None, :]).astype(
        f32
    )
    chosen = jnp.sum(one_hot * logits[:, None, :], axis=-1)
    gates = jax.nn.softmax(chosen, axis=-1)
    weighting = gates * kept
    slot_gate = jnp.sum(
        jnp.where(pick_first, weighting[:, :1], 0.0) + jnp.where(pick_second, weighting[:, 1:], 0.0),
        axis=0,
    )
    arrived = across(tn(pick_any, normed_two).astype(bf16))
    arrived_gate = lax.all_to_all(
        jnp.broadcast_to(slot_gate.reshape(expert_count, 1, capacity), (expert_count, 8, capacity)),
        "wide",
        split_axis=0,
        concat_axis=0,
        tiled=True,
    )[:, 0].reshape(slots, 1)
    weight_in, weight_out = expert_in[0], expert_out[0]
    hidden = nn(arrived, weight_in)
    active = jax.nn.gelu(hidden).astype(bf16)
    result = nn(active, weight_out).astype(bf16)
    returned = across(result)
    grad_rows = (arrived_gate * arrived_cotangent.astype(f32)).astype(bf16)
    grad_active = nt(grad_rows, weight_out)
    grad_hidden = gelu_back(hidden, grad_active).astype(bf16)
    returned_grad = across(nt(grad_hidden, weight_in).astype(bf16))
    grad_expert_in = tn(arrived, grad_hidden).astype(bf16)
    grad_expert_out = tn(active, grad_rows).astype(bf16)
    expert_in_sum = grad_expert_in.astype(f32) + swap(grad_expert_in).astype(f32)
    expert_out_sum = grad_expert_out.astype(f32) + swap(grad_expert_out).astype(f32)

    picked_first = nn(pick_first.astype(bf16), returned)
    picked_second = nn(pick_second.astype(bf16), returned)
    second_low = (
        mixed_two + weighting[:, :1] * picked_first + weighting[:, 1:] * picked_second
    ).astype(bf16)
    upstream = cotangent.astype(f32)
    grad_gates = jnp.stack(
        [jnp.sum(upstream * picked_first, axis=-1), jnp.sum(upstream * picked_second, axis=-1)],
        axis=1,
    )
    grad_chosen = gates * (grad_gates - jnp.sum(gates * grad_gates, axis=-1, keepdims=True))
    grad_logits = jnp.sum(one_hot * grad_chosen[:, :, None], axis=1).astype(bf16)
    grad_router = tn(normed_two, grad_logits)
    grad_normed_two = nn(pick_any, returned_grad) + nt(grad_logits, router_weight)
    grad_flat, grad_ffn_two = norm_back(unit_two, scale_two, gain_ffn_two, grad_normed_two)
    grad_two, grad_attn_two, grad_qkv_two, grad_proj_two = attention_backward(
        kept_two, gain_attn_two, qkv_two, proj_two, upstream + grad_flat
    )

    def halves_sum(parts):
        def half(value, which):
            size = value.shape[0] // 2
            return lax.dynamic_slice_in_dim(value, which * size, size)

        sent = [half(value, 1 - section).astype(bf16) for value in parts]
        got = [swap(value) for value in sent]
        summed = [
            (half(value, section) + other.astype(f32)).astype(bf16)
            for value, other in zip(parts, got)
        ]
        return [lax.psum(value, "wide") for value in summed]

    qkv_two_half, proj_two_half = halves_sum([grad_qkv_two, grad_proj_two])

    grad_first = grad_two.astype(bf16)
    mlp_up = grad_first.astype(f32)
    grad_mlp_out = tn(active_one, grad_first)
    grad_active_one = nt(grad_first, mlp_out)
    grad_hidden_one = gelu_back(hidden_one, grad_active_one).astype(bf16)
    grad_mlp_in = tn(normed_one, grad_hidden_one)
    mlp_out_half, mlp_in_half = halves_sum([grad_mlp_out, grad_mlp_in])
    grad_flat_one, grad_ffn_one = norm_back(
        unit_one, scale_one, gain_ffn_one, nt(grad_hidden_one, mlp_in)
    )
    grad_one, grad_attn_one, grad_qkv_one, grad_proj_one = attention_backward(
        kept_one, gain_attn_one, qkv_one, proj_one, mlp_up + grad_flat_one
    )
    qkv_one_half, proj_one_half = halves_sum([grad_qkv_one, grad_proj_one])

    def joined(half):
        other = swap(half)
        return jnp.concatenate(
            [jnp.where(is_first, half, other), jnp.where(is_first, other, half)], axis=0
        ).astype(f32)

    def own_block(half_one, half_two):
        own = jnp.where(is_first, half_one, half_two)
        other = swap(jnp.where(is_first, half_two, half_one))
        return jnp.concatenate(
            [jnp.where(is_first, own, other), jnp.where(is_first, other, own)], axis=0
        ).astype(f32)

    def own_images(value_one, value_two):
        own = jnp.where(is_first, value_one, value_two)
        other = swap(jnp.where(is_first, value_two, value_one))
        stacked = jnp.concatenate(
            [jnp.where(is_first, own, other), jnp.where(is_first, other, own)], axis=0
        )
        return stacked.reshape((1, sections * images, length, model_width))

    small = jnp.concatenate(
        [
            grad_router,
            jnp.stack([grad_attn_one, grad_attn_two, grad_ffn_one, grad_ffn_two], axis=1),
        ],
        axis=1,
    )
    small = lax.psum(small, ("section", "wide"))
    gain_sums = jnp.transpose(small[:, expert_count:])
    activations = own_images(first_low, second_low)
    input_grads = own_images(grad_one, mlp_up)
    return (
        activations,
        input_grads,
        lax.dynamic_slice_in_dim(gain_sums, section, 1),
        own_block(qkv_one_half, qkv_two_half)[None],
        own_block(proj_one_half, proj_two_half)[None],
        lax.dynamic_slice_in_dim(gain_sums, 2 + section, 1),
        joined(mlp_in_half),
        joined(mlp_out_half),
        small[:, :expert_count],
        expert_in_sum[None],
        expert_out_sum[None],
    )


def solution(mesh):
    in_specs = (
        P("wide", None, None),
        P("wide", None, None),
        P("section", None),
        P("section", None, None),
        P("section", None, None),
        P("section", None),
        P(),
        P(),
        P(),
        P("wide", None, None),
        P("wide", None, None),
        P("wide", None, None),
        P("wide", None),
    )
    out_specs = (
        P("section", "wide", None, None),
        P("section", "wide", None, None),
        P("section", None),
        P("section", None, None),
        P("section", None, None),
        P("section", None),
        P(),
        P(),
        P(),
        P("wide", None, None),
        P("wide", None, None),
    )
    return jax.shard_map(body, mesh=mesh, in_specs=in_specs, out_specs=out_specs, check_vma=False)
```

```python
import functools

import jax
import jax.numpy as jnp
from jax import lax
from jax.experimental import pallas as pl
from jax.experimental.pallas import tpu as pltpu
from jax.sharding import PartitionSpec as P

H = 12
HEAD = 64
PAIR = 2 * HEAD
STEP = 16
norm_epsilon = 1e-06
bf16 = jnp.bfloat16
f32 = jnp.float32


def dot(left, right, dims):
    return lax.dot_general(left, right, (dims, ((), ())), preferred_element_type=f32)


def nn(left, right):
    return dot(left, right, ((1,), (0,)))


def nt(left, right):
    return dot(left, right, ((1,), (1,)))


def tn(left, right):
    return dot(left, right, ((0,), (0,)))


def norm_rows(value):
    mean_value = jnp.mean(value, axis=-1, keepdims=True)
    centered = value - mean_value
    scale = lax.rsqrt(jnp.mean(centered * centered, axis=-1, keepdims=True) + norm_epsilon)
    return (centered * scale, scale)


def norm_rows_back(unit, scale, gain, upstream):
    weighted = upstream * gain
    first = jnp.mean(weighted, axis=-1, keepdims=True)
    second = jnp.mean(weighted * unit, axis=-1, keepdims=True)
    return scale * (weighted - first - unit * second)


def fetch(take, own, other, target, sem):
    @pl.when(take == 1)
    def _():
        pltpu.make_async_copy(own, target, sem).start()

    @pl.when(take != 1)
    def _():
        pltpu.make_async_copy(other, target, sem).start()


def forward_kernel(
    images,
    length,
    which,
    x_ref,
    own_qkv,
    other_qkv,
    own_proj,
    other_proj,
    gain_a,
    gain_f,
    mixed_ref,
    packed_ref,
    mix_ref,
    normed_ref,
    qkv_ref,
    proj_ref,
    low_ref,
    sems,
):
    rows, width = x_ref.shape
    pad = rows // images
    fetch(which[0], own_qkv, other_qkv, qkv_ref, sems.at[0])
    fetch(which[0], own_proj, other_proj, proj_ref, sems.at[1])

    @pl.loop(0, rows // STEP)
    def _(step):
        block = pl.ds(pl.multiple_of(step * STEP, STEP), STEP)
        unit, scale = norm_rows(x_ref[block, :].astype(f32))
        low_ref[block, :] = (unit * gain_a[...]).astype(bf16)

    pltpu.make_async_copy(own_qkv, qkv_ref, sems.at[0]).wait()

    @pl.loop(0, 3 * width // 256)
    def _(step):
        lanes = pl.ds(pl.multiple_of(step * 256, 256), 256)
        packed_ref[:, lanes] = nn(low_ref[...], qkv_ref[:, lanes]).astype(bf16)

    left = lax.broadcasted_iota(jnp.int32, (pad, PAIR), 1) < HEAD
    live = lax.broadcasted_iota(jnp.int32, (pad, pad), 1) < length

    @pl.loop(0, width // PAIR)
    def _(pair):
        def lanes(part):
            return pl.ds(pl.multiple_of(part * width + pair * PAIR, PAIR), PAIR)

        for image in range(images):
            block = slice(image * pad, (image + 1) * pad)
            queries = packed_ref[block, lanes(0)]
            keys = packed_ref[block, lanes(1)]
            values = packed_ref[block, lanes(2)]
            outs = []
            for half in (left, ~left):
                scores = nt(jnp.where(half, queries, 0.0).astype(bf16), keys) * HEAD ** (-0.5)
                scores = jnp.where(live, scores, -jnp.inf)
                powers = jnp.exp(scores - jnp.max(scores, axis=1, keepdims=True))
                weights = powers * (1.0 / jnp.sum(powers, axis=1, keepdims=True))
                outs.append(nn(weights.astype(bf16), values))
            mix_ref[block, lanes(0)] = jnp.where(left, outs[0], outs[1]).astype(bf16)

    pltpu.make_async_copy(own_proj, proj_ref, sems.at[1]).wait()

    @pl.loop(0, width // 256)
    def _(step):
        lanes = pl.ds(pl.multiple_of(step * 256, 256), 256)
        mixed_ref[:, lanes] = x_ref[:, lanes].astype(f32) + nn(mix_ref[...], proj_ref[:, lanes])

    @pl.loop(0, rows // STEP)
    def _(step):
        block = pl.ds(pl.multiple_of(step * STEP, STEP), STEP)
        unit, scale = norm_rows(mixed_ref[block, :])
        normed_ref[block, :] = (unit * gain_f[...]).astype(bf16)


def backward_kernel(
    images,
    length,
    which,
    x_ref,
    mixed_ref,
    base_ref,
    upstream_ref,
    packed_ref,
    mix_ref,
    own_qkv,
    other_qkv,
    own_proj,
    other_proj,
    gain_a,
    gain_f,
    grad_ref,
    gains_ref,
    *rest,
):
    sends, keeps = rest[:3], rest[3:6]
    qkv_ref, proj_ref, total_ref, total_low, low_ref, grad_mix, grad_packed, sems = rest[6:]
    rows, width = x_ref.shape
    pad = rows // images
    fetch(which[0], own_proj, other_proj, proj_ref, sems.at[1])
    fetch(which[0], own_qkv, other_qkv, qkv_ref, sems.at[0])
    zero = jnp.zeros((STEP, width), f32)

    def enter(step, total):
        block = pl.ds(pl.multiple_of(step * STEP, STEP), STEP)
        unit, scale = norm_rows(mixed_ref[block, :])
        upstream = upstream_ref[block, :]
        value = base_ref[block, :].astype(f32) + norm_rows_back(
            unit, scale, gain_f[...], upstream
        )
        total_ref[block, :] = value
        total_low[block, :] = value.astype(bf16)
        source_unit, source_scale = norm_rows(x_ref[block, :].astype(f32))
        low_ref[block, :] = (source_unit * gain_a[...]).astype(bf16)
        return total + upstream * unit

    gain_total = lax.fori_loop(0, rows // STEP, enter, zero)
    gains_ref[...] = jnp.zeros_like(gains_ref)
    gains_ref[1:2, :] = jnp.sum(gain_total, axis=0, keepdims=True)
    pltpu.make_async_copy(own_proj, proj_ref, sems.at[1]).wait()

    @pl.loop(0, width // 256)
    def _(step):
        lanes = pl.ds(pl.multiple_of(step * 256, 256), 256)
        grad_mix[:, lanes] = nt(total_low[...], proj_ref[lanes, :]).astype(bf16)

    left = lax.broadcasted_iota(jnp.int32, (pad, PAIR), 1) < HEAD
    live = lax.broadcasted_iota(jnp.int32, (pad, pad), 0) < length

    @pl.loop(0, width // PAIR)
    def _(pair):
        def lanes(part):
            return pl.ds(pl.multiple_of(part * width + pair * PAIR, PAIR), PAIR)

        for image in range(images):
            block = slice(image * pad, (image + 1) * pad)
            queries = packed_ref[block, lanes(0)]
            keys = packed_ref[block, lanes(1)]
            values = packed_ref[block, lanes(2)]
            grads = grad_mix[block, lanes(0)]
            sums = [0.0, 0.0, 0.0]
            for half in (left, ~left):
                some_queries = jnp.where(half, queries, 0.0).astype(bf16)
                some_keys = jnp.where(half, keys, 0.0).astype(bf16)
                some_grads = jnp.where(half, grads, 0.0).astype(bf16)
                scores = nt(keys, some_queries) * HEAD ** (-0.5)
                scores = jnp.where(live, scores, -jnp.inf)
                powers = jnp.exp(scores - jnp.max(scores, axis=0, keepdims=True))
                weights = powers * (1.0 / jnp.sum(powers, axis=0, keepdims=True))
                grad_weights = nt(values, some_grads)
                inner = jnp.sum(grad_weights * weights, axis=0, keepdims=True)
                grad_raw = (weights * (grad_weights - inner) * HEAD ** (-0.5)).astype(bf16)
                sums[0] += tn(grad_raw, some_keys)
                sums[1] += nn(grad_raw, some_queries)
                sums[2] += nn(weights.astype(bf16), some_grads)
            for part in range(3):
                grad_packed[block, lanes(part)] = sums[part].astype(bf16)

    pltpu.make_async_copy(own_qkv, qkv_ref, sems.at[0]).wait()

    @pl.loop(0, width // 256)
    def _(step):
        lanes = pl.ds(pl.multiple_of(step * 256, 256), 256)
        grad_ref[:, lanes] = nt(grad_packed[...], qkv_ref[lanes, :])

    def leave(step, total):
        block = pl.ds(pl.multiple_of(step * STEP, STEP), STEP)
        unit, scale = norm_rows(x_ref[block, :].astype(f32))
        upstream = grad_ref[block, :]
        grad_ref[block, :] = total_ref[block, :] + norm_rows_back(
            unit, scale, gain_a[...], upstream
        )
        return total + upstream * unit

    gain_total = lax.fori_loop(0, rows // STEP, leave, zero)
    gains_ref[0:1, :] = jnp.sum(gain_total, axis=0, keepdims=True)
    half_width = width // 2
    third = width // 3
    for out_refs, which_half in ((sends, 1 - which[1]), (keeps, which[1])):
        columns = pl.ds(pl.multiple_of(which_half * half_width, 128), half_width)
        left_rows = low_ref[:, columns].T
        right_rows = mix_ref[:, columns].T
        for part in range(3):
            out = out_refs[part]
            for step in range(3):
                source = slice(part * width + step * third, part * width + (step + 1) * third)
                out[:, step * third : (step + 1) * third] = nn(
                    left_rows, grad_packed[:, source]
                ).astype(bf16)
            out[:, width:] = nn(
                right_rows, total_low[:, part * third : (part + 1) * third]
            ).astype(bf16)


def whole_spec():
    return pl.BlockSpec(memory_space=pltpu.VMEM)


def attention_forward(which, x, weights, gain_a, gain_f, images, length):
    rows, width = x.shape
    far = pl.BlockSpec(memory_space=pl.ANY)
    near = whole_spec()
    return pl.pallas_call(
        functools.partial(forward_kernel, images, length),
        out_shape=(
            jax.ShapeDtypeStruct((rows, width), f32),
            jax.ShapeDtypeStruct((rows, 3 * width), bf16),
            jax.ShapeDtypeStruct((rows, width), bf16),
            jax.ShapeDtypeStruct((rows, width), bf16),
        ),
        in_specs=[pl.BlockSpec(memory_space=pltpu.SMEM), near, far, far, far, far, near, near],
        out_specs=(near, near, near, near),
        scratch_shapes=[
            pltpu.VMEM((width, 3 * width), bf16),
            pltpu.VMEM((width, width), bf16),
            pltpu.VMEM((rows, width), bf16),
            pltpu.SemaphoreType.DMA((2,)),
        ],
        compiler_params=pltpu.CompilerParams(vmem_limit_bytes=40 * 2**20),
        cost_estimate=pl.CostEstimate(
            flops=10 * rows * width * width, bytes_accessed=12 * 2**20, transcendentals=2**20
        ),
        name="attention_forward",
    )(which, x, *weights, gain_a, gain_f)


def attention_backward(
    which, x, mixed, base, upstream, packed, mix, weights, gain_a, gain_f, images, length
):
    rows, width = x.shape
    far = pl.BlockSpec(memory_space=pl.ANY)
    near = whole_spec()
    piece = jax.ShapeDtypeStruct((width // 2, width + width // 3), bf16)
    return pl.pallas_call(
        functools.partial(backward_kernel, images, length),
        out_shape=(
            jax.ShapeDtypeStruct((rows, width), f32),
            jax.ShapeDtypeStruct((8, width), f32),
        )
        + (piece,) * 6,
        in_specs=[pl.BlockSpec(memory_space=pltpu.SMEM)] + [near] * 6 + [far] * 4 + [near] * 2,
        out_specs=(near,) * 8,
        scratch_shapes=[
            pltpu.VMEM((width, 3 * width), bf16),
            pltpu.VMEM((width, width), bf16),
            pltpu.VMEM((rows, width), f32),
            pltpu.VMEM((rows, width), bf16),
            pltpu.VMEM((rows, width), bf16),
            pltpu.VMEM((rows, width), bf16),
            pltpu.VMEM((rows, 3 * width), bf16),
            pltpu.SemaphoreType.DMA((2,)),
        ],
        compiler_params=pltpu.CompilerParams(vmem_limit_bytes=52 * 2**20),
        cost_estimate=pl.CostEstimate(
            flops=20 * rows * width * width, bytes_accessed=24 * 2**20, transcendentals=2**20
        ),
        name="attention_backward",
    )(which, x, mixed, base, upstream, packed, mix, *weights, gain_a, gain_f)


def norm_stats(stream):
    mean_value = jnp.mean(stream, axis=-1, keepdims=True)
    centered = stream - mean_value
    variance = jnp.mean(centered * centered, axis=-1, keepdims=True)
    return centered * lax.rsqrt(variance + norm_epsilon)


def gelu_back(hidden, upstream):
    gelu_value, pullback = jax.vjp(jax.nn.gelu, hidden)
    return pullback(upstream)[0]


def slot_plan(ids, rank, capacity):
    before = rank[None, :] < rank[:, None]
    first, second = ids[:, 0], ids[:, 1]
    same_first = (first[:, None] == first[None, :]) & before
    same_second = (second[:, None] == second[None, :]) & before
    crossed = second[:, None] == first[None, :]
    place_first = jnp.sum(same_first.astype(jnp.int32), axis=1)
    place_second = jnp.sum(same_second.astype(jnp.int32) + crossed.astype(jnp.int32), axis=1)
    slot_first = jnp.where(place_first < capacity, first * capacity + place_first, -1)
    slot_second = jnp.where(place_second < capacity, second * capacity + place_second, -1)
    return (jnp.where(first >= 0, slot_first, -1), jnp.where(second >= 0, slot_second, -1))


def flipped(value, axis, bit):
    pairs = [(place, place ^ (1 << bit)) for place in range(lax.axis_size(axis))]
    return lax.ppermute(value, axis, pairs)


def wide_bits():
    count = lax.axis_size("wide")
    levels = count.bit_length() - 1
    assert 1 << levels == count
    third = max(1, levels // 3)
    bits = list(range(levels))
    groups = [bits[:third], bits[third : 2 * third], bits[2 * third :]]
    return [sum(groups[turn:] + groups[:turn], []) for turn in range(3)]


def wide_sum(value, order):
    place = lax.axis_index("wide")
    for bit in order:
        size = value.shape[0] // 2
        mine = (place >> bit) & 1
        sent = lax.dynamic_slice_in_dim(value, (1 - mine) * size, size)
        stays = lax.dynamic_slice_in_dim(value, mine * size, size)
        got = flipped(sent, "wide", bit)
        value = (stays.astype(f32) + got.astype(f32)).astype(bf16)
    for bit in reversed(order):
        got = flipped(value, "wide", bit)
        lower = ((place >> bit) & 1) == 0
        value = jnp.where(
            lower,
            jnp.concatenate([value, got], axis=0),
            jnp.concatenate([got, value], axis=0),
        )
    return value


def body(
    patches,
    out_cotangent,
    attn_gain,
    qkv_weight,
    proj_weight,
    ffn_gain,
    mlp_in,
    mlp_out,
    router_weight,
    expert_in,
    expert_out,
    expert_ids,
    priority,
):
    expert_count = lax.axis_size("wide")
    sections = lax.axis_size("section")
    section = lax.axis_index("section")
    own_expert = lax.axis_index("wide")
    is_first = section == 0
    images = patches.shape[0] // sections
    length, width = patches.shape[1:]
    pad = -(-length // STEP) * STEP
    rows = images * pad
    capacity = max(2, images * length // expert_count)
    slots = expert_count * capacity
    orders = wide_bits()

    def mine(whole):
        value = lax.dynamic_slice_in_dim(whole, section * images, images)
        return jnp.pad(value, ((0, 0), (0, pad - length), (0, 0))).reshape(rows, width)

    def swap(value):
        return flipped(value, "section", 0)

    def across(value):
        shape = (expert_count, capacity, value.shape[1])
        moved = lax.all_to_all(value.reshape(shape), "wide", split_axis=0, concat_axis=0, tiled=True)
        return moved.reshape(value.shape)

    other_qkv, other_proj = swap(qkv_weight[0]), swap(proj_weight[0])
    gains = jnp.concatenate([attn_gain, ffn_gain], axis=0)
    other_gains = swap(gains)
    gains_one = jnp.where(is_first, gains, other_gains)
    gains_two = jnp.where(is_first, other_gains, gains)
    weights = (qkv_weight[0], other_qkv, proj_weight[0], other_proj)
    which_one = jnp.stack([(section == 0).astype(jnp.int32), section])
    which_two = jnp.stack([(section == 1).astype(jnp.int32), section])

    ids = lax.dynamic_slice_in_dim(expert_ids, section * images, images)
    ids = jnp.pad(ids, ((0, 0), (0, pad - length), (0, 0)), constant_values=-1).reshape(rows, 2)
    rank = lax.dynamic_slice_in_dim(priority, section, 1).reshape(images, length)
    rank = jnp.pad(rank, ((0, 0), (0, pad - length))).reshape(rows)
    slot_first, slot_second = slot_plan(ids, rank, capacity)
    slot_range = jnp.arange(slots, dtype=jnp.int32)
    pick_first = slot_first[:, None] == slot_range[None, :]
    pick_second = slot_second[:, None] == slot_range[None, :]
    pick_any = (pick_first | pick_second).astype(bf16)
    kept_first = (slot_first >= 0).astype(f32)[:, None]
    kept_second = (slot_second >= 0).astype(f32)[:, None]
    rival = jnp.sum(
        jnp.where(pick_first, ids[:, 1:], 0) + jnp.where(pick_second, ids[:, :1], 0), axis=0
    )
    cotangent = mine(out_cotangent)
    packet = jnp.concatenate(
        [
            tn(pick_any, cotangent).astype(bf16),
            jnp.broadcast_to(rival.astype(bf16)[:, None], (slots, PAIR)),
        ],
        axis=1,
    )
    arrived_packet = across(packet)

    stream_one = mine(patches)
    mixed_one, packed_one, mix_one, normed_one = attention_forward(
        which_one, stream_one, weights, gains_one[:1], gains_one[1:], images, length
    )
    hidden_one = nn(normed_one, mlp_in)
    active_one = jax.nn.gelu(hidden_one).astype(bf16)
    first_low = (mixed_one + nn(active_one, mlp_out)).astype(bf16)

    mixed_two, packed_two, mix_two, normed_two = attention_forward(
        which_two, first_low, weights, gains_two[:1], gains_two[1:], images, length
    )
    arrived = across(tn(pick_any, normed_two).astype(bf16))
    weight_in, weight_out = expert_in[0], expert_out[0]
    hidden = nn(arrived, weight_in)
    active = jax.nn.gelu(hidden).astype(bf16)
    expert_range = jnp.arange(expert_count, dtype=jnp.int32)
    arrived_logits = nn(arrived, router_weight)
    arrived_rival = arrived_packet[:, width : width + 1].astype(jnp.int32)
    own_logit = jnp.sum(
        jnp.where(expert_range[None, :] == own_expert, arrived_logits, 0.0), axis=1, keepdims=True
    )
    rival_logit = jnp.sum(
        jnp.where(expert_range[None, :] == arrived_rival, arrived_logits, 0.0),
        axis=1,
        keepdims=True,
    )
    arrived_gate = jax.nn.sigmoid(own_logit - rival_logit)
    grad_rows = (arrived_gate * arrived_packet[:, :width].astype(f32)).astype(bf16)
    grad_active = nt(grad_rows, weight_out)
    grad_hidden = gelu_back(hidden, grad_active).astype(bf16)
    returned_grad = across(nt(grad_hidden, weight_in).astype(bf16))
    result = nn(active, weight_out).astype(bf16)
    returned = across(result)
    grad_expert_in = tn(arrived, grad_hidden).astype(bf16)
    grad_expert_out = tn(active, grad_rows).astype(bf16)
    expert_in_sum = grad_expert_in.astype(f32) + swap(grad_expert_in).astype(f32)
    expert_out_sum = grad_expert_out.astype(f32) + swap(grad_expert_out).astype(f32)

    logits = nn(normed_two, router_weight)
    one_hot = (ids[:, :, None] == expert_range[None, None, :]).astype(f32)
    chosen = jnp.sum(one_hot * logits[:, None, :], axis=-1)
    gates = jax.nn.softmax(chosen, axis=-1)
    picked_first = nn(pick_first.astype(bf16), returned)
    picked_second = nn(pick_second.astype(bf16), returned)
    second_low = (
        mixed_two
        + kept_first * gates[:, :1] * picked_first
        + kept_second * gates[:, 1:] * picked_second
    ).astype(bf16)
    upstream = cotangent.astype(f32)
    grad_gates = jnp.concatenate(
        [
            jnp.sum(upstream * picked_first, axis=-1, keepdims=True),
            jnp.sum(upstream * picked_second, axis=-1, keepdims=True),
        ],
        axis=1,
    )
    grad_chosen = gates * (grad_gates - jnp.sum(gates * grad_gates, axis=-1, keepdims=True))
    grad_logits = jnp.sum(one_hot * grad_chosen[:, :, None], axis=1).astype(bf16)
    grad_router = tn(grad_logits, normed_two)
    grad_normed_two = nn(pick_any, returned_grad) + nt(grad_logits, router_weight)
    grad_two, small_two, *pieces_two = attention_backward(
        which_two,
        first_low,
        mixed_two,
        cotangent,
        grad_normed_two,
        packed_two,
        mix_two,
        weights,
        gains_two[:1],
        gains_two[1:],
        images,
        length,
    )

    def pair_sum(sent, stays):
        return (stays.astype(f32) + swap(sent).astype(f32)).astype(bf16)

    def block_sums(pieces):
        return [
            wide_sum(pair_sum(sent, stays), order)
            for sent, stays, order in zip(pieces[:3], pieces[3:], orders)
        ]

    sums_two = block_sums(pieces_two)

    def half_products(left, right):
        size = left.shape[1] // 2

        def one(which):
            part = lax.dynamic_slice_in_dim(left, which * size, size, axis=1)
            return tn(part, right).astype(bf16)

        return pair_sum(one(1 - section), one(section))

    def thirds(value):
        size = value.shape[1] // 3
        return [value[:, part * size : (part + 1) * size] for part in range(3)]

    grad_first = grad_two.astype(bf16)
    grad_active_one = nt(grad_first, mlp_out)
    grad_hidden_one = gelu_back(hidden_one, grad_active_one).astype(bf16)
    grad_normed_one = nt(grad_hidden_one, mlp_in)
    mlp_in_half = half_products(normed_one, grad_hidden_one)
    mlp_out_half = half_products(active_one, grad_first)
    mlp_in_sums = [wide_sum(part, order) for part, order in zip(thirds(mlp_in_half), orders)]
    mlp_out_sums = [wide_sum(part, order) for part, order in zip(thirds(mlp_out_half), orders)]
    grad_one, small_one, *pieces_one = attention_backward(
        which_one,
        stream_one,
        mixed_one,
        grad_first,
        grad_normed_one,
        packed_one,
        mix_one,
        weights,
        gains_one[:1],
        gains_one[1:],
        images,
        length,
    )
    sums_one = block_sums(pieces_one)

    def joined(parts):
        lower, upper = [], []
        for half in parts:
            other = swap(half)
            lower.append(jnp.where(is_first, half, other))
            upper.append(jnp.where(is_first, other, half))
        return jnp.concatenate(
            [jnp.concatenate(lower, axis=1), jnp.concatenate(upper, axis=1)], axis=0
        ).astype(f32)

    qkv_parts, proj_parts = [], []
    for half_one, half_two in zip(sums_one, sums_two):
        own = jnp.where(is_first, half_one, half_two)
        other = swap(jnp.where(is_first, half_two, half_one))
        whole = jnp.concatenate(
            [jnp.where(is_first, own, other), jnp.where(is_first, other, own)], axis=0
        ).astype(f32)
        qkv_parts.append(whole[:, :width])
        proj_parts.append(whole[:, width:])

    def own_images(value_one, value_two):
        value_one, value_two = [
            value.reshape(images, pad, width)[:, :length] for value in (value_one, value_two)
        ]
        own = jnp.where(is_first, value_one, value_two)
        other = swap(jnp.where(is_first, value_two, value_one))
        return jnp.concatenate(
            [jnp.where(is_first, own, other), jnp.where(is_first, other, own)], axis=0
        )[None]

    small = jnp.concatenate([small_one, small_two, grad_router], axis=0)
    small = small + swap(small)
    for bit in sorted(orders[0]):
        small = small + flipped(small, "wide", bit)
    small_block = lax.dynamic_slice_in_dim(small, 8 * section, 8)
    return (
        own_images(first_low, second_low),
        own_images(grad_one, grad_first.astype(f32)),
        small_block[:1],
        jnp.concatenate(qkv_parts, axis=1)[None],
        jnp.concatenate(proj_parts, axis=1)[None],
        small_block[1:2],
        joined(mlp_in_sums),
        joined(mlp_out_sums),
        jnp.transpose(small[16:]),
        expert_in_sum[None],
        expert_out_sum[None],
    )


def solution(mesh):
    in_specs = (
        P("wide", None, None),
        P("wide", None, None),
        P("section", None),
        P("section", None, None),
        P("section", None, None),
        P("section", None),
        P(),
        P(),
        P(),
        P("wide", None, None),
        P("wide", None, None),
        P("wide", None, None),
        P("wide", None),
    )
    out_specs = (
        P("section", "wide", None, None),
        P("section", "wide", None, None),
        P("section", None),
        P("section", None, None),
        P("section", None, None),
        P("section", None),
        P(),
        P(),
        P(),
        P("wide", None, None),
        P("wide", None, None),
    )
    return jax.shard_map(body, mesh=mesh, in_specs=in_specs, out_specs=out_specs, check_vma=False)
```

```python
import functools

import jax
import jax.numpy as jnp
from jax import lax
from jax.experimental import pallas as pl
from jax.experimental.pallas import tpu as pltpu
from jax.sharding import PartitionSpec as P

H = 12
HEAD = 64
PAIR = 2 * HEAD
STEP = 16
norm_epsilon = 1e-06
bf16 = jnp.bfloat16
f32 = jnp.float32


def dot(left, right, dims):
    return lax.dot_general(left, right, (dims, ((), ())), preferred_element_type=f32)


def nn(left, right):
    return dot(left, right, ((1,), (0,)))


def nt(left, right):
    return dot(left, right, ((1,), (1,)))


def tn(left, right):
    return dot(left, right, ((0,), (0,)))


def norm_rows(value):
    mean_value = jnp.mean(value, axis=-1, keepdims=True)
    centered = value - mean_value
    scale = lax.rsqrt(jnp.mean(centered * centered, axis=-1, keepdims=True) + norm_epsilon)
    return (centered * scale, scale)


def norm_rows_back(unit, scale, gain, upstream):
    weighted = upstream * gain
    first = jnp.mean(weighted, axis=-1, keepdims=True)
    second = jnp.mean(weighted * unit, axis=-1, keepdims=True)
    return scale * (weighted - first - unit * second)


def fetch(take, own, other, target, sem):
    @pl.when(take == 1)
    def _():
        pltpu.make_async_copy(own, target, sem).start()

    @pl.when(take != 1)
    def _():
        pltpu.make_async_copy(other, target, sem).start()


def forward_kernel(
    images,
    length,
    which,
    x_ref,
    own_qkv,
    other_qkv,
    own_proj,
    other_proj,
    gain_a,
    gain_f,
    mixed_ref,
    packed_ref,
    mix_ref,
    normed_ref,
    qkv_ref,
    proj_ref,
    low_ref,
    sems,
):
    rows, width = x_ref.shape
    pad = rows // images
    fetch(which[0], own_qkv, other_qkv, qkv_ref, sems.at[0])
    fetch(which[0], own_proj, other_proj, proj_ref, sems.at[1])

    @pl.loop(0, rows // STEP)
    def _(step):
        block = pl.ds(pl.multiple_of(step * STEP, STEP), STEP)
        unit, scale = norm_rows(x_ref[block, :].astype(f32))
        low_ref[block, :] = (unit * gain_a[...]).astype(bf16)

    pltpu.make_async_copy(own_qkv, qkv_ref, sems.at[0]).wait()

    @pl.loop(0, 3 * width // 256)
    def _(step):
        lanes = pl.ds(pl.multiple_of(step * 256, 256), 256)
        packed_ref[:, lanes] = nn(low_ref[...], qkv_ref[:, lanes]).astype(bf16)

    left = lax.broadcasted_iota(jnp.int32, (pad, PAIR), 1) < HEAD
    live = lax.broadcasted_iota(jnp.int32, (pad, pad), 1) < length

    @pl.loop(0, width // PAIR)
    def _(pair):
        def lanes(part):
            return pl.ds(pl.multiple_of(part * width + pair * PAIR, PAIR), PAIR)

        for image in range(images):
            block = slice(image * pad, (image + 1) * pad)
            queries = packed_ref[block, lanes(0)]
            keys = packed_ref[block, lanes(1)]
            values = packed_ref[block, lanes(2)]
            outs = []
            for half in (left, ~left):
                scores = nt(jnp.where(half, queries, 0.0).astype(bf16), keys) * HEAD ** (-0.5)
                scores = jnp.where(live, scores, -jnp.inf)
                powers = jnp.exp(scores - jnp.max(scores, axis=1, keepdims=True))
                weights = powers * (1.0 / jnp.sum(powers, axis=1, keepdims=True))
                outs.append(nn(weights.astype(bf16), values))
            mix_ref[block, lanes(0)] = jnp.where(left, outs[0], outs[1]).astype(bf16)

    pltpu.make_async_copy(own_proj, proj_ref, sems.at[1]).wait()

    @pl.loop(0, width // 256)
    def _(step):
        lanes = pl.ds(pl.multiple_of(step * 256, 256), 256)
        mixed_ref[:, lanes] = x_ref[:, lanes].astype(f32) + nn(mix_ref[...], proj_ref[:, lanes])

    @pl.loop(0, rows // STEP)
    def _(step):
        block = pl.ds(pl.multiple_of(step * STEP, STEP), STEP)
        unit, scale = norm_rows(mixed_ref[block, :])
        normed_ref[block, :] = (unit * gain_f[...]).astype(bf16)


def backward_kernel(
    images,
    length,
    which,
    x_ref,
    mixed_ref,
    base_ref,
    upstream_ref,
    packed_ref,
    mix_ref,
    own_qkv,
    other_qkv,
    own_proj,
    other_proj,
    gain_a,
    gain_f,
    grad_ref,
    gains_ref,
    send_ref,
    keep_ref,
    qkv_ref,
    proj_ref,
    total_ref,
    total_low,
    low_ref,
    grad_mix,
    grad_packed,
    sems,
):
    rows, width = x_ref.shape
    pad = rows // images
    fetch(which[0], own_proj, other_proj, proj_ref, sems.at[1])
    fetch(which[0], own_qkv, other_qkv, qkv_ref, sems.at[0])
    zero = jnp.zeros((STEP, width), f32)

    def enter(step, total):
        block = pl.ds(pl.multiple_of(step * STEP, STEP), STEP)
        unit, scale = norm_rows(mixed_ref[block, :])
        upstream = upstream_ref[block, :]
        value = base_ref[block, :].astype(f32) + norm_rows_back(
            unit, scale, gain_f[...], upstream
        )
        total_ref[block, :] = value
        total_low[block, :] = value.astype(bf16)
        source_unit, source_scale = norm_rows(x_ref[block, :].astype(f32))
        low_ref[block, :] = (source_unit * gain_a[...]).astype(bf16)
        return total + upstream * unit

    gain_total = lax.fori_loop(0, rows // STEP, enter, zero)
    gains_ref[...] = jnp.zeros_like(gains_ref)
    gains_ref[1:2, :] = jnp.sum(gain_total, axis=0, keepdims=True)
    pltpu.make_async_copy(own_proj, proj_ref, sems.at[1]).wait()

    @pl.loop(0, width // 256)
    def _(step):
        lanes = pl.ds(pl.multiple_of(step * 256, 256), 256)
        grad_mix[:, lanes] = nt(total_low[...], proj_ref[lanes, :]).astype(bf16)

    left = lax.broadcasted_iota(jnp.int32, (pad, PAIR), 1) < HEAD
    live = lax.broadcasted_iota(jnp.int32, (pad, pad), 0) < length

    @pl.loop(0, width // PAIR)
    def _(pair):
        def lanes(part):
            return pl.ds(pl.multiple_of(part * width + pair * PAIR, PAIR), PAIR)

        for image in range(images):
            block = slice(image * pad, (image + 1) * pad)
            queries = packed_ref[block, lanes(0)]
            keys = packed_ref[block, lanes(1)]
            values = packed_ref[block, lanes(2)]
            grads = grad_mix[block, lanes(0)]
            sums = [0.0, 0.0, 0.0]
            for half in (left, ~left):
                some_queries = jnp.where(half, queries, 0.0).astype(bf16)
                some_keys = jnp.where(half, keys, 0.0).astype(bf16)
                some_grads = jnp.where(half, grads, 0.0).astype(bf16)
                scores = nt(keys, some_queries) * HEAD ** (-0.5)
                scores = jnp.where(live, scores, -jnp.inf)
                powers = jnp.exp(scores - jnp.max(scores, axis=0, keepdims=True))
                weights = powers * (1.0 / jnp.sum(powers, axis=0, keepdims=True))
                grad_weights = nt(values, some_grads)
                inner = jnp.sum(grad_weights * weights, axis=0, keepdims=True)
                grad_raw = (weights * (grad_weights - inner) * HEAD ** (-0.5)).astype(bf16)
                sums[0] += tn(grad_raw, some_keys)
                sums[1] += nn(grad_raw, some_queries)
                sums[2] += nn(weights.astype(bf16), some_grads)
            for part in range(3):
                grad_packed[block, lanes(part)] = sums[part].astype(bf16)

    pltpu.make_async_copy(own_qkv, qkv_ref, sems.at[0]).wait()

    @pl.loop(0, width // 256)
    def _(step):
        lanes = pl.ds(pl.multiple_of(step * 256, 256), 256)
        grad_ref[:, lanes] = nt(grad_packed[...], qkv_ref[lanes, :])

    def leave(step, total):
        block = pl.ds(pl.multiple_of(step * STEP, STEP), STEP)
        unit, scale = norm_rows(x_ref[block, :].astype(f32))
        upstream = grad_ref[block, :]
        grad_ref[block, :] = total_ref[block, :] + norm_rows_back(
            unit, scale, gain_a[...], upstream
        )
        return total + upstream * unit

    gain_total = lax.fori_loop(0, rows // STEP, leave, zero)
    gains_ref[0:1, :] = jnp.sum(gain_total, axis=0, keepdims=True)
    half_width = width // 2
    third = width // 3
    for out, which_half in ((send_ref, 1 - which[1]), (keep_ref, which[1])):
        columns = pl.ds(pl.multiple_of(which_half * half_width, 128), half_width)
        left_rows = low_ref[:, columns].T
        right_rows = mix_ref[:, columns].T
        for step in range(9):
            lanes = slice(step * third, (step + 1) * third)
            out[:, lanes] = nn(left_rows, grad_packed[:, lanes]).astype(bf16)
        for step in range(3):
            lanes = slice(step * third, (step + 1) * third)
            out[:, 3 * width + step * third : 3 * width + (step + 1) * third] = nn(
                right_rows, total_low[:, lanes]
            ).astype(bf16)


def whole_spec():
    return pl.BlockSpec(memory_space=pltpu.VMEM)


def attention_forward(which, x, weights, gain_a, gain_f, images, length):
    rows, width = x.shape
    far = pl.BlockSpec(memory_space=pl.ANY)
    near = whole_spec()
    return pl.pallas_call(
        functools.partial(forward_kernel, images, length),
        out_shape=(
            jax.ShapeDtypeStruct((rows, width), f32),
            jax.ShapeDtypeStruct((rows, 3 * width), bf16),
            jax.ShapeDtypeStruct((rows, width), bf16),
            jax.ShapeDtypeStruct((rows, width), bf16),
        ),
        in_specs=[pl.BlockSpec(memory_space=pltpu.SMEM), near, far, far, far, far, near, near],
        out_specs=(near, near, near, near),
        scratch_shapes=[
            pltpu.VMEM((width, 3 * width), bf16),
            pltpu.VMEM((width, width), bf16),
            pltpu.VMEM((rows, width), bf16),
            pltpu.SemaphoreType.DMA((2,)),
        ],
        compiler_params=pltpu.CompilerParams(vmem_limit_bytes=40 * 2**20),
        cost_estimate=pl.CostEstimate(
            flops=10 * rows * width * width, bytes_accessed=12 * 2**20, transcendentals=2**20
        ),
        name="attention_forward",
    )(which, x, *weights, gain_a, gain_f)


def attention_backward(
    which, x, mixed, base, upstream, packed, mix, weights, gain_a, gain_f, images, length
):
    rows, width = x.shape
    far = pl.BlockSpec(memory_space=pl.ANY)
    near = whole_spec()
    piece = jax.ShapeDtypeStruct((width // 2, 4 * width), bf16)
    return pl.pallas_call(
        functools.partial(backward_kernel, images, length),
        out_shape=(
            jax.ShapeDtypeStruct((rows, width), f32),
            jax.ShapeDtypeStruct((8, width), f32),
        )
        + (piece,) * 2,
        in_specs=[pl.BlockSpec(memory_space=pltpu.SMEM)] + [near] * 6 + [far] * 4 + [near] * 2,
        out_specs=(near,) * 4,
        scratch_shapes=[
            pltpu.VMEM((width, 3 * width), bf16),
            pltpu.VMEM((width, width), bf16),
            pltpu.VMEM((rows, width), f32),
            pltpu.VMEM((rows, width), bf16),
            pltpu.VMEM((rows, width), bf16),
            pltpu.VMEM((rows, width), bf16),
            pltpu.VMEM((rows, 3 * width), bf16),
            pltpu.SemaphoreType.DMA((2,)),
        ],
        compiler_params=pltpu.CompilerParams(vmem_limit_bytes=52 * 2**20),
        cost_estimate=pl.CostEstimate(
            flops=20 * rows * width * width, bytes_accessed=24 * 2**20, transcendentals=2**20
        ),
        name="attention_backward",
    )(which, x, mixed, base, upstream, packed, mix, *weights, gain_a, gain_f)


def join_kernel(section, mine_ref, other_ref, out_ref):
    @pl.when(pl.program_id(0) == section[0])
    def _():
        out_ref[...] = mine_ref[...].astype(f32)

    @pl.when(pl.program_id(0) != section[0])
    def _():
        out_ref[...] = other_ref[...].astype(f32)


def join_halves(section, mine, other):
    half, width = mine.shape
    steps = 3
    block = (half // steps, width)

    def mine_map(which, step, place):
        return (jnp.where(which == place[0], step, 0), 0)

    def other_map(which, step, place):
        return (jnp.where(which == place[0], 0, step), 0)

    return pl.pallas_call(
        join_kernel,
        grid_spec=pltpu.PrefetchScalarGridSpec(
            num_scalar_prefetch=1,
            grid=(2, steps),
            in_specs=[pl.BlockSpec(block, mine_map), pl.BlockSpec(block, other_map)],
            out_specs=pl.BlockSpec(block, lambda which, step, place: (which * steps + step, 0)),
        ),
        out_shape=jax.ShapeDtypeStruct((2 * half, width), f32),
        compiler_params=pltpu.CompilerParams(vmem_limit_bytes=24 * 2**20),
        cost_estimate=pl.CostEstimate(
            flops=0, bytes_accessed=12 * half * width, transcendentals=0
        ),
        name="join_halves",
    )(section, mine, other)


def block_kernel(section, one_ref, two_ref, from_one, from_two, qkv_out, proj_out):
    own = pl.program_id(0) == section[0]
    width = proj_out.shape[1]

    def emit(ref):
        qkv_out[...] = ref[:, : 3 * width].astype(f32)
        proj_out[...] = ref[:, 3 * width :].astype(f32)

    for place, mine_ref, other_ref in ((0, one_ref, from_one), (1, two_ref, from_two)):

        @pl.when(own & (section[0] == place))
        def _():
            emit(mine_ref)

        @pl.when(jnp.logical_not(own) & (section[0] == place))
        def _():
            emit(other_ref)


def own_block(section, one, two, from_one, from_two):
    half, joint = one.shape
    width = joint // 4
    steps = 3
    block = (half // steps, joint)

    def source(place, own):
        def index(which, step, section):
            wanted = (section[0] == place) & ((which == section[0]) == own)
            return (jnp.where(wanted, step, 0), 0)

        return pl.BlockSpec(block, index)

    def out_map(which, step, section):
        return (which * steps + step, 0)

    return pl.pallas_call(
        block_kernel,
        grid_spec=pltpu.PrefetchScalarGridSpec(
            num_scalar_prefetch=1,
            grid=(2, steps),
            in_specs=[source(0, True), source(1, True), source(0, False), source(1, False)],
            out_specs=(
                pl.BlockSpec((half // steps, 3 * width), out_map),
                pl.BlockSpec((half // steps, width), out_map),
            ),
        ),
        out_shape=(
            jax.ShapeDtypeStruct((2 * half, 3 * width), f32),
            jax.ShapeDtypeStruct((2 * half, width), f32),
        ),
        compiler_params=pltpu.CompilerParams(vmem_limit_bytes=24 * 2**20),
        cost_estimate=pl.CostEstimate(
            flops=0, bytes_accessed=12 * half * joint, transcendentals=0
        ),
        name="own_block",
    )(section, one, two, from_one, from_two)


def norm_stats(stream):
    mean_value = jnp.mean(stream, axis=-1, keepdims=True)
    centered = stream - mean_value
    variance = jnp.mean(centered * centered, axis=-1, keepdims=True)
    return centered * lax.rsqrt(variance + norm_epsilon)


def gelu_back(hidden, upstream):
    gelu_value, pullback = jax.vjp(jax.nn.gelu, hidden)
    return pullback(upstream)[0]


def slot_plan(ids, rank, capacity):
    before = rank[None, :] < rank[:, None]
    first, second = ids[:, 0], ids[:, 1]
    same_first = (first[:, None] == first[None, :]) & before
    same_second = (second[:, None] == second[None, :]) & before
    crossed = second[:, None] == first[None, :]
    place_first = jnp.sum(same_first.astype(jnp.int32), axis=1)
    place_second = jnp.sum(same_second.astype(jnp.int32) + crossed.astype(jnp.int32), axis=1)
    slot_first = jnp.where(place_first < capacity, first * capacity + place_first, -1)
    slot_second = jnp.where(place_second < capacity, second * capacity + place_second, -1)
    return (jnp.where(first >= 0, slot_first, -1), jnp.where(second >= 0, slot_second, -1))


def flipped(value, axis, bit):
    pairs = [(place, place ^ (1 << bit)) for place in range(lax.axis_size(axis))]
    return lax.ppermute(value, axis, pairs)


def wide_sum(value, turn):
    count = lax.axis_size("wide")
    order = [(place + turn) % count for place in range(count)]
    return lax.psum(value, "wide", axis_index_groups=[order])


def body(
    patches,
    out_cotangent,
    attn_gain,
    qkv_weight,
    proj_weight,
    ffn_gain,
    mlp_in,
    mlp_out,
    router_weight,
    expert_in,
    expert_out,
    expert_ids,
    priority,
):
    expert_count = lax.axis_size("wide")
    sections = lax.axis_size("section")
    section = lax.axis_index("section")
    own_expert = lax.axis_index("wide")
    is_first = section == 0
    images = patches.shape[0] // sections
    length, width = patches.shape[1:]
    pad = -(-length // STEP) * STEP
    rows = images * pad
    capacity = max(2, images * length // expert_count)
    slots = expert_count * capacity
    levels = expert_count.bit_length() - 1
    assert 1 << levels == expert_count
    place = section[None]

    def mine(whole):
        value = lax.dynamic_slice_in_dim(whole, section * images, images)
        return jnp.pad(value, ((0, 0), (0, pad - length), (0, 0))).reshape(rows, width)

    def swap(value):
        return flipped(value, "section", 0)

    def across(value):
        shape = (expert_count, capacity, value.shape[1])
        moved = lax.all_to_all(value.reshape(shape), "wide", split_axis=0, concat_axis=0, tiled=True)
        return moved.reshape(value.shape)

    other_qkv, other_proj = swap(qkv_weight[0]), swap(proj_weight[0])
    gains = jnp.concatenate([attn_gain, ffn_gain], axis=0)
    other_gains = swap(gains)
    gains_one = jnp.where(is_first, gains, other_gains)
    gains_two = jnp.where(is_first, other_gains, gains)
    weights = (qkv_weight[0], other_qkv, proj_weight[0], other_proj)
    which_one = jnp.stack([(section == 0).astype(jnp.int32), section])
    which_two = jnp.stack([(section == 1).astype(jnp.int32), section])

    ids = lax.dynamic_slice_in_dim(expert_ids, section * images, images)
    ids = jnp.pad(ids, ((0, 0), (0, pad - length), (0, 0)), constant_values=-1).reshape(rows, 2)
    rank = lax.dynamic_slice_in_dim(priority, section, 1).reshape(images, length)
    rank = jnp.pad(rank, ((0, 0), (0, pad - length))).reshape(rows)
    slot_first, slot_second = slot_plan(ids, rank, capacity)
    slot_range = jnp.arange(slots, dtype=jnp.int32)
    pick_first = slot_first[:, None] == slot_range[None, :]
    pick_second = slot_second[:, None] == slot_range[None, :]
    pick_any = (pick_first | pick_second).astype(bf16)
    kept_first = (slot_first >= 0).astype(f32)[:, None]
    kept_second = (slot_second >= 0).astype(f32)[:, None]
    rival = jnp.sum(
        jnp.where(pick_first, ids[:, 1:], 0) + jnp.where(pick_second, ids[:, :1], 0), axis=0
    )
    cotangent = mine(out_cotangent)
    packet = jnp.concatenate(
        [
            tn(pick_any, cotangent).astype(bf16),
            jnp.broadcast_to(rival.astype(bf16)[:, None], (slots, PAIR)),
        ],
        axis=1,
    )

    stream_one = mine(patches)
    mixed_one, packed_one, mix_one, normed_one = attention_forward(
        which_one, stream_one, weights, gains_one[:1], gains_one[1:], images, length
    )
    normed_one, packet = lax.optimization_barrier((normed_one, packet))
    arrived_packet = across(packet)
    hidden_one = nn(normed_one, mlp_in)
    active_one = jax.nn.gelu(hidden_one).astype(bf16)
    first_low = (mixed_one + nn(active_one, mlp_out)).astype(bf16)

    mixed_two, packed_two, mix_two, normed_two = attention_forward(
        which_two, first_low, weights, gains_two[:1], gains_two[1:], images, length
    )
    arrived = across(tn(pick_any, normed_two).astype(bf16))
    weight_in, weight_out = expert_in[0], expert_out[0]
    hidden = nn(arrived, weight_in)
    active = jax.nn.gelu(hidden).astype(bf16)
    expert_range = jnp.arange(expert_count, dtype=jnp.int32)
    arrived_logits = nn(arrived, router_weight)
    arrived_rival = arrived_packet[:, width : width + 1].astype(jnp.int32)
    own_logit = jnp.sum(
        jnp.where(expert_range[None, :] == own_expert, arrived_logits, 0.0), axis=1, keepdims=True
    )
    rival_logit = jnp.sum(
        jnp.where(expert_range[None, :] == arrived_rival, arrived_logits, 0.0),
        axis=1,
        keepdims=True,
    )
    arrived_gate = jax.nn.sigmoid(own_logit - rival_logit)
    grad_rows = (arrived_gate * arrived_packet[:, :width].astype(f32)).astype(bf16)
    grad_active = nt(grad_rows, weight_out)
    grad_hidden = gelu_back(hidden, grad_active).astype(bf16)
    result = nn(active, weight_out).astype(bf16)
    slot_grad = jnp.sum(
        arrived_packet[:, :width].astype(f32) * result.astype(f32), axis=1, keepdims=True
    )
    parts = []
    for _ in range(3):
        part = lax.reduce_precision(slot_grad, 8, 7)
        parts.append(part.astype(bf16))
        slot_grad = slot_grad - part
    parts.append(jnp.zeros((slots, PAIR - len(parts)), bf16))
    back = across(jnp.concatenate([nt(grad_hidden, weight_in).astype(bf16)] + parts, axis=1))
    result, back = lax.optimization_barrier((result, back))
    returned = across(result)
    grad_expert_in = tn(arrived, grad_hidden).astype(bf16)
    grad_expert_out = tn(active, grad_rows).astype(bf16)
    expert_in_sum = grad_expert_in.astype(f32) + swap(grad_expert_in).astype(f32)
    expert_out_sum = grad_expert_out.astype(f32) + swap(grad_expert_out).astype(f32)

    logits = nn(normed_two, router_weight)
    one_hot = (ids[:, :, None] == expert_range[None, None, :]).astype(f32)
    chosen = jnp.sum(one_hot * logits[:, None, :], axis=-1)
    gates = jax.nn.softmax(chosen, axis=-1)
    low_first, low_second = pick_first.astype(bf16), pick_second.astype(bf16)
    grad_gates = jnp.concatenate(
        [
            jnp.sum(nn(low, back[:, width:]), axis=-1, keepdims=True)
            for low in (low_first, low_second)
        ],
        axis=1,
    )
    grad_chosen = gates * (grad_gates - jnp.sum(gates * grad_gates, axis=-1, keepdims=True))
    grad_logits = jnp.sum(one_hot * grad_chosen[:, :, None], axis=1).astype(bf16)
    grad_router = tn(grad_logits, normed_two)
    grad_normed_two = nn(pick_any, back[:, :width]) + nt(grad_logits, router_weight)
    second_low = (
        mixed_two
        + kept_first * gates[:, :1] * nn(low_first, returned)
        + kept_second * gates[:, 1:] * nn(low_second, returned)
    ).astype(bf16)
    grad_two, small_two, send_two, keep_two = attention_backward(
        which_two,
        first_low,
        mixed_two,
        cotangent,
        grad_normed_two,
        packed_two,
        mix_two,
        weights,
        gains_two[:1],
        gains_two[1:],
        images,
        length,
    )

    def pair_sum(sent, stays):
        return (stays.astype(f32) + swap(sent).astype(f32)).astype(bf16)

    half_two = pair_sum(send_two, keep_two)

    def half_products(left, right):
        size = left.shape[1] // 2

        def one(which):
            part = lax.dynamic_slice_in_dim(left, which * size, size, axis=1)
            return tn(part, right).astype(bf16)

        return pair_sum(one(1 - section), one(section))

    grad_first = grad_two.astype(bf16)
    mlp_out_half = half_products(active_one, grad_first)
    grad_active_one = nt(grad_first, mlp_out)
    grad_hidden_one = gelu_back(hidden_one, grad_active_one).astype(bf16)
    grad_hidden_one, half_two, mlp_out_half = lax.optimization_barrier(
        (grad_hidden_one, half_two, mlp_out_half)
    )
    sum_two = wide_sum(half_two, 0)
    mlp_out_sum = wide_sum(mlp_out_half, 1)
    mlp_in_half = half_products(normed_one, grad_hidden_one)
    grad_normed_one = nt(grad_hidden_one, mlp_in)
    grad_normed_one, mlp_in_half = lax.optimization_barrier((grad_normed_one, mlp_in_half))
    mlp_in_sum = wide_sum(mlp_in_half, 2)
    grad_one, small_one, send_one, keep_one = attention_backward(
        which_one,
        stream_one,
        mixed_one,
        grad_first,
        grad_normed_one,
        packed_one,
        mix_one,
        weights,
        gains_one[:1],
        gains_one[1:],
        images,
        length,
    )
    sum_one = wide_sum(pair_sum(send_one, keep_one), 3)

    def joined(half):
        return join_halves(place, half, swap(half))

    from_two = lax.ppermute(sum_two, "section", [(0, 1)])
    from_one = lax.ppermute(sum_one, "section", [(1, 0)])
    qkv_grad, proj_grad = own_block(place, sum_one, sum_two, from_one, from_two)

    def own_images(value_one, value_two):
        value_one, value_two = [
            value.reshape(images, pad, width)[:, :length] for value in (value_one, value_two)
        ]
        own = jnp.where(is_first, value_one, value_two)
        other = swap(jnp.where(is_first, value_two, value_one))
        return jnp.concatenate(
            [jnp.where(is_first, own, other), jnp.where(is_first, other, own)], axis=0
        )[None]

    small = jnp.concatenate([small_one, small_two, grad_router], axis=0)
    small = small + swap(small)
    for bit in range(levels):
        small = small + flipped(small, "wide", bit)
    small_block = lax.dynamic_slice_in_dim(small, 8 * section, 8)
    return (
        own_images(first_low, second_low),
        own_images(grad_one, grad_first.astype(f32)),
        small_block[:1],
        qkv_grad[None],
        proj_grad[None],
        small_block[1:2],
        joined(mlp_in_sum),
        joined(mlp_out_sum),
        jnp.transpose(small[16:]),
        expert_in_sum[None],
        expert_out_sum[None],
    )


def solution(mesh):
    in_specs = (
        P("wide", None, None),
        P("wide", None, None),
        P("section", None),
        P("section", None, None),
        P("section", None, None),
        P("section", None),
        P(),
        P(),
        P(),
        P("wide", None, None),
        P("wide", None, None),
        P("wide", None, None),
        P("wide", None),
    )
    out_specs = (
        P("section", "wide", None, None),
        P("section", "wide", None, None),
        P("section", None),
        P("section", None, None),
        P("section", None, None),
        P("section", None),
        P(),
        P(),
        P(),
        P("wide", None, None),
        P("wide", None, None),
    )
    return jax.shard_map(body, mesh=mesh, in_specs=in_specs, out_specs=out_specs, check_vma=False)
```

```python
import functools

import jax
import jax.numpy as jnp
from jax import lax
from jax.experimental import pallas as pl
from jax.experimental.pallas import tpu as pltpu
from jax.sharding import PartitionSpec as P

H = 12
HEAD = 64
PAIR = 2 * HEAD
STEP = 16
norm_epsilon = 1e-06
bf16 = jnp.bfloat16
f32 = jnp.float32


def dot(left, right, dims):
    return lax.dot_general(left, right, (dims, ((), ())), preferred_element_type=f32)


def nn(left, right):
    return dot(left, right, ((1,), (0,)))


def nt(left, right):
    return dot(left, right, ((1,), (1,)))


def tn(left, right):
    return dot(left, right, ((0,), (0,)))


def norm_rows(value):
    mean_value = jnp.mean(value, axis=-1, keepdims=True)
    centered = value - mean_value
    scale = lax.rsqrt(jnp.mean(centered * centered, axis=-1, keepdims=True) + norm_epsilon)
    return (centered * scale, scale)


def norm_rows_back(unit, scale, gain, upstream):
    weighted = upstream * gain
    first = jnp.mean(weighted, axis=-1, keepdims=True)
    second = jnp.mean(weighted * unit, axis=-1, keepdims=True)
    return scale * (weighted - first - unit * second)


def fetch(take, own, other, target, sem):
    @pl.when(take == 1)
    def _():
        pltpu.make_async_copy(own, target, sem).start()

    @pl.when(take != 1)
    def _():
        pltpu.make_async_copy(other, target, sem).start()


def forward_kernel(
    images,
    length,
    which,
    x_ref,
    own_qkv,
    other_qkv,
    own_proj,
    other_proj,
    gain_a,
    gain_f,
    mixed_ref,
    packed_ref,
    mix_ref,
    normed_ref,
    qkv_ref,
    proj_ref,
    low_ref,
    sems,
):
    rows, width = x_ref.shape
    pad = rows // images
    fetch(which[0], own_qkv, other_qkv, qkv_ref, sems.at[0])
    fetch(which[0], own_proj, other_proj, proj_ref, sems.at[1])

    @pl.loop(0, rows // STEP)
    def _(step):
        block = pl.ds(pl.multiple_of(step * STEP, STEP), STEP)
        unit, scale = norm_rows(x_ref[block, :].astype(f32))
        low_ref[block, :] = (unit * gain_a[...]).astype(bf16)

    pltpu.make_async_copy(own_qkv, qkv_ref, sems.at[0]).wait()

    @pl.loop(0, 3 * width // 256)
    def _(step):
        lanes = pl.ds(pl.multiple_of(step * 256, 256), 256)
        packed_ref[:, lanes] = nn(low_ref[...], qkv_ref[:, lanes]).astype(bf16)

    left = lax.broadcasted_iota(jnp.int32, (pad, PAIR), 1) < HEAD
    live = lax.broadcasted_iota(jnp.int32, (pad, pad), 1) < length

    @pl.loop(0, width // PAIR)
    def _(pair):
        def lanes(part):
            return pl.ds(pl.multiple_of(part * width + pair * PAIR, PAIR), PAIR)

        for image in range(images):
            block = slice(image * pad, (image + 1) * pad)
            queries = packed_ref[block, lanes(0)]
            keys = packed_ref[block, lanes(1)]
            values = packed_ref[block, lanes(2)]
            outs = []
            for half in (left, ~left):
                scores = nt(jnp.where(half, queries, 0.0).astype(bf16), keys) * HEAD ** (-0.5)
                scores = jnp.where(live, scores, -jnp.inf)
                powers = jnp.exp(scores - jnp.max(scores, axis=1, keepdims=True))
                weights = powers * (1.0 / jnp.sum(powers, axis=1, keepdims=True))
                outs.append(nn(weights.astype(bf16), values))
            mix_ref[block, lanes(0)] = jnp.where(left, outs[0], outs[1]).astype(bf16)

    pltpu.make_async_copy(own_proj, proj_ref, sems.at[1]).wait()

    @pl.loop(0, width // 256)
    def _(step):
        lanes = pl.ds(pl.multiple_of(step * 256, 256), 256)
        mixed_ref[:, lanes] = x_ref[:, lanes].astype(f32) + nn(mix_ref[...], proj_ref[:, lanes])

    @pl.loop(0, rows // STEP)
    def _(step):
        block = pl.ds(pl.multiple_of(step * STEP, STEP), STEP)
        unit, scale = norm_rows(mixed_ref[block, :])
        normed_ref[block, :] = (unit * gain_f[...]).astype(bf16)


def backward_kernel(
    images,
    length,
    which,
    x_ref,
    mixed_ref,
    base_ref,
    upstream_ref,
    packed_ref,
    mix_ref,
    own_qkv,
    other_qkv,
    own_proj,
    other_proj,
    gain_a,
    gain_f,
    grad_ref,
    grad_low,
    gains_ref,
    grad_packed,
    total_low,
    low_ref,
    qkv_ref,
    proj_ref,
    total_ref,
    grad_mix,
    sems,
):
    rows, width = x_ref.shape
    pad = rows // images
    fetch(which[0], own_proj, other_proj, proj_ref, sems.at[1])
    fetch(which[0], own_qkv, other_qkv, qkv_ref, sems.at[0])
    zero = jnp.zeros((STEP, width), f32)

    def enter(step, total):
        block = pl.ds(pl.multiple_of(step * STEP, STEP), STEP)
        unit, scale = norm_rows(mixed_ref[block, :])
        upstream = upstream_ref[block, :]
        value = base_ref[block, :].astype(f32) + norm_rows_back(
            unit, scale, gain_f[...], upstream
        )
        total_ref[block, :] = value
        total_low[block, :] = value.astype(bf16)
        source_unit, source_scale = norm_rows(x_ref[block, :].astype(f32))
        low_ref[block, :] = (source_unit * gain_a[...]).astype(bf16)
        return total + upstream * unit

    gain_total = lax.fori_loop(0, rows // STEP, enter, zero)
    gains_ref[...] = jnp.zeros_like(gains_ref)
    gains_ref[1:2, :] = jnp.sum(gain_total, axis=0, keepdims=True)
    pltpu.make_async_copy(own_proj, proj_ref, sems.at[1]).wait()

    @pl.loop(0, width // 256)
    def _(step):
        lanes = pl.ds(pl.multiple_of(step * 256, 256), 256)
        grad_mix[:, lanes] = nt(total_low[...], proj_ref[lanes, :]).astype(bf16)

    left = lax.broadcasted_iota(jnp.int32, (pad, PAIR), 1) < HEAD
    live = lax.broadcasted_iota(jnp.int32, (pad, pad), 0) < length

    @pl.loop(0, width // PAIR)
    def _(pair):
        def lanes(part):
            return pl.ds(pl.multiple_of(part * width + pair * PAIR, PAIR), PAIR)

        for image in range(images):
            block = slice(image * pad, (image + 1) * pad)
            queries = packed_ref[block, lanes(0)]
            keys = packed_ref[block, lanes(1)]
            values = packed_ref[block, lanes(2)]
            grads = grad_mix[block, lanes(0)]
            sums = [0.0, 0.0, 0.0]
            for half in (left, ~left):
                some_queries = jnp.where(half, queries, 0.0).astype(bf16)
                some_keys = jnp.where(half, keys, 0.0).astype(bf16)
                some_grads = jnp.where(half, grads, 0.0).astype(bf16)
                scores = nt(keys, some_queries) * HEAD ** (-0.5)
                scores = jnp.where(live, scores, -jnp.inf)
                powers = jnp.exp(scores - jnp.max(scores, axis=0, keepdims=True))
                weights = powers * (1.0 / jnp.sum(powers, axis=0, keepdims=True))
                grad_weights = nt(values, some_grads)
                inner = jnp.sum(grad_weights * weights, axis=0, keepdims=True)
                grad_raw = (weights * (grad_weights - inner) * HEAD ** (-0.5)).astype(bf16)
                sums[0] += tn(grad_raw, some_keys)
                sums[1] += nn(grad_raw, some_queries)
                sums[2] += nn(weights.astype(bf16), some_grads)
            for part in range(3):
                grad_packed[block, lanes(part)] = sums[part].astype(bf16)

    pltpu.make_async_copy(own_qkv, qkv_ref, sems.at[0]).wait()

    @pl.loop(0, width // 256)
    def _(step):
        lanes = pl.ds(pl.multiple_of(step * 256, 256), 256)
        grad_ref[:, lanes] = nt(grad_packed[...], qkv_ref[lanes, :])

    def leave(step, total):
        block = pl.ds(pl.multiple_of(step * STEP, STEP), STEP)
        unit, scale = norm_rows(x_ref[block, :].astype(f32))
        upstream = grad_ref[block, :]
        value = total_ref[block, :] + norm_rows_back(unit, scale, gain_a[...], upstream)
        grad_ref[block, :] = value
        grad_low[block, :] = value.astype(bf16)
        return total + upstream * unit

    gain_total = lax.fori_loop(0, rows // STEP, leave, zero)
    gains_ref[0:1, :] = jnp.sum(gain_total, axis=0, keepdims=True)


def product_kernel(section, low_ref, mix_ref, grad_packed, total_low, *outs):
    width = low_ref.shape[1]
    half_width = width // 2
    third = width // 3
    for which_half, one, two in ((1 - section[0], *outs[:2]), (section[0], *outs[2:])):
        columns = pl.ds(pl.multiple_of(which_half * half_width, 128), half_width)
        left_rows = low_ref[:, columns].T
        right_rows = mix_ref[:, columns].T
        for step in range(12):
            if step < 9:
                value = nn(left_rows, grad_packed[:, step * third : (step + 1) * third])
            else:
                value = nn(right_rows, total_low[:, (step - 9) * third : (step - 8) * third])
            out, place = (one, step) if step < 6 else (two, step - 6)
            out[:, place * third : (place + 1) * third] = value.astype(bf16)


def attention_products(section, low, mix, grad_packed, total_low, after=()):
    width = low.shape[1]
    rows = low.shape[0]
    near = whole_spec()
    piece = jax.ShapeDtypeStruct((width // 2, 2 * width), bf16)

    def kernel(section_ref, *refs):
        product_kernel(section_ref, *refs[:4], *refs[4 + len(after) :])

    return pl.pallas_call(
        kernel,
        out_shape=(piece,) * 4,
        in_specs=[pl.BlockSpec(memory_space=pltpu.SMEM)]
        + [near] * 4
        + [pl.BlockSpec(memory_space=pl.ANY)] * len(after),
        out_specs=(near,) * 4,
        compiler_params=pltpu.CompilerParams(vmem_limit_bytes=32 * 2**20),
        cost_estimate=pl.CostEstimate(
            flops=8 * rows * width * width, bytes_accessed=12 * 2**20, transcendentals=0
        ),
        name="attention_products",
    )(section, low, mix, grad_packed, total_low, *after)


def whole_spec():
    return pl.BlockSpec(memory_space=pltpu.VMEM)


def attention_forward(which, x, weights, gain_a, gain_f, images, length):
    rows, width = x.shape
    far = pl.BlockSpec(memory_space=pl.ANY)
    near = whole_spec()
    return pl.pallas_call(
        functools.partial(forward_kernel, images, length),
        out_shape=(
            jax.ShapeDtypeStruct((rows, width), f32),
            jax.ShapeDtypeStruct((rows, 3 * width), bf16),
            jax.ShapeDtypeStruct((rows, width), bf16),
            jax.ShapeDtypeStruct((rows, width), bf16),
        ),
        in_specs=[pl.BlockSpec(memory_space=pltpu.SMEM), near, far, far, far, far, near, near],
        out_specs=(near, near, near, near),
        scratch_shapes=[
            pltpu.VMEM((width, 3 * width), bf16),
            pltpu.VMEM((width, width), bf16),
            pltpu.VMEM((rows, width), bf16),
            pltpu.SemaphoreType.DMA((2,)),
        ],
        compiler_params=pltpu.CompilerParams(vmem_limit_bytes=40 * 2**20),
        cost_estimate=pl.CostEstimate(
            flops=10 * rows * width * width, bytes_accessed=12 * 2**20, transcendentals=2**20
        ),
        name="attention_forward",
    )(which, x, *weights, gain_a, gain_f)


def attention_backward(
    which, x, mixed, base, upstream, packed, mix, weights, gain_a, gain_f, images, length, after=()
):
    rows, width = x.shape
    far = pl.BlockSpec(memory_space=pl.ANY)
    near = whole_spec()

    def kernel(*refs):
        backward_kernel(images, length, *refs[:13], *refs[13 + len(after) :])

    return pl.pallas_call(
        kernel,
        out_shape=(
            jax.ShapeDtypeStruct((rows, width), f32),
            jax.ShapeDtypeStruct((rows, width), bf16),
            jax.ShapeDtypeStruct((8, width), f32),
            jax.ShapeDtypeStruct((rows, 3 * width), bf16),
            jax.ShapeDtypeStruct((rows, width), bf16),
            jax.ShapeDtypeStruct((rows, width), bf16),
        ),
        in_specs=[pl.BlockSpec(memory_space=pltpu.SMEM)]
        + [near] * 6
        + [far] * 4
        + [near] * 2
        + [far] * len(after),
        out_specs=(near,) * 6,
        scratch_shapes=[
            pltpu.VMEM((width, 3 * width), bf16),
            pltpu.VMEM((width, width), bf16),
            pltpu.VMEM((rows, width), f32),
            pltpu.VMEM((rows, width), bf16),
            pltpu.SemaphoreType.DMA((2,)),
        ],
        compiler_params=pltpu.CompilerParams(vmem_limit_bytes=40 * 2**20),
        cost_estimate=pl.CostEstimate(
            flops=20 * rows * width * width, bytes_accessed=24 * 2**20, transcendentals=2**20
        ),
        name="attention_backward",
    )(which, x, mixed, base, upstream, packed, mix, *weights, gain_a, gain_f, *after)


def gelu_pair(hidden):
    cubic = 0.7978845608028654
    square = hidden * hidden
    curve = jnp.tanh(cubic * (hidden + 0.044715 * (square * hidden)))
    left = 0.5 * (1.0 + curve)
    slope = left + 0.5 * hidden * (1.0 - curve * curve) * (
        cubic * (1.0 + 3.0 * 0.044715 * square)
    )
    return (hidden * left, slope)


def mlp_kernel(
    section,
    x_ref,
    up_ref,
    in_ref,
    out_ref,
    grad_ref,
    in_send,
    in_keep,
    out_send,
    out_keep,
    x_turned,
):
    half = x_ref.shape[1] // 2

    @pl.when(pl.program_id(0) == 0)
    def _():
        x_turned[...] = x_ref[...].T
        grad_ref[...] = jnp.zeros_like(grad_ref)

    active, slope = gelu_pair(nn(x_ref[...], in_ref[...]))
    active = active.astype(bf16)
    grad_hidden = (nt(up_ref[...], out_ref[...]) * slope).astype(bf16)
    grad_ref[...] += nt(grad_hidden, in_ref[...])
    turned = active.T
    for which, first, second in (
        (1 - section[0], in_send, out_send),
        (section[0], in_keep, out_keep),
    ):
        block = pl.ds(pl.multiple_of(which * half, 128), half)
        first[...] = nn(x_turned[block, :], grad_hidden).astype(bf16)
        second[...] = nn(turned, up_ref[:, block]).astype(bf16)


def mlp_backward(section, x, up, weight_in, weight_out, after):
    rows, width = x.shape
    hidden = weight_in.shape[1]
    step = 512
    half = width // 2
    fixed = pl.BlockSpec((rows, width), lambda index, place: (0, 0))
    across = pl.BlockSpec((half, step), lambda index, place: (0, index))
    down = pl.BlockSpec((step, half), lambda index, place: (index, 0))

    def kernel(*refs):
        mlp_kernel(*refs[:5], *refs[5 + len(after) :])

    return pl.pallas_call(
        kernel,
        grid_spec=pltpu.PrefetchScalarGridSpec(
            num_scalar_prefetch=1,
            grid=(hidden // step,),
            in_specs=[
                fixed,
                fixed,
                pl.BlockSpec((width, step), lambda index, place: (0, index)),
                pl.BlockSpec((step, width), lambda index, place: (index, 0)),
            ]
            + [pl.BlockSpec(memory_space=pl.ANY)] * len(after),
            out_specs=(fixed, across, across, down, down),
            scratch_shapes=[pltpu.VMEM((width, rows), bf16)],
        ),
        out_shape=(
            jax.ShapeDtypeStruct((rows, width), f32),
            jax.ShapeDtypeStruct((half, hidden), bf16),
            jax.ShapeDtypeStruct((half, hidden), bf16),
            jax.ShapeDtypeStruct((hidden, half), bf16),
            jax.ShapeDtypeStruct((hidden, half), bf16),
        ),
        compiler_params=pltpu.CompilerParams(vmem_limit_bytes=40 * 2**20),
        cost_estimate=pl.CostEstimate(
            flops=10 * rows * width * hidden,
            bytes_accessed=24 * 2**20,
            transcendentals=rows * hidden,
        ),
        name="mlp_backward",
    )(section, x, up, weight_in, weight_out, *after)


def expert_kernel(
    own,
    x_ref,
    packet_ref,
    router_ref,
    in_ref,
    out_ref,
    back_ref,
    result_ref,
    in_grad,
    out_grad,
    x_turned,
    up_ref,
    total_ref,
    grad_ref,
):
    slots, width = x_ref.shape

    @pl.when(pl.program_id(0) == 0)
    def _():
        x_turned[...] = x_ref[...].T
        grad_ref[...] = jnp.zeros_like(grad_ref)
        total_ref[...] = jnp.zeros_like(total_ref)
        logits = nn(x_ref[...], router_ref[...])
        experts = lax.broadcasted_iota(jnp.int32, logits.shape, 1)
        rival = packet_ref[:, width : width + 1].astype(f32).astype(jnp.int32)
        own_logit = jnp.sum(jnp.where(experts == own[0], logits, 0.0), axis=1, keepdims=True)
        rival_logit = jnp.sum(jnp.where(experts == rival, logits, 0.0), axis=1, keepdims=True)
        top = jnp.maximum(own_logit, rival_logit)
        power = jnp.exp(own_logit - top)
        gate = power / (power + jnp.exp(rival_logit - top))
        up_ref[...] = (gate * packet_ref[:, :width].astype(f32)).astype(bf16)

    active, slope = gelu_pair(nn(x_ref[...], in_ref[0]))
    active = active.astype(bf16)
    total_ref[...] += nn(active, out_ref[0])
    grad_hidden = (nt(up_ref[...], out_ref[0]) * slope).astype(bf16)
    grad_ref[...] += nt(grad_hidden, in_ref[0])
    in_grad[...] = nn(x_turned[...], grad_hidden).astype(bf16)
    out_grad[...] = nn(active.T, up_ref[...]).astype(bf16)

    @pl.when(pl.program_id(0) == pl.num_programs(0) - 1)
    def _():
        result = total_ref[...].astype(bf16)
        result_ref[...] = result
        back_ref[:, :width] = grad_ref[...].astype(bf16)
        rest = jnp.sum(
            packet_ref[:, :width].astype(f32) * result.astype(f32), axis=1, keepdims=True
        )
        lanes = lax.broadcasted_iota(jnp.int32, (slots, PAIR), 1)
        value = jnp.zeros((slots, PAIR), f32)
        for lane in range(3):
            part = rest.astype(bf16).astype(f32)
            value = jnp.where(lanes == lane, part, value)
            rest = rest - part
        back_ref[:, width:] = value.astype(bf16)


def expert_pass(own, x, packet, router, weight_in, weight_out):
    slots, width = x.shape
    hidden = weight_in.shape[2]
    step = 512

    def fixed(shape):
        return pl.BlockSpec(shape, lambda index, place: (0, 0))

    return pl.pallas_call(
        expert_kernel,
        grid_spec=pltpu.PrefetchScalarGridSpec(
            num_scalar_prefetch=1,
            grid=(hidden // step,),
            in_specs=[
                fixed(x.shape),
                fixed(packet.shape),
                fixed(router.shape),
                pl.BlockSpec((1, width, step), lambda index, place: (0, 0, index)),
                pl.BlockSpec((1, step, width), lambda index, place: (0, index, 0)),
            ],
            out_specs=(
                fixed(packet.shape),
                fixed(x.shape),
                pl.BlockSpec((width, step), lambda index, place: (0, index)),
                pl.BlockSpec((step, width), lambda index, place: (index, 0)),
            ),
            scratch_shapes=[
                pltpu.VMEM((width, slots), bf16),
                pltpu.VMEM((slots, width), bf16),
                pltpu.VMEM((slots, width), f32),
                pltpu.VMEM((slots, width), f32),
            ],
        ),
        out_shape=(
            jax.ShapeDtypeStruct(packet.shape, bf16),
            jax.ShapeDtypeStruct(x.shape, bf16),
            jax.ShapeDtypeStruct((width, hidden), bf16),
            jax.ShapeDtypeStruct((hidden, width), bf16),
        ),
        compiler_params=pltpu.CompilerParams(vmem_limit_bytes=40 * 2**20),
        cost_estimate=pl.CostEstimate(
            flops=12 * slots * width * hidden,
            bytes_accessed=24 * 2**20,
            transcendentals=slots * hidden,
        ),
        name="expert_pass",
    )(own, x, packet, router, weight_in, weight_out)


def join_kernel(section, mine_ref, other_ref, out_ref):
    @pl.when(pl.program_id(0) == section[0])
    def _():
        out_ref[...] = mine_ref[...].astype(f32)

    @pl.when(pl.program_id(0) != section[0])
    def _():
        out_ref[...] = other_ref[...].astype(f32)


def join_halves(section, mine, other, axis):
    rows, width = mine.shape
    steps = 3
    block = (rows // steps, width)

    def mine_map(which, step, place):
        return (jnp.where(which == place[0], step, 0), 0)

    def other_map(which, step, place):
        return (jnp.where(which == place[0], 0, step), 0)

    def out_map(which, step, place):
        return (which * steps + step, 0) if axis == 0 else (step, which)

    return pl.pallas_call(
        join_kernel,
        grid_spec=pltpu.PrefetchScalarGridSpec(
            num_scalar_prefetch=1,
            grid=(2, steps),
            in_specs=[pl.BlockSpec(block, mine_map), pl.BlockSpec(block, other_map)],
            out_specs=pl.BlockSpec(block, out_map),
        ),
        out_shape=jax.ShapeDtypeStruct(
            (2 * rows, width) if axis == 0 else (rows, 2 * width), f32
        ),
        compiler_params=pltpu.CompilerParams(vmem_limit_bytes=24 * 2**20),
        cost_estimate=pl.CostEstimate(
            flops=0, bytes_accessed=12 * rows * width, transcendentals=0
        ),
        name="join_halves",
    )(section, mine, other)


def block_kernel(section, *refs):
    sources, (qkv_out, proj_out) = refs[:8], refs[8:]
    own = pl.program_id(0) == section[0]
    width = proj_out.shape[1]

    def emit(first, second):
        qkv_out[:, : 2 * width] = first[...].astype(f32)
        qkv_out[:, 2 * width :] = second[:, :width].astype(f32)
        proj_out[...] = second[:, width:].astype(f32)

    for place in range(2):
        mine, other = sources[2 * place : 2 * place + 2], sources[4 + 2 * place : 6 + 2 * place]

        @pl.when(own & (section[0] == place))
        def _():
            emit(*mine)

        @pl.when(jnp.logical_not(own) & (section[0] == place))
        def _():
            emit(*other)


def own_block(section, one, two, from_one, from_two):
    half, joint = one[0].shape
    width = joint // 2
    steps = 3
    block = (half // steps, joint)

    def source(place, own):
        def index(which, step, section):
            wanted = (section[0] == place) & ((which == section[0]) == own)
            return (jnp.where(wanted, step, 0), 0)

        return [pl.BlockSpec(block, index)] * 2

    def out_map(which, step, section):
        return (which * steps + step, 0)

    return pl.pallas_call(
        block_kernel,
        grid_spec=pltpu.PrefetchScalarGridSpec(
            num_scalar_prefetch=1,
            grid=(2, steps),
            in_specs=source(0, True) + source(1, True) + source(0, False) + source(1, False),
            out_specs=(
                pl.BlockSpec((half // steps, 3 * width), out_map),
                pl.BlockSpec((half // steps, width), out_map),
            ),
        ),
        out_shape=(
            jax.ShapeDtypeStruct((2 * half, 3 * width), f32),
            jax.ShapeDtypeStruct((2 * half, width), f32),
        ),
        compiler_params=pltpu.CompilerParams(vmem_limit_bytes=24 * 2**20),
        cost_estimate=pl.CostEstimate(
            flops=0, bytes_accessed=24 * half * joint, transcendentals=0
        ),
        name="own_block",
    )(section, *one, *two, *from_one, *from_two)


def span(axis, start, size):
    multiple = size & -size
    piece = pl.ds(pl.multiple_of(start * size, multiple), size)
    return (piece, slice(None)) if axis == 0 else (slice(None), piece)


def in_blocks(rows, work):
    size = next(size for size in (96, 64, 48, 32, 16) if rows % size == 0)
    if rows == size:
        work(slice(0, rows))
    else:

        @pl.loop(0, rows // size)
        def _(step):
            work(pl.ds(pl.multiple_of(step * size, size), size))


def combine_kernel(plans, extra, marks, *refs):
    count = len(plans)
    sources, outs = refs[: 2 * count], list(refs[2 * count + extra :])
    for index, (now, later) in enumerate(plans):
        stays, got = sources[2 * index : 2 * index + 2]
        rows, width = got.shape
        if now[0] == "gather":
            out = outs.pop(0)
            mine = marks[now[2]]
            for source, place in ((stays, mine), (got, 1 - mine)):
                target = out.at[span(now[1], place, got.shape[now[1]])]

                def move(block, source=source, target=target):
                    target[block, :] = source[block, :]

                in_blocks(rows, move)
        elif later is not None and later[0] == "reduce":
            mine = marks[later[2]]
            for place in (1 - mine, mine):
                out = outs.pop(0)
                window = span(later[1], place, out.shape[later[1]])
                first, second = stays.at[window], got.at[window]

                def add(block, first=first, second=second, out=out):
                    out[block, :] = (first[block, :].astype(f32) + second[block, :].astype(f32)).astype(
                        bf16
                    )

                in_blocks(out.shape[0], add)
        else:
            out = outs.pop(0)

            def add_all(block, stays=stays, got=got, out=out):
                out[block, :] = (stays[block, :].astype(f32) + got[block, :].astype(f32)).astype(bf16)

            in_blocks(rows, add_all)


def combine(marks, plans, pairs, after):
    near = whole_spec()
    shapes = []
    for (now, later), (stays, got) in zip(plans, pairs):
        shape = list(got.shape)
        if now[0] == "gather":
            shape[now[1]] *= 2
            shapes.append(shape)
        elif later is not None and later[0] == "reduce":
            shape[later[1]] //= 2
            shapes += [shape, shape]
        else:
            shapes.append(shape)
    values = [value for pair in pairs for value in pair]
    return pl.pallas_call(
        functools.partial(combine_kernel, plans, len(after)),
        out_shape=[jax.ShapeDtypeStruct(shape, bf16) for shape in shapes],
        in_specs=[pl.BlockSpec(memory_space=pltpu.SMEM)]
        + [near] * len(values)
        + [pl.BlockSpec(memory_space=pl.ANY)] * len(after),
        out_specs=[near] * len(shapes),
        compiler_params=pltpu.CompilerParams(vmem_limit_bytes=32 * 2**20),
        cost_estimate=pl.CostEstimate(
            flops=0, bytes_accessed=sum(4 * value.size for value in values), transcendentals=0
        ),
        name="combine",
    )(marks, *values, *after)


def combine_plainly(marks, plans, pairs):
    outs = []
    for (now, later), (stays, got) in zip(plans, pairs):
        if now[0] == "gather":
            outs.append(
                jnp.where(
                    marks[now[2]] == 0,
                    jnp.concatenate([stays, got], axis=now[1]),
                    jnp.concatenate([got, stays], axis=now[1]),
                )
            )
            continue
        total = (stays.astype(f32) + got.astype(f32)).astype(bf16)
        if later is not None and later[0] == "reduce":
            size = total.shape[later[1]] // 2
            for place in (1 - marks[later[2]], marks[later[2]]):
                outs.append(lax.dynamic_slice_in_dim(total, place * size, size, axis=later[1]))
        else:
            outs.append(total)
    return outs


def flipped(value, axis, bit):
    pairs = [(place, place ^ (1 << bit)) for place in range(lax.axis_size(axis))]
    return lax.ppermute(value, axis, pairs)


class Travel:
    def __init__(self, marks, sends, keeps, orders):
        self.marks = marks
        self.plans = []
        self.aligned = True
        for value, order in zip(sends, orders):
            shape = list(value.shape)
            steps = []
            for bit in order:
                axis = 0 if shape[0] % 32 == 0 or shape[1] % 256 else 1
                if shape[axis] % (32, 256)[axis]:
                    self.aligned = False
                steps.append((axis, bit))
                shape[axis] //= 2
            self.plans.append(
                [("pair", 0, 0)]
                + [("reduce", *step) for step in steps]
                + [("gather", *step) for step in reversed(steps)]
            )
        self.stage = 0
        self.stays = list(keeps)
        self.got = [flipped(value, "section", 0) for value in sends]

    def step(self, after=()):
        plans, pairs = [], []
        for plan, stays, got in zip(self.plans, self.stays, self.got):
            later = plan[self.stage + 1] if self.stage + 1 < len(plan) else None
            plans.append((plan[self.stage], later))
            pairs.append((stays, got))
        if self.aligned:
            outs = list(combine(self.marks, plans, pairs, after))
        else:
            outs = combine_plainly(self.marks, plans, pairs)
        self.stage += 1
        self.stays, self.got = [], []
        for now, later in plans:
            if later is not None and later[0] == "reduce":
                sent = outs.pop(0)
                self.stays.append(outs.pop(0))
            else:
                sent = outs.pop(0)
                self.stays.append(sent)
            if later is not None:
                self.got.append(flipped(sent, "wide", later[2]))
        return self.stays

    @property
    def done(self):
        return not self.got


def norm_stats(stream):
    mean_value = jnp.mean(stream, axis=-1, keepdims=True)
    centered = stream - mean_value
    variance = jnp.mean(centered * centered, axis=-1, keepdims=True)
    return centered * lax.rsqrt(variance + norm_epsilon)


def slot_plan(ids, rank, capacity):
    before = rank[None, :] < rank[:, None]
    first, second = ids[:, 0], ids[:, 1]
    same_first = (first[:, None] == first[None, :]) & before
    same_second = (second[:, None] == second[None, :]) & before
    crossed = second[:, None] == first[None, :]
    place_first = jnp.sum(same_first.astype(jnp.int32), axis=1)
    place_second = jnp.sum(same_second.astype(jnp.int32) + crossed.astype(jnp.int32), axis=1)
    slot_first = jnp.where(place_first < capacity, first * capacity + place_first, -1)
    slot_second = jnp.where(place_second < capacity, second * capacity + place_second, -1)
    return (jnp.where(first >= 0, slot_first, -1), jnp.where(second >= 0, slot_second, -1))


def body(
    patches,
    out_cotangent,
    attn_gain,
    qkv_weight,
    proj_weight,
    ffn_gain,
    mlp_in,
    mlp_out,
    router_weight,
    expert_in,
    expert_out,
    expert_ids,
    priority,
):
    expert_count = lax.axis_size("wide")
    sections = lax.axis_size("section")
    section = lax.axis_index("section")
    own_expert = lax.axis_index("wide")
    is_first = section == 0
    images = patches.shape[0] // sections
    length, width = patches.shape[1:]
    pad = -(-length // STEP) * STEP
    rows = images * pad
    capacity = max(2, images * length // expert_count)
    slots = expert_count * capacity
    levels = expert_count.bit_length() - 1
    assert 1 << levels == expert_count
    place = section[None]
    marks = (own_expert >> jnp.arange(levels, dtype=jnp.int32)) & 1
    bits = list(range(levels))
    third = max(1, levels // 3)
    orders = (bits, bits[third:] + bits[:third])

    def mine(whole):
        value = lax.dynamic_slice_in_dim(whole, section * images, images)
        return jnp.pad(value, ((0, 0), (0, pad - length), (0, 0))).reshape(rows, width)

    def swap(value):
        return flipped(value, "section", 0)

    def across(value):
        shape = (expert_count, capacity, value.shape[1])
        moved = lax.all_to_all(value.reshape(shape), "wide", split_axis=0, concat_axis=0, tiled=True)
        return moved.reshape(value.shape)

    other_qkv, other_proj = swap(qkv_weight[0]), swap(proj_weight[0])
    gains = jnp.concatenate([attn_gain, ffn_gain], axis=0)
    other_gains = swap(gains)
    gains_one = jnp.where(is_first, gains, other_gains)
    gains_two = jnp.where(is_first, other_gains, gains)
    weights = (qkv_weight[0], other_qkv, proj_weight[0], other_proj)
    which_one = jnp.stack([(section == 0).astype(jnp.int32), section])
    which_two = jnp.stack([(section == 1).astype(jnp.int32), section])

    ids = lax.dynamic_slice_in_dim(expert_ids, section * images, images)
    ids = jnp.pad(ids, ((0, 0), (0, pad - length), (0, 0)), constant_values=-1).reshape(rows, 2)
    rank = lax.dynamic_slice_in_dim(priority, section, 1).reshape(images, length)
    rank = jnp.pad(rank, ((0, 0), (0, pad - length))).reshape(rows)
    slot_first, slot_second = slot_plan(ids, rank, capacity)
    slot_range = jnp.arange(slots, dtype=jnp.int32)
    pick_first = slot_first[:, None] == slot_range[None, :]
    pick_second = slot_second[:, None] == slot_range[None, :]
    pick_any = (pick_first | pick_second).astype(bf16)
    kept_first = (slot_first >= 0).astype(f32)[:, None]
    kept_second = (slot_second >= 0).astype(f32)[:, None]
    rival = jnp.sum(
        jnp.where(pick_first, ids[:, 1:], 0) + jnp.where(pick_second, ids[:, :1], 0), axis=0
    )
    cotangent = mine(out_cotangent)
    packet = jnp.concatenate(
        [
            tn(pick_any, cotangent).astype(bf16),
            jnp.broadcast_to(rival.astype(bf16)[:, None], (slots, PAIR)),
        ],
        axis=1,
    )

    stream_one = mine(patches)
    mixed_one, packed_one, mix_one, normed_one = attention_forward(
        which_one, stream_one, weights, gains_one[:1], gains_one[1:], images, length
    )
    arrived_packet = across(packet)
    hidden_one = nn(normed_one, mlp_in)
    active_one = jax.nn.gelu(hidden_one).astype(bf16)
    first_low = (mixed_one + nn(active_one, mlp_out)).astype(bf16)

    mixed_two, packed_two, mix_two, normed_two = attention_forward(
        which_two, first_low, weights, gains_two[:1], gains_two[1:], images, length
    )
    arrived = across(tn(pick_any, normed_two).astype(bf16))
    back, result, grad_expert_in, grad_expert_out = expert_pass(
        own_expert[None], arrived, arrived_packet, router_weight, expert_in, expert_out
    )
    back = across(back)
    result, back = lax.optimization_barrier((result, back))
    returned = across(result)
    expert_in_sum = grad_expert_in.astype(f32) + swap(grad_expert_in).astype(f32)
    expert_out_sum = grad_expert_out.astype(f32) + swap(grad_expert_out).astype(f32)

    expert_range = jnp.arange(expert_count, dtype=jnp.int32)
    logits = nn(normed_two, router_weight)
    one_hot = (ids[:, :, None] == expert_range[None, None, :]).astype(f32)
    chosen = jnp.sum(one_hot * logits[:, None, :], axis=-1)
    gates = jax.nn.softmax(chosen, axis=-1)
    low_first, low_second = pick_first.astype(bf16), pick_second.astype(bf16)
    grad_gates = jnp.concatenate(
        [
            jnp.sum(nn(low, back[:, width:]), axis=-1, keepdims=True)
            for low in (low_first, low_second)
        ],
        axis=1,
    )
    grad_chosen = gates * (grad_gates - jnp.sum(gates * grad_gates, axis=-1, keepdims=True))
    grad_logits = jnp.sum(one_hot * grad_chosen[:, :, None], axis=1).astype(bf16)
    grad_router = tn(grad_logits, normed_two)
    grad_normed_two = nn(pick_any, back[:, :width]) + nt(grad_logits, router_weight)
    second_low = (
        mixed_two
        + kept_first * gates[:, :1] * nn(low_first, returned)
        + kept_second * gates[:, 1:] * nn(low_second, returned)
    ).astype(bf16)
    grad_two, grad_first, small_two, grad_packed, total_low, low = attention_backward(
        which_two,
        first_low,
        mixed_two,
        cotangent,
        grad_normed_two,
        packed_two,
        mix_two,
        weights,
        gains_two[:1],
        gains_two[1:],
        images,
        length,
    )
    pieces = attention_products(place, low, mix_two, grad_packed, total_low)
    two = Travel(marks, pieces[:2], pieces[2:], orders)
    grad_normed_one, in_send, in_keep, out_send, out_keep = mlp_backward(
        place, normed_one, grad_first, mlp_in, mlp_out, after=pieces[3:]
    )
    mlp = Travel(marks, (in_send, out_send), (in_keep, out_keep), orders)
    grad_one, _, small_one, grad_packed, total_low, low = attention_backward(
        which_one,
        stream_one,
        mixed_one,
        grad_first,
        grad_normed_one,
        packed_one,
        mix_one,
        weights,
        gains_one[:1],
        gains_one[1:],
        images,
        length,
        after=two.step(),
    )
    pieces = attention_products(
        place, low, mix_one, grad_packed, total_low, after=two.step() + mlp.step()
    )
    one = Travel(marks, pieces[:2], pieces[2:], orders)
    last = ()
    while not (one.done and two.done and mlp.done):
        for travel in (two, mlp, one):
            if not travel.done:
                last = travel.step(after=last)

    def joined(half, axis):
        return join_halves(place, half, flipped(half, "section", 0), axis)

    from_two = [lax.ppermute(value, "section", [(0, 1)]) for value in two.stays]
    from_one = [lax.ppermute(value, "section", [(1, 0)]) for value in one.stays]
    qkv_grad, proj_grad = own_block(place, one.stays, two.stays, from_one, from_two)

    def own_images(value_one, value_two):
        value_one, value_two = [
            value.reshape(images, pad, width)[:, :length] for value in (value_one, value_two)
        ]
        own = jnp.where(is_first, value_one, value_two)
        other = swap(jnp.where(is_first, value_two, value_one))
        return jnp.concatenate(
            [jnp.where(is_first, own, other), jnp.where(is_first, other, own)], axis=0
        )[None]

    small = jnp.concatenate([small_one, small_two, grad_router], axis=0)
    small = small + swap(small)
    for bit in range(levels):
        small = small + flipped(small, "wide", bit)
    small_block = lax.dynamic_slice_in_dim(small, 8 * section, 8)
    return (
        own_images(first_low, second_low),
        own_images(grad_one, grad_first.astype(f32)),
        small_block[:1],
        qkv_grad[None],
        proj_grad[None],
        small_block[1:2],
        joined(mlp.stays[0], 0),
        joined(mlp.stays[1], 1),
        jnp.transpose(small[16:]),
        expert_in_sum[None],
        expert_out_sum[None],
    )


def solution(mesh):
    in_specs = (
        P("wide", None, None),
        P("wide", None, None),
        P("section", None),
        P("section", None, None),
        P("section", None, None),
        P("section", None),
        P(),
        P(),
        P(),
        P("wide", None, None),
        P("wide", None, None),
        P("wide", None, None),
        P("wide", None),
    )
    out_specs = (
        P("section", "wide", None, None),
        P("section", "wide", None, None),
        P("section", None),
        P("section", None, None),
        P("section", None, None),
        P("section", None),
        P(),
        P(),
        P(),
        P("wide", None, None),
        P("wide", None, None),
    )
    return jax.shard_map(body, mesh=mesh, in_specs=in_specs, out_specs=out_specs, check_vma=False)
```

```python
import functools

import jax
import jax.numpy as jnp
from jax import lax
from jax.experimental import pallas as pl
from jax.experimental.pallas import tpu as pltpu
from jax.sharding import PartitionSpec as P

H = 12
HEAD = 64
PAIR = 2 * HEAD
STEP = 16
norm_epsilon = 1e-06
bf16 = jnp.bfloat16
f32 = jnp.float32


def dot(left, right, dims):
    return lax.dot_general(left, right, (dims, ((), ())), preferred_element_type=f32)


def nn(left, right):
    return dot(left, right, ((1,), (0,)))


def nt(left, right):
    return dot(left, right, ((1,), (1,)))


def tn(left, right):
    return dot(left, right, ((0,), (0,)))


def norm_rows(value):
    mean_value = jnp.mean(value, axis=-1, keepdims=True)
    centered = value - mean_value
    scale = lax.rsqrt(jnp.mean(centered * centered, axis=-1, keepdims=True) + norm_epsilon)
    return (centered * scale, scale)


def norm_rows_back(unit, scale, gain, upstream):
    weighted = upstream * gain
    first = jnp.mean(weighted, axis=-1, keepdims=True)
    second = jnp.mean(weighted * unit, axis=-1, keepdims=True)
    return scale * (weighted - first - unit * second)


def folded(value):
    rows = value.shape[0]
    return sum(value[start : start + 8] for start in range(0, rows, 8))


def row_blocks(rows):
    return [slice(start, start + STEP) for start in range(0, rows, STEP)]


def fetch(take, own, other, target, sem):
    @pl.when(take == 1)
    def _():
        pltpu.make_async_copy(own, target, sem).start()

    @pl.when(take != 1)
    def _():
        pltpu.make_async_copy(other, target, sem).start()


def forward_kernel(
    images,
    length,
    which,
    x_ref,
    own_qkv,
    other_qkv,
    own_proj,
    other_proj,
    gain_a,
    gain_f,
    mixed_ref,
    packed_ref,
    mix_ref,
    normed_ref,
    qkv_ref,
    proj_ref,
    low_ref,
    sems,
):
    rows, width = x_ref.shape
    pad = rows // images
    fetch(which[0], own_qkv, other_qkv, qkv_ref, sems.at[0])
    fetch(which[0], own_proj, other_proj, proj_ref, sems.at[1])

    for block in row_blocks(rows):
        unit, scale = norm_rows(x_ref[block, :].astype(f32))
        low_ref[block, :] = (unit * gain_a[...]).astype(bf16)

    pltpu.make_async_copy(own_qkv, qkv_ref, sems.at[0]).wait()

    @pl.loop(0, 3 * width // 256)
    def _(step):
        lanes = pl.ds(pl.multiple_of(step * 256, 256), 256)
        packed_ref[:, lanes] = nn(low_ref[...], qkv_ref[:, lanes]).astype(bf16)

    left = lax.broadcasted_iota(jnp.int32, (pad, PAIR), 1) < HEAD
    live = lax.broadcasted_iota(jnp.int32, (pad, pad), 0) < length

    @pl.loop(0, width // PAIR)
    def _(pair):
        def lanes(part):
            return pl.ds(pl.multiple_of(part * width + pair * PAIR, PAIR), PAIR)

        for image in range(images):
            block = slice(image * pad, (image + 1) * pad)
            queries = packed_ref[block, lanes(0)].astype(f32) * HEAD ** (-0.5)
            keys = packed_ref[block, lanes(1)]
            values = packed_ref[block, lanes(2)].T
            outs = []
            for half, rows_half in ((left, slice(0, HEAD)), (~left, slice(HEAD, PAIR))):
                scores = nt(keys, jnp.where(half, queries, 0.0).astype(bf16))
                scores = jnp.where(live, scores, -jnp.inf)
                powers = jnp.exp(scores - jnp.max(scores, axis=0, keepdims=True))
                share = 1.0 / jnp.sum(powers, axis=0, keepdims=True)
                outs.append(nn(values[rows_half], powers.astype(bf16)) * share)
            mix_ref[block, lanes(0)] = jnp.concatenate(outs, axis=0).T.astype(bf16)

    pltpu.make_async_copy(own_proj, proj_ref, sems.at[1]).wait()

    @pl.loop(0, width // 256)
    def _(step):
        lanes = pl.ds(pl.multiple_of(step * 256, 256), 256)
        mixed_ref[:, lanes] = x_ref[:, lanes].astype(f32) + nn(mix_ref[...], proj_ref[:, lanes])

    for block in row_blocks(rows):
        unit, scale = norm_rows(mixed_ref[block, :])
        normed_ref[block, :] = (unit * gain_f[...]).astype(bf16)


def backward_kernel(
    images,
    length,
    which,
    x_ref,
    mixed_ref,
    base_ref,
    upstream_ref,
    packed_ref,
    mix_ref,
    own_qkv,
    other_qkv,
    own_proj,
    other_proj,
    gain_a,
    gain_f,
    grad_ref,
    grad_low,
    gains_ref,
    grad_packed,
    total_low,
    low_ref,
    qkv_ref,
    proj_ref,
    total_ref,
    grad_mix,
    sems,
):
    rows, width = x_ref.shape
    pad = rows // images
    fetch(which[0], own_proj, other_proj, proj_ref, sems.at[1])
    fetch(which[0], own_qkv, other_qkv, qkv_ref, sems.at[0])
    gain_total = jnp.zeros((8, width), f32)
    for block in row_blocks(rows):
        unit, scale = norm_rows(mixed_ref[block, :])
        upstream = upstream_ref[block, :]
        value = base_ref[block, :].astype(f32) + norm_rows_back(
            unit, scale, gain_f[...], upstream
        )
        total_ref[block, :] = value
        total_low[block, :] = value.astype(bf16)
        source_unit, source_scale = norm_rows(x_ref[block, :].astype(f32))
        low_ref[block, :] = (source_unit * gain_a[...]).astype(bf16)
        gain_total = gain_total + folded(upstream * unit)
    gains_ref[...] = jnp.zeros_like(gains_ref)
    gains_ref[1:2, :] = jnp.sum(gain_total, axis=0, keepdims=True)
    pltpu.make_async_copy(own_proj, proj_ref, sems.at[1]).wait()

    @pl.loop(0, width // 256)
    def _(step):
        lanes = pl.ds(pl.multiple_of(step * 256, 256), 256)
        grad_mix[:, lanes] = nt(total_low[...], proj_ref[lanes, :]).astype(bf16)

    left = lax.broadcasted_iota(jnp.int32, (pad, PAIR), 1) < HEAD
    live = lax.broadcasted_iota(jnp.int32, (pad, pad), 0) < length

    @pl.loop(0, width // PAIR)
    def _(pair):
        def lanes(part):
            return pl.ds(pl.multiple_of(part * width + pair * PAIR, PAIR), PAIR)

        for image in range(images):
            block = slice(image * pad, (image + 1) * pad)
            queries = packed_ref[block, lanes(0)].astype(f32) * HEAD ** (-0.5)
            keys = packed_ref[block, lanes(1)]
            values = packed_ref[block, lanes(2)]
            grads = grad_mix[block, lanes(0)]
            sums = [0.0, 0.0, 0.0]
            for half in (left, ~left):
                some_queries = jnp.where(half, queries, 0.0).astype(bf16)
                some_keys = jnp.where(half, keys, 0.0).astype(bf16)
                some_grads = jnp.where(half, grads, 0.0).astype(bf16)
                scores = nt(keys, some_queries)
                scores = jnp.where(live, scores, -jnp.inf)
                powers = jnp.exp(scores - jnp.max(scores, axis=0, keepdims=True))
                weights = powers * (1.0 / jnp.sum(powers, axis=0, keepdims=True))
                grad_weights = nt(values, some_grads)
                inner = jnp.sum(grad_weights * weights, axis=0, keepdims=True)
                grad_raw = (weights * (grad_weights - inner)).astype(bf16)
                sums[0] += tn(grad_raw, some_keys)
                sums[1] += nn(grad_raw, some_queries)
                sums[2] += nn(weights.astype(bf16), some_grads)
            sums[0] = sums[0] * HEAD ** (-0.5)
            for part in range(3):
                grad_packed[block, lanes(part)] = sums[part].astype(bf16)

    pltpu.make_async_copy(own_qkv, qkv_ref, sems.at[0]).wait()

    @pl.loop(0, width // 256)
    def _(step):
        lanes = pl.ds(pl.multiple_of(step * 256, 256), 256)
        grad_ref[:, lanes] = nt(grad_packed[...], qkv_ref[lanes, :])

    gain_total = jnp.zeros((8, width), f32)
    for block in row_blocks(rows):
        unit, scale = norm_rows(x_ref[block, :].astype(f32))
        upstream = grad_ref[block, :]
        value = total_ref[block, :] + norm_rows_back(unit, scale, gain_a[...], upstream)
        grad_ref[block, :] = value
        grad_low[block, :] = value.astype(bf16)
        gain_total = gain_total + folded(upstream * unit)
    gains_ref[0:1, :] = jnp.sum(gain_total, axis=0, keepdims=True)


def product_kernel(chunks, section, low_ref, mix_ref, grad_packed, total_low, *outs):
    width = low_ref.shape[1]
    half_width = width // 2
    third = width // 3
    for which_half, targets in ((1 - section[0], outs[:chunks]), (section[0], outs[chunks:])):
        columns = pl.ds(pl.multiple_of(which_half * half_width, 128), half_width)
        left_rows = low_ref[:, columns].T
        right_rows = mix_ref[:, columns].T
        for step in range(12):
            if step < 9:
                value = nn(left_rows, grad_packed[:, step * third : (step + 1) * third])
            else:
                value = nn(right_rows, total_low[:, (step - 9) * third : (step - 8) * third])
            out, place = divmod(step, 12 // chunks)
            targets[out][:, place * third : (place + 1) * third] = value.astype(bf16)


def attention_products(section, low, mix, grad_packed, total_low, chunks, after=()):
    rows, width = low.shape
    near = whole_spec()
    piece = jax.ShapeDtypeStruct((width // 2, 4 * width // chunks), bf16)

    def kernel(section_ref, *refs):
        product_kernel(chunks, section_ref, *refs[:4], *refs[4 + len(after) :])

    return pl.pallas_call(
        kernel,
        out_shape=(piece,) * (2 * chunks),
        in_specs=[pl.BlockSpec(memory_space=pltpu.SMEM)]
        + [near] * 4
        + [pl.BlockSpec(memory_space=pl.ANY)] * len(after),
        out_specs=(near,) * (2 * chunks),
        compiler_params=pltpu.CompilerParams(vmem_limit_bytes=32 * 2**20),
        cost_estimate=pl.CostEstimate(
            flops=8 * rows * width * width, bytes_accessed=12 * 2**20, transcendentals=0
        ),
        name="attention_products",
    )(section, low, mix, grad_packed, total_low, *after)


def whole_spec():
    return pl.BlockSpec(memory_space=pltpu.VMEM)


def attention_forward(which, x, weights, gain_a, gain_f, images, length):
    rows, width = x.shape
    far = pl.BlockSpec(memory_space=pl.ANY)
    near = whole_spec()
    return pl.pallas_call(
        functools.partial(forward_kernel, images, length),
        out_shape=(
            jax.ShapeDtypeStruct((rows, width), f32),
            jax.ShapeDtypeStruct((rows, 3 * width), bf16),
            jax.ShapeDtypeStruct((rows, width), bf16),
            jax.ShapeDtypeStruct((rows, width), bf16),
        ),
        in_specs=[pl.BlockSpec(memory_space=pltpu.SMEM), near, far, far, far, far, near, near],
        out_specs=(near, near, near, near),
        scratch_shapes=[
            pltpu.VMEM((width, 3 * width), bf16),
            pltpu.VMEM((width, width), bf16),
            pltpu.VMEM((rows, width), bf16),
            pltpu.SemaphoreType.DMA((2,)),
        ],
        compiler_params=pltpu.CompilerParams(vmem_limit_bytes=40 * 2**20),
        cost_estimate=pl.CostEstimate(
            flops=10 * rows * width * width, bytes_accessed=12 * 2**20, transcendentals=2**20
        ),
        name="attention_forward",
    )(which, x, *weights, gain_a, gain_f)


def attention_backward(
    which, x, mixed, base, upstream, packed, mix, weights, gain_a, gain_f, images, length, after=()
):
    rows, width = x.shape
    far = pl.BlockSpec(memory_space=pl.ANY)
    near = whole_spec()

    def kernel(*refs):
        backward_kernel(images, length, *refs[:13], *refs[13 + len(after) :])

    return pl.pallas_call(
        kernel,
        out_shape=(
            jax.ShapeDtypeStruct((rows, width), f32),
            jax.ShapeDtypeStruct((rows, width), bf16),
            jax.ShapeDtypeStruct((8, width), f32),
            jax.ShapeDtypeStruct((rows, 3 * width), bf16),
            jax.ShapeDtypeStruct((rows, width), bf16),
            jax.ShapeDtypeStruct((rows, width), bf16),
        ),
        in_specs=[pl.BlockSpec(memory_space=pltpu.SMEM)]
        + [near] * 6
        + [far] * 4
        + [near] * 2
        + [far] * len(after),
        out_specs=(near,) * 6,
        scratch_shapes=[
            pltpu.VMEM((width, 3 * width), bf16),
            pltpu.VMEM((width, width), bf16),
            pltpu.VMEM((rows, width), f32),
            pltpu.VMEM((rows, width), bf16),
            pltpu.SemaphoreType.DMA((2,)),
        ],
        compiler_params=pltpu.CompilerParams(vmem_limit_bytes=40 * 2**20),
        cost_estimate=pl.CostEstimate(
            flops=20 * rows * width * width, bytes_accessed=24 * 2**20, transcendentals=2**20
        ),
        name="attention_backward",
    )(which, x, mixed, base, upstream, packed, mix, *weights, gain_a, gain_f, *after)


def gelu_pair(hidden):
    cubic = 0.7978845608028654
    square = hidden * hidden
    curve = jnp.tanh(cubic * (hidden + 0.044715 * (square * hidden)))
    left = 0.5 * (1.0 + curve)
    slope = left + 0.5 * hidden * (1.0 - curve * curve) * (
        cubic * (1.0 + 3.0 * 0.044715 * square)
    )
    return (hidden * left, slope)


def mlp_kernel(
    section,
    x_ref,
    up_ref,
    in_ref,
    out_ref,
    grad_ref,
    in_send,
    in_keep,
    out_send,
    out_keep,
    x_turned,
):
    half = x_ref.shape[1] // 2

    @pl.when(pl.program_id(0) == 0)
    def _():
        x_turned[...] = x_ref[...].T
        grad_ref[...] = jnp.zeros_like(grad_ref)

    active, slope = gelu_pair(nn(x_ref[...], in_ref[...]))
    active = active.astype(bf16)
    grad_hidden = (nt(up_ref[...], out_ref[...]) * slope).astype(bf16)
    grad_ref[...] += nt(grad_hidden, in_ref[...])
    turned = active.T
    for which, first, second in (
        (1 - section[0], in_send, out_send),
        (section[0], in_keep, out_keep),
    ):
        block = pl.ds(pl.multiple_of(which * half, 128), half)
        first[...] = nn(x_turned[block, :], grad_hidden).astype(bf16)
        second[...] = nn(turned, up_ref[:, block]).astype(bf16)


def mlp_backward(section, x, up, weight_in, weight_out, after):
    rows, width = x.shape
    hidden = weight_in.shape[1]
    step = 512
    half = width // 2
    fixed = pl.BlockSpec((rows, width), lambda index, place: (0, 0))
    across = pl.BlockSpec((half, step), lambda index, place: (0, index))
    down = pl.BlockSpec((step, half), lambda index, place: (index, 0))

    def kernel(*refs):
        mlp_kernel(*refs[:5], *refs[5 + len(after) :])

    return pl.pallas_call(
        kernel,
        grid_spec=pltpu.PrefetchScalarGridSpec(
            num_scalar_prefetch=1,
            grid=(hidden // step,),
            in_specs=[
                fixed,
                fixed,
                pl.BlockSpec((width, step), lambda index, place: (0, index)),
                pl.BlockSpec((step, width), lambda index, place: (index, 0)),
            ]
            + [pl.BlockSpec(memory_space=pl.ANY)] * len(after),
            out_specs=(fixed, across, across, down, down),
            scratch_shapes=[pltpu.VMEM((width, rows), bf16)],
        ),
        out_shape=(
            jax.ShapeDtypeStruct((rows, width), f32),
            jax.ShapeDtypeStruct((half, hidden), bf16),
            jax.ShapeDtypeStruct((half, hidden), bf16),
            jax.ShapeDtypeStruct((hidden, half), bf16),
            jax.ShapeDtypeStruct((hidden, half), bf16),
        ),
        compiler_params=pltpu.CompilerParams(vmem_limit_bytes=40 * 2**20),
        cost_estimate=pl.CostEstimate(
            flops=10 * rows * width * hidden,
            bytes_accessed=24 * 2**20,
            transcendentals=rows * hidden,
        ),
        name="mlp_backward",
    )(section, x, up, weight_in, weight_out, *after)


def expert_kernel(
    own,
    x_ref,
    packet_ref,
    router_ref,
    in_ref,
    out_ref,
    back_ref,
    result_ref,
    in_grad,
    out_grad,
    x_turned,
    up_ref,
    total_ref,
    grad_ref,
):
    slots, width = x_ref.shape

    @pl.when(pl.program_id(0) == 0)
    def _():
        x_turned[...] = x_ref[...].T
        grad_ref[...] = jnp.zeros_like(grad_ref)
        total_ref[...] = jnp.zeros_like(total_ref)
        logits = nn(x_ref[...], router_ref[...])
        experts = lax.broadcasted_iota(jnp.int32, logits.shape, 1)
        rival = packet_ref[:, width : width + 1].astype(f32).astype(jnp.int32)
        own_logit = jnp.sum(jnp.where(experts == own[0], logits, 0.0), axis=1, keepdims=True)
        rival_logit = jnp.sum(jnp.where(experts == rival, logits, 0.0), axis=1, keepdims=True)
        top = jnp.maximum(own_logit, rival_logit)
        power = jnp.exp(own_logit - top)
        gate = power / (power + jnp.exp(rival_logit - top))
        up_ref[...] = (gate * packet_ref[:, :width].astype(f32)).astype(bf16)

    active, slope = gelu_pair(nn(x_ref[...], in_ref[0]))
    active = active.astype(bf16)
    total_ref[...] += nn(active, out_ref[0])
    grad_hidden = (nt(up_ref[...], out_ref[0]) * slope).astype(bf16)
    grad_ref[...] += nt(grad_hidden, in_ref[0])
    in_grad[...] = nn(x_turned[...], grad_hidden).astype(bf16)
    out_grad[...] = nn(active.T, up_ref[...]).astype(bf16)

    @pl.when(pl.program_id(0) == pl.num_programs(0) - 1)
    def _():
        result = total_ref[...].astype(bf16)
        result_ref[...] = result
        back_ref[:, :width] = grad_ref[...].astype(bf16)
        rest = jnp.sum(
            packet_ref[:, :width].astype(f32) * result.astype(f32), axis=1, keepdims=True
        )
        lanes = lax.broadcasted_iota(jnp.int32, (slots, PAIR), 1)
        value = jnp.zeros((slots, PAIR), f32)
        for lane in range(3):
            part = rest.astype(bf16).astype(f32)
            value = jnp.where(lanes == lane, part, value)
            rest = rest - part
        back_ref[:, width:] = value.astype(bf16)


def expert_pass(own, x, packet, router, weight_in, weight_out):
    slots, width = x.shape
    hidden = weight_in.shape[2]
    step = 512

    def fixed(shape):
        return pl.BlockSpec(shape, lambda index, place: (0, 0))

    return pl.pallas_call(
        expert_kernel,
        grid_spec=pltpu.PrefetchScalarGridSpec(
            num_scalar_prefetch=1,
            grid=(hidden // step,),
            in_specs=[
                fixed(x.shape),
                fixed(packet.shape),
                fixed(router.shape),
                pl.BlockSpec((1, width, step), lambda index, place: (0, 0, index)),
                pl.BlockSpec((1, step, width), lambda index, place: (0, index, 0)),
            ],
            out_specs=(
                fixed(packet.shape),
                fixed(x.shape),
                pl.BlockSpec((width, step), lambda index, place: (0, index)),
                pl.BlockSpec((step, width), lambda index, place: (index, 0)),
            ),
            scratch_shapes=[
                pltpu.VMEM((width, slots), bf16),
                pltpu.VMEM((slots, width), bf16),
                pltpu.VMEM((slots, width), f32),
                pltpu.VMEM((slots, width), f32),
            ],
        ),
        out_shape=(
            jax.ShapeDtypeStruct(packet.shape, bf16),
            jax.ShapeDtypeStruct(x.shape, bf16),
            jax.ShapeDtypeStruct((width, hidden), bf16),
            jax.ShapeDtypeStruct((hidden, width), bf16),
        ),
        compiler_params=pltpu.CompilerParams(vmem_limit_bytes=40 * 2**20),
        cost_estimate=pl.CostEstimate(
            flops=12 * slots * width * hidden,
            bytes_accessed=24 * 2**20,
            transcendentals=slots * hidden,
        ),
        name="expert_pass",
    )(own, x, packet, router, weight_in, weight_out)


def join_kernel(section, mine_ref, other_ref, *rest):
    out_ref = rest[-1]

    @pl.when(pl.program_id(0) == section[0])
    def _():
        out_ref[...] = mine_ref[...].astype(f32)

    @pl.when(pl.program_id(0) != section[0])
    def _():
        out_ref[...] = other_ref[...].astype(f32)


def join_halves(section, mine, other, axis, after):
    rows, width = mine.shape
    steps = 3
    block = (rows // steps, width)

    def mine_map(which, step, place):
        return (jnp.where(which == place[0], step, 0), 0)

    def other_map(which, step, place):
        return (jnp.where(which == place[0], 0, step), 0)

    def out_map(which, step, place):
        return (which * steps + step, 0) if axis == 0 else (step, which)

    return pl.pallas_call(
        join_kernel,
        grid_spec=pltpu.PrefetchScalarGridSpec(
            num_scalar_prefetch=1,
            grid=(2, steps),
            in_specs=[pl.BlockSpec(block, mine_map), pl.BlockSpec(block, other_map)]
            + [pl.BlockSpec(memory_space=pl.ANY)] * len(after),
            out_specs=pl.BlockSpec(block, out_map),
        ),
        out_shape=jax.ShapeDtypeStruct(
            (2 * rows, width) if axis == 0 else (rows, 2 * width), f32
        ),
        compiler_params=pltpu.CompilerParams(vmem_limit_bytes=24 * 2**20),
        cost_estimate=pl.CostEstimate(
            flops=0, bytes_accessed=12 * rows * width, transcendentals=0
        ),
        name="join_halves",
    )(section, mine, other, *after)


def block_kernel(counts, section, *refs):
    refs = list(refs)
    sources = [[refs.pop(0) for _ in range(count)] for count in counts]
    qkv_out, proj_out = refs
    own = pl.program_id(0) == section[0]
    cut = qkv_out.shape[1]

    def emit(parts):
        start = 0
        for part in parts:
            size = part.shape[1]
            left = max(0, min(size, cut - start))
            if left:
                qkv_out[:, start : start + left] = part[:, :left].astype(f32)
            if left < size:
                proj_out[:, start + left - cut : start + size - cut] = part[:, left:].astype(f32)
            start += size

    for index, parts in enumerate(sources):
        place, mine = index % 2, index < 2

        @pl.when((own == mine) & (section[0] == place))
        def _():
            emit(parts)


def own_block(section, groups):
    half = groups[0][0].shape[0]
    width = sum(part.shape[1] for part in groups[0]) // 4
    steps = 3
    specs = []
    for index, parts in enumerate(groups):

        def place_map(which, step, section, place=index % 2, mine=index < 2):
            wanted = (section[0] == place) & ((which == section[0]) == mine)
            return (jnp.where(wanted, step, 0), 0)

        specs += [pl.BlockSpec((half // steps, part.shape[1]), place_map) for part in parts]

    def out_map(which, step, section):
        return (which * steps + step, 0)

    return pl.pallas_call(
        functools.partial(block_kernel, [len(parts) for parts in groups]),
        grid_spec=pltpu.PrefetchScalarGridSpec(
            num_scalar_prefetch=1,
            grid=(2, steps),
            in_specs=specs,
            out_specs=(
                pl.BlockSpec((half // steps, 3 * width), out_map),
                pl.BlockSpec((half // steps, width), out_map),
            ),
        ),
        out_shape=(
            jax.ShapeDtypeStruct((2 * half, 3 * width), f32),
            jax.ShapeDtypeStruct((2 * half, width), f32),
        ),
        compiler_params=pltpu.CompilerParams(vmem_limit_bytes=24 * 2**20),
        cost_estimate=pl.CostEstimate(
            flops=0, bytes_accessed=48 * half * width, transcendentals=0
        ),
        name="own_block",
    )(section, *[part for parts in groups for part in parts])


def total_kernel(mine_ref, other_ref, *rest):
    rest[-1][0] = mine_ref[...].astype(f32) + other_ref[...].astype(f32)


def pair_total(mine, other, after):
    rows, width = mine.shape
    steps = 6
    block = pl.BlockSpec((rows // steps, width), lambda step: (step, 0))
    return pl.pallas_call(
        total_kernel,
        grid=(steps,),
        in_specs=[block, block] + [pl.BlockSpec(memory_space=pl.ANY)] * len(after),
        out_specs=pl.BlockSpec((1, rows // steps, width), lambda step: (0, step, 0)),
        out_shape=jax.ShapeDtypeStruct((1, rows, width), f32),
        compiler_params=pltpu.CompilerParams(vmem_limit_bytes=24 * 2**20),
        cost_estimate=pl.CostEstimate(
            flops=rows * width, bytes_accessed=8 * rows * width, transcendentals=0
        ),
        name="pair_total",
    )(mine, other, *after)


def span(axis, start, size):
    multiple = size & -size
    piece = pl.ds(pl.multiple_of(start * size, multiple), size)
    return (piece, slice(None)) if axis == 0 else (slice(None), piece)


def in_blocks(rows, work):
    size = next(size for size in (96, 64, 48, 32, 16) if rows % size == 0)
    if rows == size:
        work(slice(0, rows))
    else:

        @pl.loop(0, rows // size)
        def _(step):
            work(pl.ds(pl.multiple_of(step * size, size), size))


def combine_kernel(plans, extra, marks, *refs):
    count = len(plans)
    sources, outs = refs[: 2 * count], list(refs[2 * count + extra :])
    for index, (now, later) in enumerate(plans):
        stays, got = sources[2 * index : 2 * index + 2]
        rows, width = got.shape
        if now[0] == "gather":
            out = outs.pop(0)
            mine = marks[now[2]]
            for source, place in ((stays, mine), (got, 1 - mine)):
                target = out.at[span(now[1], place, got.shape[now[1]])]

                def move(block, source=source, target=target):
                    target[block, :] = source[block, :]

                in_blocks(rows, move)
        elif later is not None and later[0] == "reduce":
            mine = marks[later[2]]
            for place in (1 - mine, mine):
                out = outs.pop(0)
                window = span(later[1], place, out.shape[later[1]])
                first, second = stays.at[window], got.at[window]

                def add(block, first=first, second=second, out=out):
                    out[block, :] = (first[block, :].astype(f32) + second[block, :].astype(f32)).astype(
                        bf16
                    )

                in_blocks(out.shape[0], add)
        else:
            out = outs.pop(0)

            def add_all(block, stays=stays, got=got, out=out):
                out[block, :] = (stays[block, :].astype(f32) + got[block, :].astype(f32)).astype(bf16)

            in_blocks(rows, add_all)


def combine(marks, plans, pairs, after):
    near = whole_spec()
    shapes = []
    for (now, later), (stays, got) in zip(plans, pairs):
        shape = list(got.shape)
        if now[0] == "gather":
            shape[now[1]] *= 2
            shapes.append(shape)
        elif later is not None and later[0] == "reduce":
            shape[later[1]] //= 2
            shapes += [shape, shape]
        else:
            shapes.append(shape)
    values = [value for pair in pairs for value in pair]
    return pl.pallas_call(
        functools.partial(combine_kernel, plans, len(after)),
        out_shape=[jax.ShapeDtypeStruct(shape, bf16) for shape in shapes],
        in_specs=[pl.BlockSpec(memory_space=pltpu.SMEM)]
        + [near] * len(values)
        + [pl.BlockSpec(memory_space=pl.ANY)] * len(after),
        out_specs=[near] * len(shapes),
        compiler_params=pltpu.CompilerParams(vmem_limit_bytes=44 * 2**20),
        cost_estimate=pl.CostEstimate(flops=0, bytes_accessed=1024, transcendentals=0),
        name="combine",
    )(marks, *values, *after)


def combine_plainly(marks, plans, pairs):
    outs = []
    for (now, later), (stays, got) in zip(plans, pairs):
        if now[0] == "gather":
            outs.append(
                jnp.where(
                    marks[now[2]] == 0,
                    jnp.concatenate([stays, got], axis=now[1]),
                    jnp.concatenate([got, stays], axis=now[1]),
                )
            )
            continue
        total = (stays.astype(f32) + got.astype(f32)).astype(bf16)
        if later is not None and later[0] == "reduce":
            size = total.shape[later[1]] // 2
            for place in (1 - marks[later[2]], marks[later[2]]):
                outs.append(lax.dynamic_slice_in_dim(total, place * size, size, axis=later[1]))
        else:
            outs.append(total)
    return outs


def flipped(value, axis, bit):
    pairs = [(place, place ^ (1 << bit)) for place in range(lax.axis_size(axis))]
    return lax.ppermute(value, axis, pairs)


class Travel:
    def __init__(self, marks, sends, keeps, orders):
        self.marks = marks
        self.plans = []
        self.aligned = True
        for value, order in zip(sends, orders):
            shape = list(value.shape)
            steps = []
            for bit in order:
                axis = 0 if shape[0] % 32 == 0 or shape[1] % 256 else 1
                if shape[axis] % (32, 256)[axis]:
                    self.aligned = False
                steps.append((axis, bit))
                shape[axis] //= 2
            self.plans.append(
                [("pair", 0, 0)]
                + [("reduce", *step) for step in steps]
                + [("gather", *step) for step in reversed(steps)]
            )
        self.stage = 0
        self.stays = list(keeps)
        self.got = [flipped(value, "section", 0) for value in sends]

    @property
    def done(self):
        return not self.got

    def pending(self):
        plans = []
        for plan in self.plans:
            later = plan[self.stage + 1] if self.stage + 1 < len(plan) else None
            plans.append((plan[self.stage], later))
        return plans, list(zip(self.stays, self.got))

    def accept(self, plans, outs):
        self.stage += 1
        self.stays, self.got = [], []
        for _, later in plans:
            sent = outs.pop(0)
            if later is not None and later[0] == "reduce":
                self.stays.append(outs.pop(0))
            else:
                self.stays.append(sent)
            if later is not None:
                self.got.append(flipped(sent, "wide", later[2]))


def joint_step(travels, after=()):
    travels = [travel for travel in travels if not travel.done]
    pending = [travel.pending() for travel in travels]
    plans = sum((item[0] for item in pending), [])
    pairs = sum((item[1] for item in pending), [])
    if all(travel.aligned for travel in travels):
        outs = list(combine(travels[0].marks, plans, pairs, after))
    else:
        outs = combine_plainly(travels[0].marks, plans, pairs)
    for travel, item in zip(travels, pending):
        travel.accept(item[0], outs)
    return sum((travel.stays for travel in travels), [])


def norm_stats(stream):
    mean_value = jnp.mean(stream, axis=-1, keepdims=True)
    centered = stream - mean_value
    variance = jnp.mean(centered * centered, axis=-1, keepdims=True)
    return centered * lax.rsqrt(variance + norm_epsilon)


def slot_plan(ids, rank, capacity):
    before = rank[None, :] < rank[:, None]
    first, second = ids[:, 0], ids[:, 1]
    same_first = (first[:, None] == first[None, :]) & before
    same_second = (second[:, None] == second[None, :]) & before
    crossed = second[:, None] == first[None, :]
    place_first = jnp.sum(same_first.astype(jnp.int32), axis=1)
    place_second = jnp.sum(same_second.astype(jnp.int32) + crossed.astype(jnp.int32), axis=1)
    slot_first = jnp.where(place_first < capacity, first * capacity + place_first, -1)
    slot_second = jnp.where(place_second < capacity, second * capacity + place_second, -1)
    return (jnp.where(first >= 0, slot_first, -1), jnp.where(second >= 0, slot_second, -1))


def body(
    patches,
    out_cotangent,
    attn_gain,
    qkv_weight,
    proj_weight,
    ffn_gain,
    mlp_in,
    mlp_out,
    router_weight,
    expert_in,
    expert_out,
    expert_ids,
    priority,
):
    expert_count = lax.axis_size("wide")
    sections = lax.axis_size("section")
    section = lax.axis_index("section")
    own_expert = lax.axis_index("wide")
    is_first = section == 0
    images = patches.shape[0] // sections
    length, width = patches.shape[1:]
    pad = -(-length // STEP) * STEP
    rows = images * pad
    capacity = max(2, images * length // expert_count)
    slots = expert_count * capacity
    levels = expert_count.bit_length() - 1
    assert 1 << levels == expert_count
    place = section[None]
    marks = (own_expert >> jnp.arange(levels, dtype=jnp.int32)) & 1
    bits = list(range(levels))
    third = max(1, levels // 3)
    groups = [bits[:third], bits[third : 2 * third], bits[2 * third : -1]]
    across_x = groups[0] + groups[1] + groups[2] + bits[-1:]
    across_y = groups[1] + groups[2] + groups[0] + bits[-1:]
    across_z = groups[2] + groups[0] + groups[1] + bits[-1:]

    def mine(whole):
        value = lax.dynamic_slice_in_dim(whole, section * images, images)
        return jnp.pad(value, ((0, 0), (0, pad - length), (0, 0))).reshape(rows, width)

    def swap(value):
        return flipped(value, "section", 0)

    def exchange(value):
        return lax.all_to_all(value, "wide", split_axis=0, concat_axis=0, tiled=True)

    def across(value):
        shape = (expert_count, capacity, value.shape[1])
        return exchange(value.reshape(shape)).reshape(value.shape)

    other_qkv, other_proj = swap(qkv_weight[0]), swap(proj_weight[0])
    gains = jnp.concatenate([attn_gain, ffn_gain], axis=0)
    other_gains = swap(gains)
    gains_one = jnp.where(is_first, gains, other_gains)
    gains_two = jnp.where(is_first, other_gains, gains)
    weights = (qkv_weight[0], other_qkv, proj_weight[0], other_proj)
    which_one = jnp.stack([(section == 0).astype(jnp.int32), section])
    which_two = jnp.stack([(section == 1).astype(jnp.int32), section])

    ids = lax.dynamic_slice_in_dim(expert_ids, section * images, images)
    ids = jnp.pad(ids, ((0, 0), (0, pad - length), (0, 0)), constant_values=-1).reshape(rows, 2)
    rank = lax.dynamic_slice_in_dim(priority, section, 1).reshape(images, length)
    rank = jnp.pad(rank, ((0, 0), (0, pad - length))).reshape(rows)
    slot_first, slot_second = slot_plan(ids, rank, capacity)
    slot_range = jnp.arange(slots, dtype=jnp.int32)
    pick_first = slot_first[:, None] == slot_range[None, :]
    pick_second = slot_second[:, None] == slot_range[None, :]
    pick_any = (pick_first | pick_second).astype(bf16)
    kept_first = (slot_first >= 0).astype(f32)[:, None]
    kept_second = (slot_second >= 0).astype(f32)[:, None]
    rival = jnp.sum(
        jnp.where(pick_first, ids[:, 1:], 0) + jnp.where(pick_second, ids[:, :1], 0), axis=0
    )
    cotangent = mine(out_cotangent)
    packet = jnp.concatenate(
        [
            tn(pick_any, cotangent).astype(bf16),
            jnp.broadcast_to(rival.astype(bf16)[:, None], (slots, PAIR)),
        ],
        axis=1,
    )

    stream_one = mine(patches)
    mixed_one, packed_one, mix_one, normed_one = attention_forward(
        which_one, stream_one, weights, gains_one[:1], gains_one[1:], images, length
    )
    arrived_packet = across(packet)
    hidden_one = nn(normed_one, mlp_in)
    active_one = jax.nn.gelu(hidden_one).astype(bf16)
    first_low = (mixed_one + nn(active_one, mlp_out)).astype(bf16)

    mixed_two, packed_two, mix_two, normed_two = attention_forward(
        which_two, first_low, weights, gains_two[:1], gains_two[1:], images, length
    )
    arrived = across(tn(pick_any, normed_two).astype(bf16))
    back, result, grad_expert_in, grad_expert_out = expert_pass(
        own_expert[None], arrived, arrived_packet, router_weight, expert_in, expert_out
    )
    back = across(back)
    result, back = lax.optimization_barrier((result, back))
    returned = across(result)
    other_expert_in, other_expert_out = swap(grad_expert_in), swap(grad_expert_out)

    expert_range = jnp.arange(expert_count, dtype=jnp.int32)
    logits = nn(normed_two, router_weight)
    one_hot = (ids[:, :, None] == expert_range[None, None, :]).astype(f32)
    chosen = jnp.sum(one_hot * logits[:, None, :], axis=-1)
    gates = jax.nn.softmax(chosen, axis=-1)
    low_first, low_second = pick_first.astype(bf16), pick_second.astype(bf16)
    grad_gates = jnp.concatenate(
        [
            jnp.sum(nn(low, back[:, width:]), axis=-1, keepdims=True)
            for low in (low_first, low_second)
        ],
        axis=1,
    )
    grad_chosen = gates * (grad_gates - jnp.sum(gates * grad_gates, axis=-1, keepdims=True))
    grad_logits = jnp.sum(one_hot * grad_chosen[:, :, None], axis=1).astype(bf16)
    grad_router = tn(grad_logits, normed_two)
    grad_normed_two = nn(pick_any, back[:, :width]) + nt(grad_logits, router_weight)
    second_low = (
        mixed_two
        + kept_first * gates[:, :1] * nn(low_first, returned)
        + kept_second * gates[:, 1:] * nn(low_second, returned)
    ).astype(bf16)
    grad_two, grad_first, small_two, grad_packed, total_low, low = attention_backward(
        which_two,
        first_low,
        mixed_two,
        cotangent,
        grad_normed_two,
        packed_two,
        mix_two,
        weights,
        gains_two[:1],
        gains_two[1:],
        images,
        length,
    )
    pieces = attention_products(
        place,
        low,
        mix_two,
        grad_packed,
        total_low,
        1,
        after=(other_expert_in, other_expert_out, returned),
    )
    two = Travel(marks, pieces[:1], pieces[1:], [across_x])
    grad_normed_one, in_send, in_keep, out_send, out_keep = mlp_backward(
        place, normed_one, grad_first, mlp_in, mlp_out, after=pieces[1:]
    )
    mlp_first = Travel(marks, [in_send], [in_keep], [across_z])
    mlp_second = Travel(marks, [out_send], [out_keep], [across_y])
    early = [two, mlp_first, mlp_second]
    grad_one, _, small_one, grad_packed, total_low, low = attention_backward(
        which_one,
        stream_one,
        mixed_one,
        grad_first,
        grad_normed_one,
        packed_one,
        mix_one,
        weights,
        gains_one[:1],
        gains_one[1:],
        images,
        length,
        after=joint_step(early),
    )
    pieces = attention_products(place, low, mix_one, grad_packed, total_low, 2)
    one = Travel(marks, pieces[:2], pieces[2:], [across_x, across_y])
    last = joint_step(early, after=pieces[2:])
    last = joint_step(early + [one], after=last)
    expert_in_sum = pair_total(grad_expert_in, other_expert_in, tuple(last))
    last = joint_step(early + [one], after=[expert_in_sum])
    expert_out_sum = pair_total(grad_expert_out, other_expert_out, tuple(last))
    last = joint_step(early + [one], after=[expert_out_sum])
    while not two.done:
        last = joint_step(early + [one], after=last)

    small = jnp.concatenate([small_one, small_two, grad_router], axis=0)
    other_small = swap(small)
    other_in, other_out = swap(mlp_first.stays[0]), swap(mlp_second.stays[0])
    last = joint_step([one], after=(other_small, other_in, other_out))
    mlp_in_sum = join_halves(place, mlp_first.stays[0], other_in, 0, tuple(last))
    mlp_out_sum = join_halves(place, mlp_second.stays[0], other_out, 1, (mlp_in_sum,))
    from_two = [lax.ppermute(value, "section", [(0, 1)]) for value in two.stays]
    last = [mlp_out_sum]
    while not one.done:
        last = joint_step([one], after=last)
    from_one = [lax.ppermute(value, "section", [(1, 0)]) for value in one.stays]
    qkv_grad, proj_grad = own_block(place, (one.stays, two.stays, from_one, from_two))

    def own_images(value_one, value_two):
        value_one, value_two = [
            value.reshape(images, pad, width)[:, :length] for value in (value_one, value_two)
        ]
        own = jnp.where(is_first, value_one, value_two)
        other = swap(jnp.where(is_first, value_two, value_one))
        return jnp.concatenate(
            [jnp.where(is_first, own, other), jnp.where(is_first, other, own)], axis=0
        )[None]

    small = small + other_small
    share = -(-small.shape[0] // expert_count)
    small = jnp.pad(small, ((0, share * expert_count - small.shape[0]), (0, 0)))
    small = jnp.sum(exchange(small.reshape(expert_count, share, width)), axis=0)
    small = exchange(jnp.broadcast_to(small[None], (expert_count, share, width)))
    small = small.reshape(expert_count * share, width)
    small_block = lax.dynamic_slice_in_dim(small, 8 * section, 8)
    return (
        own_images(first_low, second_low),
        own_images(grad_one, grad_first.astype(f32)),
        small_block[:1],
        qkv_grad[None],
        proj_grad[None],
        small_block[1:2],
        mlp_in_sum,
        mlp_out_sum,
        jnp.transpose(small[16 : 16 + expert_count]),
        expert_in_sum,
        expert_out_sum,
    )


def solution(mesh):
    in_specs = (
        P("wide", None, None),
        P("wide", None, None),
        P("section", None),
        P("section", None, None),
        P("section", None, None),
        P("section", None),
        P(),
        P(),
        P(),
        P("wide", None, None),
        P("wide", None, None),
        P("wide", None, None),
        P("wide", None),
    )
    out_specs = (
        P("section", "wide", None, None),
        P("section", "wide", None, None),
        P("section", None),
        P("section", None, None),
        P("section", None, None),
        P("section", None),
        P(),
        P(),
        P(),
        P("wide", None, None),
        P("wide", None, None),
    )
    return jax.shard_map(body, mesh=mesh, in_specs=in_specs, out_specs=out_specs, check_vma=False)
```

```python
import functools

import jax
import jax.numpy as jnp
from jax import lax
from jax.experimental import pallas as pl
from jax.experimental.pallas import tpu as pltpu
from jax.sharding import PartitionSpec as P

H = 12
HEAD = 64
PAIR = 2 * HEAD
STEP = 16
EXTRA = 256
norm_epsilon = 1e-06
bf16 = jnp.bfloat16
f32 = jnp.float32


def dot(left, right, dims):
    return lax.dot_general(left, right, (dims, ((), ())), preferred_element_type=f32)


def nn(left, right):
    return dot(left, right, ((1,), (0,)))


def nt(left, right):
    return dot(left, right, ((1,), (1,)))


def tn(left, right):
    return dot(left, right, ((0,), (0,)))


def norm_rows(value):
    mean_value = jnp.mean(value, axis=-1, keepdims=True)
    centered = value - mean_value
    scale = lax.rsqrt(jnp.mean(centered * centered, axis=-1, keepdims=True) + norm_epsilon)
    return (centered * scale, scale)


def norm_rows_back(unit, scale, gain, upstream):
    weighted = upstream * gain
    first = jnp.mean(weighted, axis=-1, keepdims=True)
    second = jnp.mean(weighted * unit, axis=-1, keepdims=True)
    return scale * (weighted - first - unit * second)


def folded(value):
    rows = value.shape[0]
    return sum(value[start : start + 8] for start in range(0, rows, 8))


def row_blocks(rows):
    return [slice(start, start + STEP) for start in range(0, rows, STEP)]


def fetch(take, own, other, target, sem):
    @pl.when(take == 1)
    def _():
        pltpu.make_async_copy(own, target, sem).start()

    @pl.when(take != 1)
    def _():
        pltpu.make_async_copy(other, target, sem).start()


def forward_kernel(
    images,
    length,
    which,
    x_ref,
    own_qkv,
    other_qkv,
    own_proj,
    other_proj,
    gain_a,
    gain_f,
    mixed_ref,
    packed_ref,
    mix_ref,
    normed_ref,
    qkv_ref,
    proj_ref,
    low_ref,
    sems,
):
    rows, width = x_ref.shape
    pad = rows // images
    fetch(which[0], own_qkv, other_qkv, qkv_ref, sems.at[0])
    fetch(which[0], own_proj, other_proj, proj_ref, sems.at[1])

    for block in row_blocks(rows):
        unit, scale = norm_rows(x_ref[block, :].astype(f32))
        low_ref[block, :] = (unit * gain_a[...]).astype(bf16)

    pltpu.make_async_copy(own_qkv, qkv_ref, sems.at[0]).wait()

    @pl.loop(0, 3 * width // 256)
    def _(step):
        lanes = pl.ds(pl.multiple_of(step * 256, 256), 256)
        packed_ref[:, lanes] = nn(low_ref[...], qkv_ref[:, lanes]).astype(bf16)

    left = lax.broadcasted_iota(jnp.int32, (pad, PAIR), 1) < HEAD
    live = lax.broadcasted_iota(jnp.int32, (pad, pad), 0) < length

    @pl.loop(0, width // PAIR)
    def _(pair):
        def lanes(part):
            return pl.ds(pl.multiple_of(part * width + pair * PAIR, PAIR), PAIR)

        for image in range(images):
            block = slice(image * pad, (image + 1) * pad)
            queries = packed_ref[block, lanes(0)].astype(f32) * HEAD ** (-0.5)
            keys = packed_ref[block, lanes(1)]
            values = packed_ref[block, lanes(2)].T
            outs = []
            for half, rows_half in ((left, slice(0, HEAD)), (~left, slice(HEAD, PAIR))):
                scores = nt(keys, jnp.where(half, queries, 0.0).astype(bf16))
                scores = jnp.where(live, scores, -jnp.inf)
                powers = jnp.exp(scores - jnp.max(scores, axis=0, keepdims=True))
                share = 1.0 / jnp.sum(powers, axis=0, keepdims=True)
                outs.append(nn(values[rows_half], powers.astype(bf16)) * share)
            mix_ref[block, lanes(0)] = jnp.concatenate(outs, axis=0).T.astype(bf16)

    pltpu.make_async_copy(own_proj, proj_ref, sems.at[1]).wait()

    @pl.loop(0, width // 256)
    def _(step):
        lanes = pl.ds(pl.multiple_of(step * 256, 256), 256)
        mixed_ref[:, lanes] = x_ref[:, lanes].astype(f32) + nn(mix_ref[...], proj_ref[:, lanes])

    for block in row_blocks(rows):
        unit, scale = norm_rows(mixed_ref[block, :])
        normed_ref[block, :] = (unit * gain_f[...]).astype(bf16)


def backward_kernel(
    images,
    length,
    which,
    x_ref,
    mixed_ref,
    base_ref,
    upstream_ref,
    packed_ref,
    mix_ref,
    own_qkv,
    other_qkv,
    own_proj,
    other_proj,
    gain_a,
    gain_f,
    grad_ref,
    grad_low,
    gains_ref,
    grad_packed,
    total_low,
    low_ref,
    qkv_ref,
    proj_ref,
    total_ref,
    grad_mix,
    sems,
):
    rows, width = x_ref.shape
    pad = rows // images
    fetch(which[0], own_proj, other_proj, proj_ref, sems.at[1])
    fetch(which[0], own_qkv, other_qkv, qkv_ref, sems.at[0])
    gain_total = jnp.zeros((8, width), f32)
    for block in row_blocks(rows):
        unit, scale = norm_rows(mixed_ref[block, :])
        upstream = upstream_ref[block, :]
        value = base_ref[block, :].astype(f32) + norm_rows_back(
            unit, scale, gain_f[...], upstream
        )
        total_ref[block, :] = value
        total_low[block, :] = value.astype(bf16)
        source_unit, source_scale = norm_rows(x_ref[block, :].astype(f32))
        low_ref[block, :] = (source_unit * gain_a[...]).astype(bf16)
        gain_total = gain_total + folded(upstream * unit)
    gains_ref[...] = jnp.zeros_like(gains_ref)
    gains_ref[1:2, :] = jnp.sum(gain_total, axis=0, keepdims=True)
    pltpu.make_async_copy(own_proj, proj_ref, sems.at[1]).wait()

    @pl.loop(0, width // 256)
    def _(step):
        lanes = pl.ds(pl.multiple_of(step * 256, 256), 256)
        grad_mix[:, lanes] = nt(total_low[...], proj_ref[lanes, :]).astype(bf16)

    left = lax.broadcasted_iota(jnp.int32, (pad, PAIR), 1) < HEAD
    live = lax.broadcasted_iota(jnp.int32, (pad, pad), 0) < length

    @pl.loop(0, width // PAIR)
    def _(pair):
        def lanes(part):
            return pl.ds(pl.multiple_of(part * width + pair * PAIR, PAIR), PAIR)

        for image in range(images):
            block = slice(image * pad, (image + 1) * pad)
            queries = packed_ref[block, lanes(0)].astype(f32) * HEAD ** (-0.5)
            keys = packed_ref[block, lanes(1)]
            values = packed_ref[block, lanes(2)]
            grads = grad_mix[block, lanes(0)]
            sums = [0.0, 0.0, 0.0]
            for half in (left, ~left):
                some_queries = jnp.where(half, queries, 0.0).astype(bf16)
                some_keys = jnp.where(half, keys, 0.0).astype(bf16)
                some_grads = jnp.where(half, grads, 0.0).astype(bf16)
                scores = nt(keys, some_queries)
                scores = jnp.where(live, scores, -jnp.inf)
                powers = jnp.exp(scores - jnp.max(scores, axis=0, keepdims=True))
                weights = powers * (1.0 / jnp.sum(powers, axis=0, keepdims=True))
                grad_weights = nt(values, some_grads)
                inner = jnp.sum(grad_weights * weights, axis=0, keepdims=True)
                grad_raw = (weights * (grad_weights - inner)).astype(bf16)
                sums[0] += tn(grad_raw, some_keys)
                sums[1] += nn(grad_raw, some_queries)
                sums[2] += nn(weights.astype(bf16), some_grads)
            sums[0] = sums[0] * HEAD ** (-0.5)
            for part in range(3):
                grad_packed[block, lanes(part)] = sums[part].astype(bf16)

    pltpu.make_async_copy(own_qkv, qkv_ref, sems.at[0]).wait()

    @pl.loop(0, width // 256)
    def _(step):
        lanes = pl.ds(pl.multiple_of(step * 256, 256), 256)
        grad_ref[:, lanes] = nt(grad_packed[...], qkv_ref[lanes, :])

    gain_total = jnp.zeros((8, width), f32)
    for block in row_blocks(rows):
        unit, scale = norm_rows(x_ref[block, :].astype(f32))
        upstream = grad_ref[block, :]
        value = total_ref[block, :] + norm_rows_back(unit, scale, gain_a[...], upstream)
        grad_ref[block, :] = value
        grad_low[block, :] = value.astype(bf16)
        gain_total = gain_total + folded(upstream * unit)
    gains_ref[0:1, :] = jnp.sum(gain_total, axis=0, keepdims=True)


def product_kernel(chunks, section, low_ref, mix_ref, grad_packed, total_low, small, outs):
    width = low_ref.shape[1]
    half_width = width // 2
    third = width // 3
    if small:
        router_ref, gains_one, gains_two, turned = small
        turned[...] = jnp.concatenate([gains_one[...], gains_two[...]], axis=0).T
    for which_half, targets in ((1 - section[0], outs[:chunks]), (section[0], outs[chunks:])):
        columns = pl.ds(pl.multiple_of(which_half * half_width, 128), half_width)
        left_rows = low_ref[:, columns].T
        right_rows = mix_ref[:, columns].T
        for step in range(12):
            if step < 9:
                value = nn(left_rows, grad_packed[:, step * third : (step + 1) * third])
            else:
                value = nn(right_rows, total_low[:, (step - 9) * third : (step - 8) * third])
            out, place = divmod(step, 12 // chunks)
            targets[out][:, place * third : (place + 1) * third] = value.astype(bf16)
        if small:
            out = targets[-1]
            start = 4 * width // chunks
            experts = router_ref.shape[1]
            out[:, start:] = jnp.zeros((half_width, EXTRA), bf16)
            out[:, start : start + experts] = router_ref[columns, :].astype(bf16)
            out[:, start + 128 : start + 144] = turned[columns, :].astype(bf16)


def attention_products(section, low, mix, grad_packed, total_low, chunks, small=(), after=()):
    rows, width = low.shape
    near = whole_spec()
    sizes = [4 * width // chunks] * chunks
    if small:
        sizes[-1] += EXTRA
    inputs = 4 + len(small)

    def kernel(section_ref, *refs):
        outs = refs[inputs + len(after) :]
        extra = (*refs[4:inputs], outs[2 * chunks]) if small else ()
        product_kernel(chunks, section_ref, *refs[:4], extra, outs[: 2 * chunks])

    return pl.pallas_call(
        kernel,
        out_shape=tuple(jax.ShapeDtypeStruct((width // 2, size), bf16) for size in sizes * 2),
        in_specs=[pl.BlockSpec(memory_space=pltpu.SMEM)]
        + [near] * inputs
        + [pl.BlockSpec(memory_space=pl.ANY)] * len(after),
        out_specs=(near,) * (2 * chunks),
        scratch_shapes=[pltpu.VMEM((width, 16), f32)] if small else [],
        compiler_params=pltpu.CompilerParams(vmem_limit_bytes=12 * 2**20),
        cost_estimate=pl.CostEstimate(
            flops=8 * rows * width * width, bytes_accessed=12 * 2**20, transcendentals=0
        ),
        name="attention_products",
    )(section, low, mix, grad_packed, total_low, *small, *after)


def whole_spec():
    return pl.BlockSpec(memory_space=pltpu.VMEM)


def attention_forward(which, x, weights, gain_a, gain_f, images, length):
    rows, width = x.shape
    far = pl.BlockSpec(memory_space=pl.ANY)
    near = whole_spec()
    return pl.pallas_call(
        functools.partial(forward_kernel, images, length),
        out_shape=(
            jax.ShapeDtypeStruct((rows, width), f32),
            jax.ShapeDtypeStruct((rows, 3 * width), bf16),
            jax.ShapeDtypeStruct((rows, width), bf16),
            jax.ShapeDtypeStruct((rows, width), bf16),
        ),
        in_specs=[pl.BlockSpec(memory_space=pltpu.SMEM), near, far, far, far, far, near, near],
        out_specs=(near, near, near, near),
        scratch_shapes=[
            pltpu.VMEM((width, 3 * width), bf16),
            pltpu.VMEM((width, width), bf16),
            pltpu.VMEM((rows, width), bf16),
            pltpu.SemaphoreType.DMA((2,)),
        ],
        compiler_params=pltpu.CompilerParams(vmem_limit_bytes=16 * 2**20),
        cost_estimate=pl.CostEstimate(
            flops=10 * rows * width * width, bytes_accessed=12 * 2**20, transcendentals=2**20
        ),
        name="attention_forward",
    )(which, x, *weights, gain_a, gain_f)


def attention_backward(
    which, x, mixed, base, upstream, packed, mix, weights, gain_a, gain_f, images, length, after=()
):
    rows, width = x.shape
    far = pl.BlockSpec(memory_space=pl.ANY)
    near = whole_spec()

    def kernel(*refs):
        backward_kernel(images, length, *refs[:13], *refs[13 + len(after) :])

    return pl.pallas_call(
        kernel,
        out_shape=(
            jax.ShapeDtypeStruct((rows, width), f32),
            jax.ShapeDtypeStruct((rows, width), bf16),
            jax.ShapeDtypeStruct((8, width), f32),
            jax.ShapeDtypeStruct((rows, 3 * width), bf16),
            jax.ShapeDtypeStruct((rows, width), bf16),
            jax.ShapeDtypeStruct((rows, width), bf16),
        ),
        in_specs=[pl.BlockSpec(memory_space=pltpu.SMEM)]
        + [near] * 6
        + [far] * 4
        + [near] * 2
        + [far] * len(after),
        out_specs=(near,) * 6,
        scratch_shapes=[
            pltpu.VMEM((width, 3 * width), bf16),
            pltpu.VMEM((width, width), bf16),
            pltpu.VMEM((rows, width), f32),
            pltpu.VMEM((rows, width), bf16),
            pltpu.SemaphoreType.DMA((2,)),
        ],
        compiler_params=pltpu.CompilerParams(vmem_limit_bytes=20 * 2**20),
        cost_estimate=pl.CostEstimate(
            flops=20 * rows * width * width, bytes_accessed=24 * 2**20, transcendentals=2**20
        ),
        name="attention_backward",
    )(which, x, mixed, base, upstream, packed, mix, *weights, gain_a, gain_f, *after)


def gelu_pair(hidden):
    cubic = 0.7978845608028654
    square = hidden * hidden
    curve = jnp.tanh(cubic * (hidden + 0.044715 * (square * hidden)))
    left = 0.5 * (1.0 + curve)
    slope = left + 0.5 * hidden * (1.0 - curve * curve) * (
        cubic * (1.0 + 3.0 * 0.044715 * square)
    )
    return (hidden * left, slope)


def mlp_kernel(
    section,
    x_ref,
    up_ref,
    in_ref,
    out_ref,
    grad_ref,
    in_send,
    in_keep,
    out_send,
    out_keep,
    x_turned,
):
    half = x_ref.shape[1] // 2

    @pl.when(pl.program_id(0) == 0)
    def _():
        x_turned[...] = x_ref[...].T
        grad_ref[...] = jnp.zeros_like(grad_ref)

    active, slope = gelu_pair(nn(x_ref[...], in_ref[...]))
    active = active.astype(bf16)
    grad_hidden = (nt(up_ref[...], out_ref[...]) * slope).astype(bf16)
    grad_ref[...] += nt(grad_hidden, in_ref[...])
    turned = active.T
    for which, first, second in (
        (1 - section[0], in_send, out_send),
        (section[0], in_keep, out_keep),
    ):
        block = pl.ds(pl.multiple_of(which * half, 128), half)
        first[...] = nn(x_turned[block, :], grad_hidden).astype(bf16)
        second[...] = nn(turned, up_ref[:, block]).astype(bf16)


def mlp_backward(section, x, up, weight_in, weight_out, after):
    rows, width = x.shape
    hidden = weight_in.shape[1]
    step = 512
    half = width // 2
    fixed = pl.BlockSpec((rows, width), lambda index, place: (0, 0))
    across = pl.BlockSpec((half, step), lambda index, place: (0, index))
    down = pl.BlockSpec((step, half), lambda index, place: (index, 0))

    def kernel(*refs):
        mlp_kernel(*refs[:5], *refs[5 + len(after) :])

    return pl.pallas_call(
        kernel,
        grid_spec=pltpu.PrefetchScalarGridSpec(
            num_scalar_prefetch=1,
            grid=(hidden // step,),
            in_specs=[
                fixed,
                fixed,
                pl.BlockSpec((width, step), lambda index, place: (0, index)),
                pl.BlockSpec((step, width), lambda index, place: (index, 0)),
            ]
            + [pl.BlockSpec(memory_space=pl.ANY)] * len(after),
            out_specs=(fixed, across, across, down, down),
            scratch_shapes=[pltpu.VMEM((width, rows), bf16)],
        ),
        out_shape=(
            jax.ShapeDtypeStruct((rows, width), f32),
            jax.ShapeDtypeStruct((half, hidden), bf16),
            jax.ShapeDtypeStruct((half, hidden), bf16),
            jax.ShapeDtypeStruct((hidden, half), bf16),
            jax.ShapeDtypeStruct((hidden, half), bf16),
        ),
        compiler_params=pltpu.CompilerParams(vmem_limit_bytes=24 * 2**20),
        cost_estimate=pl.CostEstimate(
            flops=10 * rows * width * hidden,
            bytes_accessed=24 * 2**20,
            transcendentals=rows * hidden,
        ),
        name="mlp_backward",
    )(section, x, up, weight_in, weight_out, *after)


def expert_kernel(
    own,
    x_ref,
    packet_ref,
    router_ref,
    in_ref,
    out_ref,
    back_ref,
    result_ref,
    in_grad,
    out_grad,
    x_turned,
    up_ref,
    total_ref,
    grad_ref,
):
    slots, width = x_ref.shape

    @pl.when(pl.program_id(0) == 0)
    def _():
        x_turned[...] = x_ref[...].T
        grad_ref[...] = jnp.zeros_like(grad_ref)
        total_ref[...] = jnp.zeros_like(total_ref)
        logits = nn(x_ref[...], router_ref[...])
        experts = lax.broadcasted_iota(jnp.int32, logits.shape, 1)
        rival = packet_ref[:, width : width + 1].astype(f32).astype(jnp.int32)
        own_logit = jnp.sum(jnp.where(experts == own[0], logits, 0.0), axis=1, keepdims=True)
        rival_logit = jnp.sum(jnp.where(experts == rival, logits, 0.0), axis=1, keepdims=True)
        top = jnp.maximum(own_logit, rival_logit)
        power = jnp.exp(own_logit - top)
        gate = power / (power + jnp.exp(rival_logit - top))
        up_ref[...] = (gate * packet_ref[:, :width].astype(f32)).astype(bf16)

    active, slope = gelu_pair(nn(x_ref[...], in_ref[0]))
    active = active.astype(bf16)
    total_ref[...] += nn(active, out_ref[0])
    grad_hidden = (nt(up_ref[...], out_ref[0]) * slope).astype(bf16)
    grad_ref[...] += nt(grad_hidden, in_ref[0])
    in_grad[...] = nn(x_turned[...], grad_hidden).astype(bf16)
    out_grad[...] = nn(active.T, up_ref[...]).astype(bf16)

    @pl.when(pl.program_id(0) == pl.num_programs(0) - 1)
    def _():
        result = total_ref[...].astype(bf16)
        result_ref[...] = result
        back_ref[:, :width] = grad_ref[...].astype(bf16)
        rest = jnp.sum(
            packet_ref[:, :width].astype(f32) * result.astype(f32), axis=1, keepdims=True
        )
        lanes = lax.broadcasted_iota(jnp.int32, (slots, PAIR), 1)
        value = jnp.zeros((slots, PAIR), f32)
        for lane in range(3):
            part = rest.astype(bf16).astype(f32)
            value = jnp.where(lanes == lane, part, value)
            rest = rest - part
        back_ref[:, width:] = value.astype(bf16)


def expert_pass(own, x, packet, router, weight_in, weight_out):
    slots, width = x.shape
    hidden = weight_in.shape[2]
    step = 512

    def fixed(shape):
        return pl.BlockSpec(shape, lambda index, place: (0, 0))

    return pl.pallas_call(
        expert_kernel,
        grid_spec=pltpu.PrefetchScalarGridSpec(
            num_scalar_prefetch=1,
            grid=(hidden // step,),
            in_specs=[
                fixed(x.shape),
                fixed(packet.shape),
                fixed(router.shape),
                pl.BlockSpec((1, width, step), lambda index, place: (0, 0, index)),
                pl.BlockSpec((1, step, width), lambda index, place: (0, index, 0)),
            ],
            out_specs=(
                fixed(packet.shape),
                fixed(x.shape),
                pl.BlockSpec((width, step), lambda index, place: (0, index)),
                pl.BlockSpec((step, width), lambda index, place: (index, 0)),
            ),
            scratch_shapes=[
                pltpu.VMEM((width, slots), bf16),
                pltpu.VMEM((slots, width), bf16),
                pltpu.VMEM((slots, width), f32),
                pltpu.VMEM((slots, width), f32),
            ],
        ),
        out_shape=(
            jax.ShapeDtypeStruct(packet.shape, bf16),
            jax.ShapeDtypeStruct(x.shape, bf16),
            jax.ShapeDtypeStruct((width, hidden), bf16),
            jax.ShapeDtypeStruct((hidden, width), bf16),
        ),
        compiler_params=pltpu.CompilerParams(vmem_limit_bytes=24 * 2**20),
        cost_estimate=pl.CostEstimate(
            flops=12 * slots * width * hidden,
            bytes_accessed=24 * 2**20,
            transcendentals=slots * hidden,
        ),
        name="expert_pass",
    )(own, x, packet, router, weight_in, weight_out)


def join_kernel(section, mine_ref, other_ref, *rest):
    out_ref = rest[-1]

    @pl.when(pl.program_id(0) == section[0])
    def _():
        out_ref[...] = mine_ref[...].astype(f32)

    @pl.when(pl.program_id(0) != section[0])
    def _():
        out_ref[...] = other_ref[...].astype(f32)


def join_halves(section, mine, other, axis, after):
    rows, width = mine.shape
    steps = 3
    block = (rows // steps, width)

    def mine_map(which, step, place):
        return (jnp.where(which == place[0], step, 0), 0)

    def other_map(which, step, place):
        return (jnp.where(which == place[0], 0, step), 0)

    def out_map(which, step, place):
        return (which * steps + step, 0) if axis == 0 else (step, which)

    return pl.pallas_call(
        join_kernel,
        grid_spec=pltpu.PrefetchScalarGridSpec(
            num_scalar_prefetch=1,
            grid=(2, steps),
            in_specs=[pl.BlockSpec(block, mine_map), pl.BlockSpec(block, other_map)]
            + [pl.BlockSpec(memory_space=pl.ANY)] * len(after),
            out_specs=pl.BlockSpec(block, out_map),
        ),
        out_shape=jax.ShapeDtypeStruct(
            (2 * rows, width) if axis == 0 else (rows, 2 * width), f32
        ),
        compiler_params=pltpu.CompilerParams(vmem_limit_bytes=16 * 2**20),
        cost_estimate=pl.CostEstimate(
            flops=0, bytes_accessed=12 * rows * width, transcendentals=0
        ),
        name="join_halves",
    )(section, mine, other, *after)


def block_kernel(counts, section, *refs):
    refs = list(refs)
    sources = [[refs.pop(0) for _ in range(count)] for count in counts]
    qkv_out, proj_out = refs
    own = pl.program_id(0) == section[0]
    cut = qkv_out.shape[1]

    def emit(parts):
        start = 0
        for part in parts:
            size = min(part.shape[1], cut + proj_out.shape[1] - start)
            left = max(0, min(size, cut - start))
            if left:
                qkv_out[:, start : start + left] = part[:, :left].astype(f32)
            if left < size:
                proj_out[:, start + left - cut : start + size - cut] = part[:, left:size].astype(f32)
            start += size

    for index, parts in enumerate(sources):
        place, mine = index % 2, index < 2

        @pl.when((own == mine) & (section[0] == place))
        def _():
            emit(parts)


def own_block(section, groups):
    half = groups[0][0].shape[0]
    width = 2 * half
    steps = 3
    specs = []
    for index, parts in enumerate(groups):

        def place_map(which, step, section, place=index % 2, mine=index < 2):
            wanted = (section[0] == place) & ((which == section[0]) == mine)
            return (jnp.where(wanted, step, 0), 0)

        specs += [pl.BlockSpec((half // steps, part.shape[1]), place_map) for part in parts]

    def out_map(which, step, section):
        return (which * steps + step, 0)

    return pl.pallas_call(
        functools.partial(block_kernel, [len(parts) for parts in groups]),
        grid_spec=pltpu.PrefetchScalarGridSpec(
            num_scalar_prefetch=1,
            grid=(2, steps),
            in_specs=specs,
            out_specs=(
                pl.BlockSpec((half // steps, 3 * width), out_map),
                pl.BlockSpec((half // steps, width), out_map),
            ),
        ),
        out_shape=(
            jax.ShapeDtypeStruct((2 * half, 3 * width), f32),
            jax.ShapeDtypeStruct((2 * half, width), f32),
        ),
        compiler_params=pltpu.CompilerParams(vmem_limit_bytes=16 * 2**20),
        cost_estimate=pl.CostEstimate(
            flops=0, bytes_accessed=48 * half * width, transcendentals=0
        ),
        name="own_block",
    )(section, *[part for parts in groups for part in parts])


def total_kernel(mine_ref, other_ref, *rest):
    rest[-1][0] = mine_ref[...].astype(f32) + other_ref[...].astype(f32)


def pair_total(mine, other, after):
    rows, width = mine.shape
    steps = 6
    block = pl.BlockSpec((rows // steps, width), lambda step: (step, 0))
    return pl.pallas_call(
        total_kernel,
        grid=(steps,),
        in_specs=[block, block] + [pl.BlockSpec(memory_space=pl.ANY)] * len(after),
        out_specs=pl.BlockSpec((1, rows // steps, width), lambda step: (0, step, 0)),
        out_shape=jax.ShapeDtypeStruct((1, rows, width), f32),
        compiler_params=pltpu.CompilerParams(vmem_limit_bytes=12 * 2**20),
        cost_estimate=pl.CostEstimate(
            flops=rows * width, bytes_accessed=8 * rows * width, transcendentals=0
        ),
        name="pair_total",
    )(mine, other, *after)


def span(axis, start, size):
    multiple = size & -size
    piece = pl.ds(pl.multiple_of(start * size, multiple), size)
    return (piece, slice(None)) if axis == 0 else (slice(None), piece)


def in_blocks(rows, work):
    size = next(size for size in (96, 64, 48, 32, 16) if rows % size == 0)
    if rows == size:
        work(slice(0, rows))
    else:

        @pl.loop(0, rows // size)
        def _(step):
            work(pl.ds(pl.multiple_of(step * size, size), size))


def combine_kernel(plans, extra, marks, *refs):
    count = len(plans)
    sources, outs = refs[: 2 * count], list(refs[2 * count + extra :])
    for index, (now, later) in enumerate(plans):
        stays, got = sources[2 * index : 2 * index + 2]
        rows, width = got.shape
        if now[0] == "gather":
            out = outs.pop(0)
            mine = marks[now[2]]
            for source, place in ((stays, mine), (got, 1 - mine)):
                target = out.at[span(now[1], place, got.shape[now[1]])]

                def move(block, source=source, target=target):
                    target[block, :] = source[block, :]

                in_blocks(rows, move)
        elif later is not None and later[0] == "reduce":
            mine = marks[later[2]]
            for place in (1 - mine, mine):
                out = outs.pop(0)
                window = span(later[1], place, out.shape[later[1]])
                first, second = stays.at[window], got.at[window]

                def add(block, first=first, second=second, out=out):
                    out[block, :] = first[block, :] + second[block, :]

                in_blocks(out.shape[0], add)
        else:
            out = outs.pop(0)

            def add_all(block, stays=stays, got=got, out=out):
                out[block, :] = stays[block, :] + got[block, :]

            in_blocks(rows, add_all)


def combine(marks, plans, pairs, after):
    near = whole_spec()
    shapes = []
    for (now, later), (stays, got) in zip(plans, pairs):
        shape = list(got.shape)
        if now[0] == "gather":
            shape[now[1]] *= 2
            shapes.append(shape)
        elif later is not None and later[0] == "reduce":
            shape[later[1]] //= 2
            shapes += [shape, shape]
        else:
            shapes.append(shape)
    values = [value for pair in pairs for value in pair]
    return pl.pallas_call(
        functools.partial(combine_kernel, plans, len(after)),
        out_shape=[jax.ShapeDtypeStruct(shape, bf16) for shape in shapes],
        in_specs=[pl.BlockSpec(memory_space=pltpu.SMEM)]
        + [near] * len(values)
        + [pl.BlockSpec(memory_space=pl.ANY)] * len(after),
        out_specs=[near] * len(shapes),
        compiler_params=pltpu.CompilerParams(vmem_limit_bytes=8 * 2**20),
        cost_estimate=pl.CostEstimate(flops=0, bytes_accessed=1024, transcendentals=0),
        name="combine",
    )(marks, *values, *after)


def combine_plainly(marks, plans, pairs):
    outs = []
    for (now, later), (stays, got) in zip(plans, pairs):
        if now[0] == "gather":
            outs.append(
                jnp.where(
                    marks[now[2]] == 0,
                    jnp.concatenate([stays, got], axis=now[1]),
                    jnp.concatenate([got, stays], axis=now[1]),
                )
            )
            continue
        total = stays + got
        if later is not None and later[0] == "reduce":
            size = total.shape[later[1]] // 2
            for place in (1 - marks[later[2]], marks[later[2]]):
                outs.append(lax.dynamic_slice_in_dim(total, place * size, size, axis=later[1]))
        else:
            outs.append(total)
    return outs


def flipped(value, axis, bit):
    pairs = [(place, place ^ (1 << bit)) for place in range(lax.axis_size(axis))]
    return lax.ppermute(value, axis, pairs)


class Travel:
    def __init__(self, marks, sends, keeps, orders):
        self.marks = marks
        self.plans = []
        self.aligned = True
        for value, order in zip(sends, orders):
            shape = list(value.shape)
            steps = []
            for bit in order:
                axis = 0 if shape[0] % 32 == 0 or shape[1] % 256 else 1
                if shape[axis] % (32, 256)[axis]:
                    self.aligned = False
                steps.append((axis, bit))
                shape[axis] //= 2
            self.plans.append(
                [("pair", 0, 0)]
                + [("reduce", *step) for step in steps]
                + [("gather", *step) for step in reversed(steps)]
            )
        self.stage = 0
        self.stays = list(keeps)
        self.got = [flipped(value, "section", 0) for value in sends]

    @property
    def done(self):
        return not self.got

    def pending(self):
        plans = []
        for plan in self.plans:
            later = plan[self.stage + 1] if self.stage + 1 < len(plan) else None
            plans.append((plan[self.stage], later))
        return plans, list(zip(self.stays, self.got))

    def accept(self, plans, outs):
        self.stage += 1
        self.stays, self.got = [], []
        for _, later in plans:
            sent = outs.pop(0)
            if later is not None and later[0] == "reduce":
                self.stays.append(outs.pop(0))
            else:
                self.stays.append(sent)
            if later is not None:
                self.got.append(flipped(sent, "wide", later[2]))


def joint_step(travels, after=()):
    travels = [travel for travel in travels if not travel.done]
    pending = [travel.pending() for travel in travels]
    plans = sum((item[0] for item in pending), [])
    pairs = sum((item[1] for item in pending), [])
    if all(travel.aligned for travel in travels):
        outs = list(combine(travels[0].marks, plans, pairs, after))
    else:
        outs = combine_plainly(travels[0].marks, plans, pairs)
    for travel, item in zip(travels, pending):
        travel.accept(item[0], outs)
    return sum((travel.stays for travel in travels), [])


def pad_kernel(section, x_ref, out_ref):
    out_ref[...] = jnp.zeros_like(out_ref)
    out_ref[0, : x_ref.shape[1], :] = x_ref[0]


def padded_images(section, value, images, pad):
    length, width = value.shape[1:]
    out = pl.pallas_call(
        pad_kernel,
        grid_spec=pltpu.PrefetchScalarGridSpec(
            num_scalar_prefetch=1,
            grid=(images,),
            in_specs=[
                pl.BlockSpec(
                    (1, length, width), lambda index, place: (place[0] * images + index, 0, 0)
                )
            ],
            out_specs=pl.BlockSpec((1, pad, width), lambda index, place: (index, 0, 0)),
        ),
        out_shape=jax.ShapeDtypeStruct((images, pad, width), value.dtype),
        compiler_params=pltpu.CompilerParams(vmem_limit_bytes=8 * 2**20),
        cost_estimate=pl.CostEstimate(flops=0, bytes_accessed=4 * value.size, transcendentals=0),
        name="padded_images",
    )(section, value)
    return out.reshape(images * pad, width)


def images_kernel(section, one_ref, two_ref, from_one, from_two, *rest):
    out_ref = rest[-1]
    own = pl.program_id(0) == section[0]
    for place, mine, other in ((0, one_ref, from_one), (1, two_ref, from_two)):
        for source, wanted in ((mine, own), (other, jnp.logical_not(own))):

            @pl.when(wanted & (section[0] == place))
            def _():
                out_ref[0, 0] = source[0, : out_ref.shape[2], :].astype(out_ref.dtype)


def own_images(section, one, two, from_one, from_two, images, length, dtype, after):
    rows, width = one.shape
    pad = rows // images
    sources = [value.reshape(images, pad, width) for value in (one, two, from_one, from_two)]
    specs = []
    for index in range(4):

        def place_map(which, image, section, place=index % 2, mine=index < 2):
            wanted = (section[0] == place) & ((which == section[0]) == mine)
            return (jnp.where(wanted, image, 0), 0, 0)

        specs.append(pl.BlockSpec((1, pad, width), place_map))
    return pl.pallas_call(
        images_kernel,
        grid_spec=pltpu.PrefetchScalarGridSpec(
            num_scalar_prefetch=1,
            grid=(2, images),
            in_specs=specs + [pl.BlockSpec(memory_space=pl.ANY)] * len(after),
            out_specs=pl.BlockSpec(
                (1, 1, length, width),
                lambda which, image, section: (0, which * images + image, 0, 0),
            ),
        ),
        out_shape=jax.ShapeDtypeStruct((1, 2 * images, length, width), dtype),
        compiler_params=pltpu.CompilerParams(vmem_limit_bytes=16 * 2**20),
        cost_estimate=pl.CostEstimate(flops=0, bytes_accessed=12 * one.size, transcendentals=0),
        name="own_images",
    )(section, *sources, *after)


def norm_stats(stream):
    mean_value = jnp.mean(stream, axis=-1, keepdims=True)
    centered = stream - mean_value
    variance = jnp.mean(centered * centered, axis=-1, keepdims=True)
    return centered * lax.rsqrt(variance + norm_epsilon)


def slot_plan(ids, rank, capacity):
    before = rank[None, :] < rank[:, None]
    first, second = ids[:, 0], ids[:, 1]
    same_first = (first[:, None] == first[None, :]) & before
    same_second = (second[:, None] == second[None, :]) & before
    crossed = second[:, None] == first[None, :]
    place_first = jnp.sum(same_first.astype(jnp.int32), axis=1)
    place_second = jnp.sum(same_second.astype(jnp.int32) + crossed.astype(jnp.int32), axis=1)
    slot_first = jnp.where(place_first < capacity, first * capacity + place_first, -1)
    slot_second = jnp.where(place_second < capacity, second * capacity + place_second, -1)
    return (jnp.where(first >= 0, slot_first, -1), jnp.where(second >= 0, slot_second, -1))


def body(
    patches,
    out_cotangent,
    attn_gain,
    qkv_weight,
    proj_weight,
    ffn_gain,
    mlp_in,
    mlp_out,
    router_weight,
    expert_in,
    expert_out,
    expert_ids,
    priority,
):
    expert_count = lax.axis_size("wide")
    sections = lax.axis_size("section")
    section = lax.axis_index("section")
    own_expert = lax.axis_index("wide")
    is_first = section == 0
    images = patches.shape[0] // sections
    length, width = patches.shape[1:]
    pad = -(-length // STEP) * STEP
    rows = images * pad
    capacity = max(2, images * length // expert_count)
    slots = expert_count * capacity
    levels = expert_count.bit_length() - 1
    assert 1 << levels == expert_count
    place = section[None]
    marks = (own_expert >> jnp.arange(levels, dtype=jnp.int32)) & 1
    bits = list(range(levels))
    third = max(1, levels // 3)
    groups = [bits[:third], bits[third : 2 * third], bits[2 * third : -1]]
    across_x = groups[0] + groups[1] + groups[2] + bits[-1:]
    across_y = groups[1] + groups[2] + groups[0] + bits[-1:]
    across_z = groups[2] + groups[0] + groups[1] + bits[-1:]

    def swap(value):
        return flipped(value, "section", 0)

    def exchange(value):
        return lax.all_to_all(value, "wide", split_axis=0, concat_axis=0, tiled=True)

    def across(value):
        shape = (expert_count, capacity, value.shape[1])
        return exchange(value.reshape(shape)).reshape(value.shape)

    other_qkv, other_proj = swap(qkv_weight[0]), swap(proj_weight[0])
    gains = jnp.concatenate([attn_gain, ffn_gain], axis=0)
    other_gains = swap(gains)
    gains_one = jnp.where(is_first, gains, other_gains)
    gains_two = jnp.where(is_first, other_gains, gains)
    weights = (qkv_weight[0], other_qkv, proj_weight[0], other_proj)
    which_one = jnp.stack([(section == 0).astype(jnp.int32), section])
    which_two = jnp.stack([(section == 1).astype(jnp.int32), section])

    ids = lax.dynamic_slice_in_dim(expert_ids, section * images, images)
    ids = jnp.pad(ids, ((0, 0), (0, pad - length), (0, 0)), constant_values=-1).reshape(rows, 2)
    rank = lax.dynamic_slice_in_dim(priority, section, 1).reshape(images, length)
    rank = jnp.pad(rank, ((0, 0), (0, pad - length))).reshape(rows)
    slot_first, slot_second = slot_plan(ids, rank, capacity)
    slot_range = jnp.arange(slots, dtype=jnp.int32)
    pick_first = slot_first[:, None] == slot_range[None, :]
    pick_second = slot_second[:, None] == slot_range[None, :]
    pick_any = (pick_first | pick_second).astype(bf16)
    kept_first = (slot_first >= 0).astype(f32)[:, None]
    kept_second = (slot_second >= 0).astype(f32)[:, None]
    rival = jnp.sum(
        jnp.where(pick_first, ids[:, 1:], 0) + jnp.where(pick_second, ids[:, :1], 0), axis=0
    )
    cotangent = padded_images(place, out_cotangent, images, pad)
    packet = jnp.concatenate(
        [
            tn(pick_any, cotangent).astype(bf16),
            jnp.broadcast_to(rival.astype(bf16)[:, None], (slots, PAIR)),
        ],
        axis=1,
    )

    stream_one = padded_images(place, patches, images, pad)
    mixed_one, packed_one, mix_one, normed_one = attention_forward(
        which_one, stream_one, weights, gains_one[:1], gains_one[1:], images, length
    )
    arrived_packet = across(packet)
    hidden_one = nn(normed_one, mlp_in)
    active_one = jax.nn.gelu(hidden_one).astype(bf16)
    first_low = (mixed_one + nn(active_one, mlp_out)).astype(bf16)

    mixed_two, packed_two, mix_two, normed_two = attention_forward(
        which_two, first_low, weights, gains_two[:1], gains_two[1:], images, length
    )
    arrived = across(tn(pick_any, normed_two).astype(bf16))
    back, result, grad_expert_in, grad_expert_out = expert_pass(
        own_expert[None], arrived, arrived_packet, router_weight, expert_in, expert_out
    )
    back = across(back)
    result, back = lax.optimization_barrier((result, back))
    returned = across(result)
    other_expert_in, other_expert_out = swap(grad_expert_in), swap(grad_expert_out)

    from_low_one = lax.ppermute(first_low, "section", [(1, 0)])
    expert_range = jnp.arange(expert_count, dtype=jnp.int32)
    logits = nn(normed_two, router_weight)
    one_hot = (ids[:, :, None] == expert_range[None, None, :]).astype(f32)
    chosen = jnp.sum(one_hot * logits[:, None, :], axis=-1)
    gates = jax.nn.softmax(chosen, axis=-1)
    low_first, low_second = pick_first.astype(bf16), pick_second.astype(bf16)
    grad_gates = jnp.concatenate(
        [
            jnp.sum(nn(low, back[:, width:]), axis=-1, keepdims=True)
            for low in (low_first, low_second)
        ],
        axis=1,
    )
    grad_chosen = gates * (grad_gates - jnp.sum(gates * grad_gates, axis=-1, keepdims=True))
    grad_logits = jnp.sum(one_hot * grad_chosen[:, :, None], axis=1).astype(bf16)
    grad_router = tn(normed_two, grad_logits)
    grad_normed_two = nn(pick_any, back[:, :width]) + nt(grad_logits, router_weight)
    second_low = (
        mixed_two
        + kept_first * gates[:, :1] * nn(low_first, returned)
        + kept_second * gates[:, 1:] * nn(low_second, returned)
    ).astype(bf16)
    grad_two, grad_first, small_two, grad_packed, total_low, low = attention_backward(
        which_two,
        first_low,
        mixed_two,
        cotangent,
        grad_normed_two,
        packed_two,
        mix_two,
        weights,
        gains_two[:1],
        gains_two[1:],
        images,
        length,
    )
    pieces = attention_products(
        place,
        low,
        mix_two,
        grad_packed,
        total_low,
        1,
        after=(other_expert_in, other_expert_out, returned, from_low_one),
    )
    two = Travel(marks, pieces[:1], pieces[1:], [across_x])
    grad_normed_one, in_send, in_keep, out_send, out_keep = mlp_backward(
        place, normed_one, grad_first, mlp_in, mlp_out, after=pieces[1:]
    )
    mlp_first = Travel(marks, [in_send], [in_keep], [across_z])
    mlp_second = Travel(marks, [out_send], [out_keep], [across_y])
    early = [two, mlp_first, mlp_second]
    from_grad_two = lax.ppermute(grad_first, "section", [(0, 1)])
    grad_one, _, small_one, grad_packed, total_low, low = attention_backward(
        which_one,
        stream_one,
        mixed_one,
        grad_first,
        grad_normed_one,
        packed_one,
        mix_one,
        weights,
        gains_one[:1],
        gains_one[1:],
        images,
        length,
        after=joint_step(early) + [from_grad_two],
    )
    pieces = attention_products(
        place,
        low,
        mix_one,
        grad_packed,
        total_low,
        2,
        small=(grad_router, small_one, small_two),
    )
    one = Travel(marks, pieces[:2], pieces[2:], [across_x, across_y])
    last = joint_step(early, after=pieces[2:])
    last = joint_step(early + [one], after=last)
    expert_in_sum = pair_total(grad_expert_in, other_expert_in, tuple(last))
    last = joint_step(early + [one], after=[expert_in_sum, second_low])
    expert_out_sum = pair_total(grad_expert_out, other_expert_out, tuple(last))
    last = joint_step(early + [one], after=[expert_out_sum])
    while not two.done:
        last = joint_step(early + [one], after=last)

    other_in, other_out = swap(mlp_first.stays[0]), swap(mlp_second.stays[0])
    last = joint_step([one], after=(other_in, other_out))
    late_low, late_grad, *last = lax.optimization_barrier((second_low, grad_one, *last))
    from_low_two = lax.ppermute(late_low, "section", [(0, 1)])
    from_grad_one = lax.ppermute(late_grad, "section", [(1, 0)])
    mlp_in_sum = join_halves(place, mlp_first.stays[0], other_in, 0, tuple(last))
    mlp_out_sum = join_halves(place, mlp_second.stays[0], other_out, 1, (mlp_in_sum,))
    from_two = [lax.ppermute(value, "section", [(0, 1)]) for value in two.stays]
    last = [mlp_out_sum]
    while not one.done:
        last = joint_step([one], after=last)
    activations = own_images(
        place, first_low, second_low, from_low_one, from_low_two, images, length, bf16, last
    )
    input_grads = own_images(
        place, grad_one, grad_first, from_grad_one, from_grad_two, images, length, f32, last
    )
    from_one = [lax.ppermute(value, "section", [(1, 0)]) for value in one.stays]
    qkv_grad, proj_grad = own_block(place, (one.stays, two.stays, from_one, from_two))
    small = one.stays[1][:, 2 * width :]
    other_small = swap(small)
    small = jnp.concatenate(
        [jnp.where(is_first, small, other_small), jnp.where(is_first, other_small, small)], axis=0
    ).astype(f32)
    gain_sums = jnp.transpose(small[:, 128:144])
    small_block = lax.dynamic_slice_in_dim(gain_sums, 8 * section, 8)
    return (
        activations,
        input_grads,
        small_block[:1],
        qkv_grad[None],
        proj_grad[None],
        small_block[1:2],
        mlp_in_sum,
        mlp_out_sum,
        small[:, :expert_count],
        expert_in_sum,
        expert_out_sum,
    )


def solution(mesh):
    in_specs = (
        P("wide", None, None),
        P("wide", None, None),
        P("section", None),
        P("section", None, None),
        P("section", None, None),
        P("section", None),
        P(),
        P(),
        P(),
        P("wide", None, None),
        P("wide", None, None),
        P("wide", None, None),
        P("wide", None),
    )
    out_specs = (
        P("section", "wide", None, None),
        P("section", "wide", None, None),
        P("section", None),
        P("section", None, None),
        P("section", None, None),
        P("section", None),
        P(),
        P(),
        P(),
        P("wide", None, None),
        P("wide", None, None),
    )
    return jax.shard_map(body, mesh=mesh, in_specs=in_specs, out_specs=out_specs, check_vma=False)
```

```python
import functools

import jax
import jax.numpy as jnp
from jax import lax
from jax.experimental import pallas as pl
from jax.experimental.pallas import tpu as pltpu
from jax.sharding import PartitionSpec as P

H = 12
HEAD = 64
PAIR = 2 * HEAD
STEP = 16
EXTRA = 256
norm_epsilon = 1e-06
bf16 = jnp.bfloat16
f32 = jnp.float32


def dot(left, right, dims):
    return lax.dot_general(left, right, (dims, ((), ())), preferred_element_type=f32)


def nn(left, right):
    return dot(left, right, ((1,), (0,)))


def nt(left, right):
    return dot(left, right, ((1,), (1,)))


def tn(left, right):
    return dot(left, right, ((0,), (0,)))


def norm_rows(value):
    mean_value = jnp.mean(value, axis=-1, keepdims=True)
    centered = value - mean_value
    scale = lax.rsqrt(jnp.mean(centered * centered, axis=-1, keepdims=True) + norm_epsilon)
    return (centered * scale, scale)


def norm_rows_back(unit, scale, gain, upstream):
    weighted = upstream * gain
    first = jnp.mean(weighted, axis=-1, keepdims=True)
    second = jnp.mean(weighted * unit, axis=-1, keepdims=True)
    return scale * (weighted - first - unit * second)


def folded(value):
    rows = value.shape[0]
    return sum(value[start : start + 8] for start in range(0, rows, 8))


def row_blocks(rows):
    return [slice(start, start + STEP) for start in range(0, rows, STEP)]


def fetch(take, own, other, target, sem):
    @pl.when(take == 1)
    def _():
        pltpu.make_async_copy(own, target, sem).start()

    @pl.when(take != 1)
    def _():
        pltpu.make_async_copy(other, target, sem).start()


def forward_kernel(
    images,
    length,
    which,
    x_ref,
    own_qkv,
    other_qkv,
    own_proj,
    other_proj,
    gain_a,
    gain_f,
    mixed_ref,
    packed_out,
    mix_out,
    normed_ref,
    qkv_ref,
    proj_ref,
    low_ref,
    packed_ref,
    mix_ref,
    sems,
):
    rows, width = x_ref.shape
    pad = rows // images
    packed_copy = pltpu.make_async_copy(packed_ref, packed_out, sems.at[2])
    mix_copy = pltpu.make_async_copy(mix_ref, mix_out, sems.at[3])
    fetch(which[0], own_qkv, other_qkv, qkv_ref, sems.at[0])
    fetch(which[0], own_proj, other_proj, proj_ref, sems.at[1])

    for block in row_blocks(rows):
        unit, scale = norm_rows(x_ref[block, :].astype(f32))
        low_ref[block, :] = (unit * gain_a[...]).astype(bf16)

    pltpu.make_async_copy(own_qkv, qkv_ref, sems.at[0]).wait()

    @pl.loop(0, 3 * width // 256)
    def _(step):
        lanes = pl.ds(pl.multiple_of(step * 256, 256), 256)
        packed_ref[:, lanes] = nn(low_ref[...], qkv_ref[:, lanes]).astype(bf16)

    packed_copy.start()
    left = lax.broadcasted_iota(jnp.int32, (pad, PAIR), 1) < HEAD
    live = lax.broadcasted_iota(jnp.int32, (pad, pad), 0) < length

    @pl.loop(0, width // PAIR)
    def _(pair):
        def lanes(part):
            return pl.ds(pl.multiple_of(part * width + pair * PAIR, PAIR), PAIR)

        for image in range(images):
            block = slice(image * pad, (image + 1) * pad)
            queries = packed_ref[block, lanes(0)].astype(f32) * HEAD ** (-0.5)
            keys = packed_ref[block, lanes(1)]
            values = packed_ref[block, lanes(2)].T
            outs = []
            for half, rows_half in ((left, slice(0, HEAD)), (~left, slice(HEAD, PAIR))):
                scores = nt(keys, jnp.where(half, queries, 0.0).astype(bf16))
                scores = jnp.where(live, scores, -jnp.inf)
                powers = jnp.exp(scores - jnp.max(scores, axis=0, keepdims=True))
                share = 1.0 / jnp.sum(powers, axis=0, keepdims=True)
                outs.append(nn(values[rows_half], powers.astype(bf16)) * share)
            mix_ref[block, lanes(0)] = jnp.concatenate(outs, axis=0).T.astype(bf16)

    mix_copy.start()
    pltpu.make_async_copy(own_proj, proj_ref, sems.at[1]).wait()

    @pl.loop(0, width // 256)
    def _(step):
        lanes = pl.ds(pl.multiple_of(step * 256, 256), 256)
        mixed_ref[:, lanes] = x_ref[:, lanes].astype(f32) + nn(mix_ref[...], proj_ref[:, lanes])

    for block in row_blocks(rows):
        unit, scale = norm_rows(mixed_ref[block, :])
        normed_ref[block, :] = (unit * gain_f[...]).astype(bf16)
    packed_copy.wait()
    mix_copy.wait()


def backward_kernel(
    images,
    length,
    chunks,
    which,
    x_ref,
    mixed_ref,
    base_ref,
    upstream_ref,
    packed_in,
    mix_in,
    own_qkv,
    other_qkv,
    own_proj,
    other_proj,
    gain_a,
    gain_f,
    small,
    grad_out,
    gains_ref,
    pieces,
    grad_ref,
    grad_packed,
    total_low,
    low_ref,
    qkv_ref,
    proj_ref,
    total_ref,
    grad_mix,
    packed_ref,
    mix_ref,
    staged,
    turned,
    sems,
):
    rows, width = x_ref.shape
    pad = rows // images
    packed_copy = pltpu.make_async_copy(packed_in, packed_ref, sems.at[2])
    mix_copy = pltpu.make_async_copy(mix_in, mix_ref, sems.at[3])
    packed_copy.start()
    mix_copy.start()
    fetch(which[0], own_proj, other_proj, proj_ref, sems.at[1])
    fetch(which[0], own_qkv, other_qkv, qkv_ref, sems.at[0])
    gain_total = jnp.zeros((8, width), f32)
    for block in row_blocks(rows):
        unit, scale = norm_rows(mixed_ref[block, :])
        upstream = upstream_ref[block, :]
        value = base_ref[block, :].astype(f32) + norm_rows_back(
            unit, scale, gain_f[...], upstream
        )
        total_ref[block, :] = value
        total_low[block, :] = value.astype(bf16)
        source_unit, source_scale = norm_rows(x_ref[block, :].astype(f32))
        low_ref[block, :] = (source_unit * gain_a[...]).astype(bf16)
        gain_total = gain_total + folded(upstream * unit)
    gains_ref[...] = jnp.zeros_like(gains_ref)
    gains_ref[1:2, :] = jnp.sum(gain_total, axis=0, keepdims=True)
    pltpu.make_async_copy(own_proj, proj_ref, sems.at[1]).wait()

    @pl.loop(0, width // 256)
    def _(step):
        lanes = pl.ds(pl.multiple_of(step * 256, 256), 256)
        grad_mix[:, lanes] = nt(total_low[...], proj_ref[lanes, :]).astype(bf16)

    packed_copy.wait()
    left = lax.broadcasted_iota(jnp.int32, (pad, PAIR), 1) < HEAD
    live = lax.broadcasted_iota(jnp.int32, (pad, pad), 0) < length

    @pl.loop(0, width // PAIR)
    def _(pair):
        def lanes(part):
            return pl.ds(pl.multiple_of(part * width + pair * PAIR, PAIR), PAIR)

        for image in range(images):
            block = slice(image * pad, (image + 1) * pad)
            queries = packed_ref[block, lanes(0)].astype(f32) * HEAD ** (-0.5)
            keys = packed_ref[block, lanes(1)]
            values = packed_ref[block, lanes(2)]
            grads = grad_mix[block, lanes(0)]
            sums = [0.0, 0.0, 0.0]
            for half in (left, ~left):
                some_queries = jnp.where(half, queries, 0.0).astype(bf16)
                some_keys = jnp.where(half, keys, 0.0).astype(bf16)
                some_grads = jnp.where(half, grads, 0.0).astype(bf16)
                scores = nt(keys, some_queries)
                scores = jnp.where(live, scores, -jnp.inf)
                powers = jnp.exp(scores - jnp.max(scores, axis=0, keepdims=True))
                weights = powers * (1.0 / jnp.sum(powers, axis=0, keepdims=True))
                grad_weights = nt(values, some_grads)
                inner = jnp.sum(grad_weights * weights, axis=0, keepdims=True)
                grad_raw = (weights * (grad_weights - inner)).astype(bf16)
                sums[0] += tn(grad_raw, some_keys)
                sums[1] += nn(grad_raw, some_queries)
                sums[2] += nn(weights.astype(bf16), some_grads)
            sums[0] = sums[0] * HEAD ** (-0.5)
            for part in range(3):
                grad_packed[block, lanes(part)] = sums[part].astype(bf16)

    mix_copy.wait()
    third = width // 3
    for side, place in ((0, 1 - which[1]), (1, which[1])):
        columns = pl.ds(pl.multiple_of(place * (width // 2), 128), width // 2)
        left_rows = low_ref[:, columns].T
        right_rows = mix_ref[:, columns].T
        for step in range(12):
            if step < 9:
                value = nn(left_rows, grad_packed[:, step * third : (step + 1) * third])
            else:
                value = nn(right_rows, total_low[:, (step - 9) * third : (step - 8) * third])
            out, spot = divmod(step, 12 // chunks)
            staged[side * chunks + out][:, spot * third : (spot + 1) * third] = value.astype(bf16)
        for index in range(side * chunks, (side + 1) * chunks - bool(small)):
            pltpu.make_async_copy(staged[index], pieces[index], sems.at[4 + index]).start()

    pltpu.make_async_copy(own_qkv, qkv_ref, sems.at[0]).wait()

    @pl.loop(0, width // 256)
    def _(step):
        lanes = pl.ds(pl.multiple_of(step * 256, 256), 256)
        grad_ref[:, lanes] = nt(grad_packed[...], qkv_ref[lanes, :])

    gain_total = jnp.zeros((8, width), f32)
    for block in row_blocks(rows):
        unit, scale = norm_rows(x_ref[block, :].astype(f32))
        upstream = grad_ref[block, :]
        value = total_ref[block, :] + norm_rows_back(unit, scale, gain_a[...], upstream)
        grad_out[block, :] = value.astype(grad_out.dtype)
        gain_total = gain_total + folded(upstream * unit)
    gains_ref[0:1, :] = jnp.sum(gain_total, axis=0, keepdims=True)
    half_width = width // 2
    if small:
        turned[...] = jnp.concatenate([gains_ref[...], small[1][...]], axis=0).T
        for index, place in ((chunks - 1, 1 - which[1]), (2 * chunks - 1, which[1])):
            block = pl.ds(pl.multiple_of(place * half_width, 128), half_width)
            out = staged[index]
            start = out.shape[1] - EXTRA
            out[:, start:] = jnp.zeros((half_width, EXTRA), bf16)
            out[:, start : start + small[0].shape[1]] = small[0][block, :].astype(bf16)
            out[:, start + 128 : start + 144] = turned[block, :].astype(bf16)
        for index in (chunks - 1, 2 * chunks - 1):
            pltpu.make_async_copy(staged[index], pieces[index], sems.at[4 + index]).start()
    for index in range(2 * chunks):
        pltpu.make_async_copy(staged[index], pieces[index], sems.at[4 + index]).wait()


def whole_spec():
    return pl.BlockSpec(memory_space=pltpu.VMEM)


def kept_far(value):
    return pltpu.with_memory_space_constraint(value, pltpu.HBM)


def attention_forward(which, x, weights, gain_a, gain_f, images, length):
    rows, width = x.shape
    far = pl.BlockSpec(memory_space=pltpu.HBM)
    near = whole_spec()
    return pl.pallas_call(
        functools.partial(forward_kernel, images, length),
        out_shape=(
            jax.ShapeDtypeStruct((rows, width), f32),
            pltpu.HBM((rows, 3 * width), bf16),
            pltpu.HBM((rows, width), bf16),
            jax.ShapeDtypeStruct((rows, width), bf16),
        ),
        in_specs=[pl.BlockSpec(memory_space=pltpu.SMEM), near, far, far, far, far, near, near],
        out_specs=(near, far, far, near),
        scratch_shapes=[
            pltpu.VMEM((width, 3 * width), bf16),
            pltpu.VMEM((width, width), bf16),
            pltpu.VMEM((rows, width), bf16),
            pltpu.VMEM((rows, 3 * width), bf16),
            pltpu.VMEM((rows, width), bf16),
            pltpu.SemaphoreType.DMA((4,)),
        ],
        compiler_params=pltpu.CompilerParams(vmem_limit_bytes=24 * 2**20),
        cost_estimate=pl.CostEstimate(
            flops=10 * rows * width * width, bytes_accessed=12 * 2**20, transcendentals=2**20
        ),
        name="attention_forward",
    )(which, x, *[kept_far(value) for value in weights], gain_a, gain_f)


def attention_backward(
    which,
    x,
    mixed,
    base,
    upstream,
    packed,
    mix,
    weights,
    gain_a,
    gain_f,
    images,
    length,
    chunks,
    dtype,
    small=(),
    after=(),
):
    rows, width = x.shape
    far = pl.BlockSpec(memory_space=pltpu.HBM)
    near = whole_spec()
    sizes = [4 * width // chunks] * chunks
    if small:
        sizes[-1] += EXTRA
    sizes = sizes * 2
    first_out = 13 + len(small) + len(after)

    def kernel(*refs):
        outs = refs[first_out : first_out + 2 + 2 * chunks]
        scratch = refs[first_out + 2 + 2 * chunks :]
        backward_kernel(
            images,
            length,
            chunks,
            *refs[:13],
            refs[13 : 13 + len(small)],
            outs[0],
            outs[1],
            outs[2:],
            *scratch[:10],
            scratch[10 : 10 + 2 * chunks],
            *scratch[10 + 2 * chunks :],
        )

    return pl.pallas_call(
        kernel,
        out_shape=(
            jax.ShapeDtypeStruct((rows, width), dtype),
            jax.ShapeDtypeStruct((8, width), f32),
        )
        + tuple(pltpu.HBM((width // 2, size), bf16) for size in sizes),
        in_specs=[pl.BlockSpec(memory_space=pltpu.SMEM)]
        + [near] * 4
        + [far] * 6
        + [near] * (2 + len(small))
        + [pl.BlockSpec(memory_space=pl.ANY)] * len(after),
        out_specs=(near, near) + (far,) * (2 * chunks),
        scratch_shapes=[
            pltpu.VMEM((rows, width), f32),
            pltpu.VMEM((rows, 3 * width), bf16),
            pltpu.VMEM((rows, width), bf16),
            pltpu.VMEM((rows, width), bf16),
            pltpu.VMEM((width, 3 * width), bf16),
            pltpu.VMEM((width, width), bf16),
            pltpu.VMEM((rows, width), f32),
            pltpu.VMEM((rows, width), bf16),
            pltpu.VMEM((rows, 3 * width), bf16),
            pltpu.VMEM((rows, width), bf16),
        ]
        + [pltpu.VMEM((width // 2, size), bf16) for size in sizes]
        + [pltpu.VMEM((width, 16), f32), pltpu.SemaphoreType.DMA((4 + 2 * chunks,))],
        compiler_params=pltpu.CompilerParams(vmem_limit_bytes=32 * 2**20),
        cost_estimate=pl.CostEstimate(
            flops=28 * rows * width * width, bytes_accessed=24 * 2**20, transcendentals=2**20
        ),
        name="attention_backward",
    )(
        which,
        x,
        mixed,
        base,
        upstream,
        *[kept_far(value) for value in (packed, mix, *weights)],
        gain_a,
        gain_f,
        *small,
        *after,
    )


def gelu_pair(hidden):
    cubic = 0.7978845608028654
    square = hidden * hidden
    curve = jnp.tanh(cubic * (hidden + 0.044715 * (square * hidden)))
    left = 0.5 * (1.0 + curve)
    slope = left + 0.5 * hidden * (1.0 - curve * curve) * (
        cubic * (1.0 + 3.0 * 0.044715 * square)
    )
    return (hidden * left, slope)


def mlp_kernel(
    section,
    x_ref,
    up_ref,
    in_ref,
    out_ref,
    grad_ref,
    in_send,
    in_keep,
    out_send,
    out_keep,
    x_turned,
):
    half = x_ref.shape[1] // 2

    @pl.when(pl.program_id(0) == 0)
    def _():
        x_turned[...] = x_ref[...].T
        grad_ref[...] = jnp.zeros_like(grad_ref)

    active, slope = gelu_pair(nn(x_ref[...], in_ref[...]))
    active = active.astype(bf16)
    grad_hidden = (nt(up_ref[...], out_ref[...]) * slope).astype(bf16)
    grad_ref[...] += nt(grad_hidden, in_ref[...])
    turned = active.T
    for which, first, second in (
        (1 - section[0], in_send, out_send),
        (section[0], in_keep, out_keep),
    ):
        block = pl.ds(pl.multiple_of(which * half, 128), half)
        first[...] = nn(x_turned[block, :], grad_hidden).astype(bf16)
        second[...] = nn(turned, up_ref[:, block]).astype(bf16)


def mlp_backward(section, x, up, weight_in, weight_out, after):
    rows, width = x.shape
    hidden = weight_in.shape[1]
    step = 512
    half = width // 2
    fixed = pl.BlockSpec((rows, width), lambda index, place: (0, 0))
    across = pl.BlockSpec((half, step), lambda index, place: (0, index))
    down = pl.BlockSpec((step, half), lambda index, place: (index, 0))

    def kernel(*refs):
        mlp_kernel(*refs[:5], *refs[5 + len(after) :])

    return pl.pallas_call(
        kernel,
        grid_spec=pltpu.PrefetchScalarGridSpec(
            num_scalar_prefetch=1,
            grid=(hidden // step,),
            in_specs=[
                fixed,
                fixed,
                pl.BlockSpec((width, step), lambda index, place: (0, index)),
                pl.BlockSpec((step, width), lambda index, place: (index, 0)),
            ]
            + [pl.BlockSpec(memory_space=pl.ANY)] * len(after),
            out_specs=(fixed, across, across, down, down),
            scratch_shapes=[pltpu.VMEM((width, rows), bf16)],
        ),
        out_shape=(
            jax.ShapeDtypeStruct((rows, width), f32),
            pltpu.HBM((half, hidden), bf16),
            pltpu.HBM((half, hidden), bf16),
            pltpu.HBM((hidden, half), bf16),
            pltpu.HBM((hidden, half), bf16),
        ),
        compiler_params=pltpu.CompilerParams(vmem_limit_bytes=44 * 2**20),
        cost_estimate=pl.CostEstimate(
            flops=10 * rows * width * hidden,
            bytes_accessed=24 * 2**20,
            transcendentals=rows * hidden,
        ),
        name="mlp_backward",
    )(section, x, up, weight_in, weight_out, *after)


def expert_kernel(
    own,
    x_ref,
    packet_ref,
    router_ref,
    in_ref,
    out_ref,
    back_ref,
    result_ref,
    in_grad,
    out_grad,
    x_turned,
    up_ref,
    total_ref,
    grad_ref,
):
    slots, width = x_ref.shape

    @pl.when(pl.program_id(0) == 0)
    def _():
        x_turned[...] = x_ref[...].T
        grad_ref[...] = jnp.zeros_like(grad_ref)
        total_ref[...] = jnp.zeros_like(total_ref)
        logits = nn(x_ref[...], router_ref[...])
        experts = lax.broadcasted_iota(jnp.int32, logits.shape, 1)
        rival = packet_ref[:, width : width + 1].astype(f32).astype(jnp.int32)
        own_logit = jnp.sum(jnp.where(experts == own[0], logits, 0.0), axis=1, keepdims=True)
        rival_logit = jnp.sum(jnp.where(experts == rival, logits, 0.0), axis=1, keepdims=True)
        top = jnp.maximum(own_logit, rival_logit)
        power = jnp.exp(own_logit - top)
        gate = power / (power + jnp.exp(rival_logit - top))
        up_ref[...] = (gate * packet_ref[:, :width].astype(f32)).astype(bf16)

    active, slope = gelu_pair(nn(x_ref[...], in_ref[0]))
    active = active.astype(bf16)
    total_ref[...] += nn(active, out_ref[0])
    grad_hidden = (nt(up_ref[...], out_ref[0]) * slope).astype(bf16)
    grad_ref[...] += nt(grad_hidden, in_ref[0])
    in_grad[...] = nn(x_turned[...], grad_hidden).astype(bf16)
    out_grad[...] = nn(active.T, up_ref[...]).astype(bf16)

    @pl.when(pl.program_id(0) == pl.num_programs(0) - 1)
    def _():
        result = total_ref[...].astype(bf16)
        result_ref[...] = result
        back_ref[:, :width] = grad_ref[...].astype(bf16)
        rest = jnp.sum(
            packet_ref[:, :width].astype(f32) * result.astype(f32), axis=1, keepdims=True
        )
        lanes = lax.broadcasted_iota(jnp.int32, (slots, PAIR), 1)
        value = jnp.zeros((slots, PAIR), f32)
        for lane in range(3):
            part = rest.astype(bf16).astype(f32)
            value = jnp.where(lanes == lane, part, value)
            rest = rest - part
        back_ref[:, width:] = value.astype(bf16)


def expert_pass(own, x, packet, router, weight_in, weight_out):
    slots, width = x.shape
    hidden = weight_in.shape[2]
    step = 512

    def fixed(shape):
        return pl.BlockSpec(shape, lambda index, place: (0, 0))

    return pl.pallas_call(
        expert_kernel,
        grid_spec=pltpu.PrefetchScalarGridSpec(
            num_scalar_prefetch=1,
            grid=(hidden // step,),
            in_specs=[
                fixed(x.shape),
                fixed(packet.shape),
                fixed(router.shape),
                pl.BlockSpec((1, width, step), lambda index, place: (0, 0, index)),
                pl.BlockSpec((1, step, width), lambda index, place: (0, index, 0)),
            ],
            out_specs=(
                fixed(packet.shape),
                fixed(x.shape),
                pl.BlockSpec((width, step), lambda index, place: (0, index)),
                pl.BlockSpec((step, width), lambda index, place: (index, 0)),
            ),
            scratch_shapes=[
                pltpu.VMEM((width, slots), bf16),
                pltpu.VMEM((slots, width), bf16),
                pltpu.VMEM((slots, width), f32),
                pltpu.VMEM((slots, width), f32),
            ],
        ),
        out_shape=(
            jax.ShapeDtypeStruct(packet.shape, bf16),
            jax.ShapeDtypeStruct(x.shape, bf16),
            pltpu.HBM((width, hidden), bf16),
            pltpu.HBM((hidden, width), bf16),
        ),
        compiler_params=pltpu.CompilerParams(vmem_limit_bytes=44 * 2**20),
        cost_estimate=pl.CostEstimate(
            flops=12 * slots * width * hidden,
            bytes_accessed=24 * 2**20,
            transcendentals=slots * hidden,
        ),
        name="expert_pass",
    )(own, x, packet, router, weight_in, weight_out)


def join_kernel(section, mine_ref, other_ref, *rest):
    out_ref = rest[-1]

    @pl.when(pl.program_id(0) == section[0])
    def _():
        out_ref[...] = mine_ref[...].astype(f32)

    @pl.when(pl.program_id(0) != section[0])
    def _():
        out_ref[...] = other_ref[...].astype(f32)


def join_halves(section, mine, other, axis, after):
    rows, width = mine.shape
    steps = 3
    block = (rows // steps, width)

    def mine_map(which, step, place):
        return (jnp.where(which == place[0], step, 0), 0)

    def other_map(which, step, place):
        return (jnp.where(which == place[0], 0, step), 0)

    def out_map(which, step, place):
        return (which * steps + step, 0) if axis == 0 else (step, which)

    return pl.pallas_call(
        join_kernel,
        grid_spec=pltpu.PrefetchScalarGridSpec(
            num_scalar_prefetch=1,
            grid=(2, steps),
            in_specs=[pl.BlockSpec(block, mine_map), pl.BlockSpec(block, other_map)]
            + [pl.BlockSpec(memory_space=pl.ANY)] * len(after),
            out_specs=pl.BlockSpec(block, out_map),
        ),
        out_shape=pltpu.HBM((2 * rows, width) if axis == 0 else (rows, 2 * width), f32),
        compiler_params=pltpu.CompilerParams(vmem_limit_bytes=44 * 2**20),
        cost_estimate=pl.CostEstimate(
            flops=0, bytes_accessed=12 * rows * width, transcendentals=0
        ),
        name="join_halves",
    )(section, mine, other, *after)


def block_kernel(counts, section, *refs):
    refs = list(refs)
    sources = [[refs.pop(0) for _ in range(count)] for count in counts]
    qkv_out, proj_out = refs
    own = pl.program_id(0) == section[0]
    cut = qkv_out.shape[1]

    def emit(parts):
        start = 0
        for part in parts:
            size = min(part.shape[1], cut + proj_out.shape[1] - start)
            left = max(0, min(size, cut - start))
            if left:
                qkv_out[:, start : start + left] = part[:, :left].astype(f32)
            if left < size:
                proj_out[:, start + left - cut : start + size - cut] = part[:, left:size].astype(f32)
            start += size

    for index, parts in enumerate(sources):
        place, mine = index % 2, index < 2

        @pl.when((own == mine) & (section[0] == place))
        def _():
            emit(parts)


def own_block(section, groups):
    half = groups[0][0].shape[0]
    width = 2 * half
    steps = 3
    specs = []
    for index, parts in enumerate(groups):

        def place_map(which, step, section, place=index % 2, mine=index < 2):
            wanted = (section[0] == place) & ((which == section[0]) == mine)
            return (jnp.where(wanted, step, 0), 0)

        specs += [pl.BlockSpec((half // steps, part.shape[1]), place_map) for part in parts]

    def out_map(which, step, section):
        return (which * steps + step, 0)

    return pl.pallas_call(
        functools.partial(block_kernel, [len(parts) for parts in groups]),
        grid_spec=pltpu.PrefetchScalarGridSpec(
            num_scalar_prefetch=1,
            grid=(2, steps),
            in_specs=specs,
            out_specs=(
                pl.BlockSpec((half // steps, 3 * width), out_map),
                pl.BlockSpec((half // steps, width), out_map),
            ),
        ),
        out_shape=(
            pltpu.HBM((2 * half, 3 * width), f32),
            pltpu.HBM((2 * half, width), f32),
        ),
        compiler_params=pltpu.CompilerParams(vmem_limit_bytes=44 * 2**20),
        cost_estimate=pl.CostEstimate(
            flops=0, bytes_accessed=48 * half * width, transcendentals=0
        ),
        name="own_block",
    )(section, *[part for parts in groups for part in parts])


def total_kernel(mine_ref, other_ref, *rest):
    rest[-1][0] = mine_ref[...].astype(f32) + other_ref[...].astype(f32)


def pair_total(mine, other, after):
    rows, width = mine.shape
    steps = 6
    block = pl.BlockSpec((rows // steps, width), lambda step: (step, 0))
    return pl.pallas_call(
        total_kernel,
        grid=(steps,),
        in_specs=[block, block] + [pl.BlockSpec(memory_space=pl.ANY)] * len(after),
        out_specs=pl.BlockSpec((1, rows // steps, width), lambda step: (0, step, 0)),
        out_shape=pltpu.HBM((1, rows, width), f32),
        compiler_params=pltpu.CompilerParams(vmem_limit_bytes=44 * 2**20),
        cost_estimate=pl.CostEstimate(
            flops=rows * width, bytes_accessed=8 * rows * width, transcendentals=0
        ),
        name="pair_total",
    )(mine, other, *after)


def span(axis, start, size):
    multiple = size & -size
    piece = pl.ds(pl.multiple_of(start * size, multiple), size)
    return (piece, slice(None)) if axis == 0 else (slice(None), piece)


def in_blocks(rows, work):
    size = next(size for size in (96, 64, 48, 32, 16) if rows % size == 0)
    if rows == size:
        work(slice(0, rows))
    else:

        @pl.loop(0, rows // size)
        def _(step):
            work(pl.ds(pl.multiple_of(step * size, size), size))


def combine_kernel(plans, extra, marks, *refs):
    count = len(plans)
    sources, outs = refs[: 2 * count], list(refs[2 * count + extra :])
    for index, (now, later) in enumerate(plans):
        stays, got = sources[2 * index : 2 * index + 2]
        rows, width = got.shape
        if now[0] == "gather":
            out = outs.pop(0)
            mine = marks[now[2]]
            for source, place in ((stays, mine), (got, 1 - mine)):
                target = out.at[span(now[1], place, got.shape[now[1]])]

                def move(block, source=source, target=target):
                    target[block, :] = source[block, :]

                in_blocks(rows, move)
        elif later is not None and later[0] == "reduce":
            mine = marks[later[2]]
            for place in (1 - mine, mine):
                out = outs.pop(0)
                window = span(later[1], place, out.shape[later[1]])
                first, second = stays.at[window], got.at[window]

                def add(block, first=first, second=second, out=out):
                    out[block, :] = first[block, :] + second[block, :]

                in_blocks(out.shape[0], add)
        else:
            out = outs.pop(0)

            def add_all(block, stays=stays, got=got, out=out):
                out[block, :] = stays[block, :] + got[block, :]

            in_blocks(rows, add_all)


def combine(marks, plans, pairs, after):
    near = whole_spec()
    shapes = []
    for (now, later), (stays, got) in zip(plans, pairs):
        shape = list(got.shape)
        if now[0] == "gather":
            shape[now[1]] *= 2
            shapes.append(shape)
        elif later is not None and later[0] == "reduce":
            shape[later[1]] //= 2
            shapes += [shape, shape]
        else:
            shapes.append(shape)
    values = [value for pair in pairs for value in pair]
    return pl.pallas_call(
        functools.partial(combine_kernel, plans, len(after)),
        out_shape=[jax.ShapeDtypeStruct(shape, bf16) for shape in shapes],
        in_specs=[pl.BlockSpec(memory_space=pltpu.SMEM)]
        + [near] * len(values)
        + [pl.BlockSpec(memory_space=pl.ANY)] * len(after),
        out_specs=[near] * len(shapes),
        compiler_params=pltpu.CompilerParams(vmem_limit_bytes=8 * 2**20),
        cost_estimate=pl.CostEstimate(flops=0, bytes_accessed=1024, transcendentals=0),
        name="combine",
    )(marks, *values, *after)


def combine_plainly(marks, plans, pairs):
    outs = []
    for (now, later), (stays, got) in zip(plans, pairs):
        if now[0] == "gather":
            outs.append(
                jnp.where(
                    marks[now[2]] == 0,
                    jnp.concatenate([stays, got], axis=now[1]),
                    jnp.concatenate([got, stays], axis=now[1]),
                )
            )
            continue
        total = stays + got
        if later is not None and later[0] == "reduce":
            size = total.shape[later[1]] // 2
            for place in (1 - marks[later[2]], marks[later[2]]):
                outs.append(lax.dynamic_slice_in_dim(total, place * size, size, axis=later[1]))
        else:
            outs.append(total)
    return outs


def flipped(value, axis, bit):
    pairs = [(place, place ^ (1 << bit)) for place in range(lax.axis_size(axis))]
    return lax.ppermute(value, axis, pairs)


class Travel:
    def __init__(self, marks, sends, keeps, orders):
        self.marks = marks
        self.plans = []
        self.aligned = True
        for value, order in zip(sends, orders):
            shape = list(value.shape)
            steps = []
            for bit in order:
                axis = 0 if shape[0] % 32 == 0 or shape[1] % 256 else 1
                if shape[axis] % (32, 256)[axis]:
                    self.aligned = False
                steps.append((axis, bit))
                shape[axis] //= 2
            self.plans.append(
                [("pair", 0, 0)]
                + [("reduce", *step) for step in steps]
                + [("gather", *step) for step in reversed(steps)]
            )
        self.stage = 0
        self.stays = list(keeps)
        self.got = [flipped(value, "section", 0) for value in sends]

    @property
    def done(self):
        return not self.got

    def pending(self):
        plans = []
        for plan in self.plans:
            later = plan[self.stage + 1] if self.stage + 1 < len(plan) else None
            plans.append((plan[self.stage], later))
        return plans, list(zip(self.stays, self.got))

    def accept(self, plans, outs):
        self.stage += 1
        self.stays, self.got = [], []
        for _, later in plans:
            sent = outs.pop(0)
            if later is not None and later[0] == "reduce":
                self.stays.append(outs.pop(0))
            else:
                self.stays.append(sent)
            if later is not None:
                self.got.append(flipped(sent, "wide", later[2]))


def joint_step(travels, after=()):
    travels = [travel for travel in travels if not travel.done]
    pending = [travel.pending() for travel in travels]
    plans = sum((item[0] for item in pending), [])
    pairs = sum((item[1] for item in pending), [])
    if all(travel.aligned for travel in travels):
        outs = list(combine(travels[0].marks, plans, pairs, after))
    else:
        outs = combine_plainly(travels[0].marks, plans, pairs)
    for travel, item in zip(travels, pending):
        travel.accept(item[0], outs)
    return sum((travel.stays for travel in travels), [])


def pad_kernel(section, x_ref, out_ref):
    out_ref[...] = jnp.zeros_like(out_ref)
    out_ref[0, : x_ref.shape[1], :] = x_ref[0]


def padded_images(section, value, images, pad):
    length, width = value.shape[1:]
    out = pl.pallas_call(
        pad_kernel,
        grid_spec=pltpu.PrefetchScalarGridSpec(
            num_scalar_prefetch=1,
            grid=(images,),
            in_specs=[
                pl.BlockSpec(
                    (1, length, width), lambda index, place: (place[0] * images + index, 0, 0)
                )
            ],
            out_specs=pl.BlockSpec((1, pad, width), lambda index, place: (index, 0, 0)),
        ),
        out_shape=jax.ShapeDtypeStruct((images, pad, width), value.dtype),
        compiler_params=pltpu.CompilerParams(vmem_limit_bytes=44 * 2**20),
        cost_estimate=pl.CostEstimate(flops=0, bytes_accessed=4 * value.size, transcendentals=0),
        name="padded_images",
    )(section, value)
    return out.reshape(images * pad, width)


def images_kernel(section, one_ref, two_ref, from_one, from_two, *rest):
    out_ref = rest[-1]
    own = pl.program_id(0) == section[0]
    for place, mine, other in ((0, one_ref, from_one), (1, two_ref, from_two)):
        for source, wanted in ((mine, own), (other, jnp.logical_not(own))):

            @pl.when(wanted & (section[0] == place))
            def _():
                out_ref[0, 0] = source[0, : out_ref.shape[2], :].astype(out_ref.dtype)


def own_images(section, one, two, from_one, from_two, images, length, dtype, after):
    rows, width = one.shape
    pad = rows // images
    sources = [value.reshape(images, pad, width) for value in (one, two, from_one, from_two)]
    specs = []
    for index in range(4):

        def place_map(which, image, section, place=index % 2, mine=index < 2):
            wanted = (section[0] == place) & ((which == section[0]) == mine)
            return (jnp.where(wanted, image, 0), 0, 0)

        specs.append(pl.BlockSpec((1, pad, width), place_map))
    return pl.pallas_call(
        images_kernel,
        grid_spec=pltpu.PrefetchScalarGridSpec(
            num_scalar_prefetch=1,
            grid=(2, images),
            in_specs=specs + [pl.BlockSpec(memory_space=pl.ANY)] * len(after),
            out_specs=pl.BlockSpec(
                (1, 1, length, width),
                lambda which, image, section: (0, which * images + image, 0, 0),
            ),
        ),
        out_shape=pltpu.HBM((1, 2 * images, length, width), dtype),
        compiler_params=pltpu.CompilerParams(vmem_limit_bytes=44 * 2**20),
        cost_estimate=pl.CostEstimate(flops=0, bytes_accessed=12 * one.size, transcendentals=0),
        name="own_images",
    )(section, *sources, *after)


def norm_stats(stream):
    mean_value = jnp.mean(stream, axis=-1, keepdims=True)
    centered = stream - mean_value
    variance = jnp.mean(centered * centered, axis=-1, keepdims=True)
    return centered * lax.rsqrt(variance + norm_epsilon)


def slot_plan(ids, rank, capacity):
    before = rank[None, :] < rank[:, None]
    first, second = ids[:, 0], ids[:, 1]
    same_first = (first[:, None] == first[None, :]) & before
    same_second = (second[:, None] == second[None, :]) & before
    crossed = second[:, None] == first[None, :]
    place_first = jnp.sum(same_first.astype(jnp.int32), axis=1)
    place_second = jnp.sum(same_second.astype(jnp.int32) + crossed.astype(jnp.int32), axis=1)
    slot_first = jnp.where(place_first < capacity, first * capacity + place_first, -1)
    slot_second = jnp.where(place_second < capacity, second * capacity + place_second, -1)
    return (jnp.where(first >= 0, slot_first, -1), jnp.where(second >= 0, slot_second, -1))


def body(
    patches,
    out_cotangent,
    attn_gain,
    qkv_weight,
    proj_weight,
    ffn_gain,
    mlp_in,
    mlp_out,
    router_weight,
    expert_in,
    expert_out,
    expert_ids,
    priority,
):
    expert_count = lax.axis_size("wide")
    sections = lax.axis_size("section")
    section = lax.axis_index("section")
    own_expert = lax.axis_index("wide")
    is_first = section == 0
    images = patches.shape[0] // sections
    length, width = patches.shape[1:]
    pad = -(-length // STEP) * STEP
    rows = images * pad
    capacity = max(2, images * length // expert_count)
    slots = expert_count * capacity
    levels = expert_count.bit_length() - 1
    assert 1 << levels == expert_count
    place = section[None]
    marks = (own_expert >> jnp.arange(levels, dtype=jnp.int32)) & 1
    bits = list(range(levels))
    third = max(1, levels // 3)
    groups = [bits[:third], bits[third : 2 * third], bits[2 * third : -1]]
    across_x = groups[0] + groups[1] + groups[2] + bits[-1:]
    across_y = groups[1] + groups[2] + groups[0] + bits[-1:]
    across_z = groups[2] + groups[0] + groups[1] + bits[-1:]

    def swap(value):
        return flipped(value, "section", 0)

    def exchange(value):
        return lax.all_to_all(value, "wide", split_axis=0, concat_axis=0, tiled=True)

    def across(value):
        shape = (expert_count, capacity, value.shape[1])
        return exchange(value.reshape(shape)).reshape(value.shape)

    other_qkv, other_proj = swap(qkv_weight[0]), swap(proj_weight[0])
    gains = jnp.concatenate([attn_gain, ffn_gain], axis=0)
    other_gains = swap(gains)
    gains_one = jnp.where(is_first, gains, other_gains)
    gains_two = jnp.where(is_first, other_gains, gains)
    weights = (qkv_weight[0], other_qkv, proj_weight[0], other_proj)
    which_one = jnp.stack([(section == 0).astype(jnp.int32), section])
    which_two = jnp.stack([(section == 1).astype(jnp.int32), section])

    ids = lax.dynamic_slice_in_dim(expert_ids, section * images, images)
    ids = jnp.pad(ids, ((0, 0), (0, pad - length), (0, 0)), constant_values=-1).reshape(rows, 2)
    rank = lax.dynamic_slice_in_dim(priority, section, 1).reshape(images, length)
    rank = jnp.pad(rank, ((0, 0), (0, pad - length))).reshape(rows)
    slot_first, slot_second = slot_plan(ids, rank, capacity)
    slot_range = jnp.arange(slots, dtype=jnp.int32)
    pick_first = slot_first[:, None] == slot_range[None, :]
    pick_second = slot_second[:, None] == slot_range[None, :]
    pick_any = (pick_first | pick_second).astype(bf16)
    kept_first = (slot_first >= 0).astype(f32)[:, None]
    kept_second = (slot_second >= 0).astype(f32)[:, None]
    rival = jnp.sum(
        jnp.where(pick_first, ids[:, 1:], 0) + jnp.where(pick_second, ids[:, :1], 0), axis=0
    )
    cotangent = padded_images(place, out_cotangent, images, pad)
    packet = jnp.concatenate(
        [
            tn(pick_any, cotangent).astype(bf16),
            jnp.broadcast_to(rival.astype(bf16)[:, None], (slots, PAIR)),
        ],
        axis=1,
    )

    stream_one = padded_images(place, patches, images, pad)
    mixed_one, packed_one, mix_one, normed_one = attention_forward(
        which_one, stream_one, weights, gains_one[:1], gains_one[1:], images, length
    )
    arrived_packet = across(packet)
    hidden_one = nn(normed_one, mlp_in)
    active_one = jax.nn.gelu(hidden_one).astype(bf16)
    first_low = (mixed_one + nn(active_one, mlp_out)).astype(bf16)

    mixed_two, packed_two, mix_two, normed_two = attention_forward(
        which_two, first_low, weights, gains_two[:1], gains_two[1:], images, length
    )
    arrived = across(tn(pick_any, normed_two).astype(bf16))
    back, result, grad_expert_in, grad_expert_out = expert_pass(
        own_expert[None], arrived, arrived_packet, router_weight, expert_in, expert_out
    )
    back = across(back)
    result, back = lax.optimization_barrier((result, back))
    returned = across(result)
    other_expert_in, other_expert_out = swap(grad_expert_in), swap(grad_expert_out)

    from_low_one = lax.ppermute(first_low, "section", [(1, 0)])
    expert_range = jnp.arange(expert_count, dtype=jnp.int32)
    logits = nn(normed_two, router_weight)
    one_hot = (ids[:, :, None] == expert_range[None, None, :]).astype(f32)
    chosen = jnp.sum(one_hot * logits[:, None, :], axis=-1)
    gates = jax.nn.softmax(chosen, axis=-1)
    low_first, low_second = pick_first.astype(bf16), pick_second.astype(bf16)
    grad_gates = jnp.concatenate(
        [
            jnp.sum(nn(low, back[:, width:]), axis=-1, keepdims=True)
            for low in (low_first, low_second)
        ],
        axis=1,
    )
    grad_chosen = gates * (grad_gates - jnp.sum(gates * grad_gates, axis=-1, keepdims=True))
    grad_logits = jnp.sum(one_hot * grad_chosen[:, :, None], axis=1).astype(bf16)
    grad_router = tn(normed_two, grad_logits)
    grad_normed_two = nn(pick_any, back[:, :width]) + nt(grad_logits, router_weight)
    second_low = (
        mixed_two
        + kept_first * gates[:, :1] * nn(low_first, returned)
        + kept_second * gates[:, 1:] * nn(low_second, returned)
    ).astype(bf16)
    grad_first, small_two, *pieces = attention_backward(
        which_two,
        first_low,
        mixed_two,
        cotangent,
        grad_normed_two,
        packed_two,
        mix_two,
        weights,
        gains_two[:1],
        gains_two[1:],
        images,
        length,
        1,
        bf16,
    )
    two = Travel(marks, pieces[:1], pieces[1:], [across_x])
    grad_normed_one, in_send, in_keep, out_send, out_keep = mlp_backward(
        place, normed_one, grad_first, mlp_in, mlp_out, after=(kept_far(other_expert_in), kept_far(other_expert_out), second_low, from_low_one)
    )
    mlp_first = Travel(marks, [in_send], [in_keep], [across_z])
    mlp_second = Travel(marks, [out_send], [out_keep], [across_y])
    early = [two, mlp_first, mlp_second]
    from_low_two = lax.ppermute(second_low, "section", [(0, 1)])
    from_grad_two = lax.ppermute(grad_first, "section", [(0, 1)])
    grad_one, small_one, *pieces = attention_backward(
        which_one,
        stream_one,
        mixed_one,
        grad_first,
        grad_normed_one,
        packed_one,
        mix_one,
        weights,
        gains_one[:1],
        gains_one[1:],
        images,
        length,
        2,
        f32,
        small=(grad_router, small_two),
        after=joint_step(early) + [from_grad_two, from_low_two],
    )
    one = Travel(marks, pieces[:2], pieces[2:], [across_x, across_y])
    last = joint_step(early, after=pieces[2:])
    activations = own_images(
        place, first_low, second_low, from_low_one, from_low_two, images, length, bf16, last
    )
    last = joint_step(early + [one], after=[kept_far(activations)])
    expert_in_sum = pair_total(grad_expert_in, other_expert_in, tuple(last))
    last = joint_step(early + [one], after=[kept_far(expert_in_sum)])
    expert_out_sum = pair_total(grad_expert_out, other_expert_out, tuple(last))
    last = joint_step(early + [one], after=[kept_far(expert_out_sum)])
    while not two.done:
        last = joint_step(early + [one], after=last)

    other_in, other_out = swap(mlp_first.stays[0]), swap(mlp_second.stays[0])
    last = joint_step([one], after=(other_in, other_out))
    late_grad, *last = lax.optimization_barrier((grad_one, *last))
    from_grad_one = lax.ppermute(late_grad, "section", [(1, 0)])
    mlp_in_sum = join_halves(place, mlp_first.stays[0], other_in, 0, tuple(last))
    mlp_out_sum = join_halves(place, mlp_second.stays[0], other_out, 1, (kept_far(mlp_in_sum),))
    from_two = [lax.ppermute(value, "section", [(0, 1)]) for value in two.stays]
    input_grads = own_images(
        place,
        grad_one,
        grad_first,
        from_grad_one,
        from_grad_two,
        images,
        length,
        f32,
        (kept_far(mlp_out_sum),),
    )
    last = [kept_far(input_grads)]
    while not one.done:
        last = joint_step([one], after=last)
    from_one = [lax.ppermute(value, "section", [(1, 0)]) for value in one.stays]
    qkv_grad, proj_grad = own_block(place, (one.stays, two.stays, from_one, from_two))
    small = one.stays[1][:, 2 * width :]
    other_small = swap(small)
    small = jnp.concatenate(
        [jnp.where(is_first, small, other_small), jnp.where(is_first, other_small, small)], axis=0
    ).astype(f32)
    gain_sums = jnp.transpose(small[:, 128:144])
    small_block = lax.dynamic_slice_in_dim(gain_sums, 8 * section, 8)
    return (
        activations,
        input_grads,
        small_block[:1],
        qkv_grad[None],
        proj_grad[None],
        small_block[1:2],
        mlp_in_sum,
        mlp_out_sum,
        small[:, :expert_count],
        expert_in_sum,
        expert_out_sum,
    )


def solution(mesh):
    in_specs = (
        P("wide", None, None),
        P("wide", None, None),
        P("section", None),
        P("section", None, None),
        P("section", None, None),
        P("section", None),
        P(),
        P(),
        P(),
        P("wide", None, None),
        P("wide", None, None),
        P("wide", None, None),
        P("wide", None),
    )
    out_specs = (
        P("section", "wide", None, None),
        P("section", "wide", None, None),
        P("section", None),
        P("section", None, None),
        P("section", None, None),
        P("section", None),
        P(),
        P(),
        P(),
        P("wide", None, None),
        P("wide", None, None),
    )
    return jax.shard_map(body, mesh=mesh, in_specs=in_specs, out_specs=out_specs, check_vma=False)
```

```python
import functools

import jax
import jax.numpy as jnp
from jax import lax
from jax.experimental import pallas as pl
from jax.experimental.pallas import tpu as pltpu
from jax.sharding import PartitionSpec as P

H = 12
HEAD = 64
PAIR = 2 * HEAD
STEP = 16
EXTRA = 256
norm_epsilon = 1e-06
bf16 = jnp.bfloat16
f32 = jnp.float32


def dot(left, right, dims):
    return lax.dot_general(left, right, (dims, ((), ())), preferred_element_type=f32)


def nn(left, right):
    return dot(left, right, ((1,), (0,)))


def nt(left, right):
    return dot(left, right, ((1,), (1,)))


def tn(left, right):
    return dot(left, right, ((0,), (0,)))


def norm_rows(value):
    mean_value = jnp.mean(value, axis=-1, keepdims=True)
    centered = value - mean_value
    scale = lax.rsqrt(jnp.mean(centered * centered, axis=-1, keepdims=True) + norm_epsilon)
    return (centered * scale, scale)


def norm_rows_back(unit, scale, gain, upstream):
    weighted = upstream * gain
    first = jnp.mean(weighted, axis=-1, keepdims=True)
    second = jnp.mean(weighted * unit, axis=-1, keepdims=True)
    return scale * (weighted - first - unit * second)


def folded(value):
    rows = value.shape[0]
    return sum(value[start : start + 8] for start in range(0, rows, 8))


def row_blocks(rows):
    return [slice(start, start + STEP) for start in range(0, rows, STEP)]


def fetch(take, own, other, target, sem):
    @pl.when(take == 1)
    def _():
        pltpu.make_async_copy(own, target, sem).start()

    @pl.when(take != 1)
    def _():
        pltpu.make_async_copy(other, target, sem).start()


def forward_kernel(
    images,
    length,
    which,
    x_ref,
    own_qkv,
    other_qkv,
    own_proj,
    other_proj,
    gain_a,
    gain_f,
    mixed_ref,
    packed_out,
    mix_out,
    normed_ref,
    qkv_ref,
    proj_ref,
    low_ref,
    packed_ref,
    mix_ref,
    sems,
):
    rows, width = x_ref.shape
    pad = rows // images
    packed_copy = pltpu.make_async_copy(packed_ref, packed_out, sems.at[2])
    mix_copy = pltpu.make_async_copy(mix_ref, mix_out, sems.at[3])
    fetch(which[0], own_qkv, other_qkv, qkv_ref, sems.at[0])
    fetch(which[0], own_proj, other_proj, proj_ref, sems.at[1])

    for block in row_blocks(rows):
        unit, scale = norm_rows(x_ref[block, :].astype(f32))
        low_ref[block, :] = (unit * gain_a[...]).astype(bf16)

    pltpu.make_async_copy(own_qkv, qkv_ref, sems.at[0]).wait()

    @pl.loop(0, 3 * width // 256)
    def _(step):
        lanes = pl.ds(pl.multiple_of(step * 256, 256), 256)
        packed_ref[:, lanes] = nn(low_ref[...], qkv_ref[:, lanes]).astype(bf16)

    packed_copy.start()
    left = lax.broadcasted_iota(jnp.int32, (pad, PAIR), 1) < HEAD
    live = lax.broadcasted_iota(jnp.int32, (pad, pad), 0) < length

    @pl.loop(0, width // PAIR)
    def _(pair):
        def lanes(part):
            return pl.ds(pl.multiple_of(part * width + pair * PAIR, PAIR), PAIR)

        for image in range(images):
            block = slice(image * pad, (image + 1) * pad)
            queries = packed_ref[block, lanes(0)].astype(f32) * HEAD ** (-0.5)
            keys = packed_ref[block, lanes(1)]
            values = packed_ref[block, lanes(2)].T
            outs = []
            for half, rows_half in ((left, slice(0, HEAD)), (~left, slice(HEAD, PAIR))):
                scores = nt(keys, jnp.where(half, queries, 0.0).astype(bf16))
                scores = jnp.where(live, scores, -jnp.inf)
                powers = jnp.exp(scores - jnp.max(scores, axis=0, keepdims=True))
                share = 1.0 / jnp.sum(powers, axis=0, keepdims=True)
                outs.append(nn(values[rows_half], powers.astype(bf16)) * share)
            mix_ref[block, lanes(0)] = jnp.concatenate(outs, axis=0).T.astype(bf16)

    mix_copy.start()
    pltpu.make_async_copy(own_proj, proj_ref, sems.at[1]).wait()

    @pl.loop(0, width // 256)
    def _(step):
        lanes = pl.ds(pl.multiple_of(step * 256, 256), 256)
        mixed_ref[:, lanes] = x_ref[:, lanes].astype(f32) + nn(mix_ref[...], proj_ref[:, lanes])

    for block in row_blocks(rows):
        unit, scale = norm_rows(mixed_ref[block, :])
        normed_ref[block, :] = (unit * gain_f[...]).astype(bf16)
    packed_copy.wait()
    mix_copy.wait()


def backward_kernel(
    images,
    length,
    chunks,
    which,
    x_ref,
    mixed_ref,
    base_ref,
    upstream_ref,
    packed_in,
    mix_in,
    own_qkv,
    other_qkv,
    own_proj,
    other_proj,
    gain_a,
    gain_f,
    small,
    grad_out,
    gains_ref,
    pieces,
    grad_ref,
    grad_packed,
    total_low,
    low_ref,
    qkv_ref,
    proj_ref,
    total_ref,
    grad_mix,
    packed_ref,
    mix_ref,
    staged,
    turned,
    sems,
):
    rows, width = x_ref.shape
    pad = rows // images
    packed_copy = pltpu.make_async_copy(packed_in, packed_ref, sems.at[2])
    mix_copy = pltpu.make_async_copy(mix_in, mix_ref, sems.at[3])
    packed_copy.start()
    mix_copy.start()
    fetch(which[0], own_proj, other_proj, proj_ref, sems.at[1])
    fetch(which[0], own_qkv, other_qkv, qkv_ref, sems.at[0])
    gain_total = jnp.zeros((8, width), f32)
    for block in row_blocks(rows):
        unit, scale = norm_rows(mixed_ref[block, :])
        upstream = upstream_ref[block, :]
        value = base_ref[block, :].astype(f32) + norm_rows_back(
            unit, scale, gain_f[...], upstream
        )
        total_ref[block, :] = value
        total_low[block, :] = value.astype(bf16)
        source_unit, source_scale = norm_rows(x_ref[block, :].astype(f32))
        low_ref[block, :] = (source_unit * gain_a[...]).astype(bf16)
        gain_total = gain_total + folded(upstream * unit)
    gains_ref[...] = jnp.zeros_like(gains_ref)
    gains_ref[1:2, :] = jnp.sum(gain_total, axis=0, keepdims=True)
    pltpu.make_async_copy(own_proj, proj_ref, sems.at[1]).wait()

    @pl.loop(0, width // 256)
    def _(step):
        lanes = pl.ds(pl.multiple_of(step * 256, 256), 256)
        grad_mix[:, lanes] = nt(total_low[...], proj_ref[lanes, :]).astype(bf16)

    packed_copy.wait()
    left = lax.broadcasted_iota(jnp.int32, (pad, PAIR), 1) < HEAD
    live = lax.broadcasted_iota(jnp.int32, (pad, pad), 0) < length

    @pl.loop(0, width // PAIR)
    def _(pair):
        def lanes(part):
            return pl.ds(pl.multiple_of(part * width + pair * PAIR, PAIR), PAIR)

        for image in range(images):
            block = slice(image * pad, (image + 1) * pad)
            queries = packed_ref[block, lanes(0)].astype(f32) * HEAD ** (-0.5)
            keys = packed_ref[block, lanes(1)]
            values = packed_ref[block, lanes(2)]
            grads = grad_mix[block, lanes(0)]
            sums = [0.0, 0.0, 0.0]
            for half in (left, ~left):
                some_queries = jnp.where(half, queries, 0.0).astype(bf16)
                some_keys = jnp.where(half, keys, 0.0).astype(bf16)
                some_grads = jnp.where(half, grads, 0.0).astype(bf16)
                scores = nt(keys, some_queries)
                scores = jnp.where(live, scores, -jnp.inf)
                powers = jnp.exp(scores - jnp.max(scores, axis=0, keepdims=True))
                weights = powers * (1.0 / jnp.sum(powers, axis=0, keepdims=True))
                grad_weights = nt(values, some_grads)
                inner = jnp.sum(grad_weights * weights, axis=0, keepdims=True)
                grad_raw = (weights * (grad_weights - inner)).astype(bf16)
                sums[0] += tn(grad_raw, some_keys)
                sums[1] += nn(grad_raw, some_queries)
                sums[2] += nn(weights.astype(bf16), some_grads)
            sums[0] = sums[0] * HEAD ** (-0.5)
            for part in range(3):
                grad_packed[block, lanes(part)] = sums[part].astype(bf16)

    mix_copy.wait()
    third = width // 3
    for side, place in ((0, 1 - which[1]), (1, which[1])):
        columns = pl.ds(pl.multiple_of(place * (width // 2), 128), width // 2)
        left_rows = low_ref[:, columns].T
        right_rows = mix_ref[:, columns].T
        for step in range(12):
            if step < 9:
                value = nn(left_rows, grad_packed[:, step * third : (step + 1) * third])
            else:
                value = nn(right_rows, total_low[:, (step - 9) * third : (step - 8) * third])
            out, spot = divmod(step, 12 // chunks)
            staged[side * chunks + out][:, spot * third : (spot + 1) * third] = value.astype(bf16)
        for index in range(side * chunks, (side + 1) * chunks - bool(small)):
            pltpu.make_async_copy(staged[index], pieces[index], sems.at[4 + index]).start()

    pltpu.make_async_copy(own_qkv, qkv_ref, sems.at[0]).wait()

    @pl.loop(0, width // 256)
    def _(step):
        lanes = pl.ds(pl.multiple_of(step * 256, 256), 256)
        grad_ref[:, lanes] = nt(grad_packed[...], qkv_ref[lanes, :])

    gain_total = jnp.zeros((8, width), f32)
    for block in row_blocks(rows):
        unit, scale = norm_rows(x_ref[block, :].astype(f32))
        upstream = grad_ref[block, :]
        value = total_ref[block, :] + norm_rows_back(unit, scale, gain_a[...], upstream)
        grad_out[block, :] = value.astype(grad_out.dtype)
        gain_total = gain_total + folded(upstream * unit)
    gains_ref[0:1, :] = jnp.sum(gain_total, axis=0, keepdims=True)
    half_width = width // 2
    if small:
        turned[...] = jnp.concatenate([gains_ref[...], small[1][...]], axis=0).T
        for index, place in ((chunks - 1, 1 - which[1]), (2 * chunks - 1, which[1])):
            block = pl.ds(pl.multiple_of(place * half_width, 128), half_width)
            out = staged[index]
            start = out.shape[1] - EXTRA
            out[:, start:] = jnp.zeros((half_width, EXTRA), bf16)
            out[:, start : start + small[0].shape[1]] = small[0][block, :].astype(bf16)
            out[:, start + 128 : start + 144] = turned[block, :].astype(bf16)
        for index in (chunks - 1, 2 * chunks - 1):
            pltpu.make_async_copy(staged[index], pieces[index], sems.at[4 + index]).start()
    for index in range(2 * chunks):
        pltpu.make_async_copy(staged[index], pieces[index], sems.at[4 + index]).wait()


def whole_spec():
    return pl.BlockSpec(memory_space=pltpu.VMEM)


def kept_far(value):
    return pltpu.with_memory_space_constraint(value, pltpu.HBM)


def attention_forward(which, x, weights, gain_a, gain_f, images, length):
    rows, width = x.shape
    far = pl.BlockSpec(memory_space=pltpu.HBM)
    near = whole_spec()
    return pl.pallas_call(
        functools.partial(forward_kernel, images, length),
        out_shape=(
            jax.ShapeDtypeStruct((rows, width), f32),
            pltpu.HBM((rows, 3 * width), bf16),
            pltpu.HBM((rows, width), bf16),
            jax.ShapeDtypeStruct((rows, width), bf16),
        ),
        in_specs=[pl.BlockSpec(memory_space=pltpu.SMEM), near, far, far, far, far, near, near],
        out_specs=(near, far, far, near),
        scratch_shapes=[
            pltpu.VMEM((width, 3 * width), bf16),
            pltpu.VMEM((width, width), bf16),
            pltpu.VMEM((rows, width), bf16),
            pltpu.VMEM((rows, 3 * width), bf16),
            pltpu.VMEM((rows, width), bf16),
            pltpu.SemaphoreType.DMA((4,)),
        ],
        compiler_params=pltpu.CompilerParams(vmem_limit_bytes=24 * 2**20),
        cost_estimate=pl.CostEstimate(
            flops=10 * rows * width * width, bytes_accessed=12 * 2**20, transcendentals=2**20
        ),
        name="attention_forward",
    )(which, x, *[kept_far(value) for value in weights], gain_a, gain_f)


def attention_backward(
    which,
    x,
    mixed,
    base,
    upstream,
    packed,
    mix,
    weights,
    gain_a,
    gain_f,
    images,
    length,
    chunks,
    dtype,
    small=(),
    after=(),
):
    rows, width = x.shape
    far = pl.BlockSpec(memory_space=pltpu.HBM)
    near = whole_spec()
    sizes = [4 * width // chunks] * chunks
    if small:
        sizes[-1] += EXTRA
    sizes = sizes * 2
    first_out = 13 + len(small) + len(after)

    def kernel(*refs):
        outs = refs[first_out : first_out + 2 + 2 * chunks]
        scratch = refs[first_out + 2 + 2 * chunks :]
        backward_kernel(
            images,
            length,
            chunks,
            *refs[:13],
            refs[13 : 13 + len(small)],
            outs[0],
            outs[1],
            outs[2:],
            *scratch[:10],
            scratch[10 : 10 + 2 * chunks],
            *scratch[10 + 2 * chunks :],
        )

    return pl.pallas_call(
        kernel,
        out_shape=(
            jax.ShapeDtypeStruct((rows, width), dtype),
            jax.ShapeDtypeStruct((8, width), f32),
        )
        + tuple(pltpu.HBM((width // 2, size), bf16) for size in sizes),
        in_specs=[pl.BlockSpec(memory_space=pltpu.SMEM)]
        + [near] * 4
        + [far] * 6
        + [near] * (2 + len(small))
        + [pl.BlockSpec(memory_space=pl.ANY)] * len(after),
        out_specs=(near, near) + (far,) * (2 * chunks),
        scratch_shapes=[
            pltpu.VMEM((rows, width), f32),
            pltpu.VMEM((rows, 3 * width), bf16),
            pltpu.VMEM((rows, width), bf16),
            pltpu.VMEM((rows, width), bf16),
            pltpu.VMEM((width, 3 * width), bf16),
            pltpu.VMEM((width, width), bf16),
            pltpu.VMEM((rows, width), f32),
            pltpu.VMEM((rows, width), bf16),
            pltpu.VMEM((rows, 3 * width), bf16),
            pltpu.VMEM((rows, width), bf16),
        ]
        + [pltpu.VMEM((width // 2, size), bf16) for size in sizes]
        + [pltpu.VMEM((width, 16), f32), pltpu.SemaphoreType.DMA((4 + 2 * chunks,))],
        compiler_params=pltpu.CompilerParams(vmem_limit_bytes=32 * 2**20),
        cost_estimate=pl.CostEstimate(
            flops=28 * rows * width * width, bytes_accessed=24 * 2**20, transcendentals=2**20
        ),
        name="attention_backward",
    )(
        which,
        x,
        mixed,
        base,
        upstream,
        *[kept_far(value) for value in (packed, mix, *weights)],
        gain_a,
        gain_f,
        *small,
        *after,
    )


def gelu_pair(hidden):
    cubic = 0.7978845608028654
    square = hidden * hidden
    curve = jnp.tanh(cubic * (hidden + 0.044715 * (square * hidden)))
    left = 0.5 * (1.0 + curve)
    slope = left + 0.5 * hidden * (1.0 - curve * curve) * (
        cubic * (1.0 + 3.0 * 0.044715 * square)
    )
    return (hidden * left, slope)


def refresh_kernel(x_ref, in_ref, *rest):
    active_ref, slope_ref = rest[-2:]
    active, slope = gelu_pair(nn(x_ref[...], in_ref[...]))
    active_ref[...] = active.astype(bf16)
    slope_ref[...] = slope.astype(bf16)


def mlp_refresh(x, weight_in, after):
    rows, width = x.shape
    hidden = weight_in.shape[1]
    step = 512
    block = pl.BlockSpec((rows, step), lambda index: (0, index))
    return pl.pallas_call(
        refresh_kernel,
        grid=(hidden // step,),
        in_specs=[
            pl.BlockSpec((rows, width), lambda index: (0, 0)),
            pl.BlockSpec((width, step), lambda index: (0, index)),
        ]
        + [pl.BlockSpec(memory_space=pl.ANY)] * len(after),
        out_specs=(block, block),
        out_shape=(pltpu.HBM((rows, hidden), bf16),) * 2,
        compiler_params=pltpu.CompilerParams(vmem_limit_bytes=44 * 2**20),
        cost_estimate=pl.CostEstimate(
            flops=2 * rows * width * hidden,
            bytes_accessed=10 * 2**20,
            transcendentals=rows * hidden,
        ),
        name="mlp_refresh",
    )(x, weight_in, *after)


def mlp_kernel(
    section,
    x_ref,
    up_ref,
    in_ref,
    out_ref,
    active_ref,
    slope_ref,
    grad_ref,
    in_send,
    in_keep,
    out_send,
    out_keep,
    x_turned,
):
    half = x_ref.shape[1] // 2

    @pl.when(pl.program_id(0) == 0)
    def _():
        x_turned[...] = x_ref[...].T
        grad_ref[...] = jnp.zeros_like(grad_ref)

    grad_hidden = (nt(up_ref[...], out_ref[...]) * slope_ref[...].astype(f32)).astype(bf16)
    grad_ref[...] += nt(grad_hidden, in_ref[...])
    turned = active_ref[...].T
    for which, first, second in (
        (1 - section[0], in_send, out_send),
        (section[0], in_keep, out_keep),
    ):
        block = pl.ds(pl.multiple_of(which * half, 128), half)
        first[...] = nn(x_turned[block, :], grad_hidden).astype(bf16)
        second[...] = nn(turned, up_ref[:, block]).astype(bf16)


def mlp_backward(section, x, up, weight_in, weight_out, active, slope, after):
    rows, width = x.shape
    hidden = weight_in.shape[1]
    step = 512
    half = width // 2
    fixed = pl.BlockSpec((rows, width), lambda index, place: (0, 0))
    saved = pl.BlockSpec((rows, step), lambda index, place: (0, index))
    across = pl.BlockSpec((half, step), lambda index, place: (0, index))
    down = pl.BlockSpec((step, half), lambda index, place: (index, 0))

    def kernel(*refs):
        mlp_kernel(*refs[:7], *refs[7 + len(after) :])

    return pl.pallas_call(
        kernel,
        grid_spec=pltpu.PrefetchScalarGridSpec(
            num_scalar_prefetch=1,
            grid=(hidden // step,),
            in_specs=[
                fixed,
                fixed,
                pl.BlockSpec((width, step), lambda index, place: (0, index)),
                pl.BlockSpec((step, width), lambda index, place: (index, 0)),
                saved,
                saved,
            ]
            + [pl.BlockSpec(memory_space=pl.ANY)] * len(after),
            out_specs=(fixed, across, across, down, down),
            scratch_shapes=[pltpu.VMEM((width, rows), bf16)],
        ),
        out_shape=(
            jax.ShapeDtypeStruct((rows, width), f32),
            pltpu.HBM((half, hidden), bf16),
            pltpu.HBM((half, hidden), bf16),
            pltpu.HBM((hidden, half), bf16),
            pltpu.HBM((hidden, half), bf16),
        ),
        compiler_params=pltpu.CompilerParams(vmem_limit_bytes=44 * 2**20),
        cost_estimate=pl.CostEstimate(
            flops=8 * rows * width * hidden, bytes_accessed=28 * 2**20, transcendentals=0
        ),
        name="mlp_backward",
    )(section, x, up, weight_in, weight_out, active, slope, *after)


def expert_kernel(
    own,
    x_ref,
    packet_ref,
    router_ref,
    in_ref,
    out_ref,
    *rest,
):
    back_ref, result_ref, active_ref, hidden_ref, up_ref, total_ref, grad_ref = rest[-7:]
    slots, width = x_ref.shape

    @pl.when(pl.program_id(0) == 0)
    def _():
        grad_ref[...] = jnp.zeros_like(grad_ref)
        total_ref[...] = jnp.zeros_like(total_ref)
        logits = nn(x_ref[...], router_ref[...])
        experts = lax.broadcasted_iota(jnp.int32, logits.shape, 1)
        rival = packet_ref[:, width : width + 1].astype(f32).astype(jnp.int32)
        own_logit = jnp.sum(jnp.where(experts == own[0], logits, 0.0), axis=1, keepdims=True)
        rival_logit = jnp.sum(jnp.where(experts == rival, logits, 0.0), axis=1, keepdims=True)
        top = jnp.maximum(own_logit, rival_logit)
        power = jnp.exp(own_logit - top)
        gate = power / (power + jnp.exp(rival_logit - top))
        up_ref[...] = (gate * packet_ref[:, :width].astype(f32)).astype(bf16)

    active, slope = gelu_pair(nn(x_ref[...], in_ref[0]))
    active = active.astype(bf16)
    total_ref[...] += nn(active, out_ref[0])
    grad_hidden = (nt(up_ref[...], out_ref[0]) * slope).astype(bf16)
    grad_ref[...] += nt(grad_hidden, in_ref[0])
    active_ref[...] = active
    hidden_ref[...] = grad_hidden

    @pl.when(pl.program_id(0) == pl.num_programs(0) - 1)
    def _():
        result = total_ref[...].astype(bf16)
        result_ref[...] = result
        back_ref[:, :width] = grad_ref[...].astype(bf16)
        rest = jnp.sum(
            packet_ref[:, :width].astype(f32) * result.astype(f32), axis=1, keepdims=True
        )
        lanes = lax.broadcasted_iota(jnp.int32, (slots, PAIR), 1)
        value = jnp.zeros((slots, PAIR), f32)
        for lane in range(3):
            part = rest.astype(bf16).astype(f32)
            value = jnp.where(lanes == lane, part, value)
            rest = rest - part
        back_ref[:, width:] = value.astype(bf16)


def expert_pass(own, x, packet, router, weight_in, weight_out, after):
    slots, width = x.shape
    hidden = weight_in.shape[2]
    step = 512

    def fixed(shape):
        return pl.BlockSpec(shape, lambda index, place: (0, 0))

    saved = pl.BlockSpec((slots, step), lambda index, place: (0, index))
    return pl.pallas_call(
        expert_kernel,
        grid_spec=pltpu.PrefetchScalarGridSpec(
            num_scalar_prefetch=1,
            grid=(hidden // step,),
            in_specs=[
                fixed(x.shape),
                fixed(packet.shape),
                fixed(router.shape),
                pl.BlockSpec((1, width, step), lambda index, place: (0, 0, index)),
                pl.BlockSpec((1, step, width), lambda index, place: (0, index, 0)),
            ]
            + [pl.BlockSpec(memory_space=pl.ANY)] * len(after),
            out_specs=(fixed(packet.shape), fixed(x.shape), saved, saved, fixed(x.shape)),
            scratch_shapes=[
                pltpu.VMEM((slots, width), f32),
                pltpu.VMEM((slots, width), f32),
            ],
        ),
        out_shape=(
            jax.ShapeDtypeStruct(packet.shape, bf16),
            jax.ShapeDtypeStruct(x.shape, bf16),
            pltpu.HBM((slots, hidden), bf16),
            pltpu.HBM((slots, hidden), bf16),
            jax.ShapeDtypeStruct(x.shape, bf16),
        ),
        compiler_params=pltpu.CompilerParams(vmem_limit_bytes=44 * 2**20),
        cost_estimate=pl.CostEstimate(
            flops=8 * slots * width * hidden,
            bytes_accessed=16 * 2**20,
            transcendentals=slots * hidden,
        ),
        name="expert_pass",
    )(own, x, packet, router, weight_in, weight_out, *after)


def expert_product_kernel(
    x_ref, up_ref, active_ref, hidden_ref, in_grad, out_grad, x_turned
):
    @pl.when(pl.program_id(0) == 0)
    def _():
        x_turned[...] = x_ref[...].T

    in_grad[...] = nn(x_turned[...], hidden_ref[...]).astype(bf16)
    out_grad[...] = nn(active_ref[...].T, up_ref[...]).astype(bf16)


def expert_products(x, up, active, grad_hidden):
    slots, width = x.shape
    hidden = active.shape[1]
    step = 512
    fixed = pl.BlockSpec((slots, width), lambda index: (0, 0))
    saved = pl.BlockSpec((slots, step), lambda index: (0, index))
    return pl.pallas_call(
        expert_product_kernel,
        grid=(hidden // step,),
        in_specs=[fixed, fixed, saved, saved],
        out_specs=(
            pl.BlockSpec((width, step), lambda index: (0, index)),
            pl.BlockSpec((step, width), lambda index: (index, 0)),
        ),
        out_shape=(pltpu.HBM((width, hidden), bf16), pltpu.HBM((hidden, width), bf16)),
        scratch_shapes=[pltpu.VMEM((width, slots), bf16)],
        compiler_params=pltpu.CompilerParams(vmem_limit_bytes=44 * 2**20),
        cost_estimate=pl.CostEstimate(
            flops=4 * slots * width * hidden, bytes_accessed=16 * 2**20, transcendentals=0
        ),
        name="expert_products",
    )(x, up, active, grad_hidden)


def join_kernel(section, mine_ref, other_ref, *rest):
    out_ref = rest[-1]

    @pl.when(pl.program_id(0) == section[0])
    def _():
        out_ref[...] = mine_ref[...].astype(f32)

    @pl.when(pl.program_id(0) != section[0])
    def _():
        out_ref[...] = other_ref[...].astype(f32)


def join_halves(section, mine, other, axis, after):
    rows, width = mine.shape
    steps = 3
    block = (rows // steps, width)

    def mine_map(which, step, place):
        return (jnp.where(which == place[0], step, 0), 0)

    def other_map(which, step, place):
        return (jnp.where(which == place[0], 0, step), 0)

    def out_map(which, step, place):
        return (which * steps + step, 0) if axis == 0 else (step, which)

    return pl.pallas_call(
        join_kernel,
        grid_spec=pltpu.PrefetchScalarGridSpec(
            num_scalar_prefetch=1,
            grid=(2, steps),
            in_specs=[pl.BlockSpec(block, mine_map), pl.BlockSpec(block, other_map)]
            + [pl.BlockSpec(memory_space=pl.ANY)] * len(after),
            out_specs=pl.BlockSpec(block, out_map),
        ),
        out_shape=pltpu.HBM((2 * rows, width) if axis == 0 else (rows, 2 * width), f32),
        compiler_params=pltpu.CompilerParams(vmem_limit_bytes=44 * 2**20),
        cost_estimate=pl.CostEstimate(
            flops=0, bytes_accessed=12 * rows * width, transcendentals=0
        ),
        name="join_halves",
    )(section, mine, other, *after)


def block_kernel(counts, section, *refs):
    refs = list(refs)
    sources = [[refs.pop(0) for _ in range(count)] for count in counts]
    own_small, other_small, qkv_out, proj_out, router_out, gains_out = refs
    own = pl.program_id(0) == section[0]
    cut = qkv_out.shape[1]

    def emit_small(part):
        value = part[:, part.shape[1] - EXTRA :].astype(f32)
        router_out[...] = value[:, : router_out.shape[1]]
        gains_out[...] = value[:, 128:].T[:16]

    @pl.when(own)
    def _():
        emit_small(own_small)

    @pl.when(jnp.logical_not(own))
    def _():
        emit_small(other_small)

    def emit(parts):
        start = 0
        for part in parts:
            size = min(part.shape[1], cut + proj_out.shape[1] - start)
            left = max(0, min(size, cut - start))
            if left:
                qkv_out[:, start : start + left] = part[:, :left].astype(f32)
            if left < size:
                proj_out[:, start + left - cut : start + size - cut] = part[:, left:size].astype(f32)
            start += size

    for index, parts in enumerate(sources):
        place, mine = index % 2, index < 2

        @pl.when((own == mine) & (section[0] == place))
        def _():
            emit(parts)


def own_block(section, groups, own_small, other_small, experts):
    half = groups[0][0].shape[0]
    width = 2 * half
    steps = 3
    specs = []
    for index, parts in enumerate(groups):

        def place_map(which, step, section, place=index % 2, mine=index < 2):
            wanted = (section[0] == place) & ((which == section[0]) == mine)
            return (jnp.where(wanted, step, 0), 0)

        specs += [pl.BlockSpec((half // steps, part.shape[1]), place_map) for part in parts]

    for value, mine in ((own_small, True), (other_small, False)):

        def small_map(which, step, section, mine=mine):
            return (jnp.where((which == section[0]) == mine, step, 0), 0)

        specs.append(pl.BlockSpec((half // steps, value.shape[1]), small_map))

    def out_map(which, step, section):
        return (which * steps + step, 0)

    return pl.pallas_call(
        functools.partial(block_kernel, [len(parts) for parts in groups]),
        grid_spec=pltpu.PrefetchScalarGridSpec(
            num_scalar_prefetch=1,
            grid=(2, steps),
            in_specs=specs,
            out_specs=(
                pl.BlockSpec((half // steps, 3 * width), out_map),
                pl.BlockSpec((half // steps, width), out_map),
                pl.BlockSpec((half // steps, experts), out_map),
                pl.BlockSpec(
                    (16, half // steps), lambda which, step, section: (0, which * steps + step)
                ),
            ),
        ),
        out_shape=(
            pltpu.HBM((2 * half, 3 * width), f32),
            pltpu.HBM((2 * half, width), f32),
            jax.ShapeDtypeStruct((2 * half, experts), f32),
            jax.ShapeDtypeStruct((16, 2 * half), f32),
        ),
        compiler_params=pltpu.CompilerParams(vmem_limit_bytes=44 * 2**20),
        cost_estimate=pl.CostEstimate(
            flops=0, bytes_accessed=48 * half * width, transcendentals=0
        ),
        name="own_block",
    )(section, *[part for parts in groups for part in parts], own_small, other_small)


def total_kernel(mine_ref, other_ref, *rest):
    rest[-1][0] = mine_ref[...].astype(f32) + other_ref[...].astype(f32)


def pair_total(mine, other, after):
    rows, width = mine.shape
    steps = 6
    block = pl.BlockSpec((rows // steps, width), lambda step: (step, 0))
    return pl.pallas_call(
        total_kernel,
        grid=(steps,),
        in_specs=[block, block] + [pl.BlockSpec(memory_space=pl.ANY)] * len(after),
        out_specs=pl.BlockSpec((1, rows // steps, width), lambda step: (0, step, 0)),
        out_shape=pltpu.HBM((1, rows, width), f32),
        compiler_params=pltpu.CompilerParams(vmem_limit_bytes=44 * 2**20),
        cost_estimate=pl.CostEstimate(
            flops=rows * width, bytes_accessed=8 * rows * width, transcendentals=0
        ),
        name="pair_total",
    )(mine, other, *after)


def span(axis, start, size):
    multiple = size & -size
    piece = pl.ds(pl.multiple_of(start * size, multiple), size)
    return (piece, slice(None)) if axis == 0 else (slice(None), piece)


def in_blocks(rows, work):
    size = next(size for size in (96, 64, 48, 32, 16) if rows % size == 0)
    if rows == size:
        work(slice(0, rows))
    else:

        @pl.loop(0, rows // size)
        def _(step):
            work(pl.ds(pl.multiple_of(step * size, size), size))


def combine_kernel(plans, extra, marks, *refs):
    count = len(plans)
    sources, outs = refs[: 2 * count], list(refs[2 * count + extra :])
    for index, (now, later) in enumerate(plans):
        stays, got = sources[2 * index : 2 * index + 2]
        rows, width = got.shape
        if now[0] == "gather":
            out = outs.pop(0)
            mine = marks[now[2]]
            for source, place in ((stays, mine), (got, 1 - mine)):
                target = out.at[span(now[1], place, got.shape[now[1]])]

                def move(block, source=source, target=target):
                    target[block, :] = source[block, :]

                in_blocks(rows, move)
        elif later is not None and later[0] == "reduce":
            mine = marks[later[2]]
            for place in (1 - mine, mine):
                out = outs.pop(0)
                window = span(later[1], place, out.shape[later[1]])
                first, second = stays.at[window], got.at[window]

                def add(block, first=first, second=second, out=out):
                    out[block, :] = first[block, :] + second[block, :]

                in_blocks(out.shape[0], add)
        else:
            out = outs.pop(0)

            def add_all(block, stays=stays, got=got, out=out):
                out[block, :] = stays[block, :] + got[block, :]

            in_blocks(rows, add_all)


def combine(marks, plans, pairs, after):
    near = whole_spec()
    shapes = []
    for (now, later), (stays, got) in zip(plans, pairs):
        shape = list(got.shape)
        if now[0] == "gather":
            shape[now[1]] *= 2
            shapes.append(shape)
        elif later is not None and later[0] == "reduce":
            shape[later[1]] //= 2
            shapes += [shape, shape]
        else:
            shapes.append(shape)
    values = [value for pair in pairs for value in pair]
    return pl.pallas_call(
        functools.partial(combine_kernel, plans, len(after)),
        out_shape=[jax.ShapeDtypeStruct(shape, bf16) for shape in shapes],
        in_specs=[pl.BlockSpec(memory_space=pltpu.SMEM)]
        + [near] * len(values)
        + [pl.BlockSpec(memory_space=pl.ANY)] * len(after),
        out_specs=[near] * len(shapes),
        compiler_params=pltpu.CompilerParams(vmem_limit_bytes=8 * 2**20),
        cost_estimate=pl.CostEstimate(flops=0, bytes_accessed=1024, transcendentals=0),
        name="combine",
    )(marks, *values, *after)


def combine_plainly(marks, plans, pairs):
    outs = []
    for (now, later), (stays, got) in zip(plans, pairs):
        if now[0] == "gather":
            outs.append(
                jnp.where(
                    marks[now[2]] == 0,
                    jnp.concatenate([stays, got], axis=now[1]),
                    jnp.concatenate([got, stays], axis=now[1]),
                )
            )
            continue
        total = stays + got
        if later is not None and later[0] == "reduce":
            size = total.shape[later[1]] // 2
            for place in (1 - marks[later[2]], marks[later[2]]):
                outs.append(lax.dynamic_slice_in_dim(total, place * size, size, axis=later[1]))
        else:
            outs.append(total)
    return outs


def flipped(value, axis, bit):
    pairs = [(place, place ^ (1 << bit)) for place in range(lax.axis_size(axis))]
    return lax.ppermute(value, axis, pairs)


class Travel:
    def __init__(self, marks, sends, keeps, orders):
        self.marks = marks
        self.plans = []
        self.aligned = True
        for value, order in zip(sends, orders):
            shape = list(value.shape)
            steps = []
            for bit in order:
                axis = 0 if shape[0] % 32 == 0 or shape[1] % 256 else 1
                if shape[axis] % (32, 256)[axis]:
                    self.aligned = False
                steps.append((axis, bit))
                shape[axis] //= 2
            self.plans.append(
                [("pair", 0, 0)]
                + [("reduce", *step) for step in steps]
                + [("gather", *step) for step in reversed(steps)]
            )
        self.stage = 0
        self.stays = list(keeps)
        self.got = [flipped(value, "section", 0) for value in sends]

    @property
    def done(self):
        return not self.got

    def pending(self):
        plans = []
        for plan in self.plans:
            later = plan[self.stage + 1] if self.stage + 1 < len(plan) else None
            plans.append((plan[self.stage], later))
        return plans, list(zip(self.stays, self.got))

    def accept(self, plans, outs):
        self.stage += 1
        self.stays, self.got = [], []
        for _, later in plans:
            sent = outs.pop(0)
            if later is not None and later[0] == "reduce":
                self.stays.append(outs.pop(0))
            else:
                self.stays.append(sent)
            if later is not None:
                self.got.append(flipped(sent, "wide", later[2]))


def joint_step(travels, after=()):
    travels = [travel for travel in travels if not travel.done]
    pending = [travel.pending() for travel in travels]
    plans = sum((item[0] for item in pending), [])
    pairs = sum((item[1] for item in pending), [])
    if all(travel.aligned for travel in travels):
        outs = list(combine(travels[0].marks, plans, pairs, after))
    else:
        outs = combine_plainly(travels[0].marks, plans, pairs)
    for travel, item in zip(travels, pending):
        travel.accept(item[0], outs)
    return sum((travel.stays for travel in travels), [])


def pad_kernel(section, x_ref, out_ref):
    out_ref[...] = jnp.zeros_like(out_ref)
    out_ref[0, : x_ref.shape[1], :] = x_ref[0]


def padded_images(section, value, images, pad):
    length, width = value.shape[1:]
    out = pl.pallas_call(
        pad_kernel,
        grid_spec=pltpu.PrefetchScalarGridSpec(
            num_scalar_prefetch=1,
            grid=(images,),
            in_specs=[
                pl.BlockSpec(
                    (1, length, width), lambda index, place: (place[0] * images + index, 0, 0)
                )
            ],
            out_specs=pl.BlockSpec((1, pad, width), lambda index, place: (index, 0, 0)),
        ),
        out_shape=jax.ShapeDtypeStruct((images, pad, width), value.dtype),
        compiler_params=pltpu.CompilerParams(vmem_limit_bytes=44 * 2**20),
        cost_estimate=pl.CostEstimate(flops=0, bytes_accessed=4 * value.size, transcendentals=0),
        name="padded_images",
    )(section, value)
    return out.reshape(images * pad, width)


def images_kernel(section, one_ref, two_ref, from_one, from_two, *rest):
    out_ref = rest[-1]
    own = pl.program_id(0) == section[0]
    for place, mine, other in ((0, one_ref, from_one), (1, two_ref, from_two)):
        for source, wanted in ((mine, own), (other, jnp.logical_not(own))):

            @pl.when(wanted & (section[0] == place))
            def _():
                out_ref[0, 0] = source[0, : out_ref.shape[2], :].astype(out_ref.dtype)


def own_images(section, one, two, from_one, from_two, images, length, dtype, after):
    rows, width = one.shape
    pad = rows // images
    sources = [value.reshape(images, pad, width) for value in (one, two, from_one, from_two)]
    specs = []
    for index in range(4):

        def place_map(which, image, section, place=index % 2, mine=index < 2):
            wanted = (section[0] == place) & ((which == section[0]) == mine)
            return (jnp.where(wanted, image, 0), 0, 0)

        specs.append(pl.BlockSpec((1, pad, width), place_map))
    return pl.pallas_call(
        images_kernel,
        grid_spec=pltpu.PrefetchScalarGridSpec(
            num_scalar_prefetch=1,
            grid=(2, images),
            in_specs=specs + [pl.BlockSpec(memory_space=pl.ANY)] * len(after),
            out_specs=pl.BlockSpec(
                (1, 1, length, width),
                lambda which, image, section: (0, which * images + image, 0, 0),
            ),
        ),
        out_shape=pltpu.HBM((1, 2 * images, length, width), dtype),
        compiler_params=pltpu.CompilerParams(vmem_limit_bytes=44 * 2**20),
        cost_estimate=pl.CostEstimate(flops=0, bytes_accessed=12 * one.size, transcendentals=0),
        name="own_images",
    )(section, *sources, *after)


def norm_stats(stream):
    mean_value = jnp.mean(stream, axis=-1, keepdims=True)
    centered = stream - mean_value
    variance = jnp.mean(centered * centered, axis=-1, keepdims=True)
    return centered * lax.rsqrt(variance + norm_epsilon)


def slot_plan(ids, rank, capacity):
    before = rank[None, :] < rank[:, None]
    first, second = ids[:, 0], ids[:, 1]
    same_first = (first[:, None] == first[None, :]) & before
    same_second = (second[:, None] == second[None, :]) & before
    crossed = second[:, None] == first[None, :]
    place_first = jnp.sum(same_first.astype(jnp.int32), axis=1)
    place_second = jnp.sum(same_second.astype(jnp.int32) + crossed.astype(jnp.int32), axis=1)
    slot_first = jnp.where(place_first < capacity, first * capacity + place_first, -1)
    slot_second = jnp.where(place_second < capacity, second * capacity + place_second, -1)
    return (jnp.where(first >= 0, slot_first, -1), jnp.where(second >= 0, slot_second, -1))


def body(
    patches,
    out_cotangent,
    attn_gain,
    qkv_weight,
    proj_weight,
    ffn_gain,
    mlp_in,
    mlp_out,
    router_weight,
    expert_in,
    expert_out,
    expert_ids,
    priority,
):
    expert_count = lax.axis_size("wide")
    sections = lax.axis_size("section")
    section = lax.axis_index("section")
    own_expert = lax.axis_index("wide")
    is_first = section == 0
    images = patches.shape[0] // sections
    length, width = patches.shape[1:]
    pad = -(-length // STEP) * STEP
    rows = images * pad
    capacity = max(2, images * length // expert_count)
    slots = expert_count * capacity
    levels = expert_count.bit_length() - 1
    assert 1 << levels == expert_count
    place = section[None]
    marks = (own_expert >> jnp.arange(levels, dtype=jnp.int32)) & 1
    bits = list(range(levels))
    third = max(1, levels // 3)
    groups = [bits[:third], bits[third : 2 * third], bits[2 * third : -1]]
    across_x = groups[0] + groups[1] + groups[2] + bits[-1:]
    across_y = groups[1] + groups[2] + groups[0] + bits[-1:]
    across_z = groups[2] + groups[0] + groups[1] + bits[-1:]

    def swap(value):
        return flipped(value, "section", 0)

    def exchange(value):
        return lax.all_to_all(value, "wide", split_axis=0, concat_axis=0, tiled=True)

    def across(value):
        shape = (expert_count, capacity, value.shape[1])
        return exchange(value.reshape(shape)).reshape(value.shape)

    other_qkv, other_proj = swap(qkv_weight[0]), swap(proj_weight[0])
    gains = jnp.concatenate([attn_gain, ffn_gain], axis=0)
    other_gains = swap(gains)
    gains_one = jnp.where(is_first, gains, other_gains)
    gains_two = jnp.where(is_first, other_gains, gains)
    weights = (qkv_weight[0], other_qkv, proj_weight[0], other_proj)
    which_one = jnp.stack([(section == 0).astype(jnp.int32), section])
    which_two = jnp.stack([(section == 1).astype(jnp.int32), section])

    ids = lax.dynamic_slice_in_dim(expert_ids, section * images, images)
    ids = jnp.pad(ids, ((0, 0), (0, pad - length), (0, 0)), constant_values=-1).reshape(rows, 2)
    rank = lax.dynamic_slice_in_dim(priority, section, 1).reshape(images, length)
    rank = jnp.pad(rank, ((0, 0), (0, pad - length))).reshape(rows)
    slot_first, slot_second = slot_plan(ids, rank, capacity)
    slot_range = jnp.arange(slots, dtype=jnp.int32)
    pick_first = slot_first[:, None] == slot_range[None, :]
    pick_second = slot_second[:, None] == slot_range[None, :]
    pick_any = (pick_first | pick_second).astype(bf16)
    kept_first = (slot_first >= 0).astype(f32)[:, None]
    kept_second = (slot_second >= 0).astype(f32)[:, None]
    rival = jnp.sum(
        jnp.where(pick_first, ids[:, 1:], 0) + jnp.where(pick_second, ids[:, :1], 0), axis=0
    )
    cotangent = padded_images(place, out_cotangent, images, pad)
    packet = jnp.concatenate(
        [
            tn(pick_any, cotangent).astype(bf16),
            jnp.broadcast_to(rival.astype(bf16)[:, None], (slots, PAIR)),
        ],
        axis=1,
    )

    stream_one = padded_images(place, patches, images, pad)
    mixed_one, packed_one, mix_one, normed_one = attention_forward(
        which_one, stream_one, weights, gains_one[:1], gains_one[1:], images, length
    )
    arrived_packet = across(packet)
    active_first = jax.nn.gelu(nn(normed_one, mlp_in)).astype(bf16)
    first_low = (mixed_one + nn(active_first, mlp_out)).astype(bf16)

    mixed_two, packed_two, mix_two, normed_two = attention_forward(
        which_two, first_low, weights, gains_two[:1], gains_two[1:], images, length
    )
    leaving = tn(pick_any, normed_two).astype(bf16)
    arrived = across(leaving)
    active_one, slope_one = mlp_refresh(normed_one, mlp_in, (leaving,))
    back, result, active, grad_hidden, grad_rows = expert_pass(
        own_expert[None],
        arrived,
        arrived_packet,
        router_weight,
        expert_in,
        expert_out,
        (active_one, slope_one),
    )
    grad_expert_in, grad_expert_out = expert_products(arrived, grad_rows, active, grad_hidden)
    back = across(back)
    result, back = lax.optimization_barrier((result, back))
    returned = across(result)
    other_expert_in, other_expert_out = swap(grad_expert_in), swap(grad_expert_out)

    from_low_one = lax.ppermute(first_low, "section", [(1, 0)])
    expert_range = jnp.arange(expert_count, dtype=jnp.int32)
    logits = nn(normed_two, router_weight)
    one_hot = (ids[:, :, None] == expert_range[None, None, :]).astype(f32)
    chosen = jnp.sum(one_hot * logits[:, None, :], axis=-1)
    gates = jax.nn.softmax(chosen, axis=-1)
    low_first, low_second = pick_first.astype(bf16), pick_second.astype(bf16)
    grad_gates = jnp.concatenate(
        [
            jnp.sum(nn(low, back[:, width:]), axis=-1, keepdims=True)
            for low in (low_first, low_second)
        ],
        axis=1,
    )
    grad_chosen = gates * (grad_gates - jnp.sum(gates * grad_gates, axis=-1, keepdims=True))
    grad_logits = jnp.sum(one_hot * grad_chosen[:, :, None], axis=1).astype(bf16)
    grad_router = tn(normed_two, grad_logits)
    grad_normed_two = nn(pick_any, back[:, :width]) + nt(grad_logits, router_weight)
    second_low = (
        mixed_two
        + kept_first * gates[:, :1] * nn(low_first, returned)
        + kept_second * gates[:, 1:] * nn(low_second, returned)
    ).astype(bf16)
    grad_first, small_two, *pieces = attention_backward(
        which_two,
        first_low,
        mixed_two,
        cotangent,
        grad_normed_two,
        packed_two,
        mix_two,
        weights,
        gains_two[:1],
        gains_two[1:],
        images,
        length,
        1,
        bf16,
        after=(grad_expert_in, grad_expert_out),
    )
    two = Travel(marks, pieces[:1], pieces[1:], [across_x])
    grad_normed_one, in_send, in_keep, out_send, out_keep = mlp_backward(
        place,
        normed_one,
        grad_first,
        mlp_in,
        mlp_out,
        active_one,
        slope_one,
        after=(kept_far(other_expert_in), kept_far(other_expert_out), from_low_one),
    )
    mlp_first = Travel(marks, [in_send], [in_keep], [across_z])
    mlp_second = Travel(marks, [out_send], [out_keep], [across_y])
    early = [two, mlp_first, mlp_second]
    from_low_two = lax.ppermute(second_low, "section", [(0, 1)])
    from_grad_two = lax.ppermute(grad_first, "section", [(0, 1)])
    grad_one, small_one, *pieces = attention_backward(
        which_one,
        stream_one,
        mixed_one,
        grad_first,
        grad_normed_one,
        packed_one,
        mix_one,
        weights,
        gains_one[:1],
        gains_one[1:],
        images,
        length,
        2,
        f32,
        small=(grad_router, small_two),
        after=joint_step(early, after=[second_low]),
    )
    one = Travel(marks, pieces[:2], pieces[2:], [across_x, across_y])
    last = joint_step(early, after=[from_low_two, from_grad_two])

    def settled(value):
        return lax.optimization_barrier(jnp.transpose(value[0], (1, 0, 2)))

    activations = settled(
        own_images(
            place, first_low, second_low, from_low_one, from_low_two, images, length, bf16, last
        )
    )
    last = joint_step(early + [one], after=[kept_far(activations)])
    expert_in_sum = pair_total(grad_expert_in, other_expert_in, tuple(last))
    last = joint_step(early + [one], after=[kept_far(expert_in_sum)])
    expert_out_sum = pair_total(grad_expert_out, other_expert_out, tuple(last))
    last = joint_step(early + [one], after=[kept_far(expert_out_sum)])
    while not two.done:
        last = joint_step(early + [one], after=last)

    other_in, other_out = swap(mlp_first.stays[0]), swap(mlp_second.stays[0])
    late_grad, *last = lax.optimization_barrier((grad_one, *last))
    from_grad_one = lax.ppermute(late_grad, "section", [(1, 0)])
    input_grads = settled(
        own_images(
            place, grad_one, grad_first, from_grad_one, from_grad_two, images, length, f32, last
        )
    )
    last = joint_step([one], after=(other_in, other_out, kept_far(input_grads)))
    mlp_in_sum = join_halves(place, mlp_first.stays[0], other_in, 0, tuple(last))
    mlp_out_sum = join_halves(
        place, mlp_second.stays[0], other_out, 1, (kept_far(mlp_in_sum),)
    )
    from_two = [lax.ppermute(value, "section", [(0, 1)]) for value in two.stays]
    last = [kept_far(mlp_out_sum)]
    while not one.done:
        last = joint_step([one], after=last)
    from_one = [lax.ppermute(value, "section", [(1, 0)]) for value in one.stays]
    other_small = swap(one.stays[1][:, 2 * width :])
    qkv_grad, proj_grad, sum_router, gain_sums = own_block(
        place,
        (one.stays, two.stays, from_one, from_two),
        one.stays[1],
        other_small,
        expert_count,
    )
    small_block = lax.dynamic_slice_in_dim(gain_sums, 8 * section, 8)
    return (
        jnp.transpose(activations, (1, 0, 2))[None],
        jnp.transpose(input_grads, (1, 0, 2))[None],
        small_block[:1],
        qkv_grad[None],
        proj_grad[None],
        small_block[1:2],
        mlp_in_sum,
        mlp_out_sum,
        sum_router,
        expert_in_sum,
        expert_out_sum,
    )


def solution(mesh):
    in_specs = (
        P("wide", None, None),
        P("wide", None, None),
        P("section", None),
        P("section", None, None),
        P("section", None, None),
        P("section", None),
        P(),
        P(),
        P(),
        P("wide", None, None),
        P("wide", None, None),
        P("wide", None, None),
        P("wide", None),
    )
    out_specs = (
        P("section", "wide", None, None),
        P("section", "wide", None, None),
        P("section", None),
        P("section", None, None),
        P("section", None, None),
        P("section", None),
        P(),
        P(),
        P(),
        P("wide", None, None),
        P("wide", None, None),
    )
    return jax.shard_map(body, mesh=mesh, in_specs=in_specs, out_specs=out_specs, check_vma=False)
```

```python
import functools

import jax
import jax.numpy as jnp
from jax import lax
from jax.experimental import pallas as pl
from jax.experimental.pallas import tpu as pltpu
from jax.sharding import PartitionSpec as P

H = 12
HEAD = 64
PAIR = 2 * HEAD
STEP = 16
EXTRA = 256
norm_epsilon = 1e-06
bf16 = jnp.bfloat16
f32 = jnp.float32


def dot(left, right, dims):
    return lax.dot_general(left, right, (dims, ((), ())), preferred_element_type=f32)


def nn(left, right):
    return dot(left, right, ((1,), (0,)))


def nt(left, right):
    return dot(left, right, ((1,), (1,)))


def tn(left, right):
    return dot(left, right, ((0,), (0,)))


def norm_rows(value):
    mean_value = jnp.mean(value, axis=-1, keepdims=True)
    centered = value - mean_value
    scale = lax.rsqrt(jnp.mean(centered * centered, axis=-1, keepdims=True) + norm_epsilon)
    return (centered * scale, scale)


def norm_rows_back(unit, scale, gain, upstream):
    weighted = upstream * gain
    first = jnp.mean(weighted, axis=-1, keepdims=True)
    second = jnp.mean(weighted * unit, axis=-1, keepdims=True)
    return scale * (weighted - first - unit * second)


def folded(value):
    rows = value.shape[0]
    return sum(value[start : start + 8] for start in range(0, rows, 8))


def row_blocks(rows):
    return [slice(start, start + STEP) for start in range(0, rows, STEP)]


def fetch(take, own, other, target, sem):
    @pl.when(take == 1)
    def _():
        pltpu.make_async_copy(own, target, sem).start()

    @pl.when(take != 1)
    def _():
        pltpu.make_async_copy(other, target, sem).start()


def forward_kernel(
    images,
    length,
    which,
    x_ref,
    own_qkv,
    other_qkv,
    own_proj,
    other_proj,
    gain_a,
    gain_f,
    mixed_ref,
    packed_out,
    mix_out,
    normed_ref,
    qkv_ref,
    proj_ref,
    low_ref,
    packed_ref,
    mix_ref,
    sems,
):
    rows, width = x_ref.shape
    pad = rows // images
    packed_copy = pltpu.make_async_copy(packed_ref, packed_out, sems.at[2])
    mix_copy = pltpu.make_async_copy(mix_ref, mix_out, sems.at[3])
    fetch(which[0], own_qkv, other_qkv, qkv_ref, sems.at[0])
    fetch(which[0], own_proj, other_proj, proj_ref, sems.at[1])

    for block in row_blocks(rows):
        unit, scale = norm_rows(x_ref[block, :].astype(f32))
        low_ref[block, :] = (unit * gain_a[...]).astype(bf16)

    pltpu.make_async_copy(own_qkv, qkv_ref, sems.at[0]).wait()

    @pl.loop(0, 3 * width // 256)
    def _(step):
        lanes = pl.ds(pl.multiple_of(step * 256, 256), 256)
        packed_ref[:, lanes] = nn(low_ref[...], qkv_ref[:, lanes]).astype(bf16)

    packed_copy.start()
    left = lax.broadcasted_iota(jnp.int32, (pad, PAIR), 1) < HEAD
    live = lax.broadcasted_iota(jnp.int32, (pad, pad), 0) < length

    @pl.loop(0, width // PAIR)
    def _(pair):
        def lanes(part):
            return pl.ds(pl.multiple_of(part * width + pair * PAIR, PAIR), PAIR)

        for image in range(images):
            block = slice(image * pad, (image + 1) * pad)
            queries = packed_ref[block, lanes(0)].astype(f32) * HEAD ** (-0.5)
            keys = packed_ref[block, lanes(1)]
            values = packed_ref[block, lanes(2)].T
            outs = []
            for half, rows_half in ((left, slice(0, HEAD)), (~left, slice(HEAD, PAIR))):
                scores = nt(keys, jnp.where(half, queries, 0.0).astype(bf16))
                scores = jnp.where(live, scores, -jnp.inf)
                powers = jnp.exp(scores - jnp.max(scores, axis=0, keepdims=True))
                share = 1.0 / jnp.sum(powers, axis=0, keepdims=True)
                outs.append(nn(values[rows_half], powers.astype(bf16)) * share)
            mix_ref[block, lanes(0)] = jnp.concatenate(outs, axis=0).T.astype(bf16)

    mix_copy.start()
    pltpu.make_async_copy(own_proj, proj_ref, sems.at[1]).wait()

    @pl.loop(0, width // 256)
    def _(step):
        lanes = pl.ds(pl.multiple_of(step * 256, 256), 256)
        mixed_ref[:, lanes] = x_ref[:, lanes].astype(f32) + nn(mix_ref[...], proj_ref[:, lanes])

    for block in row_blocks(rows):
        unit, scale = norm_rows(mixed_ref[block, :])
        normed_ref[block, :] = (unit * gain_f[...]).astype(bf16)
    packed_copy.wait()
    mix_copy.wait()


def backward_kernel(
    images,
    length,
    chunks,
    which,
    x_ref,
    mixed_ref,
    base_ref,
    upstream_ref,
    packed_in,
    mix_in,
    own_qkv,
    other_qkv,
    own_proj,
    other_proj,
    gain_a,
    gain_f,
    small,
    grad_out,
    gains_ref,
    pieces,
    grad_ref,
    grad_packed,
    total_low,
    low_ref,
    qkv_ref,
    proj_ref,
    total_ref,
    grad_mix,
    packed_ref,
    mix_ref,
    staged,
    turned,
    sems,
):
    rows, width = x_ref.shape
    pad = rows // images
    packed_copy = pltpu.make_async_copy(packed_in, packed_ref, sems.at[2])
    mix_copy = pltpu.make_async_copy(mix_in, mix_ref, sems.at[3])
    packed_copy.start()
    mix_copy.start()
    fetch(which[0], own_proj, other_proj, proj_ref, sems.at[1])
    fetch(which[0], own_qkv, other_qkv, qkv_ref, sems.at[0])
    gain_total = jnp.zeros((8, width), f32)
    for block in row_blocks(rows):
        unit, scale = norm_rows(mixed_ref[block, :])
        upstream = upstream_ref[block, :]
        value = base_ref[block, :].astype(f32) + norm_rows_back(
            unit, scale, gain_f[...], upstream
        )
        total_ref[block, :] = value
        total_low[block, :] = value.astype(bf16)
        source_unit, source_scale = norm_rows(x_ref[block, :].astype(f32))
        low_ref[block, :] = (source_unit * gain_a[...]).astype(bf16)
        gain_total = gain_total + folded(upstream * unit)
    gains_ref[...] = jnp.zeros_like(gains_ref)
    gains_ref[1:2, :] = jnp.sum(gain_total, axis=0, keepdims=True)
    pltpu.make_async_copy(own_proj, proj_ref, sems.at[1]).wait()

    @pl.loop(0, width // 256)
    def _(step):
        lanes = pl.ds(pl.multiple_of(step * 256, 256), 256)
        grad_mix[:, lanes] = nt(total_low[...], proj_ref[lanes, :]).astype(bf16)

    packed_copy.wait()
    left = lax.broadcasted_iota(jnp.int32, (pad, PAIR), 1) < HEAD
    live = lax.broadcasted_iota(jnp.int32, (pad, pad), 0) < length

    @pl.loop(0, width // PAIR)
    def _(pair):
        def lanes(part):
            return pl.ds(pl.multiple_of(part * width + pair * PAIR, PAIR), PAIR)

        for image in range(images):
            block = slice(image * pad, (image + 1) * pad)
            queries = packed_ref[block, lanes(0)].astype(f32) * HEAD ** (-0.5)
            keys = packed_ref[block, lanes(1)]
            values = packed_ref[block, lanes(2)]
            grads = grad_mix[block, lanes(0)]
            sums = [0.0, 0.0, 0.0]
            for half in (left, ~left):
                some_queries = jnp.where(half, queries, 0.0).astype(bf16)
                some_keys = jnp.where(half, keys, 0.0).astype(bf16)
                some_grads = jnp.where(half, grads, 0.0).astype(bf16)
                scores = nt(keys, some_queries)
                scores = jnp.where(live, scores, -jnp.inf)
                powers = jnp.exp(scores - jnp.max(scores, axis=0, keepdims=True))
                weights = powers * (1.0 / jnp.sum(powers, axis=0, keepdims=True))
                grad_weights = nt(values, some_grads)
                inner = jnp.sum(grad_weights * weights, axis=0, keepdims=True)
                grad_raw = (weights * (grad_weights - inner)).astype(bf16)
                sums[0] += tn(grad_raw, some_keys)
                sums[1] += nn(grad_raw, some_queries)
                sums[2] += nn(weights.astype(bf16), some_grads)
            sums[0] = sums[0] * HEAD ** (-0.5)
            for part in range(3):
                grad_packed[block, lanes(part)] = sums[part].astype(bf16)

    mix_copy.wait()
    third = width // 3
    for side, place in ((0, 1 - which[1]), (1, which[1])):
        columns = pl.ds(pl.multiple_of(place * (width // 2), 128), width // 2)
        left_rows = low_ref[:, columns].T
        right_rows = mix_ref[:, columns].T
        for step in range(12):
            if step < 9:
                value = nn(left_rows, grad_packed[:, step * third : (step + 1) * third])
            else:
                value = nn(right_rows, total_low[:, (step - 9) * third : (step - 8) * third])
            out, spot = divmod(step, 12 // chunks)
            staged[side * chunks + out][:, spot * third : (spot + 1) * third] = value.astype(bf16)
        for index in range(side * chunks, (side + 1) * chunks - bool(small)):
            pltpu.make_async_copy(staged[index], pieces[index], sems.at[4 + index]).start()

    pltpu.make_async_copy(own_qkv, qkv_ref, sems.at[0]).wait()

    @pl.loop(0, width // 256)
    def _(step):
        lanes = pl.ds(pl.multiple_of(step * 256, 256), 256)
        grad_ref[:, lanes] = nt(grad_packed[...], qkv_ref[lanes, :])

    gain_total = jnp.zeros((8, width), f32)
    for block in row_blocks(rows):
        unit, scale = norm_rows(x_ref[block, :].astype(f32))
        upstream = grad_ref[block, :]
        value = total_ref[block, :] + norm_rows_back(unit, scale, gain_a[...], upstream)
        grad_out[block, :] = value.astype(grad_out.dtype)
        gain_total = gain_total + folded(upstream * unit)
    gains_ref[0:1, :] = jnp.sum(gain_total, axis=0, keepdims=True)
    half_width = width // 2
    if small:
        turned[...] = jnp.concatenate([gains_ref[...], small[1][...]], axis=0).T
        for index, place in ((chunks - 1, 1 - which[1]), (2 * chunks - 1, which[1])):
            block = pl.ds(pl.multiple_of(place * half_width, 128), half_width)
            out = staged[index]
            start = out.shape[1] - EXTRA
            out[:, start:] = jnp.zeros((half_width, EXTRA), bf16)
            out[:, start : start + small[0].shape[1]] = small[0][block, :].astype(bf16)
            out[:, start + 128 : start + 144] = turned[block, :].astype(bf16)
        for index in (chunks - 1, 2 * chunks - 1):
            pltpu.make_async_copy(staged[index], pieces[index], sems.at[4 + index]).start()
    for index in range(2 * chunks):
        pltpu.make_async_copy(staged[index], pieces[index], sems.at[4 + index]).wait()


def whole_spec():
    return pl.BlockSpec(memory_space=pltpu.VMEM)


def kept_far(value):
    return pltpu.with_memory_space_constraint(value, pltpu.HBM)


def attention_forward(which, x, weights, gain_a, gain_f, images, length):
    rows, width = x.shape
    far = pl.BlockSpec(memory_space=pltpu.HBM)
    near = whole_spec()
    return pl.pallas_call(
        functools.partial(forward_kernel, images, length),
        out_shape=(
            jax.ShapeDtypeStruct((rows, width), f32),
            pltpu.HBM((rows, 3 * width), bf16),
            pltpu.HBM((rows, width), bf16),
            jax.ShapeDtypeStruct((rows, width), bf16),
        ),
        in_specs=[pl.BlockSpec(memory_space=pltpu.SMEM), near, far, far, far, far, near, near],
        out_specs=(near, far, far, near),
        scratch_shapes=[
            pltpu.VMEM((width, 3 * width), bf16),
            pltpu.VMEM((width, width), bf16),
            pltpu.VMEM((rows, width), bf16),
            pltpu.VMEM((rows, 3 * width), bf16),
            pltpu.VMEM((rows, width), bf16),
            pltpu.SemaphoreType.DMA((4,)),
        ],
        compiler_params=pltpu.CompilerParams(vmem_limit_bytes=24 * 2**20),
        cost_estimate=pl.CostEstimate(
            flops=10 * rows * width * width, bytes_accessed=12 * 2**20, transcendentals=2**20
        ),
        name="attention_forward",
    )(which, x, *[kept_far(value) for value in weights], gain_a, gain_f)


def attention_backward(
    which,
    x,
    mixed,
    base,
    upstream,
    packed,
    mix,
    weights,
    gain_a,
    gain_f,
    images,
    length,
    chunks,
    dtype,
    small=(),
    after=(),
):
    rows, width = x.shape
    far = pl.BlockSpec(memory_space=pltpu.HBM)
    near = whole_spec()
    sizes = [4 * width // chunks] * chunks
    if small:
        sizes[-1] += EXTRA
    sizes = sizes * 2
    first_out = 13 + len(small) + len(after)

    def kernel(*refs):
        outs = refs[first_out : first_out + 2 + 2 * chunks]
        scratch = refs[first_out + 2 + 2 * chunks :]
        backward_kernel(
            images,
            length,
            chunks,
            *refs[:13],
            refs[13 : 13 + len(small)],
            outs[0],
            outs[1],
            outs[2:],
            *scratch[:10],
            scratch[10 : 10 + 2 * chunks],
            *scratch[10 + 2 * chunks :],
        )

    return pl.pallas_call(
        kernel,
        out_shape=(
            jax.ShapeDtypeStruct((rows, width), dtype),
            jax.ShapeDtypeStruct((8, width), f32),
        )
        + tuple(pltpu.HBM((width // 2, size), bf16) for size in sizes),
        in_specs=[pl.BlockSpec(memory_space=pltpu.SMEM)]
        + [near] * 4
        + [far] * 6
        + [near] * (2 + len(small))
        + [pl.BlockSpec(memory_space=pl.ANY)] * len(after),
        out_specs=(near, near) + (far,) * (2 * chunks),
        scratch_shapes=[
            pltpu.VMEM((rows, width), f32),
            pltpu.VMEM((rows, 3 * width), bf16),
            pltpu.VMEM((rows, width), bf16),
            pltpu.VMEM((rows, width), bf16),
            pltpu.VMEM((width, 3 * width), bf16),
            pltpu.VMEM((width, width), bf16),
            pltpu.VMEM((rows, width), f32),
            pltpu.VMEM((rows, width), bf16),
            pltpu.VMEM((rows, 3 * width), bf16),
            pltpu.VMEM((rows, width), bf16),
        ]
        + [pltpu.VMEM((width // 2, size), bf16) for size in sizes]
        + [pltpu.VMEM((width, 16), f32), pltpu.SemaphoreType.DMA((4 + 2 * chunks,))],
        compiler_params=pltpu.CompilerParams(vmem_limit_bytes=32 * 2**20),
        cost_estimate=pl.CostEstimate(
            flops=28 * rows * width * width, bytes_accessed=24 * 2**20, transcendentals=2**20
        ),
        name="attention_backward",
    )(
        which,
        x,
        mixed,
        base,
        upstream,
        *[kept_far(value) for value in (packed, mix, *weights)],
        gain_a,
        gain_f,
        *small,
        *after,
    )


def gelu_pair(hidden):
    cubic = 0.7978845608028654
    square = hidden * hidden
    curve = jnp.tanh(cubic * (hidden + 0.044715 * (square * hidden)))
    left = 0.5 * (1.0 + curve)
    slope = left + 0.5 * hidden * (1.0 - curve * curve) * (
        cubic * (1.0 + 3.0 * 0.044715 * square)
    )
    return (hidden * left, slope)


def refresh_kernel(x_ref, in_ref, *rest):
    active_ref, slope_ref = rest[-2:]
    active, slope = gelu_pair(nn(x_ref[...], in_ref[...]))
    active_ref[...] = active.astype(bf16)
    slope_ref[...] = slope.astype(bf16)


def mlp_refresh(x, weight_in, after):
    rows, width = x.shape
    hidden = weight_in.shape[1]
    step = 512
    block = pl.BlockSpec((rows, step), lambda index: (0, index))
    return pl.pallas_call(
        refresh_kernel,
        grid=(hidden // step,),
        in_specs=[
            pl.BlockSpec((rows, width), lambda index: (0, 0)),
            pl.BlockSpec((width, step), lambda index: (0, index)),
        ]
        + [pl.BlockSpec(memory_space=pl.ANY)] * len(after),
        out_specs=(block, block),
        out_shape=(pltpu.HBM((rows, hidden), bf16),) * 2,
        compiler_params=pltpu.CompilerParams(vmem_limit_bytes=44 * 2**20),
        cost_estimate=pl.CostEstimate(
            flops=2 * rows * width * hidden,
            bytes_accessed=10 * 2**20,
            transcendentals=rows * hidden,
        ),
        name="mlp_refresh",
    )(x, weight_in, *after)


def mlp_kernel(
    section,
    x_ref,
    up_ref,
    in_ref,
    out_ref,
    active_ref,
    slope_ref,
    grad_ref,
    in_send,
    in_keep,
    out_send,
    out_keep,
    x_turned,
):
    half = x_ref.shape[1] // 2

    @pl.when(pl.program_id(0) == 0)
    def _():
        x_turned[...] = x_ref[...].T
        grad_ref[...] = jnp.zeros_like(grad_ref)

    grad_hidden = (nt(up_ref[...], out_ref[...]) * slope_ref[...].astype(f32)).astype(bf16)
    grad_ref[...] += nt(grad_hidden, in_ref[...])
    turned = active_ref[...].T
    for which, first, second in (
        (1 - section[0], in_send, out_send),
        (section[0], in_keep, out_keep),
    ):
        block = pl.ds(pl.multiple_of(which * half, 128), half)
        first[...] = nn(x_turned[block, :], grad_hidden).astype(bf16)
        second[...] = nn(turned, up_ref[:, block]).astype(bf16)


def mlp_backward(section, x, up, weight_in, weight_out, active, slope, after):
    rows, width = x.shape
    hidden = weight_in.shape[1]
    step = 512
    half = width // 2
    fixed = pl.BlockSpec((rows, width), lambda index, place: (0, 0))
    saved = pl.BlockSpec((rows, step), lambda index, place: (0, index))
    across = pl.BlockSpec((half, step), lambda index, place: (0, index))
    down = pl.BlockSpec((step, half), lambda index, place: (index, 0))

    def kernel(*refs):
        mlp_kernel(*refs[:7], *refs[7 + len(after) :])

    return pl.pallas_call(
        kernel,
        grid_spec=pltpu.PrefetchScalarGridSpec(
            num_scalar_prefetch=1,
            grid=(hidden // step,),
            in_specs=[
                fixed,
                fixed,
                pl.BlockSpec((width, step), lambda index, place: (0, index)),
                pl.BlockSpec((step, width), lambda index, place: (index, 0)),
                saved,
                saved,
            ]
            + [pl.BlockSpec(memory_space=pl.ANY)] * len(after),
            out_specs=(fixed, across, across, down, down),
            scratch_shapes=[pltpu.VMEM((width, rows), bf16)],
        ),
        out_shape=(
            jax.ShapeDtypeStruct((rows, width), f32),
            pltpu.HBM((half, hidden), bf16),
            pltpu.HBM((half, hidden), bf16),
            pltpu.HBM((hidden, half), bf16),
            pltpu.HBM((hidden, half), bf16),
        ),
        compiler_params=pltpu.CompilerParams(vmem_limit_bytes=44 * 2**20),
        cost_estimate=pl.CostEstimate(
            flops=8 * rows * width * hidden, bytes_accessed=28 * 2**20, transcendentals=0
        ),
        name="mlp_backward",
    )(section, x, up, weight_in, weight_out, kept_far(active), kept_far(slope), *after)


def expert_kernel(
    own,
    x_ref,
    packet_ref,
    router_ref,
    in_ref,
    out_ref,
    *rest,
):
    back_ref, result_ref, active_ref, hidden_ref, up_ref, total_ref, grad_ref = rest[-7:]
    slots, width = x_ref.shape

    @pl.when(pl.program_id(0) == 0)
    def _():
        grad_ref[...] = jnp.zeros_like(grad_ref)
        total_ref[...] = jnp.zeros_like(total_ref)
        logits = nn(x_ref[...], router_ref[...])
        experts = lax.broadcasted_iota(jnp.int32, logits.shape, 1)
        rival = packet_ref[:, width : width + 1].astype(f32).astype(jnp.int32)
        own_logit = jnp.sum(jnp.where(experts == own[0], logits, 0.0), axis=1, keepdims=True)
        rival_logit = jnp.sum(jnp.where(experts == rival, logits, 0.0), axis=1, keepdims=True)
        top = jnp.maximum(own_logit, rival_logit)
        power = jnp.exp(own_logit - top)
        gate = power / (power + jnp.exp(rival_logit - top))
        up_ref[...] = (gate * packet_ref[:, :width].astype(f32)).astype(bf16)

    active, slope = gelu_pair(nn(x_ref[...], in_ref[0]))
    active = active.astype(bf16)
    total_ref[...] += nn(active, out_ref[0])
    grad_hidden = (nt(up_ref[...], out_ref[0]) * slope).astype(bf16)
    grad_ref[...] += nt(grad_hidden, in_ref[0])
    active_ref[...] = active
    hidden_ref[...] = grad_hidden

    @pl.when(pl.program_id(0) == pl.num_programs(0) - 1)
    def _():
        result = total_ref[...].astype(bf16)
        result_ref[...] = result
        back_ref[:, :width] = grad_ref[...].astype(bf16)
        rest = jnp.sum(
            packet_ref[:, :width].astype(f32) * result.astype(f32), axis=1, keepdims=True
        )
        lanes = lax.broadcasted_iota(jnp.int32, (slots, PAIR), 1)
        value = jnp.zeros((slots, PAIR), f32)
        for lane in range(3):
            part = rest.astype(bf16).astype(f32)
            value = jnp.where(lanes == lane, part, value)
            rest = rest - part
        back_ref[:, width:] = value.astype(bf16)


def expert_pass(own, x, packet, router, weight_in, weight_out, after):
    slots, width = x.shape
    hidden = weight_in.shape[2]
    step = 512

    def fixed(shape):
        return pl.BlockSpec(shape, lambda index, place: (0, 0))

    saved = pl.BlockSpec((slots, step), lambda index, place: (0, index))
    return pl.pallas_call(
        expert_kernel,
        grid_spec=pltpu.PrefetchScalarGridSpec(
            num_scalar_prefetch=1,
            grid=(hidden // step,),
            in_specs=[
                fixed(x.shape),
                fixed(packet.shape),
                fixed(router.shape),
                pl.BlockSpec((1, width, step), lambda index, place: (0, 0, index)),
                pl.BlockSpec((1, step, width), lambda index, place: (0, index, 0)),
            ]
            + [pl.BlockSpec(memory_space=pl.ANY)] * len(after),
            out_specs=(fixed(packet.shape), fixed(x.shape), saved, saved, fixed(x.shape)),
            scratch_shapes=[
                pltpu.VMEM((slots, width), f32),
                pltpu.VMEM((slots, width), f32),
            ],
        ),
        out_shape=(
            jax.ShapeDtypeStruct(packet.shape, bf16),
            jax.ShapeDtypeStruct(x.shape, bf16),
            pltpu.HBM((slots, hidden), bf16),
            pltpu.HBM((slots, hidden), bf16),
            jax.ShapeDtypeStruct(x.shape, bf16),
        ),
        compiler_params=pltpu.CompilerParams(vmem_limit_bytes=44 * 2**20),
        cost_estimate=pl.CostEstimate(
            flops=8 * slots * width * hidden,
            bytes_accessed=16 * 2**20,
            transcendentals=slots * hidden,
        ),
        name="expert_pass",
    )(own, x, packet, router, weight_in, weight_out, *after)


def expert_product_kernel(
    x_ref, up_ref, active_ref, hidden_ref, in_grad, out_grad, x_turned
):
    @pl.when(pl.program_id(0) == 0)
    def _():
        x_turned[...] = x_ref[...].T

    in_grad[...] = nn(x_turned[...], hidden_ref[...]).astype(bf16)
    out_grad[...] = nn(active_ref[...].T, up_ref[...]).astype(bf16)


def expert_products(x, up, active, grad_hidden):
    slots, width = x.shape
    hidden = active.shape[1]
    step = 512
    fixed = pl.BlockSpec((slots, width), lambda index: (0, 0))
    saved = pl.BlockSpec((slots, step), lambda index: (0, index))
    return pl.pallas_call(
        expert_product_kernel,
        grid=(hidden // step,),
        in_specs=[fixed, fixed, saved, saved],
        out_specs=(
            pl.BlockSpec((width, step), lambda index: (0, index)),
            pl.BlockSpec((step, width), lambda index: (index, 0)),
        ),
        out_shape=(pltpu.HBM((width, hidden), bf16), pltpu.HBM((hidden, width), bf16)),
        scratch_shapes=[pltpu.VMEM((width, slots), bf16)],
        compiler_params=pltpu.CompilerParams(vmem_limit_bytes=44 * 2**20),
        cost_estimate=pl.CostEstimate(
            flops=4 * slots * width * hidden, bytes_accessed=16 * 2**20, transcendentals=0
        ),
        name="expert_products",
    )(x, up, kept_far(active), kept_far(grad_hidden))


def join_kernel(section, mine_ref, other_ref, *rest):
    out_ref = rest[-1]

    @pl.when(pl.program_id(0) == section[0])
    def _():
        out_ref[...] = mine_ref[...].astype(f32)

    @pl.when(pl.program_id(0) != section[0])
    def _():
        out_ref[...] = other_ref[...].astype(f32)


def held_step(which, step, wanted, steps):
    return jnp.where(which == wanted, step, jnp.where(which > wanted, steps - 1, 0))


def join_halves(section, mine, other, axis, after):
    rows, width = mine.shape
    steps = 3
    block = (rows // steps, width)

    def mine_map(which, step, place):
        return (held_step(which, step, place[0], steps), 0)

    def other_map(which, step, place):
        return (held_step(which, step, 1 - place[0], steps), 0)

    def out_map(which, step, place):
        return (which * steps + step, 0) if axis == 0 else (step, which)

    return pl.pallas_call(
        join_kernel,
        grid_spec=pltpu.PrefetchScalarGridSpec(
            num_scalar_prefetch=1,
            grid=(2, steps),
            in_specs=[pl.BlockSpec(block, mine_map), pl.BlockSpec(block, other_map)]
            + [pl.BlockSpec(memory_space=pl.ANY)] * len(after),
            out_specs=pl.BlockSpec(block, out_map),
        ),
        out_shape=pltpu.HBM((2 * rows, width) if axis == 0 else (rows, 2 * width), f32),
        compiler_params=pltpu.CompilerParams(vmem_limit_bytes=44 * 2**20),
        cost_estimate=pl.CostEstimate(
            flops=0, bytes_accessed=12 * rows * width, transcendentals=0
        ),
        name="join_halves",
    )(section, mine, other, *after)


def block_kernel(counts, section, *refs):
    refs = list(refs)
    sources = [[refs.pop(0) for _ in range(count)] for count in counts]
    own_small, other_small, qkv_out, proj_out, router_out, gains_out = refs
    own = pl.program_id(0) == section[0]
    cut = qkv_out.shape[1]

    def emit_small(part):
        value = part[:, part.shape[1] - EXTRA :].astype(f32)
        router_out[...] = value[:, : router_out.shape[1]]
        gains_out[...] = value[:, 128:].T[:16]

    @pl.when(own)
    def _():
        emit_small(own_small)

    @pl.when(jnp.logical_not(own))
    def _():
        emit_small(other_small)

    def emit(parts):
        start = 0
        for part in parts:
            size = min(part.shape[1], cut + proj_out.shape[1] - start)
            left = max(0, min(size, cut - start))
            if left:
                qkv_out[:, start : start + left] = part[:, :left].astype(f32)
            if left < size:
                proj_out[:, start + left - cut : start + size - cut] = part[:, left:size].astype(f32)
            start += size

    for index, parts in enumerate(sources):
        place, mine = index % 2, index < 2

        @pl.when((own == mine) & (section[0] == place))
        def _():
            emit(parts)


def own_block(section, groups, own_small, other_small, experts):
    half = groups[0][0].shape[0]
    width = 2 * half
    steps = 3
    specs = []
    for index, parts in enumerate(groups):

        def place_map(which, step, section, place=index % 2, mine=index < 2):
            wanted = section[0] if mine else 1 - section[0]
            held = held_step(which, step, wanted, steps)
            return (jnp.where(section[0] == place, held, 0), 0)

        specs += [pl.BlockSpec((half // steps, part.shape[1]), place_map) for part in parts]

    for value, mine in ((own_small, True), (other_small, False)):

        def small_map(which, step, section, mine=mine):
            return (held_step(which, step, section[0] if mine else 1 - section[0], steps), 0)

        specs.append(pl.BlockSpec((half // steps, value.shape[1]), small_map))

    def out_map(which, step, section):
        return (which * steps + step, 0)

    return pl.pallas_call(
        functools.partial(block_kernel, [len(parts) for parts in groups]),
        grid_spec=pltpu.PrefetchScalarGridSpec(
            num_scalar_prefetch=1,
            grid=(2, steps),
            in_specs=specs,
            out_specs=(
                pl.BlockSpec((half // steps, 3 * width), out_map),
                pl.BlockSpec((half // steps, width), out_map),
                pl.BlockSpec((half // steps, experts), out_map),
                pl.BlockSpec(
                    (16, half // steps), lambda which, step, section: (0, which * steps + step)
                ),
            ),
        ),
        out_shape=(
            pltpu.HBM((2 * half, 3 * width), f32),
            pltpu.HBM((2 * half, width), f32),
            jax.ShapeDtypeStruct((2 * half, experts), f32),
            jax.ShapeDtypeStruct((16, 2 * half), f32),
        ),
        compiler_params=pltpu.CompilerParams(vmem_limit_bytes=44 * 2**20),
        cost_estimate=pl.CostEstimate(
            flops=0, bytes_accessed=48 * half * width, transcendentals=0
        ),
        name="own_block",
    )(section, *[part for parts in groups for part in parts], own_small, other_small)


def total_kernel(mine_ref, other_ref, *rest):
    rest[-1][0] = mine_ref[...].astype(f32) + other_ref[...].astype(f32)


def pair_total(mine, other, after):
    rows, width = mine.shape
    steps = 6
    block = pl.BlockSpec((rows // steps, width), lambda step: (step, 0))
    return pl.pallas_call(
        total_kernel,
        grid=(steps,),
        in_specs=[block, block] + [pl.BlockSpec(memory_space=pl.ANY)] * len(after),
        out_specs=pl.BlockSpec((1, rows // steps, width), lambda step: (0, step, 0)),
        out_shape=pltpu.HBM((1, rows, width), f32),
        compiler_params=pltpu.CompilerParams(vmem_limit_bytes=44 * 2**20),
        cost_estimate=pl.CostEstimate(
            flops=rows * width, bytes_accessed=8 * rows * width, transcendentals=0
        ),
        name="pair_total",
    )(mine, other, *after)


def span(axis, start, size):
    multiple = size & -size
    piece = pl.ds(pl.multiple_of(start * size, multiple), size)
    return (piece, slice(None)) if axis == 0 else (slice(None), piece)


def in_blocks(rows, work):
    size = next(size for size in (96, 64, 48, 32, 16) if rows % size == 0)
    if rows == size:
        work(slice(0, rows))
    else:

        @pl.loop(0, rows // size)
        def _(step):
            work(pl.ds(pl.multiple_of(step * size, size), size))


def combine_kernel(plans, extra, marks, *refs):
    count = len(plans)
    sources, outs = refs[: 2 * count], list(refs[2 * count + extra :])
    for index, (now, later) in enumerate(plans):
        stays, got = sources[2 * index : 2 * index + 2]
        rows, width = got.shape
        if now[0] == "gather":
            out = outs.pop(0)
            mine = marks[now[2]]
            for source, place in ((stays, mine), (got, 1 - mine)):
                target = out.at[span(now[1], place, got.shape[now[1]])]

                def move(block, source=source, target=target):
                    target[block, :] = source[block, :]

                in_blocks(rows, move)
        elif later is not None and later[0] == "reduce":
            mine = marks[later[2]]
            for place in (1 - mine, mine):
                out = outs.pop(0)
                window = span(later[1], place, out.shape[later[1]])
                first, second = stays.at[window], got.at[window]

                def add(block, first=first, second=second, out=out):
                    out[block, :] = first[block, :] + second[block, :]

                in_blocks(out.shape[0], add)
        else:
            out = outs.pop(0)

            def add_all(block, stays=stays, got=got, out=out):
                out[block, :] = stays[block, :] + got[block, :]

            in_blocks(rows, add_all)


def combine(marks, plans, pairs, after):
    near = whole_spec()
    shapes = []
    for (now, later), (stays, got) in zip(plans, pairs):
        shape = list(got.shape)
        if now[0] == "gather":
            shape[now[1]] *= 2
            shapes.append(shape)
        elif later is not None and later[0] == "reduce":
            shape[later[1]] //= 2
            shapes += [shape, shape]
        else:
            shapes.append(shape)
    values = [value for pair in pairs for value in pair]
    return pl.pallas_call(
        functools.partial(combine_kernel, plans, len(after)),
        out_shape=[jax.ShapeDtypeStruct(shape, bf16) for shape in shapes],
        in_specs=[pl.BlockSpec(memory_space=pltpu.SMEM)]
        + [near] * len(values)
        + [pl.BlockSpec(memory_space=pl.ANY)] * len(after),
        out_specs=[near] * len(shapes),
        compiler_params=pltpu.CompilerParams(vmem_limit_bytes=8 * 2**20),
        cost_estimate=pl.CostEstimate(flops=0, bytes_accessed=1024, transcendentals=0),
        name="combine",
    )(marks, *values, *after)


def combine_plainly(marks, plans, pairs):
    outs = []
    for (now, later), (stays, got) in zip(plans, pairs):
        if now[0] == "gather":
            outs.append(
                jnp.where(
                    marks[now[2]] == 0,
                    jnp.concatenate([stays, got], axis=now[1]),
                    jnp.concatenate([got, stays], axis=now[1]),
                )
            )
            continue
        total = stays + got
        if later is not None and later[0] == "reduce":
            size = total.shape[later[1]] // 2
            for place in (1 - marks[later[2]], marks[later[2]]):
                outs.append(lax.dynamic_slice_in_dim(total, place * size, size, axis=later[1]))
        else:
            outs.append(total)
    return outs


def flipped(value, axis, bit):
    pairs = [(place, place ^ (1 << bit)) for place in range(lax.axis_size(axis))]
    return lax.ppermute(value, axis, pairs)


class Travel:
    def __init__(self, marks, sends, keeps, orders):
        self.marks = marks
        self.plans = []
        self.aligned = True
        for value, order in zip(sends, orders):
            shape = list(value.shape)
            steps = []
            for bit in order:
                axis = 0 if shape[0] % 32 == 0 or shape[1] % 256 else 1
                if shape[axis] % (32, 256)[axis]:
                    self.aligned = False
                steps.append((axis, bit))
                shape[axis] //= 2
            self.plans.append(
                [("pair", 0, 0)]
                + [("reduce", *step) for step in steps]
                + [("gather", *step) for step in reversed(steps)]
            )
        self.stage = 0
        self.stays = list(keeps)
        self.got = [flipped(value, "section", 0) for value in sends]

    @property
    def done(self):
        return not self.got

    def pending(self):
        plans = []
        for plan in self.plans:
            later = plan[self.stage + 1] if self.stage + 1 < len(plan) else None
            plans.append((plan[self.stage], later))
        return plans, list(zip(self.stays, self.got))

    def accept(self, plans, outs):
        self.stage += 1
        self.stays, self.got = [], []
        for _, later in plans:
            sent = outs.pop(0)
            if later is not None and later[0] == "reduce":
                self.stays.append(outs.pop(0))
            else:
                self.stays.append(sent)
            if later is not None:
                self.got.append(flipped(sent, "wide", later[2]))


def joint_step(travels, after=()):
    travels = [travel for travel in travels if not travel.done]
    pending = [travel.pending() for travel in travels]
    plans = sum((item[0] for item in pending), [])
    pairs = sum((item[1] for item in pending), [])
    if all(travel.aligned for travel in travels):
        outs = list(combine(travels[0].marks, plans, pairs, after))
    else:
        outs = combine_plainly(travels[0].marks, plans, pairs)
    for travel, item in zip(travels, pending):
        travel.accept(item[0], outs)
    return sum((travel.stays for travel in travels), [])


def pad_kernel(section, x_ref, out_ref):
    out_ref[...] = jnp.zeros_like(out_ref)
    out_ref[0, : x_ref.shape[1], :] = x_ref[0]


def padded_images(section, value, images, pad):
    length, width = value.shape[1:]
    out = pl.pallas_call(
        pad_kernel,
        grid_spec=pltpu.PrefetchScalarGridSpec(
            num_scalar_prefetch=1,
            grid=(images,),
            in_specs=[
                pl.BlockSpec(
                    (1, length, width), lambda index, place: (place[0] * images + index, 0, 0)
                )
            ],
            out_specs=pl.BlockSpec((1, pad, width), lambda index, place: (index, 0, 0)),
        ),
        out_shape=jax.ShapeDtypeStruct((images, pad, width), value.dtype),
        compiler_params=pltpu.CompilerParams(vmem_limit_bytes=44 * 2**20),
        cost_estimate=pl.CostEstimate(flops=0, bytes_accessed=4 * value.size, transcendentals=0),
        name="padded_images",
    )(section, value)
    return out.reshape(images * pad, width)


def images_kernel(section, one_ref, two_ref, from_one, from_two, *rest):
    out_ref = rest[-1]
    own = pl.program_id(0) == section[0]
    for place, mine, other in ((0, one_ref, from_one), (1, two_ref, from_two)):
        for source, wanted in ((mine, own), (other, jnp.logical_not(own))):

            @pl.when(wanted & (section[0] == place))
            def _():
                out_ref[0, 0] = source[0, : out_ref.shape[2], :].astype(out_ref.dtype)


def own_images(section, one, two, from_one, from_two, images, length, dtype, after):
    rows, width = one.shape
    pad = rows // images
    sources = [value.reshape(images, pad, width) for value in (one, two, from_one, from_two)]
    specs = []
    for index in range(4):

        def place_map(which, image, section, place=index % 2, mine=index < 2):
            wanted = (section[0] == place) & ((which == section[0]) == mine)
            return (jnp.where(wanted, image, 0), 0, 0)

        specs.append(pl.BlockSpec((1, pad, width), place_map))
    return pl.pallas_call(
        images_kernel,
        grid_spec=pltpu.PrefetchScalarGridSpec(
            num_scalar_prefetch=1,
            grid=(2, images),
            in_specs=specs + [pl.BlockSpec(memory_space=pl.ANY)] * len(after),
            out_specs=pl.BlockSpec(
                (1, 1, length, width),
                lambda which, image, section: (0, which * images + image, 0, 0),
            ),
        ),
        out_shape=pltpu.HBM((1, 2 * images, length, width), dtype),
        compiler_params=pltpu.CompilerParams(vmem_limit_bytes=44 * 2**20),
        cost_estimate=pl.CostEstimate(flops=0, bytes_accessed=12 * one.size, transcendentals=0),
        name="own_images",
    )(section, *sources, *after)


def norm_stats(stream):
    mean_value = jnp.mean(stream, axis=-1, keepdims=True)
    centered = stream - mean_value
    variance = jnp.mean(centered * centered, axis=-1, keepdims=True)
    return centered * lax.rsqrt(variance + norm_epsilon)


def slot_plan(ids, rank, capacity):
    before = rank[None, :] < rank[:, None]
    first, second = ids[:, 0], ids[:, 1]
    same_first = (first[:, None] == first[None, :]) & before
    same_second = (second[:, None] == second[None, :]) & before
    crossed = second[:, None] == first[None, :]
    place_first = jnp.sum(same_first.astype(jnp.int32), axis=1)
    place_second = jnp.sum(same_second.astype(jnp.int32) + crossed.astype(jnp.int32), axis=1)
    slot_first = jnp.where(place_first < capacity, first * capacity + place_first, -1)
    slot_second = jnp.where(place_second < capacity, second * capacity + place_second, -1)
    return (jnp.where(first >= 0, slot_first, -1), jnp.where(second >= 0, slot_second, -1))


def body(
    patches,
    out_cotangent,
    attn_gain,
    qkv_weight,
    proj_weight,
    ffn_gain,
    mlp_in,
    mlp_out,
    router_weight,
    expert_in,
    expert_out,
    expert_ids,
    priority,
):
    expert_count = lax.axis_size("wide")
    sections = lax.axis_size("section")
    section = lax.axis_index("section")
    own_expert = lax.axis_index("wide")
    is_first = section == 0
    images = patches.shape[0] // sections
    length, width = patches.shape[1:]
    pad = -(-length // STEP) * STEP
    rows = images * pad
    capacity = max(2, images * length // expert_count)
    slots = expert_count * capacity
    levels = expert_count.bit_length() - 1
    assert 1 << levels == expert_count
    place = section[None]
    marks = (own_expert >> jnp.arange(levels, dtype=jnp.int32)) & 1
    bits = list(range(levels))
    third = max(1, levels // 3)
    groups = [bits[:third], bits[third : 2 * third], bits[2 * third : -1]]
    across_x = groups[0] + groups[1] + groups[2] + bits[-1:]
    across_y = groups[1] + groups[2] + groups[0] + bits[-1:]
    across_z = groups[2] + groups[0] + groups[1] + bits[-1:]

    def swap(value):
        return flipped(value, "section", 0)

    def exchange(value):
        return lax.all_to_all(value, "wide", split_axis=0, concat_axis=0, tiled=True)

    def across(value):
        shape = (expert_count, capacity, value.shape[1])
        return exchange(value.reshape(shape)).reshape(value.shape)

    other_qkv, other_proj = swap(qkv_weight[0]), swap(proj_weight[0])
    gains = jnp.concatenate([attn_gain, ffn_gain], axis=0)
    other_gains = swap(gains)
    gains_one = jnp.where(is_first, gains, other_gains)
    gains_two = jnp.where(is_first, other_gains, gains)
    weights = (qkv_weight[0], other_qkv, proj_weight[0], other_proj)
    which_one = jnp.stack([(section == 0).astype(jnp.int32), section])
    which_two = jnp.stack([(section == 1).astype(jnp.int32), section])

    ids = lax.dynamic_slice_in_dim(expert_ids, section * images, images)
    ids = jnp.pad(ids, ((0, 0), (0, pad - length), (0, 0)), constant_values=-1).reshape(rows, 2)
    rank = lax.dynamic_slice_in_dim(priority, section, 1).reshape(images, length)
    rank = jnp.pad(rank, ((0, 0), (0, pad - length))).reshape(rows)
    slot_first, slot_second = slot_plan(ids, rank, capacity)
    slot_range = jnp.arange(slots, dtype=jnp.int32)
    pick_first = slot_first[:, None] == slot_range[None, :]
    pick_second = slot_second[:, None] == slot_range[None, :]
    pick_any = (pick_first | pick_second).astype(bf16)
    kept_first = (slot_first >= 0).astype(f32)[:, None]
    kept_second = (slot_second >= 0).astype(f32)[:, None]
    rival = jnp.sum(
        jnp.where(pick_first, ids[:, 1:], 0) + jnp.where(pick_second, ids[:, :1], 0), axis=0
    )
    cotangent = padded_images(place, out_cotangent, images, pad)
    packet = jnp.concatenate(
        [
            tn(pick_any, cotangent).astype(bf16),
            jnp.broadcast_to(rival.astype(bf16)[:, None], (slots, PAIR)),
        ],
        axis=1,
    )

    stream_one = padded_images(place, patches, images, pad)
    mixed_one, packed_one, mix_one, normed_one = attention_forward(
        which_one, stream_one, weights, gains_one[:1], gains_one[1:], images, length
    )
    arrived_packet = across(packet)
    active_first = jax.nn.gelu(nn(normed_one, mlp_in)).astype(bf16)
    first_low = (mixed_one + nn(active_first, mlp_out)).astype(bf16)

    mixed_two, packed_two, mix_two, normed_two = attention_forward(
        which_two, first_low, weights, gains_two[:1], gains_two[1:], images, length
    )
    leaving = tn(pick_any, normed_two).astype(bf16)
    arrived = across(leaving)
    active_one, slope_one = mlp_refresh(normed_one, mlp_in, (leaving,))
    back, result, active, grad_hidden, grad_rows = expert_pass(
        own_expert[None],
        arrived,
        arrived_packet,
        router_weight,
        expert_in,
        expert_out,
        (kept_far(active_one), kept_far(slope_one)),
    )
    grad_expert_in, grad_expert_out = expert_products(arrived, grad_rows, active, grad_hidden)
    back = across(back)
    result, back, _ = lax.optimization_barrier((result, back, grad_expert_out[:16, :128]))
    returned = across(result)
    other_expert_in, other_expert_out = swap(grad_expert_in), swap(grad_expert_out)

    from_low_one = lax.ppermute(first_low, "section", [(1, 0)])
    expert_range = jnp.arange(expert_count, dtype=jnp.int32)
    logits = nn(normed_two, router_weight)
    one_hot = (ids[:, :, None] == expert_range[None, None, :]).astype(f32)
    chosen = jnp.sum(one_hot * logits[:, None, :], axis=-1)
    gates = jax.nn.softmax(chosen, axis=-1)
    low_first, low_second = pick_first.astype(bf16), pick_second.astype(bf16)
    grad_gates = jnp.concatenate(
        [
            jnp.sum(nn(low, back[:, width:]), axis=-1, keepdims=True)
            for low in (low_first, low_second)
        ],
        axis=1,
    )
    grad_chosen = gates * (grad_gates - jnp.sum(gates * grad_gates, axis=-1, keepdims=True))
    grad_logits = jnp.sum(one_hot * grad_chosen[:, :, None], axis=1).astype(bf16)
    grad_router = tn(normed_two, grad_logits)
    grad_normed_two = nn(pick_any, back[:, :width]) + nt(grad_logits, router_weight)
    second_low = (
        mixed_two
        + kept_first * gates[:, :1] * nn(low_first, returned)
        + kept_second * gates[:, 1:] * nn(low_second, returned)
    ).astype(bf16)
    grad_first, small_two, *pieces = attention_backward(
        which_two,
        first_low,
        mixed_two,
        cotangent,
        grad_normed_two,
        packed_two,
        mix_two,
        weights,
        gains_two[:1],
        gains_two[1:],
        images,
        length,
        1,
        bf16,
    )
    two = Travel(marks, pieces[:1], pieces[1:], [across_x])
    grad_normed_one, in_send, in_keep, out_send, out_keep = mlp_backward(
        place,
        normed_one,
        grad_first,
        mlp_in,
        mlp_out,
        active_one,
        slope_one,
        after=(kept_far(other_expert_in), kept_far(other_expert_out), from_low_one, returned),
    )
    mlp_first = Travel(marks, [in_send], [in_keep], [across_z])
    mlp_second = Travel(marks, [out_send], [out_keep], [across_y])
    early = [two, mlp_first, mlp_second]
    from_low_two = lax.ppermute(second_low, "section", [(0, 1)])
    from_grad_two = lax.ppermute(grad_first, "section", [(0, 1)])
    grad_one, small_one, *pieces = attention_backward(
        which_one,
        stream_one,
        mixed_one,
        grad_first,
        grad_normed_one,
        packed_one,
        mix_one,
        weights,
        gains_one[:1],
        gains_one[1:],
        images,
        length,
        2,
        f32,
        small=(grad_router, small_two),
        after=joint_step(early, after=[second_low]),
    )
    one = Travel(marks, pieces[:2], pieces[2:], [across_x, across_y])
    last = joint_step(early, after=[from_low_two, from_grad_two])

    def settled(value):
        return lax.optimization_barrier(jnp.transpose(value[0], (1, 0, 2)))

    activations = settled(
        own_images(
            place, first_low, second_low, from_low_one, from_low_two, images, length, bf16, last
        )
    )
    last = joint_step(early + [one], after=[kept_far(activations)])
    expert_in_sum = pair_total(grad_expert_in, other_expert_in, tuple(last))
    last = joint_step(early + [one], after=[kept_far(expert_in_sum)])
    expert_out_sum = pair_total(grad_expert_out, other_expert_out, tuple(last))
    last = joint_step(early + [one], after=[kept_far(expert_out_sum)])
    late_grad, *last = lax.optimization_barrier((grad_one, *last))
    from_grad_one = lax.ppermute(late_grad, "section", [(1, 0)])
    last = joint_step(early + [one], after=[*last, from_grad_one])
    last = joint_step(early + [one], after=last)
    last = joint_step(early + [one], after=last)
    input_grads = settled(
        own_images(
            place, grad_one, grad_first, from_grad_one, from_grad_two, images, length, f32, last
        )
    )
    last = [kept_far(input_grads)]
    while not two.done:
        last = joint_step(early + [one], after=last)

    other_in, other_out = swap(mlp_first.stays[0]), swap(mlp_second.stays[0])
    last = joint_step([one], after=(other_in, other_out))
    mlp_in_sum = join_halves(place, mlp_first.stays[0], other_in, 0, tuple(last))
    mlp_out_sum = join_halves(
        place, mlp_second.stays[0], other_out, 1, (kept_far(mlp_in_sum),)
    )
    from_two = [lax.ppermute(value, "section", [(0, 1)]) for value in two.stays]
    last = [kept_far(mlp_out_sum)]
    while not one.done:
        last = joint_step([one], after=last)
    from_one = [lax.ppermute(one.stays[0], "section", [(1, 0)]), swap(one.stays[1])]
    qkv_grad, proj_grad, sum_router, gain_sums = own_block(
        place,
        (one.stays, two.stays, from_one, from_two),
        one.stays[1],
        from_one[1],
        expert_count,
    )
    small_block = lax.dynamic_slice_in_dim(gain_sums, 8 * section, 8)
    return (
        jnp.transpose(activations, (1, 0, 2))[None],
        jnp.transpose(input_grads, (1, 0, 2))[None],
        small_block[:1],
        qkv_grad[None],
        proj_grad[None],
        small_block[1:2],
        mlp_in_sum,
        mlp_out_sum,
        sum_router,
        expert_in_sum,
        expert_out_sum,
    )


def solution(mesh):
    in_specs = (
        P("wide", None, None),
        P("wide", None, None),
        P("section", None),
        P("section", None, None),
        P("section", None, None),
        P("section", None),
        P(),
        P(),
        P(),
        P("wide", None, None),
        P("wide", None, None),
        P("wide", None, None),
        P("wide", None),
    )
    out_specs = (
        P("section", "wide", None, None),
        P("section", "wide", None, None),
        P("section", None),
        P("section", None, None),
        P("section", None, None),
        P("section", None),
        P(),
        P(),
        P(),
        P("wide", None, None),
        P("wide", None, None),
    )
    return jax.shard_map(body, mesh=mesh, in_specs=in_specs, out_specs=out_specs, check_vma=False)
```

```python
import functools

import jax
import jax.numpy as jnp
from jax import lax
from jax.experimental import pallas as pl
from jax.experimental.pallas import tpu as pltpu
from jax.sharding import PartitionSpec as P

H = 12
HEAD = 64
PAIR = 2 * HEAD
STEP = 16
EXTRA = 256
norm_epsilon = 1e-06
bf16 = jnp.bfloat16
f32 = jnp.float32


def dot(left, right, dims):
    return lax.dot_general(left, right, (dims, ((), ())), preferred_element_type=f32)


def nn(left, right):
    return dot(left, right, ((1,), (0,)))


def nt(left, right):
    return dot(left, right, ((1,), (1,)))


def tn(left, right):
    return dot(left, right, ((0,), (0,)))


def norm_rows(value):
    mean_value = jnp.mean(value, axis=-1, keepdims=True)
    centered = value - mean_value
    scale = lax.rsqrt(jnp.mean(centered * centered, axis=-1, keepdims=True) + norm_epsilon)
    return (centered * scale, scale)


def norm_rows_back(unit, scale, gain, upstream):
    weighted = upstream * gain
    first = jnp.mean(weighted, axis=-1, keepdims=True)
    second = jnp.mean(weighted * unit, axis=-1, keepdims=True)
    return scale * (weighted - first - unit * second)


def folded(value):
    rows = value.shape[0]
    return sum(value[start : start + 8] for start in range(0, rows, 8))


def row_blocks(rows):
    return [slice(start, start + STEP) for start in range(0, rows, STEP)]


def fetch(take, own, other, target, sem):
    @pl.when(take == 1)
    def _():
        pltpu.make_async_copy(own, target, sem).start()

    @pl.when(take != 1)
    def _():
        pltpu.make_async_copy(other, target, sem).start()


def forward_kernel(
    images,
    length,
    which,
    x_ref,
    own_qkv,
    other_qkv,
    own_proj,
    other_proj,
    gain_a,
    gain_f,
    mixed_ref,
    packed_out,
    mix_out,
    normed_ref,
    qkv_ref,
    proj_ref,
    low_ref,
    packed_ref,
    mix_ref,
    sems,
):
    rows, width = x_ref.shape
    pad = rows // images
    packed_copy = pltpu.make_async_copy(packed_ref, packed_out, sems.at[2])
    mix_copy = pltpu.make_async_copy(mix_ref, mix_out, sems.at[3])
    fetch(which[0], own_qkv, other_qkv, qkv_ref, sems.at[0])
    fetch(which[0], own_proj, other_proj, proj_ref, sems.at[1])

    for block in row_blocks(rows):
        unit, scale = norm_rows(x_ref[block, :].astype(f32))
        low_ref[block, :] = (unit * gain_a[...]).astype(bf16)

    pltpu.make_async_copy(own_qkv, qkv_ref, sems.at[0]).wait()

    @pl.loop(0, 3 * width // 256)
    def _(step):
        lanes = pl.ds(pl.multiple_of(step * 256, 256), 256)
        packed_ref[:, lanes] = nn(low_ref[...], qkv_ref[:, lanes]).astype(bf16)

    packed_copy.start()
    left = lax.broadcasted_iota(jnp.int32, (pad, PAIR), 1) < HEAD
    live = lax.broadcasted_iota(jnp.int32, (pad, pad), 0) < length

    @pl.loop(0, width // PAIR)
    def _(pair):
        def lanes(part):
            return pl.ds(pl.multiple_of(part * width + pair * PAIR, PAIR), PAIR)

        for image in range(images):
            block = slice(image * pad, (image + 1) * pad)
            queries = packed_ref[block, lanes(0)].astype(f32) * HEAD ** (-0.5)
            keys = packed_ref[block, lanes(1)]
            values = packed_ref[block, lanes(2)].T
            outs = []
            for half, rows_half in ((left, slice(0, HEAD)), (~left, slice(HEAD, PAIR))):
                scores = nt(keys, jnp.where(half, queries, 0.0).astype(bf16))
                scores = jnp.where(live, scores, -jnp.inf)
                powers = jnp.exp(scores - jnp.max(scores, axis=0, keepdims=True))
                share = 1.0 / jnp.sum(powers, axis=0, keepdims=True)
                outs.append(nn(values[rows_half], powers.astype(bf16)) * share)
            mix_ref[block, lanes(0)] = jnp.concatenate(outs, axis=0).T.astype(bf16)

    mix_copy.start()
    pltpu.make_async_copy(own_proj, proj_ref, sems.at[1]).wait()

    @pl.loop(0, width // 256)
    def _(step):
        lanes = pl.ds(pl.multiple_of(step * 256, 256), 256)
        mixed_ref[:, lanes] = x_ref[:, lanes].astype(f32) + nn(mix_ref[...], proj_ref[:, lanes])

    for block in row_blocks(rows):
        unit, scale = norm_rows(mixed_ref[block, :])
        normed_ref[block, :] = (unit * gain_f[...]).astype(bf16)
    packed_copy.wait()
    mix_copy.wait()


def backward_kernel(
    images,
    length,
    chunks,
    which,
    x_ref,
    mixed_ref,
    base_ref,
    upstream_ref,
    packed_in,
    mix_in,
    own_qkv,
    other_qkv,
    own_proj,
    other_proj,
    gain_a,
    gain_f,
    small,
    grad_out,
    gains_ref,
    pieces,
    grad_ref,
    grad_packed,
    total_low,
    low_ref,
    qkv_ref,
    proj_ref,
    total_ref,
    grad_mix,
    packed_ref,
    mix_ref,
    staged,
    turned,
    sems,
):
    rows, width = x_ref.shape
    pad = rows // images
    packed_copy = pltpu.make_async_copy(packed_in, packed_ref, sems.at[2])
    mix_copy = pltpu.make_async_copy(mix_in, mix_ref, sems.at[3])
    packed_copy.start()
    mix_copy.start()
    fetch(which[0], own_proj, other_proj, proj_ref, sems.at[1])
    fetch(which[0], own_qkv, other_qkv, qkv_ref, sems.at[0])
    gain_total = jnp.zeros((8, width), f32)
    for block in row_blocks(rows):
        unit, scale = norm_rows(mixed_ref[block, :])
        upstream = upstream_ref[block, :]
        value = base_ref[block, :].astype(f32) + norm_rows_back(
            unit, scale, gain_f[...], upstream
        )
        total_ref[block, :] = value
        total_low[block, :] = value.astype(bf16)
        source_unit, source_scale = norm_rows(x_ref[block, :].astype(f32))
        low_ref[block, :] = (source_unit * gain_a[...]).astype(bf16)
        gain_total = gain_total + folded(upstream * unit)
    gains_ref[...] = jnp.zeros_like(gains_ref)
    gains_ref[1:2, :] = jnp.sum(gain_total, axis=0, keepdims=True)
    pltpu.make_async_copy(own_proj, proj_ref, sems.at[1]).wait()

    @pl.loop(0, width // 256)
    def _(step):
        lanes = pl.ds(pl.multiple_of(step * 256, 256), 256)
        grad_mix[:, lanes] = nt(total_low[...], proj_ref[lanes, :]).astype(bf16)

    packed_copy.wait()
    left = lax.broadcasted_iota(jnp.int32, (pad, PAIR), 1) < HEAD
    live = lax.broadcasted_iota(jnp.int32, (pad, pad), 0) < length

    @pl.loop(0, width // PAIR)
    def _(pair):
        def lanes(part):
            return pl.ds(pl.multiple_of(part * width + pair * PAIR, PAIR), PAIR)

        for image in range(images):
            block = slice(image * pad, (image + 1) * pad)
            queries = packed_ref[block, lanes(0)].astype(f32) * HEAD ** (-0.5)
            keys = packed_ref[block, lanes(1)]
            values = packed_ref[block, lanes(2)]
            grads = grad_mix[block, lanes(0)]
            sums = [0.0, 0.0, 0.0]
            for half in (left, ~left):
                some_queries = jnp.where(half, queries, 0.0).astype(bf16)
                some_keys = jnp.where(half, keys, 0.0).astype(bf16)
                some_grads = jnp.where(half, grads, 0.0).astype(bf16)
                scores = nt(keys, some_queries)
                scores = jnp.where(live, scores, -jnp.inf)
                powers = jnp.exp(scores - jnp.max(scores, axis=0, keepdims=True))
                weights = powers * (1.0 / jnp.sum(powers, axis=0, keepdims=True))
                grad_weights = nt(values, some_grads)
                inner = jnp.sum(grad_weights * weights, axis=0, keepdims=True)
                grad_raw = (weights * (grad_weights - inner)).astype(bf16)
                sums[0] += tn(grad_raw, some_keys)
                sums[1] += nn(grad_raw, some_queries)
                sums[2] += nn(weights.astype(bf16), some_grads)
            sums[0] = sums[0] * HEAD ** (-0.5)
            for part in range(3):
                grad_packed[block, lanes(part)] = sums[part].astype(bf16)

    mix_copy.wait()
    third = width // 3
    for side, place in ((0, 1 - which[1]), (1, which[1])):
        columns = pl.ds(pl.multiple_of(place * (width // 2), 128), width // 2)
        left_rows = low_ref[:, columns].T
        right_rows = mix_ref[:, columns].T
        for step in range(12):
            if step < 9:
                value = nn(left_rows, grad_packed[:, step * third : (step + 1) * third])
            else:
                value = nn(right_rows, total_low[:, (step - 9) * third : (step - 8) * third])
            out, spot = divmod(step, 12 // chunks)
            staged[side * chunks + out][:, spot * third : (spot + 1) * third] = value.astype(bf16)
        for index in range(side * chunks, (side + 1) * chunks - bool(small)):
            pltpu.make_async_copy(staged[index], pieces[index], sems.at[4 + index]).start()

    pltpu.make_async_copy(own_qkv, qkv_ref, sems.at[0]).wait()

    @pl.loop(0, width // 256)
    def _(step):
        lanes = pl.ds(pl.multiple_of(step * 256, 256), 256)
        grad_ref[:, lanes] = nt(grad_packed[...], qkv_ref[lanes, :])

    gain_total = jnp.zeros((8, width), f32)
    for block in row_blocks(rows):
        unit, scale = norm_rows(x_ref[block, :].astype(f32))
        upstream = grad_ref[block, :]
        value = total_ref[block, :] + norm_rows_back(unit, scale, gain_a[...], upstream)
        grad_out[block, :] = value.astype(grad_out.dtype)
        gain_total = gain_total + folded(upstream * unit)
    gains_ref[0:1, :] = jnp.sum(gain_total, axis=0, keepdims=True)
    half_width = width // 2
    if small:
        turned[...] = jnp.concatenate([gains_ref[...], small[1][...]], axis=0).T
        for index, place in ((chunks - 1, 1 - which[1]), (2 * chunks - 1, which[1])):
            block = pl.ds(pl.multiple_of(place * half_width, 128), half_width)
            out = staged[index]
            start = out.shape[1] - EXTRA
            out[:, start:] = jnp.zeros((half_width, EXTRA), bf16)
            out[:, start : start + small[0].shape[1]] = small[0][block, :].astype(bf16)
            out[:, start + 128 : start + 144] = turned[block, :].astype(bf16)
        for index in (chunks - 1, 2 * chunks - 1):
            pltpu.make_async_copy(staged[index], pieces[index], sems.at[4 + index]).start()
    for index in range(2 * chunks):
        pltpu.make_async_copy(staged[index], pieces[index], sems.at[4 + index]).wait()


def whole_spec():
    return pl.BlockSpec(memory_space=pltpu.VMEM)


def kept_far(value):
    return pltpu.with_memory_space_constraint(value, pltpu.HBM)


def attention_forward(which, x, weights, gain_a, gain_f, images, length):
    rows, width = x.shape
    far = pl.BlockSpec(memory_space=pltpu.HBM)
    near = whole_spec()
    return pl.pallas_call(
        functools.partial(forward_kernel, images, length),
        out_shape=(
            jax.ShapeDtypeStruct((rows, width), f32),
            pltpu.HBM((rows, 3 * width), bf16),
            pltpu.HBM((rows, width), bf16),
            jax.ShapeDtypeStruct((rows, width), bf16),
        ),
        in_specs=[pl.BlockSpec(memory_space=pltpu.SMEM), near, far, far, far, far, near, near],
        out_specs=(near, far, far, near),
        scratch_shapes=[
            pltpu.VMEM((width, 3 * width), bf16),
            pltpu.VMEM((width, width), bf16),
            pltpu.VMEM((rows, width), bf16),
            pltpu.VMEM((rows, 3 * width), bf16),
            pltpu.VMEM((rows, width), bf16),
            pltpu.SemaphoreType.DMA((4,)),
        ],
        compiler_params=pltpu.CompilerParams(vmem_limit_bytes=24 * 2**20),
        cost_estimate=pl.CostEstimate(
            flops=10 * rows * width * width, bytes_accessed=12 * 2**20, transcendentals=2**20
        ),
        name="attention_forward",
    )(which, x, *[kept_far(value) for value in weights], gain_a, gain_f)


def attention_backward(
    which,
    x,
    mixed,
    base,
    upstream,
    packed,
    mix,
    weights,
    gain_a,
    gain_f,
    images,
    length,
    chunks,
    dtype,
    small=(),
    after=(),
):
    rows, width = x.shape
    far = pl.BlockSpec(memory_space=pltpu.HBM)
    near = whole_spec()
    sizes = [4 * width // chunks] * chunks
    if small:
        sizes[-1] += EXTRA
    sizes = sizes * 2
    first_out = 13 + len(small) + len(after)

    def kernel(*refs):
        outs = refs[first_out : first_out + 2 + 2 * chunks]
        scratch = refs[first_out + 2 + 2 * chunks :]
        backward_kernel(
            images,
            length,
            chunks,
            *refs[:13],
            refs[13 : 13 + len(small)],
            outs[0],
            outs[1],
            outs[2:],
            *scratch[:10],
            scratch[10 : 10 + 2 * chunks],
            *scratch[10 + 2 * chunks :],
        )

    return pl.pallas_call(
        kernel,
        out_shape=(
            jax.ShapeDtypeStruct((rows, width), dtype),
            jax.ShapeDtypeStruct((8, width), f32),
        )
        + tuple(pltpu.HBM((width // 2, size), bf16) for size in sizes),
        in_specs=[pl.BlockSpec(memory_space=pltpu.SMEM)]
        + [near] * 4
        + [far] * 6
        + [near] * (2 + len(small))
        + [pl.BlockSpec(memory_space=pl.ANY)] * len(after),
        out_specs=(near, near) + (far,) * (2 * chunks),
        scratch_shapes=[
            pltpu.VMEM((rows, width), f32),
            pltpu.VMEM((rows, 3 * width), bf16),
            pltpu.VMEM((rows, width), bf16),
            pltpu.VMEM((rows, width), bf16),
            pltpu.VMEM((width, 3 * width), bf16),
            pltpu.VMEM((width, width), bf16),
            pltpu.VMEM((rows, width), f32),
            pltpu.VMEM((rows, width), bf16),
            pltpu.VMEM((rows, 3 * width), bf16),
            pltpu.VMEM((rows, width), bf16),
        ]
        + [pltpu.VMEM((width // 2, size), bf16) for size in sizes]
        + [pltpu.VMEM((width, 16), f32), pltpu.SemaphoreType.DMA((4 + 2 * chunks,))],
        compiler_params=pltpu.CompilerParams(vmem_limit_bytes=32 * 2**20),
        cost_estimate=pl.CostEstimate(
            flops=28 * rows * width * width, bytes_accessed=24 * 2**20, transcendentals=2**20
        ),
        name="attention_backward",
    )(
        which,
        x,
        mixed,
        base,
        upstream,
        *[kept_far(value) for value in (packed, mix, *weights)],
        gain_a,
        gain_f,
        *small,
        *after,
    )


def gelu_pair(hidden):
    cubic = 0.7978845608028654
    square = hidden * hidden
    curve = jnp.tanh(cubic * (hidden + 0.044715 * (square * hidden)))
    left = 0.5 * (1.0 + curve)
    slope = left + 0.5 * hidden * (1.0 - curve * curve) * (
        cubic * (1.0 + 3.0 * 0.044715 * square)
    )
    return (hidden * left, slope)


def refresh_kernel(x_ref, in_ref, *rest):
    active_ref, slope_ref = rest[-2:]
    active, slope = gelu_pair(nn(x_ref[...], in_ref[...]))
    active_ref[...] = active.astype(bf16)
    slope_ref[...] = slope.astype(bf16)


def mlp_refresh(x, weight_in, after):
    rows, width = x.shape
    hidden = weight_in.shape[1]
    step = 512
    block = pl.BlockSpec((rows, step), lambda index: (0, index))
    return pl.pallas_call(
        refresh_kernel,
        grid=(hidden // step,),
        in_specs=[
            pl.BlockSpec((rows, width), lambda index: (0, 0)),
            pl.BlockSpec((width, step), lambda index: (0, index)),
        ]
        + [pl.BlockSpec(memory_space=pl.ANY)] * len(after),
        out_specs=(block, block),
        out_shape=(pltpu.HBM((rows, hidden), bf16),) * 2,
        compiler_params=pltpu.CompilerParams(vmem_limit_bytes=44 * 2**20),
        cost_estimate=pl.CostEstimate(
            flops=2 * rows * width * hidden,
            bytes_accessed=10 * 2**20,
            transcendentals=rows * hidden,
        ),
        name="mlp_refresh",
    )(x, kept_far(weight_in), *after)


def mlp_kernel(
    section,
    x_ref,
    up_ref,
    in_ref,
    out_ref,
    active_ref,
    slope_ref,
    grad_ref,
    in_send,
    in_keep,
    out_send,
    out_keep,
    x_turned,
):
    half = x_ref.shape[1] // 2

    @pl.when(pl.program_id(0) == 0)
    def _():
        x_turned[...] = x_ref[...].T
        grad_ref[...] = jnp.zeros_like(grad_ref)

    grad_hidden = (nt(up_ref[...], out_ref[...]) * slope_ref[...].astype(f32)).astype(bf16)
    grad_ref[...] += nt(grad_hidden, in_ref[...])
    turned = active_ref[...].T
    for which, first, second in (
        (1 - section[0], in_send, out_send),
        (section[0], in_keep, out_keep),
    ):
        block = pl.ds(pl.multiple_of(which * half, 128), half)
        first[...] = nn(x_turned[block, :], grad_hidden).astype(bf16)
        second[...] = nn(turned, up_ref[:, block]).astype(bf16)


def mlp_backward(section, x, up, weight_in, weight_out, active, slope, after):
    rows, width = x.shape
    hidden = weight_in.shape[1]
    step = 512
    half = width // 2
    fixed = pl.BlockSpec((rows, width), lambda index, place: (0, 0))
    saved = pl.BlockSpec((rows, step), lambda index, place: (0, index))
    across = pl.BlockSpec((half, step), lambda index, place: (0, index))
    down = pl.BlockSpec((step, half), lambda index, place: (index, 0))

    def kernel(*refs):
        mlp_kernel(*refs[:7], *refs[7 + len(after) :])

    return pl.pallas_call(
        kernel,
        grid_spec=pltpu.PrefetchScalarGridSpec(
            num_scalar_prefetch=1,
            grid=(hidden // step,),
            in_specs=[
                fixed,
                fixed,
                pl.BlockSpec((width, step), lambda index, place: (0, index)),
                pl.BlockSpec((step, width), lambda index, place: (index, 0)),
                saved,
                saved,
            ]
            + [pl.BlockSpec(memory_space=pl.ANY)] * len(after),
            out_specs=(fixed, across, across, down, down),
            scratch_shapes=[pltpu.VMEM((width, rows), bf16)],
        ),
        out_shape=(
            jax.ShapeDtypeStruct((rows, width), f32),
            pltpu.HBM((half, hidden), bf16),
            pltpu.HBM((half, hidden), bf16),
            pltpu.HBM((hidden, half), bf16),
            pltpu.HBM((hidden, half), bf16),
        ),
        compiler_params=pltpu.CompilerParams(vmem_limit_bytes=44 * 2**20),
        cost_estimate=pl.CostEstimate(
            flops=8 * rows * width * hidden, bytes_accessed=28 * 2**20, transcendentals=0
        ),
        name="mlp_backward",
    )(
        section,
        x,
        up,
        *[kept_far(value) for value in (weight_in, weight_out, active, slope)],
        *after,
    )


def expert_kernel(
    own,
    x_ref,
    packet_ref,
    router_ref,
    in_ref,
    out_ref,
    *rest,
):
    back_ref, result_ref, active_ref, hidden_ref, up_ref, total_ref, grad_ref = rest[-7:]
    slots, width = x_ref.shape

    @pl.when(pl.program_id(0) == 0)
    def _():
        grad_ref[...] = jnp.zeros_like(grad_ref)
        total_ref[...] = jnp.zeros_like(total_ref)
        logits = nn(x_ref[...], router_ref[...])
        experts = lax.broadcasted_iota(jnp.int32, logits.shape, 1)
        rival = packet_ref[:, width : width + 1].astype(f32).astype(jnp.int32)
        own_logit = jnp.sum(jnp.where(experts == own[0], logits, 0.0), axis=1, keepdims=True)
        rival_logit = jnp.sum(jnp.where(experts == rival, logits, 0.0), axis=1, keepdims=True)
        top = jnp.maximum(own_logit, rival_logit)
        power = jnp.exp(own_logit - top)
        gate = power / (power + jnp.exp(rival_logit - top))
        up_ref[...] = (gate * packet_ref[:, :width].astype(f32)).astype(bf16)

    active, slope = gelu_pair(nn(x_ref[...], in_ref[0]))
    active = active.astype(bf16)
    total_ref[...] += nn(active, out_ref[0])
    grad_hidden = (nt(up_ref[...], out_ref[0]) * slope).astype(bf16)
    grad_ref[...] += nt(grad_hidden, in_ref[0])
    active_ref[...] = active
    hidden_ref[...] = grad_hidden

    @pl.when(pl.program_id(0) == pl.num_programs(0) - 1)
    def _():
        result = total_ref[...].astype(bf16)
        result_ref[...] = result
        back_ref[:, :width] = grad_ref[...].astype(bf16)
        rest = jnp.sum(
            packet_ref[:, :width].astype(f32) * result.astype(f32), axis=1, keepdims=True
        )
        lanes = lax.broadcasted_iota(jnp.int32, (slots, PAIR), 1)
        value = jnp.zeros((slots, PAIR), f32)
        for lane in range(3):
            part = rest.astype(bf16).astype(f32)
            value = jnp.where(lanes == lane, part, value)
            rest = rest - part
        back_ref[:, width:] = value.astype(bf16)


def expert_pass(own, x, packet, router, weight_in, weight_out, after):
    slots, width = x.shape
    hidden = weight_in.shape[2]
    step = 512

    def fixed(shape):
        return pl.BlockSpec(shape, lambda index, place: (0, 0))

    saved = pl.BlockSpec((slots, step), lambda index, place: (0, index))
    return pl.pallas_call(
        expert_kernel,
        grid_spec=pltpu.PrefetchScalarGridSpec(
            num_scalar_prefetch=1,
            grid=(hidden // step,),
            in_specs=[
                fixed(x.shape),
                fixed(packet.shape),
                fixed(router.shape),
                pl.BlockSpec((1, width, step), lambda index, place: (0, 0, index)),
                pl.BlockSpec((1, step, width), lambda index, place: (0, index, 0)),
            ]
            + [pl.BlockSpec(memory_space=pl.ANY)] * len(after),
            out_specs=(fixed(packet.shape), fixed(x.shape), saved, saved, fixed(x.shape)),
            scratch_shapes=[
                pltpu.VMEM((slots, width), f32),
                pltpu.VMEM((slots, width), f32),
            ],
        ),
        out_shape=(
            jax.ShapeDtypeStruct(packet.shape, bf16),
            jax.ShapeDtypeStruct(x.shape, bf16),
            pltpu.HBM((slots, hidden), bf16),
            pltpu.HBM((slots, hidden), bf16),
            jax.ShapeDtypeStruct(x.shape, bf16),
        ),
        compiler_params=pltpu.CompilerParams(vmem_limit_bytes=44 * 2**20),
        cost_estimate=pl.CostEstimate(
            flops=8 * slots * width * hidden,
            bytes_accessed=16 * 2**20,
            transcendentals=slots * hidden,
        ),
        name="expert_pass",
    )(own, x, packet, router, kept_far(weight_in), kept_far(weight_out), *after)


def expert_product_kernel(
    x_ref, up_ref, active_ref, hidden_ref, in_grad, out_grad, x_turned
):
    @pl.when(pl.program_id(0) == 0)
    def _():
        x_turned[...] = x_ref[...].T

    in_grad[...] = nn(x_turned[...], hidden_ref[...]).astype(bf16)
    out_grad[...] = nn(active_ref[...].T, up_ref[...]).astype(bf16)


def expert_products(x, up, active, grad_hidden):
    slots, width = x.shape
    hidden = active.shape[1]
    step = 512
    fixed = pl.BlockSpec((slots, width), lambda index: (0, 0))
    saved = pl.BlockSpec((slots, step), lambda index: (0, index))
    return pl.pallas_call(
        expert_product_kernel,
        grid=(hidden // step,),
        in_specs=[fixed, fixed, saved, saved],
        out_specs=(
            pl.BlockSpec((width, step), lambda index: (0, index)),
            pl.BlockSpec((step, width), lambda index: (index, 0)),
        ),
        out_shape=(pltpu.HBM((width, hidden), bf16), pltpu.HBM((hidden, width), bf16)),
        scratch_shapes=[pltpu.VMEM((width, slots), bf16)],
        compiler_params=pltpu.CompilerParams(vmem_limit_bytes=44 * 2**20),
        cost_estimate=pl.CostEstimate(
            flops=4 * slots * width * hidden, bytes_accessed=16 * 2**20, transcendentals=0
        ),
        name="expert_products",
    )(x, up, kept_far(active), kept_far(grad_hidden))


def join_kernel(section, mine_ref, other_ref, *rest):
    out_ref = rest[-1]

    @pl.when(pl.program_id(0) == section[0])
    def _():
        out_ref[...] = mine_ref[...].astype(f32)

    @pl.when(pl.program_id(0) != section[0])
    def _():
        out_ref[...] = other_ref[...].astype(f32)


def held_step(which, step, wanted, steps):
    return jnp.where(which == wanted, step, jnp.where(which > wanted, steps - 1, 0))


def join_halves(section, mine, other, axis, after):
    rows, width = mine.shape
    steps = 3
    block = (rows // steps, width)

    def mine_map(which, step, place):
        return (held_step(which, step, place[0], steps), 0)

    def other_map(which, step, place):
        return (held_step(which, step, 1 - place[0], steps), 0)

    def out_map(which, step, place):
        return (which * steps + step, 0) if axis == 0 else (step, which)

    return pl.pallas_call(
        join_kernel,
        grid_spec=pltpu.PrefetchScalarGridSpec(
            num_scalar_prefetch=1,
            grid=(2, steps),
            in_specs=[pl.BlockSpec(block, mine_map), pl.BlockSpec(block, other_map)]
            + [pl.BlockSpec(memory_space=pl.ANY)] * len(after),
            out_specs=pl.BlockSpec(block, out_map),
        ),
        out_shape=pltpu.HBM((2 * rows, width) if axis == 0 else (rows, 2 * width), f32),
        compiler_params=pltpu.CompilerParams(vmem_limit_bytes=44 * 2**20),
        cost_estimate=pl.CostEstimate(
            flops=0, bytes_accessed=12 * rows * width, transcendentals=0
        ),
        name="join_halves",
    )(section, mine, other, *after)


def block_kernel(counts, section, *refs):
    refs = list(refs)
    sources = [[refs.pop(0) for _ in range(count)] for count in counts]
    own_small, other_small, qkv_out, proj_out, router_out, gains_out = refs
    own = pl.program_id(0) == section[0]
    cut = qkv_out.shape[1]

    def emit_small(part):
        value = part[:, part.shape[1] - EXTRA :].astype(f32)
        router_out[...] = value[:, : router_out.shape[1]]
        gains_out[...] = value[:, 128:].T[:16]

    @pl.when(own)
    def _():
        emit_small(own_small)

    @pl.when(jnp.logical_not(own))
    def _():
        emit_small(other_small)

    def emit(parts):
        start = 0
        for part in parts:
            size = min(part.shape[1], cut + proj_out.shape[1] - start)
            left = max(0, min(size, cut - start))
            if left:
                qkv_out[:, start : start + left] = part[:, :left].astype(f32)
            if left < size:
                proj_out[:, start + left - cut : start + size - cut] = part[:, left:size].astype(f32)
            start += size

    for index, parts in enumerate(sources):
        place, mine = index % 2, index < 2

        @pl.when((own == mine) & (section[0] == place))
        def _():
            emit(parts)


def own_block(section, groups, own_small, other_small, experts):
    half = groups[0][0].shape[0]
    width = 2 * half
    steps = 3
    specs = []
    for index, parts in enumerate(groups):

        def place_map(which, step, section, place=index % 2, mine=index < 2):
            wanted = section[0] if mine else 1 - section[0]
            held = held_step(which, step, wanted, steps)
            return (jnp.where(section[0] == place, held, 0), 0)

        specs += [pl.BlockSpec((half // steps, part.shape[1]), place_map) for part in parts]

    for value, mine in ((own_small, True), (other_small, False)):

        def small_map(which, step, section, mine=mine):
            return (held_step(which, step, section[0] if mine else 1 - section[0], steps), 0)

        specs.append(pl.BlockSpec((half // steps, value.shape[1]), small_map))

    def out_map(which, step, section):
        return (which * steps + step, 0)

    return pl.pallas_call(
        functools.partial(block_kernel, [len(parts) for parts in groups]),
        grid_spec=pltpu.PrefetchScalarGridSpec(
            num_scalar_prefetch=1,
            grid=(2, steps),
            in_specs=specs,
            out_specs=(
                pl.BlockSpec((half // steps, 3 * width), out_map),
                pl.BlockSpec((half // steps, width), out_map),
                pl.BlockSpec((half // steps, experts), out_map),
                pl.BlockSpec(
                    (16, half // steps), lambda which, step, section: (0, which * steps + step)
                ),
            ),
        ),
        out_shape=(
            pltpu.HBM((2 * half, 3 * width), f32),
            pltpu.HBM((2 * half, width), f32),
            jax.ShapeDtypeStruct((2 * half, experts), f32),
            jax.ShapeDtypeStruct((16, 2 * half), f32),
        ),
        compiler_params=pltpu.CompilerParams(vmem_limit_bytes=44 * 2**20),
        cost_estimate=pl.CostEstimate(
            flops=0, bytes_accessed=48 * half * width, transcendentals=0
        ),
        name="own_block",
    )(section, *[part for parts in groups for part in parts], own_small, other_small)


def total_kernel(mine_ref, other_ref, *rest):
    rest[-1][0] = mine_ref[...].astype(f32) + other_ref[...].astype(f32)


def pair_total(mine, other, after):
    rows, width = mine.shape
    steps = 6
    block = pl.BlockSpec((rows // steps, width), lambda step: (step, 0))
    return pl.pallas_call(
        total_kernel,
        grid=(steps,),
        in_specs=[block, block] + [pl.BlockSpec(memory_space=pl.ANY)] * len(after),
        out_specs=pl.BlockSpec((1, rows // steps, width), lambda step: (0, step, 0)),
        out_shape=pltpu.HBM((1, rows, width), f32),
        compiler_params=pltpu.CompilerParams(vmem_limit_bytes=44 * 2**20),
        cost_estimate=pl.CostEstimate(
            flops=rows * width, bytes_accessed=8 * rows * width, transcendentals=0
        ),
        name="pair_total",
    )(mine, other, *after)


def span(axis, start, size):
    multiple = size & -size
    piece = pl.ds(pl.multiple_of(start * size, multiple), size)
    return (piece, slice(None)) if axis == 0 else (slice(None), piece)


def in_blocks(rows, work):
    size = next(size for size in (96, 64, 48, 32, 16) if rows % size == 0)
    if rows == size:
        work(slice(0, rows))
    else:

        @pl.loop(0, rows // size)
        def _(step):
            work(pl.ds(pl.multiple_of(step * size, size), size))


def combine_kernel(plans, extra, marks, *refs):
    count = len(plans)
    sources, outs = refs[: 2 * count], list(refs[2 * count + extra :])
    for index, (now, later) in enumerate(plans):
        stays, got = sources[2 * index : 2 * index + 2]
        rows, width = got.shape
        if now[0] == "gather":
            out = outs.pop(0)
            mine = marks[now[2]]
            for source, place in ((stays, mine), (got, 1 - mine)):
                target = out.at[span(now[1], place, got.shape[now[1]])]

                def move(block, source=source, target=target):
                    target[block, :] = source[block, :]

                in_blocks(rows, move)
        elif later is not None and later[0] == "reduce":
            mine = marks[later[2]]
            for place in (1 - mine, mine):
                out = outs.pop(0)
                window = span(later[1], place, out.shape[later[1]])
                first, second = stays.at[window], got.at[window]

                def add(block, first=first, second=second, out=out):
                    out[block, :] = first[block, :] + second[block, :]

                in_blocks(out.shape[0], add)
        else:
            out = outs.pop(0)

            def add_all(block, stays=stays, got=got, out=out):
                out[block, :] = stays[block, :] + got[block, :]

            in_blocks(rows, add_all)


def combine(marks, plans, pairs, after):
    near = whole_spec()
    shapes = []
    for (now, later), (stays, got) in zip(plans, pairs):
        shape = list(got.shape)
        if now[0] == "gather":
            shape[now[1]] *= 2
            shapes.append(shape)
        elif later is not None and later[0] == "reduce":
            shape[later[1]] //= 2
            shapes += [shape, shape]
        else:
            shapes.append(shape)
    values = [value for pair in pairs for value in pair]
    return pl.pallas_call(
        functools.partial(combine_kernel, plans, len(after)),
        out_shape=[jax.ShapeDtypeStruct(shape, bf16) for shape in shapes],
        in_specs=[pl.BlockSpec(memory_space=pltpu.SMEM)]
        + [near] * len(values)
        + [pl.BlockSpec(memory_space=pl.ANY)] * len(after),
        out_specs=[near] * len(shapes),
        compiler_params=pltpu.CompilerParams(vmem_limit_bytes=8 * 2**20),
        cost_estimate=pl.CostEstimate(flops=0, bytes_accessed=1024, transcendentals=0),
        name="combine",
    )(marks, *values, *after)


def combine_plainly(marks, plans, pairs):
    outs = []
    for (now, later), (stays, got) in zip(plans, pairs):
        if now[0] == "gather":
            outs.append(
                jnp.where(
                    marks[now[2]] == 0,
                    jnp.concatenate([stays, got], axis=now[1]),
                    jnp.concatenate([got, stays], axis=now[1]),
                )
            )
            continue
        total = stays + got
        if later is not None and later[0] == "reduce":
            size = total.shape[later[1]] // 2
            for place in (1 - marks[later[2]], marks[later[2]]):
                outs.append(lax.dynamic_slice_in_dim(total, place * size, size, axis=later[1]))
        else:
            outs.append(total)
    return outs


def flipped(value, axis, bit):
    pairs = [(place, place ^ (1 << bit)) for place in range(lax.axis_size(axis))]
    return lax.ppermute(value, axis, pairs)


class Travel:
    def __init__(self, marks, sends, keeps, orders):
        self.marks = marks
        self.plans = []
        self.aligned = True
        for value, order in zip(sends, orders):
            shape = list(value.shape)
            steps = []
            for bit in order:
                axis = 0 if shape[0] % 32 == 0 or shape[1] % 256 else 1
                if shape[axis] % (32, 256)[axis]:
                    self.aligned = False
                steps.append((axis, bit))
                shape[axis] //= 2
            self.plans.append(
                [("pair", 0, 0)]
                + [("reduce", *step) for step in steps]
                + [("gather", *step) for step in reversed(steps)]
            )
        self.stage = 0
        self.stays = list(keeps)
        self.got = [flipped(value, "section", 0) for value in sends]

    @property
    def done(self):
        return not self.got

    def pending(self):
        plans = []
        for plan in self.plans:
            later = plan[self.stage + 1] if self.stage + 1 < len(plan) else None
            plans.append((plan[self.stage], later))
        return plans, list(zip(self.stays, self.got))

    def accept(self, plans, outs):
        self.stage += 1
        self.stays, self.got = [], []
        for _, later in plans:
            sent = outs.pop(0)
            if later is not None and later[0] == "reduce":
                self.stays.append(outs.pop(0))
            else:
                self.stays.append(sent)
            if later is not None:
                self.got.append(flipped(sent, "wide", later[2]))


def joint_step(travels, after=()):
    travels = [travel for travel in travels if not travel.done]
    pending = [travel.pending() for travel in travels]
    plans = sum((item[0] for item in pending), [])
    pairs = sum((item[1] for item in pending), [])
    if all(travel.aligned for travel in travels):
        outs = list(combine(travels[0].marks, plans, pairs, after))
    else:
        outs = combine_plainly(travels[0].marks, plans, pairs)
    for travel, item in zip(travels, pending):
        travel.accept(item[0], outs)
    return sum((travel.stays for travel in travels), [])


def pad_kernel(section, x_ref, out_ref):
    out_ref[...] = jnp.zeros_like(out_ref)
    out_ref[0, : x_ref.shape[1], :] = x_ref[0]


def padded_images(section, value, images, pad):
    length, width = value.shape[1:]
    out = pl.pallas_call(
        pad_kernel,
        grid_spec=pltpu.PrefetchScalarGridSpec(
            num_scalar_prefetch=1,
            grid=(images,),
            in_specs=[
                pl.BlockSpec(
                    (1, length, width), lambda index, place: (place[0] * images + index, 0, 0)
                )
            ],
            out_specs=pl.BlockSpec((1, pad, width), lambda index, place: (index, 0, 0)),
        ),
        out_shape=jax.ShapeDtypeStruct((images, pad, width), value.dtype),
        compiler_params=pltpu.CompilerParams(vmem_limit_bytes=44 * 2**20),
        cost_estimate=pl.CostEstimate(flops=0, bytes_accessed=4 * value.size, transcendentals=0),
        name="padded_images",
    )(section, value)
    return out.reshape(images * pad, width)


def images_kernel(section, one_ref, two_ref, from_one, from_two, *rest):
    out_ref = rest[-1]
    own = pl.program_id(0) == section[0]
    for place, mine, other in ((0, one_ref, from_one), (1, two_ref, from_two)):
        for source, wanted in ((mine, own), (other, jnp.logical_not(own))):

            @pl.when(wanted & (section[0] == place))
            def _():
                out_ref[0, 0] = source[0, : out_ref.shape[2], :].astype(out_ref.dtype)


def own_images(section, one, two, from_one, from_two, images, length, dtype, after):
    rows, width = one.shape
    pad = rows // images
    sources = [value.reshape(images, pad, width) for value in (one, two, from_one, from_two)]
    specs = []
    for index in range(4):

        def place_map(which, image, section, place=index % 2, mine=index < 2):
            wanted = (section[0] == place) & ((which == section[0]) == mine)
            return (jnp.where(wanted, image, 0), 0, 0)

        specs.append(pl.BlockSpec((1, pad, width), place_map))
    return pl.pallas_call(
        images_kernel,
        grid_spec=pltpu.PrefetchScalarGridSpec(
            num_scalar_prefetch=1,
            grid=(2, images),
            in_specs=specs + [pl.BlockSpec(memory_space=pl.ANY)] * len(after),
            out_specs=pl.BlockSpec(
                (1, 1, length, width),
                lambda which, image, section: (0, which * images + image, 0, 0),
            ),
        ),
        out_shape=pltpu.HBM((1, 2 * images, length, width), dtype),
        compiler_params=pltpu.CompilerParams(vmem_limit_bytes=44 * 2**20),
        cost_estimate=pl.CostEstimate(flops=0, bytes_accessed=12 * one.size, transcendentals=0),
        name="own_images",
    )(section, *sources, *after)


def norm_stats(stream):
    mean_value = jnp.mean(stream, axis=-1, keepdims=True)
    centered = stream - mean_value
    variance = jnp.mean(centered * centered, axis=-1, keepdims=True)
    return centered * lax.rsqrt(variance + norm_epsilon)


def slot_plan(ids, rank, capacity):
    before = rank[None, :] < rank[:, None]
    first, second = ids[:, 0], ids[:, 1]
    same_first = (first[:, None] == first[None, :]) & before
    same_second = (second[:, None] == second[None, :]) & before
    crossed = second[:, None] == first[None, :]
    place_first = jnp.sum(same_first.astype(jnp.int32), axis=1)
    place_second = jnp.sum(same_second.astype(jnp.int32) + crossed.astype(jnp.int32), axis=1)
    slot_first = jnp.where(place_first < capacity, first * capacity + place_first, -1)
    slot_second = jnp.where(place_second < capacity, second * capacity + place_second, -1)
    return (jnp.where(first >= 0, slot_first, -1), jnp.where(second >= 0, slot_second, -1))


def body(
    patches,
    out_cotangent,
    attn_gain,
    qkv_weight,
    proj_weight,
    ffn_gain,
    mlp_in,
    mlp_out,
    router_weight,
    expert_in,
    expert_out,
    expert_ids,
    priority,
):
    expert_count = lax.axis_size("wide")
    sections = lax.axis_size("section")
    section = lax.axis_index("section")
    own_expert = lax.axis_index("wide")
    is_first = section == 0
    images = patches.shape[0] // sections
    length, width = patches.shape[1:]
    pad = -(-length // STEP) * STEP
    rows = images * pad
    capacity = max(2, images * length // expert_count)
    slots = expert_count * capacity
    levels = expert_count.bit_length() - 1
    assert 1 << levels == expert_count
    place = section[None]
    marks = (own_expert >> jnp.arange(levels, dtype=jnp.int32)) & 1
    bits = list(range(levels))
    third = max(1, levels // 3)
    groups = [bits[:third], bits[third : 2 * third], bits[2 * third : -1]]
    across_x = groups[0] + groups[1] + groups[2] + bits[-1:]
    across_y = groups[1] + groups[2] + groups[0] + bits[-1:]
    across_z = groups[2] + groups[0] + groups[1] + bits[-1:]

    def swap(value):
        return flipped(value, "section", 0)

    def exchange(value):
        return lax.all_to_all(value, "wide", split_axis=0, concat_axis=0, tiled=True)

    def across(value):
        shape = (expert_count, capacity, value.shape[1])
        return exchange(value.reshape(shape)).reshape(value.shape)

    other_qkv, other_proj = swap(qkv_weight[0]), swap(proj_weight[0])
    gains = jnp.concatenate([attn_gain, ffn_gain], axis=0)
    other_gains = swap(gains)
    gains_one = jnp.where(is_first, gains, other_gains)
    gains_two = jnp.where(is_first, other_gains, gains)
    weights = (qkv_weight[0], other_qkv, proj_weight[0], other_proj)
    which_one = jnp.stack([(section == 0).astype(jnp.int32), section])
    which_two = jnp.stack([(section == 1).astype(jnp.int32), section])

    ids = lax.dynamic_slice_in_dim(expert_ids, section * images, images)
    ids = jnp.pad(ids, ((0, 0), (0, pad - length), (0, 0)), constant_values=-1).reshape(rows, 2)
    rank = lax.dynamic_slice_in_dim(priority, section, 1).reshape(images, length)
    rank = jnp.pad(rank, ((0, 0), (0, pad - length))).reshape(rows)
    slot_first, slot_second = slot_plan(ids, rank, capacity)
    slot_range = jnp.arange(slots, dtype=jnp.int32)
    pick_first = slot_first[:, None] == slot_range[None, :]
    pick_second = slot_second[:, None] == slot_range[None, :]
    pick_any = (pick_first | pick_second).astype(bf16)
    kept_first = (slot_first >= 0).astype(f32)[:, None]
    kept_second = (slot_second >= 0).astype(f32)[:, None]
    rival = jnp.sum(
        jnp.where(pick_first, ids[:, 1:], 0) + jnp.where(pick_second, ids[:, :1], 0), axis=0
    )
    cotangent = padded_images(place, out_cotangent, images, pad)
    packet = jnp.concatenate(
        [
            tn(pick_any, cotangent).astype(bf16),
            jnp.broadcast_to(rival.astype(bf16)[:, None], (slots, PAIR)),
        ],
        axis=1,
    )

    stream_one = padded_images(place, patches, images, pad)
    mixed_one, packed_one, mix_one, normed_one = attention_forward(
        which_one, stream_one, weights, gains_one[:1], gains_one[1:], images, length
    )
    arrived_packet = across(packet)
    active_first = jax.nn.gelu(nn(normed_one, mlp_in)).astype(bf16)
    first_low = (mixed_one + nn(active_first, mlp_out)).astype(bf16)

    mixed_two, packed_two, mix_two, normed_two = attention_forward(
        which_two, first_low, weights, gains_two[:1], gains_two[1:], images, length
    )
    leaving = tn(pick_any, normed_two).astype(bf16)
    arrived = across(leaving)
    active_one, slope_one = mlp_refresh(normed_one, mlp_in, (leaving,))
    from_low_one = lax.ppermute(first_low, "section", [(1, 0)])
    expert_range = jnp.arange(expert_count, dtype=jnp.int32)
    logits = nn(normed_two, router_weight)
    one_hot = (ids[:, :, None] == expert_range[None, None, :]).astype(f32)
    chosen = jnp.sum(one_hot * logits[:, None, :], axis=-1)
    gates = jax.nn.softmax(chosen, axis=-1)
    back, result, active, grad_hidden, grad_rows = expert_pass(
        own_expert[None],
        arrived,
        arrived_packet,
        router_weight,
        expert_in,
        expert_out,
        (kept_far(active_one), kept_far(slope_one), gates, from_low_one),
    )
    grad_expert_in, grad_expert_out = expert_products(arrived, grad_rows, active, grad_hidden)
    back = across(back)
    result, back, _ = lax.optimization_barrier((result, back, grad_expert_out[:16, :128]))
    returned = across(result)
    other_expert_in, other_expert_out = swap(grad_expert_in), swap(grad_expert_out)

    low_first, low_second = pick_first.astype(bf16), pick_second.astype(bf16)
    grad_gates = jnp.concatenate(
        [
            jnp.sum(nn(low, back[:, width:]), axis=-1, keepdims=True)
            for low in (low_first, low_second)
        ],
        axis=1,
    )
    grad_chosen = gates * (grad_gates - jnp.sum(gates * grad_gates, axis=-1, keepdims=True))
    grad_logits = jnp.sum(one_hot * grad_chosen[:, :, None], axis=1).astype(bf16)
    grad_router = tn(normed_two, grad_logits)
    grad_normed_two = nn(pick_any, back[:, :width]) + nt(grad_logits, router_weight)
    second_low = (
        mixed_two
        + kept_first * gates[:, :1] * nn(low_first, returned)
        + kept_second * gates[:, 1:] * nn(low_second, returned)
    ).astype(bf16)
    grad_first, small_two, *pieces = attention_backward(
        which_two,
        first_low,
        mixed_two,
        cotangent,
        grad_normed_two,
        packed_two,
        mix_two,
        weights,
        gains_two[:1],
        gains_two[1:],
        images,
        length,
        1,
        bf16,
    )
    two = Travel(marks, pieces[:1], pieces[1:], [across_x])
    grad_normed_one, in_send, in_keep, out_send, out_keep = mlp_backward(
        place,
        normed_one,
        grad_first,
        mlp_in,
        mlp_out,
        active_one,
        slope_one,
        after=(kept_far(other_expert_in), kept_far(other_expert_out), from_low_one, returned),
    )
    mlp_first = Travel(marks, [in_send], [in_keep], [across_z])
    mlp_second = Travel(marks, [out_send], [out_keep], [across_y])
    early = [two, mlp_first, mlp_second]
    from_low_two = lax.ppermute(second_low, "section", [(0, 1)])
    from_grad_two = lax.ppermute(grad_first, "section", [(0, 1)])
    grad_one, small_one, *pieces = attention_backward(
        which_one,
        stream_one,
        mixed_one,
        grad_first,
        grad_normed_one,
        packed_one,
        mix_one,
        weights,
        gains_one[:1],
        gains_one[1:],
        images,
        length,
        2,
        f32,
        small=(grad_router, small_two),
        after=joint_step(early, after=[second_low]),
    )
    one = Travel(marks, pieces[:2], pieces[2:], [across_x, across_y])
    last = joint_step(early, after=[from_low_two, from_grad_two])

    def settled(value):
        return lax.optimization_barrier(jnp.transpose(value[0], (1, 0, 2)))

    activations = settled(
        own_images(
            place, first_low, second_low, from_low_one, from_low_two, images, length, bf16, last
        )
    )
    last = joint_step(early + [one], after=[kept_far(activations)])
    expert_in_sum = pair_total(grad_expert_in, other_expert_in, tuple(last))
    last = joint_step(early + [one], after=[kept_far(expert_in_sum)])
    expert_out_sum = pair_total(grad_expert_out, other_expert_out, tuple(last))
    last = joint_step(early + [one], after=[kept_far(expert_out_sum)])
    while not two.done:
        last = joint_step(early + [one], after=last)

    other_in, other_out = swap(mlp_first.stays[0]), swap(mlp_second.stays[0])
    late_grad, *last = lax.optimization_barrier((grad_one, *last))
    from_grad_one = lax.ppermute(late_grad, "section", [(1, 0)])
    last = joint_step([one], after=(other_in, other_out, from_grad_one))
    late_two, *last = lax.optimization_barrier((two.stays[0], *last))
    from_two = [lax.ppermute(late_two, "section", [(0, 1)])]
    mlp_in_sum = join_halves(place, mlp_first.stays[0], other_in, 0, tuple(last))
    mlp_out_sum = join_halves(
        place, mlp_second.stays[0], other_out, 1, (kept_far(mlp_in_sum),)
    )
    input_grads = settled(
        own_images(
            place,
            grad_one,
            grad_first,
            from_grad_one,
            from_grad_two,
            images,
            length,
            f32,
            (kept_far(mlp_out_sum),),
        )
    )
    last = [kept_far(input_grads)]
    while not one.done:
        last = joint_step([one], after=last)
    from_one = [lax.ppermute(one.stays[0], "section", [(1, 0)]), swap(one.stays[1])]
    qkv_grad, proj_grad, sum_router, gain_sums = own_block(
        place,
        (one.stays, two.stays, from_one, from_two),
        one.stays[1],
        from_one[1],
        expert_count,
    )
    small_block = lax.dynamic_slice_in_dim(gain_sums, 8 * section, 8)
    return (
        jnp.transpose(activations, (1, 0, 2))[None],
        jnp.transpose(input_grads, (1, 0, 2))[None],
        small_block[:1],
        qkv_grad[None],
        proj_grad[None],
        small_block[1:2],
        mlp_in_sum,
        mlp_out_sum,
        sum_router,
        expert_in_sum,
        expert_out_sum,
    )


def solution(mesh):
    in_specs = (
        P("wide", None, None),
        P("wide", None, None),
        P("section", None),
        P("section", None, None),
        P("section", None, None),
        P("section", None),
        P(),
        P(),
        P(),
        P("wide", None, None),
        P("wide", None, None),
        P("wide", None, None),
        P("wide", None),
    )
    out_specs = (
        P("section", "wide", None, None),
        P("section", "wide", None, None),
        P("section", None),
        P("section", None, None),
        P("section", None, None),
        P("section", None),
        P(),
        P(),
        P(),
        P("wide", None, None),
        P("wide", None, None),
    )
    return jax.shard_map(body, mesh=mesh, in_specs=in_specs, out_specs=out_specs, check_vma=False)
```

```python
import functools

import jax
import jax.numpy as jnp
from jax import lax
from jax.experimental import pallas as pl
from jax.experimental.pallas import tpu as pltpu
from jax.sharding import PartitionSpec as P

H = 12
HEAD = 64
PAIR = 2 * HEAD
STEP = 16
EXTRA = 256
norm_epsilon = 1e-06
bf16 = jnp.bfloat16
f32 = jnp.float32


def dot(left, right, dims):
    return lax.dot_general(left, right, (dims, ((), ())), preferred_element_type=f32)


def nn(left, right):
    return dot(left, right, ((1,), (0,)))


def nt(left, right):
    return dot(left, right, ((1,), (1,)))


def tn(left, right):
    return dot(left, right, ((0,), (0,)))


def norm_rows(value):
    mean_value = jnp.mean(value, axis=-1, keepdims=True)
    centered = value - mean_value
    scale = lax.rsqrt(jnp.mean(centered * centered, axis=-1, keepdims=True) + norm_epsilon)
    return (centered * scale, scale)


def norm_rows_back(unit, scale, gain, upstream):
    weighted = upstream * gain
    first = jnp.mean(weighted, axis=-1, keepdims=True)
    second = jnp.mean(weighted * unit, axis=-1, keepdims=True)
    return scale * (weighted - first - unit * second)


def folded(value):
    rows = value.shape[0]
    return sum(value[start : start + 8] for start in range(0, rows, 8))


def row_blocks(rows):
    return [slice(start, start + STEP) for start in range(0, rows, STEP)]


def fetch(take, own, other, target, sem):
    @pl.when(take == 1)
    def _():
        pltpu.make_async_copy(own, target, sem).start()

    @pl.when(take != 1)
    def _():
        pltpu.make_async_copy(other, target, sem).start()


def forward_kernel(
    images,
    length,
    which,
    x_ref,
    own_qkv,
    other_qkv,
    own_proj,
    other_proj,
    gain_a,
    gain_f,
    mixed_ref,
    packed_out,
    mix_out,
    normed_ref,
    qkv_ref,
    proj_ref,
    low_ref,
    packed_ref,
    mix_ref,
    sems,
):
    rows, width = x_ref.shape
    pad = rows // images
    packed_copy = pltpu.make_async_copy(packed_ref, packed_out, sems.at[2])
    mix_copy = pltpu.make_async_copy(mix_ref, mix_out, sems.at[3])
    fetch(which[0], own_qkv, other_qkv, qkv_ref, sems.at[0])
    fetch(which[0], own_proj, other_proj, proj_ref, sems.at[1])

    for block in row_blocks(rows):
        unit, scale = norm_rows(x_ref[block, :].astype(f32))
        low_ref[block, :] = (unit * gain_a[...]).astype(bf16)

    pltpu.make_async_copy(own_qkv, qkv_ref, sems.at[0]).wait()

    @pl.loop(0, 3 * width // 256)
    def _(step):
        lanes = pl.ds(pl.multiple_of(step * 256, 256), 256)
        packed_ref[:, lanes] = nn(low_ref[...], qkv_ref[:, lanes]).astype(bf16)

    packed_copy.start()
    left = lax.broadcasted_iota(jnp.int32, (pad, PAIR), 1) < HEAD
    live = lax.broadcasted_iota(jnp.int32, (pad, pad), 0) < length

    @pl.loop(0, width // PAIR)
    def _(pair):
        def lanes(part):
            return pl.ds(pl.multiple_of(part * width + pair * PAIR, PAIR), PAIR)

        for image in range(images):
            block = slice(image * pad, (image + 1) * pad)
            queries = packed_ref[block, lanes(0)].astype(f32) * HEAD ** (-0.5)
            keys = packed_ref[block, lanes(1)]
            values = packed_ref[block, lanes(2)].T
            outs = []
            for half, rows_half in ((left, slice(0, HEAD)), (~left, slice(HEAD, PAIR))):
                scores = nt(keys, jnp.where(half, queries, 0.0).astype(bf16))
                scores = jnp.where(live, scores, -jnp.inf)
                powers = jnp.exp(scores - jnp.max(scores, axis=0, keepdims=True))
                share = 1.0 / jnp.sum(powers, axis=0, keepdims=True)
                outs.append(nn(values[rows_half], powers.astype(bf16)) * share)
            mix_ref[block, lanes(0)] = jnp.concatenate(outs, axis=0).T.astype(bf16)

    mix_copy.start()
    pltpu.make_async_copy(own_proj, proj_ref, sems.at[1]).wait()

    @pl.loop(0, width // 256)
    def _(step):
        lanes = pl.ds(pl.multiple_of(step * 256, 256), 256)
        mixed_ref[:, lanes] = x_ref[:, lanes].astype(f32) + nn(mix_ref[...], proj_ref[:, lanes])

    for block in row_blocks(rows):
        unit, scale = norm_rows(mixed_ref[block, :])
        normed_ref[block, :] = (unit * gain_f[...]).astype(bf16)
    packed_copy.wait()
    mix_copy.wait()


def backward_kernel(
    images,
    length,
    chunks,
    which,
    x_ref,
    mixed_ref,
    base_ref,
    upstream_ref,
    packed_in,
    mix_in,
    own_qkv,
    other_qkv,
    own_proj,
    other_proj,
    gain_a,
    gain_f,
    small,
    grad_out,
    gains_ref,
    pieces,
    grad_ref,
    grad_packed,
    total_low,
    low_ref,
    qkv_ref,
    proj_ref,
    total_ref,
    grad_mix,
    packed_ref,
    mix_ref,
    staged,
    turned,
    sems,
):
    rows, width = x_ref.shape
    pad = rows // images
    packed_copy = pltpu.make_async_copy(packed_in, packed_ref, sems.at[2])
    mix_copy = pltpu.make_async_copy(mix_in, mix_ref, sems.at[3])
    packed_copy.start()
    mix_copy.start()
    fetch(which[0], own_proj, other_proj, proj_ref, sems.at[1])
    fetch(which[0], own_qkv, other_qkv, qkv_ref, sems.at[0])
    gain_total = jnp.zeros((8, width), f32)
    for block in row_blocks(rows):
        unit, scale = norm_rows(mixed_ref[block, :])
        upstream = upstream_ref[block, :]
        value = base_ref[block, :].astype(f32) + norm_rows_back(
            unit, scale, gain_f[...], upstream
        )
        total_ref[block, :] = value
        total_low[block, :] = value.astype(bf16)
        source_unit, source_scale = norm_rows(x_ref[block, :].astype(f32))
        low_ref[block, :] = (source_unit * gain_a[...]).astype(bf16)
        gain_total = gain_total + folded(upstream * unit)
    gains_ref[...] = jnp.zeros_like(gains_ref)
    gains_ref[1:2, :] = jnp.sum(gain_total, axis=0, keepdims=True)
    pltpu.make_async_copy(own_proj, proj_ref, sems.at[1]).wait()

    @pl.loop(0, width // 256)
    def _(step):
        lanes = pl.ds(pl.multiple_of(step * 256, 256), 256)
        grad_mix[:, lanes] = nt(total_low[...], proj_ref[lanes, :]).astype(bf16)

    packed_copy.wait()
    left = lax.broadcasted_iota(jnp.int32, (pad, PAIR), 1) < HEAD
    live = lax.broadcasted_iota(jnp.int32, (pad, pad), 0) < length

    @pl.loop(0, width // PAIR)
    def _(pair):
        def lanes(part):
            return pl.ds(pl.multiple_of(part * width + pair * PAIR, PAIR), PAIR)

        for image in range(images):
            block = slice(image * pad, (image + 1) * pad)
            queries = packed_ref[block, lanes(0)].astype(f32) * HEAD ** (-0.5)
            keys = packed_ref[block, lanes(1)]
            values = packed_ref[block, lanes(2)]
            grads = grad_mix[block, lanes(0)]
            sums = [0.0, 0.0, 0.0]
            for half in (left, ~left):
                some_queries = jnp.where(half, queries, 0.0).astype(bf16)
                some_keys = jnp.where(half, keys, 0.0).astype(bf16)
                some_grads = jnp.where(half, grads, 0.0).astype(bf16)
                scores = nt(keys, some_queries)
                scores = jnp.where(live, scores, -jnp.inf)
                powers = jnp.exp(scores - jnp.max(scores, axis=0, keepdims=True))
                weights = powers * (1.0 / jnp.sum(powers, axis=0, keepdims=True))
                grad_weights = nt(values, some_grads)
                inner = jnp.sum(grad_weights * weights, axis=0, keepdims=True)
                grad_raw = (weights * (grad_weights - inner)).astype(bf16)
                sums[0] += tn(grad_raw, some_keys)
                sums[1] += nn(grad_raw, some_queries)
                sums[2] += nn(weights.astype(bf16), some_grads)
            sums[0] = sums[0] * HEAD ** (-0.5)
            for part in range(3):
                grad_packed[block, lanes(part)] = sums[part].astype(bf16)

    mix_copy.wait()
    third = width // 3
    for side, place in ((0, 1 - which[1]), (1, which[1])):
        columns = pl.ds(pl.multiple_of(place * (width // 2), 128), width // 2)
        left_rows = low_ref[:, columns].T
        right_rows = mix_ref[:, columns].T
        for step in range(12):
            if step < 9:
                value = nn(left_rows, grad_packed[:, step * third : (step + 1) * third])
            else:
                value = nn(right_rows, total_low[:, (step - 9) * third : (step - 8) * third])
            out, spot = divmod(step, 12 // chunks)
            staged[side * chunks + out][:, spot * third : (spot + 1) * third] = value.astype(bf16)
        for index in range(side * chunks, (side + 1) * chunks - bool(small)):
            pltpu.make_async_copy(staged[index], pieces[index], sems.at[4 + index]).start()

    pltpu.make_async_copy(own_qkv, qkv_ref, sems.at[0]).wait()

    @pl.loop(0, width // 256)
    def _(step):
        lanes = pl.ds(pl.multiple_of(step * 256, 256), 256)
        grad_ref[:, lanes] = nt(grad_packed[...], qkv_ref[lanes, :])

    gain_total = jnp.zeros((8, width), f32)
    for block in row_blocks(rows):
        unit, scale = norm_rows(x_ref[block, :].astype(f32))
        upstream = grad_ref[block, :]
        value = total_ref[block, :] + norm_rows_back(unit, scale, gain_a[...], upstream)
        grad_out[block, :] = value.astype(grad_out.dtype)
        gain_total = gain_total + folded(upstream * unit)
    gains_ref[0:1, :] = jnp.sum(gain_total, axis=0, keepdims=True)
    half_width = width // 2
    if small:
        turned[...] = jnp.concatenate([gains_ref[...], small[1][...]], axis=0).T
        for index, place in ((chunks - 1, 1 - which[1]), (2 * chunks - 1, which[1])):
            block = pl.ds(pl.multiple_of(place * half_width, 128), half_width)
            out = staged[index]
            start = out.shape[1] - EXTRA
            out[:, start:] = jnp.zeros((half_width, EXTRA), bf16)
            out[:, start : start + small[0].shape[1]] = small[0][block, :].astype(bf16)
            out[:, start + 128 : start + 144] = turned[block, :].astype(bf16)
        for index in (chunks - 1, 2 * chunks - 1):
            pltpu.make_async_copy(staged[index], pieces[index], sems.at[4 + index]).start()
    for index in range(2 * chunks):
        pltpu.make_async_copy(staged[index], pieces[index], sems.at[4 + index]).wait()


def whole_spec():
    return pl.BlockSpec(memory_space=pltpu.VMEM)


def kept_far(value):
    return pltpu.with_memory_space_constraint(value, pltpu.HBM)


def attention_forward(which, x, weights, gain_a, gain_f, images, length):
    rows, width = x.shape
    far = pl.BlockSpec(memory_space=pltpu.HBM)
    near = whole_spec()
    return pl.pallas_call(
        functools.partial(forward_kernel, images, length),
        out_shape=(
            jax.ShapeDtypeStruct((rows, width), f32),
            pltpu.HBM((rows, 3 * width), bf16),
            pltpu.HBM((rows, width), bf16),
            jax.ShapeDtypeStruct((rows, width), bf16),
        ),
        in_specs=[pl.BlockSpec(memory_space=pltpu.SMEM), near, far, far, far, far, near, near],
        out_specs=(near, far, far, near),
        scratch_shapes=[
            pltpu.VMEM((width, 3 * width), bf16),
            pltpu.VMEM((width, width), bf16),
            pltpu.VMEM((rows, width), bf16),
            pltpu.VMEM((rows, 3 * width), bf16),
            pltpu.VMEM((rows, width), bf16),
            pltpu.SemaphoreType.DMA((4,)),
        ],
        compiler_params=pltpu.CompilerParams(vmem_limit_bytes=24 * 2**20),
        cost_estimate=pl.CostEstimate(
            flops=10 * rows * width * width, bytes_accessed=12 * 2**20, transcendentals=2**20
        ),
        name="attention_forward",
    )(which, x, *[kept_far(value) for value in weights], gain_a, gain_f)


def attention_backward(
    which,
    x,
    mixed,
    base,
    upstream,
    packed,
    mix,
    weights,
    gain_a,
    gain_f,
    images,
    length,
    chunks,
    dtype,
    small=(),
    after=(),
):
    rows, width = x.shape
    far = pl.BlockSpec(memory_space=pltpu.HBM)
    near = whole_spec()
    sizes = [4 * width // chunks] * chunks
    if small:
        sizes[-1] += EXTRA
    sizes = sizes * 2
    first_out = 13 + len(small) + len(after)

    def kernel(*refs):
        outs = refs[first_out : first_out + 2 + 2 * chunks]
        scratch = refs[first_out + 2 + 2 * chunks :]
        backward_kernel(
            images,
            length,
            chunks,
            *refs[:13],
            refs[13 : 13 + len(small)],
            outs[0],
            outs[1],
            outs[2:],
            *scratch[:10],
            scratch[10 : 10 + 2 * chunks],
            *scratch[10 + 2 * chunks :],
        )

    return pl.pallas_call(
        kernel,
        out_shape=(
            jax.ShapeDtypeStruct((rows, width), dtype),
            jax.ShapeDtypeStruct((8, width), f32),
        )
        + tuple(pltpu.HBM((width // 2, size), bf16) for size in sizes),
        in_specs=[pl.BlockSpec(memory_space=pltpu.SMEM)]
        + [near] * 4
        + [far] * 6
        + [near] * (2 + len(small))
        + [pl.BlockSpec(memory_space=pl.ANY)] * len(after),
        out_specs=(near, near) + (far,) * (2 * chunks),
        scratch_shapes=[
            pltpu.VMEM((rows, width), f32),
            pltpu.VMEM((rows, 3 * width), bf16),
            pltpu.VMEM((rows, width), bf16),
            pltpu.VMEM((rows, width), bf16),
            pltpu.VMEM((width, 3 * width), bf16),
            pltpu.VMEM((width, width), bf16),
            pltpu.VMEM((rows, width), f32),
            pltpu.VMEM((rows, width), bf16),
            pltpu.VMEM((rows, 3 * width), bf16),
            pltpu.VMEM((rows, width), bf16),
        ]
        + [pltpu.VMEM((width // 2, size), bf16) for size in sizes]
        + [pltpu.VMEM((width, 16), f32), pltpu.SemaphoreType.DMA((4 + 2 * chunks,))],
        compiler_params=pltpu.CompilerParams(vmem_limit_bytes=32 * 2**20),
        cost_estimate=pl.CostEstimate(
            flops=28 * rows * width * width, bytes_accessed=24 * 2**20, transcendentals=2**20
        ),
        name="attention_backward",
    )(
        which,
        x,
        mixed,
        base,
        upstream,
        *[kept_far(value) for value in (packed, mix, *weights)],
        gain_a,
        gain_f,
        *small,
        *after,
    )


def gelu_pair(hidden):
    cubic = 0.7978845608028654
    square = hidden * hidden
    curve = jnp.tanh(cubic * (hidden + 0.044715 * (square * hidden)))
    left = 0.5 * (1.0 + curve)
    slope = left + 0.5 * hidden * (1.0 - curve * curve) * (
        cubic * (1.0 + 3.0 * 0.044715 * square)
    )
    return (hidden * left, slope)


def refresh_kernel(x_ref, in_ref, *rest):
    active_ref, slope_ref = rest[-2:]
    active, slope = gelu_pair(nn(x_ref[...], in_ref[...]))
    active_ref[...] = active.astype(bf16)
    slope_ref[...] = slope.astype(bf16)


def mlp_refresh(x, weight_in, after):
    rows, width = x.shape
    hidden = weight_in.shape[1]
    step = 512
    block = pl.BlockSpec((rows, step), lambda index: (0, index))
    return pl.pallas_call(
        refresh_kernel,
        grid=(hidden // step,),
        in_specs=[
            pl.BlockSpec((rows, width), lambda index: (0, 0)),
            pl.BlockSpec((width, step), lambda index: (0, index)),
        ]
        + [pl.BlockSpec(memory_space=pl.ANY)] * len(after),
        out_specs=(block, block),
        out_shape=(pltpu.HBM((rows, hidden), bf16),) * 2,
        compiler_params=pltpu.CompilerParams(vmem_limit_bytes=44 * 2**20),
        cost_estimate=pl.CostEstimate(
            flops=2 * rows * width * hidden,
            bytes_accessed=10 * 2**20,
            transcendentals=rows * hidden,
        ),
        name="mlp_refresh",
    )(x, kept_far(weight_in), *after)


def mlp_kernel(
    section,
    x_ref,
    up_ref,
    in_ref,
    out_ref,
    active_ref,
    slope_ref,
    grad_ref,
    in_send,
    in_keep,
    out_send,
    out_keep,
    x_turned,
):
    half = x_ref.shape[1] // 2

    @pl.when(pl.program_id(0) == 0)
    def _():
        x_turned[...] = x_ref[...].T
        grad_ref[...] = jnp.zeros_like(grad_ref)

    grad_hidden = (nt(up_ref[...], out_ref[...]) * slope_ref[...].astype(f32)).astype(bf16)
    grad_ref[...] += nt(grad_hidden, in_ref[...])
    turned = active_ref[...].T
    for which, first, second in (
        (1 - section[0], in_send, out_send),
        (section[0], in_keep, out_keep),
    ):
        block = pl.ds(pl.multiple_of(which * half, 128), half)
        first[...] = nn(x_turned[block, :], grad_hidden).astype(bf16)
        second[...] = nn(turned, up_ref[:, block]).astype(bf16)


def mlp_backward(section, x, up, weight_in, weight_out, active, slope, after):
    rows, width = x.shape
    hidden = weight_in.shape[1]
    step = 512
    half = width // 2
    fixed = pl.BlockSpec((rows, width), lambda index, place: (0, 0))
    saved = pl.BlockSpec((rows, step), lambda index, place: (0, index))
    across = pl.BlockSpec((half, step), lambda index, place: (0, index))
    down = pl.BlockSpec((step, half), lambda index, place: (index, 0))

    def kernel(*refs):
        mlp_kernel(*refs[:7], *refs[7 + len(after) :])

    return pl.pallas_call(
        kernel,
        grid_spec=pltpu.PrefetchScalarGridSpec(
            num_scalar_prefetch=1,
            grid=(hidden // step,),
            in_specs=[
                fixed,
                fixed,
                pl.BlockSpec((width, step), lambda index, place: (0, index)),
                pl.BlockSpec((step, width), lambda index, place: (index, 0)),
                saved,
                saved,
            ]
            + [pl.BlockSpec(memory_space=pl.ANY)] * len(after),
            out_specs=(fixed, across, across, down, down),
            scratch_shapes=[pltpu.VMEM((width, rows), bf16)],
        ),
        out_shape=(
            jax.ShapeDtypeStruct((rows, width), f32),
            pltpu.HBM((half, hidden), bf16),
            pltpu.HBM((half, hidden), bf16),
            pltpu.HBM((hidden, half), bf16),
            pltpu.HBM((hidden, half), bf16),
        ),
        compiler_params=pltpu.CompilerParams(vmem_limit_bytes=44 * 2**20),
        cost_estimate=pl.CostEstimate(
            flops=8 * rows * width * hidden, bytes_accessed=28 * 2**20, transcendentals=0
        ),
        name="mlp_backward",
    )(
        section,
        x,
        up,
        *[kept_far(value) for value in (weight_in, weight_out, active, slope)],
        *after,
    )


def expert_kernel(
    own,
    x_ref,
    packet_ref,
    router_ref,
    in_ref,
    out_ref,
    *rest,
):
    back_ref, result_ref, active_ref, hidden_ref, up_ref, total_ref, grad_ref = rest[-7:]
    slots, width = x_ref.shape

    @pl.when(pl.program_id(0) == 0)
    def _():
        grad_ref[...] = jnp.zeros_like(grad_ref)
        total_ref[...] = jnp.zeros_like(total_ref)
        logits = nn(x_ref[...], router_ref[...])
        experts = lax.broadcasted_iota(jnp.int32, logits.shape, 1)
        rival = packet_ref[:, width : width + 1].astype(f32).astype(jnp.int32)
        own_logit = jnp.sum(jnp.where(experts == own[0], logits, 0.0), axis=1, keepdims=True)
        rival_logit = jnp.sum(jnp.where(experts == rival, logits, 0.0), axis=1, keepdims=True)
        top = jnp.maximum(own_logit, rival_logit)
        power = jnp.exp(own_logit - top)
        gate = power / (power + jnp.exp(rival_logit - top))
        up_ref[...] = (gate * packet_ref[:, :width].astype(f32)).astype(bf16)

    active, slope = gelu_pair(nn(x_ref[...], in_ref[0]))
    active = active.astype(bf16)
    total_ref[...] += nn(active, out_ref[0])
    grad_hidden = (nt(up_ref[...], out_ref[0]) * slope).astype(bf16)
    grad_ref[...] += nt(grad_hidden, in_ref[0])
    active_ref[...] = active
    hidden_ref[...] = grad_hidden

    @pl.when(pl.program_id(0) == pl.num_programs(0) - 1)
    def _():
        result = total_ref[...].astype(bf16)
        result_ref[...] = result
        back_ref[:, :width] = grad_ref[...].astype(bf16)
        rest = jnp.sum(
            packet_ref[:, :width].astype(f32) * result.astype(f32), axis=1, keepdims=True
        )
        lanes = lax.broadcasted_iota(jnp.int32, (slots, PAIR), 1)
        value = jnp.zeros((slots, PAIR), f32)
        for lane in range(3):
            part = rest.astype(bf16).astype(f32)
            value = jnp.where(lanes == lane, part, value)
            rest = rest - part
        back_ref[:, width:] = value.astype(bf16)


def expert_pass(own, x, packet, router, weight_in, weight_out, after):
    slots, width = x.shape
    hidden = weight_in.shape[2]
    step = 512

    def fixed(shape):
        return pl.BlockSpec(shape, lambda index, place: (0, 0))

    saved = pl.BlockSpec((slots, step), lambda index, place: (0, index))
    return pl.pallas_call(
        expert_kernel,
        grid_spec=pltpu.PrefetchScalarGridSpec(
            num_scalar_prefetch=1,
            grid=(hidden // step,),
            in_specs=[
                fixed(x.shape),
                fixed(packet.shape),
                fixed(router.shape),
                pl.BlockSpec((1, width, step), lambda index, place: (0, 0, index)),
                pl.BlockSpec((1, step, width), lambda index, place: (0, index, 0)),
            ]
            + [pl.BlockSpec(memory_space=pl.ANY)] * len(after),
            out_specs=(fixed(packet.shape), fixed(x.shape), saved, saved, fixed(x.shape)),
            scratch_shapes=[
                pltpu.VMEM((slots, width), f32),
                pltpu.VMEM((slots, width), f32),
            ],
        ),
        out_shape=(
            jax.ShapeDtypeStruct(packet.shape, bf16),
            jax.ShapeDtypeStruct(x.shape, bf16),
            pltpu.HBM((slots, hidden), bf16),
            pltpu.HBM((slots, hidden), bf16),
            jax.ShapeDtypeStruct(x.shape, bf16),
        ),
        compiler_params=pltpu.CompilerParams(vmem_limit_bytes=44 * 2**20),
        cost_estimate=pl.CostEstimate(
            flops=8 * slots * width * hidden,
            bytes_accessed=16 * 2**20,
            transcendentals=slots * hidden,
        ),
        name="expert_pass",
    )(own, x, packet, router, kept_far(weight_in), kept_far(weight_out), *after)


def expert_product_kernel(
    x_ref, up_ref, active_ref, hidden_ref, in_grad, out_grad, x_turned
):
    @pl.when(pl.program_id(0) == 0)
    def _():
        x_turned[...] = x_ref[...].T

    in_grad[...] = nn(x_turned[...], hidden_ref[...]).astype(bf16)
    out_grad[...] = nn(active_ref[...].T, up_ref[...]).astype(bf16)


def expert_products(x, up, active, grad_hidden):
    slots, width = x.shape
    hidden = active.shape[1]
    step = 512
    fixed = pl.BlockSpec((slots, width), lambda index: (0, 0))
    saved = pl.BlockSpec((slots, step), lambda index: (0, index))
    return pl.pallas_call(
        expert_product_kernel,
        grid=(hidden // step,),
        in_specs=[fixed, fixed, saved, saved],
        out_specs=(
            pl.BlockSpec((width, step), lambda index: (0, index)),
            pl.BlockSpec((step, width), lambda index: (index, 0)),
        ),
        out_shape=(pltpu.HBM((width, hidden), bf16), pltpu.HBM((hidden, width), bf16)),
        scratch_shapes=[pltpu.VMEM((width, slots), bf16)],
        compiler_params=pltpu.CompilerParams(vmem_limit_bytes=44 * 2**20),
        cost_estimate=pl.CostEstimate(
            flops=4 * slots * width * hidden, bytes_accessed=16 * 2**20, transcendentals=0
        ),
        name="expert_products",
    )(x, up, kept_far(active), kept_far(grad_hidden))


def join_kernel(section, mine_ref, other_ref, *rest):
    out_ref = rest[-1]

    @pl.when(pl.program_id(0) == section[0])
    def _():
        out_ref[...] = mine_ref[...].astype(f32)

    @pl.when(pl.program_id(0) != section[0])
    def _():
        out_ref[...] = other_ref[...].astype(f32)


def gather_kernel(
    pick_first, pick_second, back_ref, gates_ref, ids_ref, router_ref, normed_ref, *rest
):
    grad_ref, router_grad = rest[-2:]
    width = normed_ref.shape[1]
    first, second = pick_first[...], pick_second[...]
    extra = back_ref[:, width:]
    slot_first = jnp.sum(nn(first, extra), axis=1, keepdims=True)
    slot_second = jnp.sum(nn(second, extra), axis=1, keepdims=True)
    gate_first, gate_second = gates_ref[:, 0:1], gates_ref[:, 1:2]
    total = gate_first * slot_first + gate_second * slot_second
    experts = lax.broadcasted_iota(jnp.int32, (first.shape[0], router_ref.shape[1]), 1)
    logits = jnp.where(experts == ids_ref[:, 0:1], gate_first * (slot_first - total), 0.0)
    logits += jnp.where(experts == ids_ref[:, 1:2], gate_second * (slot_second - total), 0.0)
    logits = logits.astype(bf16)
    grad_ref[...] = nn(first + second, back_ref[:, :width]) + nt(logits, router_ref[...])
    router_grad[...] = tn(normed_ref[...], logits)


def gather_back(pick_first, pick_second, back, gates, ids, router, normed, after):
    rows, width = normed.shape
    near = whole_spec()
    return pl.pallas_call(
        gather_kernel,
        out_shape=(
            jax.ShapeDtypeStruct((rows, width), f32),
            jax.ShapeDtypeStruct(router.shape, f32),
        ),
        in_specs=[near] * 7 + [pl.BlockSpec(memory_space=pl.ANY)] * len(after),
        out_specs=(near, near),
        compiler_params=pltpu.CompilerParams(vmem_limit_bytes=16 * 2**20),
        cost_estimate=pl.CostEstimate(
            flops=2 * rows * back.shape[0] * width, bytes_accessed=4 * 2**20, transcendentals=0
        ),
        name="gather_back",
    )(pick_first, pick_second, back, gates, ids, router, normed, *after)


def held_step(which, step, wanted, steps):
    return jnp.where(which == wanted, step, jnp.where(which > wanted, steps - 1, 0))


def join_halves(section, mine, other, axis, after):
    rows, width = mine.shape
    steps = 3
    block = (rows // steps, width)

    def mine_map(which, step, place):
        return (held_step(which, step, place[0], steps), 0)

    def other_map(which, step, place):
        return (held_step(which, step, 1 - place[0], steps), 0)

    def out_map(which, step, place):
        return (which * steps + step, 0) if axis == 0 else (step, which)

    return pl.pallas_call(
        join_kernel,
        grid_spec=pltpu.PrefetchScalarGridSpec(
            num_scalar_prefetch=1,
            grid=(2, steps),
            in_specs=[pl.BlockSpec(block, mine_map), pl.BlockSpec(block, other_map)]
            + [pl.BlockSpec(memory_space=pl.ANY)] * len(after),
            out_specs=pl.BlockSpec(block, out_map),
        ),
        out_shape=pltpu.HBM((2 * rows, width) if axis == 0 else (rows, 2 * width), f32),
        compiler_params=pltpu.CompilerParams(vmem_limit_bytes=44 * 2**20),
        cost_estimate=pl.CostEstimate(
            flops=0, bytes_accessed=12 * rows * width, transcendentals=0
        ),
        name="join_halves",
    )(section, mine, other, *after)


def block_kernel(counts, section, *refs):
    refs = list(refs)
    sources = [[refs.pop(0) for _ in range(count)] for count in counts]
    own_small, other_small, qkv_out, proj_out, router_out, gains_out = refs
    own = pl.program_id(0) == section[0]
    cut = qkv_out.shape[1]

    def emit_small(part):
        value = part[:, part.shape[1] - EXTRA :].astype(f32)
        router_out[...] = value[:, : router_out.shape[1]]
        gains_out[...] = value[:, 128:].T[:16]

    @pl.when(own)
    def _():
        emit_small(own_small)

    @pl.when(jnp.logical_not(own))
    def _():
        emit_small(other_small)

    def emit(parts):
        start = 0
        for part in parts:
            size = min(part.shape[1], cut + proj_out.shape[1] - start)
            left = max(0, min(size, cut - start))
            if left:
                qkv_out[:, start : start + left] = part[:, :left].astype(f32)
            if left < size:
                proj_out[:, start + left - cut : start + size - cut] = part[:, left:size].astype(f32)
            start += size

    for index, parts in enumerate(sources):
        place, mine = index % 2, index < 2

        @pl.when((own == mine) & (section[0] == place))
        def _():
            emit(parts)


def own_block(section, groups, own_small, other_small, experts):
    half = groups[0][0].shape[0]
    width = 2 * half
    steps = 3
    specs = []
    for index, parts in enumerate(groups):

        def place_map(which, step, section, place=index % 2, mine=index < 2):
            wanted = section[0] if mine else 1 - section[0]
            held = held_step(which, step, wanted, steps)
            return (jnp.where(section[0] == place, held, 0), 0)

        specs += [pl.BlockSpec((half // steps, part.shape[1]), place_map) for part in parts]

    for value, mine in ((own_small, True), (other_small, False)):

        def small_map(which, step, section, mine=mine):
            return (held_step(which, step, section[0] if mine else 1 - section[0], steps), 0)

        specs.append(pl.BlockSpec((half // steps, value.shape[1]), small_map))

    def out_map(which, step, section):
        return (which * steps + step, 0)

    return pl.pallas_call(
        functools.partial(block_kernel, [len(parts) for parts in groups]),
        grid_spec=pltpu.PrefetchScalarGridSpec(
            num_scalar_prefetch=1,
            grid=(2, steps),
            in_specs=specs,
            out_specs=(
                pl.BlockSpec((half // steps, 3 * width), out_map),
                pl.BlockSpec((half // steps, width), out_map),
                pl.BlockSpec((half // steps, experts), out_map),
                pl.BlockSpec(
                    (16, half // steps), lambda which, step, section: (0, which * steps + step)
                ),
            ),
        ),
        out_shape=(
            pltpu.HBM((2 * half, 3 * width), f32),
            pltpu.HBM((2 * half, width), f32),
            jax.ShapeDtypeStruct((2 * half, experts), f32),
            jax.ShapeDtypeStruct((16, 2 * half), f32),
        ),
        compiler_params=pltpu.CompilerParams(vmem_limit_bytes=44 * 2**20),
        cost_estimate=pl.CostEstimate(
            flops=0, bytes_accessed=48 * half * width, transcendentals=0
        ),
        name="own_block",
    )(section, *[part for parts in groups for part in parts], own_small, other_small)


def total_kernel(mine_ref, other_ref, *rest):
    rest[-1][0] = mine_ref[...].astype(f32) + other_ref[...].astype(f32)


def pair_total(mine, other, after):
    rows, width = mine.shape
    steps = 6
    block = pl.BlockSpec((rows // steps, width), lambda step: (step, 0))
    return pl.pallas_call(
        total_kernel,
        grid=(steps,),
        in_specs=[block, block] + [pl.BlockSpec(memory_space=pl.ANY)] * len(after),
        out_specs=pl.BlockSpec((1, rows // steps, width), lambda step: (0, step, 0)),
        out_shape=pltpu.HBM((1, rows, width), f32),
        compiler_params=pltpu.CompilerParams(vmem_limit_bytes=44 * 2**20),
        cost_estimate=pl.CostEstimate(
            flops=rows * width, bytes_accessed=8 * rows * width, transcendentals=0
        ),
        name="pair_total",
    )(mine, other, *after)


def span(axis, start, size):
    multiple = size & -size
    piece = pl.ds(pl.multiple_of(start * size, multiple), size)
    return (piece, slice(None)) if axis == 0 else (slice(None), piece)


def in_blocks(rows, work):
    size = next(size for size in (96, 64, 48, 32, 16) if rows % size == 0)
    if rows == size:
        work(slice(0, rows))
    else:

        @pl.loop(0, rows // size)
        def _(step):
            work(pl.ds(pl.multiple_of(step * size, size), size))


def combine_kernel(plans, extra, marks, *refs):
    count = len(plans)
    sources, outs = refs[: 2 * count], list(refs[2 * count + extra :])
    for index, (now, later) in enumerate(plans):
        stays, got = sources[2 * index : 2 * index + 2]
        rows, width = got.shape
        if now[0] == "gather":
            out = outs.pop(0)
            mine = marks[now[2]]
            for source, place in ((stays, mine), (got, 1 - mine)):
                target = out.at[span(now[1], place, got.shape[now[1]])]

                def move(block, source=source, target=target):
                    target[block, :] = source[block, :]

                in_blocks(rows, move)
        elif later is not None and later[0] == "reduce":
            mine = marks[later[2]]
            for place in (1 - mine, mine):
                out = outs.pop(0)
                window = span(later[1], place, out.shape[later[1]])
                first, second = stays.at[window], got.at[window]

                def add(block, first=first, second=second, out=out):
                    out[block, :] = first[block, :] + second[block, :]

                in_blocks(out.shape[0], add)
        else:
            out = outs.pop(0)

            def add_all(block, stays=stays, got=got, out=out):
                out[block, :] = stays[block, :] + got[block, :]

            in_blocks(rows, add_all)


def combine(marks, plans, pairs, after):
    near = whole_spec()
    shapes = []
    for (now, later), (stays, got) in zip(plans, pairs):
        shape = list(got.shape)
        if now[0] == "gather":
            shape[now[1]] *= 2
            shapes.append(shape)
        elif later is not None and later[0] == "reduce":
            shape[later[1]] //= 2
            shapes += [shape, shape]
        else:
            shapes.append(shape)
    values = [value for pair in pairs for value in pair]
    return pl.pallas_call(
        functools.partial(combine_kernel, plans, len(after)),
        out_shape=[jax.ShapeDtypeStruct(shape, bf16) for shape in shapes],
        in_specs=[pl.BlockSpec(memory_space=pltpu.SMEM)]
        + [near] * len(values)
        + [pl.BlockSpec(memory_space=pl.ANY)] * len(after),
        out_specs=[near] * len(shapes),
        compiler_params=pltpu.CompilerParams(vmem_limit_bytes=8 * 2**20),
        cost_estimate=pl.CostEstimate(flops=0, bytes_accessed=1024, transcendentals=0),
        name="combine",
    )(marks, *values, *after)


def combine_plainly(marks, plans, pairs):
    outs = []
    for (now, later), (stays, got) in zip(plans, pairs):
        if now[0] == "gather":
            outs.append(
                jnp.where(
                    marks[now[2]] == 0,
                    jnp.concatenate([stays, got], axis=now[1]),
                    jnp.concatenate([got, stays], axis=now[1]),
                )
            )
            continue
        total = stays + got
        if later is not None and later[0] == "reduce":
            size = total.shape[later[1]] // 2
            for place in (1 - marks[later[2]], marks[later[2]]):
                outs.append(lax.dynamic_slice_in_dim(total, place * size, size, axis=later[1]))
        else:
            outs.append(total)
    return outs


def flipped(value, axis, bit):
    pairs = [(place, place ^ (1 << bit)) for place in range(lax.axis_size(axis))]
    return lax.ppermute(value, axis, pairs)


class Travel:
    def __init__(self, marks, sends, keeps, orders):
        self.marks = marks
        self.plans = []
        self.aligned = True
        for value, order in zip(sends, orders):
            shape = list(value.shape)
            steps = []
            for bit in order:
                axis = 0 if shape[0] % 32 == 0 or shape[1] % 256 else 1
                if shape[axis] % (32, 256)[axis]:
                    self.aligned = False
                steps.append((axis, bit))
                shape[axis] //= 2
            self.plans.append(
                [("pair", 0, 0)]
                + [("reduce", *step) for step in steps]
                + [("gather", *step) for step in reversed(steps)]
            )
        self.stage = 0
        self.stays = list(keeps)
        self.got = [flipped(value, "section", 0) for value in sends]

    @property
    def done(self):
        return not self.got

    def pending(self):
        plans = []
        for plan in self.plans:
            later = plan[self.stage + 1] if self.stage + 1 < len(plan) else None
            plans.append((plan[self.stage], later))
        return plans, list(zip(self.stays, self.got))

    def accept(self, plans, outs):
        self.stage += 1
        self.stays, self.got = [], []
        for _, later in plans:
            sent = outs.pop(0)
            if later is not None and later[0] == "reduce":
                self.stays.append(outs.pop(0))
            else:
                self.stays.append(sent)
            if later is not None:
                self.got.append(flipped(sent, "wide", later[2]))


def joint_step(travels, after=()):
    travels = [travel for travel in travels if not travel.done]
    pending = [travel.pending() for travel in travels]
    plans = sum((item[0] for item in pending), [])
    pairs = sum((item[1] for item in pending), [])
    if all(travel.aligned for travel in travels):
        outs = list(combine(travels[0].marks, plans, pairs, after))
    else:
        outs = combine_plainly(travels[0].marks, plans, pairs)
    for travel, item in zip(travels, pending):
        travel.accept(item[0], outs)
    return sum((travel.stays for travel in travels), [])


def pad_kernel(section, x_ref, out_ref):
    out_ref[...] = jnp.zeros_like(out_ref)
    out_ref[0, : x_ref.shape[1], :] = x_ref[0]


def padded_images(section, value, images, pad):
    length, width = value.shape[1:]
    out = pl.pallas_call(
        pad_kernel,
        grid_spec=pltpu.PrefetchScalarGridSpec(
            num_scalar_prefetch=1,
            grid=(images,),
            in_specs=[
                pl.BlockSpec(
                    (1, length, width), lambda index, place: (place[0] * images + index, 0, 0)
                )
            ],
            out_specs=pl.BlockSpec((1, pad, width), lambda index, place: (index, 0, 0)),
        ),
        out_shape=jax.ShapeDtypeStruct((images, pad, width), value.dtype),
        compiler_params=pltpu.CompilerParams(vmem_limit_bytes=44 * 2**20),
        cost_estimate=pl.CostEstimate(flops=0, bytes_accessed=4 * value.size, transcendentals=0),
        name="padded_images",
    )(section, value)
    return out.reshape(images * pad, width)


def images_kernel(section, one_ref, two_ref, from_one, from_two, *rest):
    out_ref = rest[-1]
    own = pl.program_id(0) == section[0]
    for place, mine, other in ((0, one_ref, from_one), (1, two_ref, from_two)):
        for source, wanted in ((mine, own), (other, jnp.logical_not(own))):

            @pl.when(wanted & (section[0] == place))
            def _():
                out_ref[0, 0] = source[0, : out_ref.shape[2], :].astype(out_ref.dtype)


def own_images(section, one, two, from_one, from_two, images, length, dtype, after):
    rows, width = one.shape
    pad = rows // images
    sources = [value.reshape(images, pad, width) for value in (one, two, from_one, from_two)]
    specs = []
    for index in range(4):

        def place_map(which, image, section, place=index % 2, mine=index < 2):
            wanted = (section[0] == place) & ((which == section[0]) == mine)
            return (jnp.where(wanted, image, 0), 0, 0)

        specs.append(pl.BlockSpec((1, pad, width), place_map))
    return pl.pallas_call(
        images_kernel,
        grid_spec=pltpu.PrefetchScalarGridSpec(
            num_scalar_prefetch=1,
            grid=(2, images),
            in_specs=specs + [pl.BlockSpec(memory_space=pl.ANY)] * len(after),
            out_specs=pl.BlockSpec(
                (1, 1, length, width),
                lambda which, image, section: (0, which * images + image, 0, 0),
            ),
        ),
        out_shape=pltpu.HBM((1, 2 * images, length, width), dtype),
        compiler_params=pltpu.CompilerParams(vmem_limit_bytes=44 * 2**20),
        cost_estimate=pl.CostEstimate(flops=0, bytes_accessed=12 * one.size, transcendentals=0),
        name="own_images",
    )(section, *sources, *after)


def norm_stats(stream):
    mean_value = jnp.mean(stream, axis=-1, keepdims=True)
    centered = stream - mean_value
    variance = jnp.mean(centered * centered, axis=-1, keepdims=True)
    return centered * lax.rsqrt(variance + norm_epsilon)


def slot_plan(ids, rank, capacity):
    before = rank[None, :] < rank[:, None]
    first, second = ids[:, 0], ids[:, 1]
    same_first = (first[:, None] == first[None, :]) & before
    same_second = (second[:, None] == second[None, :]) & before
    crossed = second[:, None] == first[None, :]
    place_first = jnp.sum(same_first.astype(jnp.int32), axis=1)
    place_second = jnp.sum(same_second.astype(jnp.int32) + crossed.astype(jnp.int32), axis=1)
    slot_first = jnp.where(place_first < capacity, first * capacity + place_first, -1)
    slot_second = jnp.where(place_second < capacity, second * capacity + place_second, -1)
    return (jnp.where(first >= 0, slot_first, -1), jnp.where(second >= 0, slot_second, -1))


def body(
    patches,
    out_cotangent,
    attn_gain,
    qkv_weight,
    proj_weight,
    ffn_gain,
    mlp_in,
    mlp_out,
    router_weight,
    expert_in,
    expert_out,
    expert_ids,
    priority,
):
    expert_count = lax.axis_size("wide")
    sections = lax.axis_size("section")
    section = lax.axis_index("section")
    own_expert = lax.axis_index("wide")
    is_first = section == 0
    images = patches.shape[0] // sections
    length, width = patches.shape[1:]
    pad = -(-length // STEP) * STEP
    rows = images * pad
    capacity = max(2, images * length // expert_count)
    slots = expert_count * capacity
    levels = expert_count.bit_length() - 1
    assert 1 << levels == expert_count
    place = section[None]
    marks = (own_expert >> jnp.arange(levels, dtype=jnp.int32)) & 1
    bits = list(range(levels))
    third = max(1, levels // 3)
    groups = [bits[:third], bits[third : 2 * third], bits[2 * third : -1]]
    across_x = groups[0] + groups[1] + groups[2] + bits[-1:]
    across_y = groups[1] + groups[2] + groups[0] + bits[-1:]
    across_z = groups[2] + groups[0] + groups[1] + bits[-1:]

    def swap(value):
        return flipped(value, "section", 0)

    def exchange(value):
        return lax.all_to_all(value, "wide", split_axis=0, concat_axis=0, tiled=True)

    def across(value):
        shape = (expert_count, capacity, value.shape[1])
        return exchange(value.reshape(shape)).reshape(value.shape)

    other_qkv, other_proj = swap(qkv_weight[0]), swap(proj_weight[0])
    gains = jnp.concatenate([attn_gain, ffn_gain], axis=0)
    other_gains = swap(gains)
    gains_one = jnp.where(is_first, gains, other_gains)
    gains_two = jnp.where(is_first, other_gains, gains)
    weights = (qkv_weight[0], other_qkv, proj_weight[0], other_proj)
    which_one = jnp.stack([(section == 0).astype(jnp.int32), section])
    which_two = jnp.stack([(section == 1).astype(jnp.int32), section])

    ids = lax.dynamic_slice_in_dim(expert_ids, section * images, images)
    ids = jnp.pad(ids, ((0, 0), (0, pad - length), (0, 0)), constant_values=-1).reshape(rows, 2)
    rank = lax.dynamic_slice_in_dim(priority, section, 1).reshape(images, length)
    rank = jnp.pad(rank, ((0, 0), (0, pad - length))).reshape(rows)
    slot_first, slot_second = slot_plan(ids, rank, capacity)
    slot_range = jnp.arange(slots, dtype=jnp.int32)
    pick_first = slot_first[:, None] == slot_range[None, :]
    pick_second = slot_second[:, None] == slot_range[None, :]
    pick_any = (pick_first | pick_second).astype(bf16)
    kept_first = (slot_first >= 0).astype(f32)[:, None]
    kept_second = (slot_second >= 0).astype(f32)[:, None]
    rival = jnp.sum(
        jnp.where(pick_first, ids[:, 1:], 0) + jnp.where(pick_second, ids[:, :1], 0), axis=0
    )
    cotangent = padded_images(place, out_cotangent, images, pad)
    packet = jnp.concatenate(
        [
            tn(pick_any, cotangent).astype(bf16),
            jnp.broadcast_to(rival.astype(bf16)[:, None], (slots, PAIR)),
        ],
        axis=1,
    )

    stream_one = padded_images(place, patches, images, pad)
    mixed_one, packed_one, mix_one, normed_one = attention_forward(
        which_one, stream_one, weights, gains_one[:1], gains_one[1:], images, length
    )
    arrived_packet = across(packet)
    active_first = jax.nn.gelu(nn(normed_one, mlp_in)).astype(bf16)
    first_low = (mixed_one + nn(active_first, mlp_out)).astype(bf16)

    mixed_two, packed_two, mix_two, normed_two = attention_forward(
        which_two, first_low, weights, gains_two[:1], gains_two[1:], images, length
    )
    leaving = tn(pick_any, normed_two).astype(bf16)
    arrived = across(leaving)
    active_one, slope_one = mlp_refresh(normed_one, mlp_in, (leaving,))
    from_low_one = lax.ppermute(first_low, "section", [(1, 0)])
    expert_range = jnp.arange(expert_count, dtype=jnp.int32)
    logits = nn(normed_two, router_weight)
    one_hot = (ids[:, :, None] == expert_range[None, None, :]).astype(f32)
    chosen = jnp.sum(one_hot * logits[:, None, :], axis=-1)
    gates = jax.nn.softmax(chosen, axis=-1)
    back, result, active, grad_hidden, grad_rows = expert_pass(
        own_expert[None],
        arrived,
        arrived_packet,
        router_weight,
        expert_in,
        expert_out,
        (kept_far(active_one), kept_far(slope_one), gates, from_low_one),
    )
    grad_expert_in, grad_expert_out = expert_products(arrived, grad_rows, active, grad_hidden)
    back = across(back)
    result, back = lax.optimization_barrier((result, back))
    returned = across(result)
    other_expert_in, other_expert_out = swap(grad_expert_in), swap(grad_expert_out)

    low_first, low_second = pick_first.astype(bf16), pick_second.astype(bf16)
    grad_normed_two, grad_router = gather_back(
        low_first,
        low_second,
        back,
        gates,
        ids,
        router_weight,
        normed_two,
        (kept_far(grad_expert_in), kept_far(grad_expert_out)),
    )
    second_low = (
        mixed_two
        + kept_first * gates[:, :1] * nn(low_first, returned)
        + kept_second * gates[:, 1:] * nn(low_second, returned)
    ).astype(bf16)
    grad_first, small_two, *pieces = attention_backward(
        which_two,
        first_low,
        mixed_two,
        cotangent,
        grad_normed_two,
        packed_two,
        mix_two,
        weights,
        gains_two[:1],
        gains_two[1:],
        images,
        length,
        1,
        bf16,
    )
    two = Travel(marks, pieces[:1], pieces[1:], [across_x])
    grad_normed_one, in_send, in_keep, out_send, out_keep = mlp_backward(
        place,
        normed_one,
        grad_first,
        mlp_in,
        mlp_out,
        active_one,
        slope_one,
        after=(kept_far(other_expert_in), kept_far(other_expert_out), from_low_one, returned),
    )
    mlp_first = Travel(marks, [in_send], [in_keep], [across_z])
    mlp_second = Travel(marks, [out_send], [out_keep], [across_y])
    early = [two, mlp_first, mlp_second]
    from_low_two = lax.ppermute(second_low, "section", [(0, 1)])
    from_grad_two = lax.ppermute(grad_first, "section", [(0, 1)])
    grad_one, small_one, *pieces = attention_backward(
        which_one,
        stream_one,
        mixed_one,
        grad_first,
        grad_normed_one,
        packed_one,
        mix_one,
        weights,
        gains_one[:1],
        gains_one[1:],
        images,
        length,
        2,
        f32,
        small=(grad_router, small_two),
        after=joint_step(early, after=[second_low]),
    )
    one = Travel(marks, pieces[:2], pieces[2:], [across_x, across_y])
    last = joint_step(early, after=[from_low_two, from_grad_two])

    def settled(value):
        return lax.optimization_barrier(jnp.transpose(value[0], (1, 0, 2)))

    activations = settled(
        own_images(
            place, first_low, second_low, from_low_one, from_low_two, images, length, bf16, last
        )
    )
    last = joint_step(early + [one], after=[kept_far(activations)])
    expert_in_sum = pair_total(grad_expert_in, other_expert_in, tuple(last))
    last = joint_step(early + [one], after=[kept_far(expert_in_sum)])
    expert_out_sum = pair_total(grad_expert_out, other_expert_out, tuple(last))
    last = joint_step(early + [one], after=[kept_far(expert_out_sum)])
    while not two.done:
        last = joint_step(early + [one], after=last)

    other_in, other_out = swap(mlp_first.stays[0]), swap(mlp_second.stays[0])
    late_grad, *last = lax.optimization_barrier((grad_one, *last))
    from_grad_one = lax.ppermute(late_grad, "section", [(1, 0)])
    last = joint_step([one], after=(other_in, other_out, from_grad_one))
    late_two, *last = lax.optimization_barrier((two.stays[0], *last))
    from_two = [lax.ppermute(late_two, "section", [(0, 1)])]
    mlp_in_sum = join_halves(place, mlp_first.stays[0], other_in, 0, tuple(last))
    mlp_out_sum = join_halves(
        place, mlp_second.stays[0], other_out, 1, (kept_far(mlp_in_sum),)
    )
    input_grads = settled(
        own_images(
            place,
            grad_one,
            grad_first,
            from_grad_one,
            from_grad_two,
            images,
            length,
            f32,
            (kept_far(mlp_out_sum),),
        )
    )
    last = [kept_far(input_grads)]
    while not one.done:
        last = joint_step([one], after=last)
    from_one = [lax.ppermute(one.stays[0], "section", [(1, 0)]), swap(one.stays[1])]
    qkv_grad, proj_grad, sum_router, gain_sums = own_block(
        place,
        (one.stays, two.stays, from_one, from_two),
        one.stays[1],
        from_one[1],
        expert_count,
    )
    small_block = lax.dynamic_slice_in_dim(gain_sums, 8 * section, 8)
    return (
        jnp.transpose(activations, (1, 0, 2))[None],
        jnp.transpose(input_grads, (1, 0, 2))[None],
        small_block[:1],
        qkv_grad[None],
        proj_grad[None],
        small_block[1:2],
        mlp_in_sum,
        mlp_out_sum,
        sum_router,
        expert_in_sum,
        expert_out_sum,
    )


def solution(mesh):
    in_specs = (
        P("wide", None, None),
        P("wide", None, None),
        P("section", None),
        P("section", None, None),
        P("section", None, None),
        P("section", None),
        P(),
        P(),
        P(),
        P("wide", None, None),
        P("wide", None, None),
        P("wide", None, None),
        P("wide", None),
    )
    out_specs = (
        P("section", "wide", None, None),
        P("section", "wide", None, None),
        P("section", None),
        P("section", None, None),
        P("section", None, None),
        P("section", None),
        P(),
        P(),
        P(),
        P("wide", None, None),
        P("wide", None, None),
    )
    return jax.shard_map(body, mesh=mesh, in_specs=in_specs, out_specs=out_specs, check_vma=False)
```

```python
import functools

import jax
import jax.numpy as jnp
from jax import lax
from jax.experimental import pallas as pl
from jax.experimental.pallas import tpu as pltpu
from jax.sharding import PartitionSpec as P

H = 12
HEAD = 64
PAIR = 2 * HEAD
STEP = 16
EXTRA = 256
norm_epsilon = 1e-06
bf16 = jnp.bfloat16
f32 = jnp.float32


def dot(left, right, dims):
    return lax.dot_general(left, right, (dims, ((), ())), preferred_element_type=f32)


def nn(left, right):
    return dot(left, right, ((1,), (0,)))


def nt(left, right):
    return dot(left, right, ((1,), (1,)))


def tn(left, right):
    return dot(left, right, ((0,), (0,)))


def norm_rows(value):
    mean_value = jnp.mean(value, axis=-1, keepdims=True)
    centered = value - mean_value
    scale = lax.rsqrt(jnp.mean(centered * centered, axis=-1, keepdims=True) + norm_epsilon)
    return (centered * scale, scale)


def norm_rows_back(unit, scale, gain, upstream):
    weighted = upstream * gain
    first = jnp.mean(weighted, axis=-1, keepdims=True)
    second = jnp.mean(weighted * unit, axis=-1, keepdims=True)
    return scale * (weighted - first - unit * second)


def folded(value):
    rows = value.shape[0]
    return sum(value[start : start + 8] for start in range(0, rows, 8))


def row_blocks(rows):
    return [slice(start, start + STEP) for start in range(0, rows, STEP)]


def fetch(take, own, other, target, sem):
    @pl.when(take == 1)
    def _():
        pltpu.make_async_copy(own, target, sem).start()

    @pl.when(take != 1)
    def _():
        pltpu.make_async_copy(other, target, sem).start()


def forward_kernel(
    images,
    length,
    which,
    x_ref,
    own_qkv,
    other_qkv,
    own_proj,
    other_proj,
    gain_a,
    gain_f,
    mixed_ref,
    packed_out,
    mix_out,
    normed_ref,
    qkv_ref,
    proj_ref,
    low_ref,
    packed_ref,
    mix_ref,
    sems,
):
    rows, width = x_ref.shape
    pad = rows // images
    packed_copy = pltpu.make_async_copy(packed_ref, packed_out, sems.at[2])
    mix_copy = pltpu.make_async_copy(mix_ref, mix_out, sems.at[3])
    fetch(which[0], own_qkv, other_qkv, qkv_ref, sems.at[0])
    fetch(which[0], own_proj, other_proj, proj_ref, sems.at[1])

    for block in row_blocks(rows):
        unit, scale = norm_rows(x_ref[block, :].astype(f32))
        low_ref[block, :] = (unit * gain_a[...]).astype(bf16)

    pltpu.make_async_copy(own_qkv, qkv_ref, sems.at[0]).wait()

    @pl.loop(0, 3 * width // 256)
    def _(step):
        lanes = pl.ds(pl.multiple_of(step * 256, 256), 256)
        packed_ref[:, lanes] = nn(low_ref[...], qkv_ref[:, lanes]).astype(bf16)

    packed_copy.start()
    left = lax.broadcasted_iota(jnp.int32, (pad, PAIR), 1) < HEAD
    live = lax.broadcasted_iota(jnp.int32, (pad, pad), 0) < length

    @pl.loop(0, width // PAIR)
    def _(pair):
        def lanes(part):
            return pl.ds(pl.multiple_of(part * width + pair * PAIR, PAIR), PAIR)

        for image in range(images):
            block = slice(image * pad, (image + 1) * pad)
            queries = packed_ref[block, lanes(0)].astype(f32) * HEAD ** (-0.5)
            keys = packed_ref[block, lanes(1)]
            values = packed_ref[block, lanes(2)].T
            outs = []
            for half, rows_half in ((left, slice(0, HEAD)), (~left, slice(HEAD, PAIR))):
                scores = nt(keys, jnp.where(half, queries, 0.0).astype(bf16))
                scores = jnp.where(live, scores, -jnp.inf)
                powers = jnp.exp(scores - jnp.max(scores, axis=0, keepdims=True))
                share = 1.0 / jnp.sum(powers, axis=0, keepdims=True)
                outs.append(nn(values[rows_half], powers.astype(bf16)) * share)
            mix_ref[block, lanes(0)] = jnp.concatenate(outs, axis=0).T.astype(bf16)

    mix_copy.start()
    pltpu.make_async_copy(own_proj, proj_ref, sems.at[1]).wait()

    @pl.loop(0, width // 256)
    def _(step):
        lanes = pl.ds(pl.multiple_of(step * 256, 256), 256)
        mixed_ref[:, lanes] = x_ref[:, lanes].astype(f32) + nn(mix_ref[...], proj_ref[:, lanes])

    for block in row_blocks(rows):
        unit, scale = norm_rows(mixed_ref[block, :])
        normed_ref[block, :] = (unit * gain_f[...]).astype(bf16)
    packed_copy.wait()
    mix_copy.wait()


def backward_kernel(
    images,
    length,
    chunks,
    which,
    x_ref,
    mixed_ref,
    base_ref,
    upstream_ref,
    packed_in,
    mix_in,
    own_qkv,
    other_qkv,
    own_proj,
    other_proj,
    gain_a,
    gain_f,
    small,
    grad_out,
    gains_ref,
    pieces,
    grad_ref,
    grad_packed,
    total_low,
    low_ref,
    qkv_ref,
    proj_ref,
    total_ref,
    grad_mix,
    packed_ref,
    mix_ref,
    staged,
    turned,
    sems,
):
    rows, width = x_ref.shape
    pad = rows // images
    packed_copy = pltpu.make_async_copy(packed_in, packed_ref, sems.at[2])
    mix_copy = pltpu.make_async_copy(mix_in, mix_ref, sems.at[3])
    packed_copy.start()
    mix_copy.start()
    fetch(which[0], own_proj, other_proj, proj_ref, sems.at[1])
    fetch(which[0], own_qkv, other_qkv, qkv_ref, sems.at[0])
    gain_total = jnp.zeros((8, width), f32)
    for block in row_blocks(rows):
        unit, scale = norm_rows(mixed_ref[block, :])
        upstream = upstream_ref[block, :]
        value = base_ref[block, :].astype(f32) + norm_rows_back(
            unit, scale, gain_f[...], upstream
        )
        total_ref[block, :] = value
        total_low[block, :] = value.astype(bf16)
        source_unit, source_scale = norm_rows(x_ref[block, :].astype(f32))
        low_ref[block, :] = (source_unit * gain_a[...]).astype(bf16)
        gain_total = gain_total + folded(upstream * unit)
    gains_ref[...] = jnp.zeros_like(gains_ref)
    gains_ref[1:2, :] = jnp.sum(gain_total, axis=0, keepdims=True)
    pltpu.make_async_copy(own_proj, proj_ref, sems.at[1]).wait()

    @pl.loop(0, width // 256)
    def _(step):
        lanes = pl.ds(pl.multiple_of(step * 256, 256), 256)
        grad_mix[:, lanes] = nt(total_low[...], proj_ref[lanes, :]).astype(bf16)

    packed_copy.wait()
    left = lax.broadcasted_iota(jnp.int32, (pad, PAIR), 1) < HEAD
    live = lax.broadcasted_iota(jnp.int32, (pad, pad), 0) < length

    @pl.loop(0, width // PAIR)
    def _(pair):
        def lanes(part):
            return pl.ds(pl.multiple_of(part * width + pair * PAIR, PAIR), PAIR)

        for image in range(images):
            block = slice(image * pad, (image + 1) * pad)
            queries = packed_ref[block, lanes(0)].astype(f32) * HEAD ** (-0.5)
            keys = packed_ref[block, lanes(1)]
            values = packed_ref[block, lanes(2)]
            grads = grad_mix[block, lanes(0)]
            sums = [0.0, 0.0, 0.0]
            for half in (left, ~left):
                some_queries = jnp.where(half, queries, 0.0).astype(bf16)
                some_keys = jnp.where(half, keys, 0.0).astype(bf16)
                some_grads = jnp.where(half, grads, 0.0).astype(bf16)
                scores = nt(keys, some_queries)
                scores = jnp.where(live, scores, -jnp.inf)
                powers = jnp.exp(scores - jnp.max(scores, axis=0, keepdims=True))
                weights = powers * (1.0 / jnp.sum(powers, axis=0, keepdims=True))
                grad_weights = nt(values, some_grads)
                inner = jnp.sum(grad_weights * weights, axis=0, keepdims=True)
                grad_raw = (weights * (grad_weights - inner)).astype(bf16)
                sums[0] += tn(grad_raw, some_keys)
                sums[1] += nn(grad_raw, some_queries)
                sums[2] += nn(weights.astype(bf16), some_grads)
            sums[0] = sums[0] * HEAD ** (-0.5)
            for part in range(3):
                grad_packed[block, lanes(part)] = sums[part].astype(bf16)

    mix_copy.wait()
    third = width // 3
    for side, place in ((0, 1 - which[1]), (1, which[1])):
        columns = pl.ds(pl.multiple_of(place * (width // 2), 128), width // 2)
        left_rows = low_ref[:, columns].T
        right_rows = mix_ref[:, columns].T
        for step in range(12):
            if step < 9:
                value = nn(left_rows, grad_packed[:, step * third : (step + 1) * third])
            else:
                value = nn(right_rows, total_low[:, (step - 9) * third : (step - 8) * third])
            out, spot = divmod(step, 12 // chunks)
            staged[side * chunks + out][:, spot * third : (spot + 1) * third] = value.astype(bf16)
        for index in range(side * chunks, (side + 1) * chunks - bool(small)):
            pltpu.make_async_copy(staged[index], pieces[index], sems.at[4 + index]).start()

    pltpu.make_async_copy(own_qkv, qkv_ref, sems.at[0]).wait()

    @pl.loop(0, width // 256)
    def _(step):
        lanes = pl.ds(pl.multiple_of(step * 256, 256), 256)
        grad_ref[:, lanes] = nt(grad_packed[...], qkv_ref[lanes, :])

    gain_total = jnp.zeros((8, width), f32)
    for block in row_blocks(rows):
        unit, scale = norm_rows(x_ref[block, :].astype(f32))
        upstream = grad_ref[block, :]
        value = total_ref[block, :] + norm_rows_back(unit, scale, gain_a[...], upstream)
        grad_out[block, :] = value.astype(grad_out.dtype)
        gain_total = gain_total + folded(upstream * unit)
    gains_ref[0:1, :] = jnp.sum(gain_total, axis=0, keepdims=True)
    half_width = width // 2
    if small:
        turned[...] = jnp.concatenate([gains_ref[...], small[1][...]], axis=0).T
        for index, place in ((chunks - 1, 1 - which[1]), (2 * chunks - 1, which[1])):
            block = pl.ds(pl.multiple_of(place * half_width, 128), half_width)
            out = staged[index]
            start = out.shape[1] - EXTRA
            out[:, start:] = jnp.zeros((half_width, EXTRA), bf16)
            out[:, start : start + small[0].shape[1]] = small[0][block, :].astype(bf16)
            out[:, start + 128 : start + 144] = turned[block, :].astype(bf16)
        for index in (chunks - 1, 2 * chunks - 1):
            pltpu.make_async_copy(staged[index], pieces[index], sems.at[4 + index]).start()
    for index in range(2 * chunks):
        pltpu.make_async_copy(staged[index], pieces[index], sems.at[4 + index]).wait()


def whole_spec():
    return pl.BlockSpec(memory_space=pltpu.VMEM)


def kept_far(value):
    return pltpu.with_memory_space_constraint(value, pltpu.HBM)


def attention_forward(which, x, weights, gain_a, gain_f, images, length):
    rows, width = x.shape
    far = pl.BlockSpec(memory_space=pltpu.HBM)
    near = whole_spec()
    return pl.pallas_call(
        functools.partial(forward_kernel, images, length),
        out_shape=(
            jax.ShapeDtypeStruct((rows, width), f32),
            pltpu.HBM((rows, 3 * width), bf16),
            pltpu.HBM((rows, width), bf16),
            jax.ShapeDtypeStruct((rows, width), bf16),
        ),
        in_specs=[pl.BlockSpec(memory_space=pltpu.SMEM), near, far, far, far, far, near, near],
        out_specs=(near, far, far, near),
        scratch_shapes=[
            pltpu.VMEM((width, 3 * width), bf16),
            pltpu.VMEM((width, width), bf16),
            pltpu.VMEM((rows, width), bf16),
            pltpu.VMEM((rows, 3 * width), bf16),
            pltpu.VMEM((rows, width), bf16),
            pltpu.SemaphoreType.DMA((4,)),
        ],
        compiler_params=pltpu.CompilerParams(vmem_limit_bytes=24 * 2**20),
        cost_estimate=pl.CostEstimate(
            flops=10 * rows * width * width, bytes_accessed=12 * 2**20, transcendentals=2**20
        ),
        name="attention_forward",
    )(which, x, *[kept_far(value) for value in weights], gain_a, gain_f)


def attention_backward(
    which,
    x,
    mixed,
    base,
    upstream,
    packed,
    mix,
    weights,
    gain_a,
    gain_f,
    images,
    length,
    chunks,
    dtype,
    small=(),
    after=(),
):
    rows, width = x.shape
    far = pl.BlockSpec(memory_space=pltpu.HBM)
    near = whole_spec()
    sizes = [4 * width // chunks] * chunks
    if small:
        sizes[-1] += EXTRA
    sizes = sizes * 2
    first_out = 13 + len(small) + len(after)

    def kernel(*refs):
        outs = refs[first_out : first_out + 2 + 2 * chunks]
        scratch = refs[first_out + 2 + 2 * chunks :]
        backward_kernel(
            images,
            length,
            chunks,
            *refs[:13],
            refs[13 : 13 + len(small)],
            outs[0],
            outs[1],
            outs[2:],
            *scratch[:10],
            scratch[10 : 10 + 2 * chunks],
            *scratch[10 + 2 * chunks :],
        )

    return pl.pallas_call(
        kernel,
        out_shape=(
            jax.ShapeDtypeStruct((rows, width), dtype),
            jax.ShapeDtypeStruct((8, width), f32),
        )
        + tuple(pltpu.HBM((width // 2, size), bf16) for size in sizes),
        in_specs=[pl.BlockSpec(memory_space=pltpu.SMEM)]
        + [near] * 4
        + [far] * 6
        + [near] * (2 + len(small))
        + [pl.BlockSpec(memory_space=pl.ANY)] * len(after),
        out_specs=(near, near) + (far,) * (2 * chunks),
        scratch_shapes=[
            pltpu.VMEM((rows, width), f32),
            pltpu.VMEM((rows, 3 * width), bf16),
            pltpu.VMEM((rows, width), bf16),
            pltpu.VMEM((rows, width), bf16),
            pltpu.VMEM((width, 3 * width), bf16),
            pltpu.VMEM((width, width), bf16),
            pltpu.VMEM((rows, width), f32),
            pltpu.VMEM((rows, width), bf16),
            pltpu.VMEM((rows, 3 * width), bf16),
            pltpu.VMEM((rows, width), bf16),
        ]
        + [pltpu.VMEM((width // 2, size), bf16) for size in sizes]
        + [pltpu.VMEM((width, 16), f32), pltpu.SemaphoreType.DMA((4 + 2 * chunks,))],
        compiler_params=pltpu.CompilerParams(vmem_limit_bytes=32 * 2**20),
        cost_estimate=pl.CostEstimate(
            flops=28 * rows * width * width, bytes_accessed=24 * 2**20, transcendentals=2**20
        ),
        name="attention_backward",
    )(
        which,
        x,
        mixed,
        base,
        upstream,
        *[kept_far(value) for value in (packed, mix, *weights)],
        gain_a,
        gain_f,
        *small,
        *after,
    )


def gelu_pair(hidden):
    cubic = 0.7978845608028654
    square = hidden * hidden
    curve = jnp.tanh(cubic * (hidden + 0.044715 * (square * hidden)))
    left = 0.5 * (1.0 + curve)
    slope = left + 0.5 * hidden * (1.0 - curve * curve) * (
        cubic * (1.0 + 3.0 * 0.044715 * square)
    )
    return (hidden * left, slope)


def refresh_kernel(x_ref, in_ref, *rest):
    active_ref, slope_ref = rest[-2:]
    active, slope = gelu_pair(nn(x_ref[...], in_ref[...]))
    active_ref[...] = active.astype(bf16)
    slope_ref[...] = slope.astype(bf16)


def mlp_refresh(x, weight_in, after):
    rows, width = x.shape
    hidden = weight_in.shape[1]
    step = 512
    block = pl.BlockSpec((rows, step), lambda index: (0, index))
    return pl.pallas_call(
        refresh_kernel,
        grid=(hidden // step,),
        in_specs=[
            pl.BlockSpec((rows, width), lambda index: (0, 0)),
            pl.BlockSpec((width, step), lambda index: (0, index)),
        ]
        + [pl.BlockSpec(memory_space=pl.ANY)] * len(after),
        out_specs=(block, block),
        out_shape=(pltpu.HBM((rows, hidden), bf16),) * 2,
        compiler_params=pltpu.CompilerParams(vmem_limit_bytes=44 * 2**20),
        cost_estimate=pl.CostEstimate(
            flops=2 * rows * width * hidden,
            bytes_accessed=10 * 2**20,
            transcendentals=rows * hidden,
        ),
        name="mlp_refresh",
    )(x, weight_in, *after)


def mlp_kernel(
    section,
    x_ref,
    up_ref,
    in_ref,
    out_ref,
    active_ref,
    slope_ref,
    grad_ref,
    in_send,
    in_keep,
    out_send,
    out_keep,
    x_turned,
):
    half = x_ref.shape[1] // 2

    @pl.when(pl.program_id(0) == 0)
    def _():
        x_turned[...] = x_ref[...].T
        grad_ref[...] = jnp.zeros_like(grad_ref)

    grad_hidden = (nt(up_ref[...], out_ref[...]) * slope_ref[...].astype(f32)).astype(bf16)
    grad_ref[...] += nt(grad_hidden, in_ref[...])
    turned = active_ref[...].T
    for which, first, second in (
        (1 - section[0], in_send, out_send),
        (section[0], in_keep, out_keep),
    ):
        block = pl.ds(pl.multiple_of(which * half, 128), half)
        first[...] = nn(x_turned[block, :], grad_hidden).astype(bf16)
        second[...] = nn(turned, up_ref[:, block]).astype(bf16)


def mlp_backward(section, x, up, weight_in, weight_out, active, slope, after):
    rows, width = x.shape
    hidden = weight_in.shape[1]
    step = 512
    half = width // 2
    fixed = pl.BlockSpec((rows, width), lambda index, place: (0, 0))
    saved = pl.BlockSpec((rows, step), lambda index, place: (0, index))
    across = pl.BlockSpec((half, step), lambda index, place: (0, index))
    down = pl.BlockSpec((step, half), lambda index, place: (index, 0))

    def kernel(*refs):
        mlp_kernel(*refs[:7], *refs[7 + len(after) :])

    return pl.pallas_call(
        kernel,
        grid_spec=pltpu.PrefetchScalarGridSpec(
            num_scalar_prefetch=1,
            grid=(hidden // step,),
            in_specs=[
                fixed,
                fixed,
                pl.BlockSpec((width, step), lambda index, place: (0, index)),
                pl.BlockSpec((step, width), lambda index, place: (index, 0)),
                saved,
                saved,
            ]
            + [pl.BlockSpec(memory_space=pl.ANY)] * len(after),
            out_specs=(fixed, across, across, down, down),
            scratch_shapes=[pltpu.VMEM((width, rows), bf16)],
        ),
        out_shape=(
            jax.ShapeDtypeStruct((rows, width), f32),
            pltpu.HBM((half, hidden), bf16),
            pltpu.HBM((half, hidden), bf16),
            pltpu.HBM((hidden, half), bf16),
            pltpu.HBM((hidden, half), bf16),
        ),
        compiler_params=pltpu.CompilerParams(vmem_limit_bytes=44 * 2**20),
        cost_estimate=pl.CostEstimate(
            flops=8 * rows * width * hidden, bytes_accessed=28 * 2**20, transcendentals=0
        ),
        name="mlp_backward",
    )(section, x, up, weight_in, weight_out, kept_far(active), kept_far(slope), *after)


def expert_kernel(
    own,
    x_ref,
    packet_ref,
    router_ref,
    in_ref,
    out_ref,
    *rest,
):
    back_ref, result_ref, active_ref, hidden_ref, up_ref, total_ref, grad_ref = rest[-7:]
    slots, width = x_ref.shape

    @pl.when(pl.program_id(0) == 0)
    def _():
        grad_ref[...] = jnp.zeros_like(grad_ref)
        total_ref[...] = jnp.zeros_like(total_ref)
        logits = nn(x_ref[...], router_ref[...])
        experts = lax.broadcasted_iota(jnp.int32, logits.shape, 1)
        rival = packet_ref[:, width : width + 1].astype(f32).astype(jnp.int32)
        own_logit = jnp.sum(jnp.where(experts == own[0], logits, 0.0), axis=1, keepdims=True)
        rival_logit = jnp.sum(jnp.where(experts == rival, logits, 0.0), axis=1, keepdims=True)
        top = jnp.maximum(own_logit, rival_logit)
        power = jnp.exp(own_logit - top)
        gate = power / (power + jnp.exp(rival_logit - top))
        up_ref[...] = (gate * packet_ref[:, :width].astype(f32)).astype(bf16)

    active, slope = gelu_pair(nn(x_ref[...], in_ref[0]))
    active = active.astype(bf16)
    total_ref[...] += nn(active, out_ref[0])
    grad_hidden = (nt(up_ref[...], out_ref[0]) * slope).astype(bf16)
    grad_ref[...] += nt(grad_hidden, in_ref[0])
    active_ref[...] = active
    hidden_ref[...] = grad_hidden

    @pl.when(pl.program_id(0) == pl.num_programs(0) - 1)
    def _():
        result = total_ref[...].astype(bf16)
        result_ref[...] = result
        back_ref[:, :width] = grad_ref[...].astype(bf16)
        rest = jnp.sum(
            packet_ref[:, :width].astype(f32) * result.astype(f32), axis=1, keepdims=True
        )
        lanes = lax.broadcasted_iota(jnp.int32, (slots, PAIR), 1)
        value = jnp.zeros((slots, PAIR), f32)
        for lane in range(3):
            part = rest.astype(bf16).astype(f32)
            value = jnp.where(lanes == lane, part, value)
            rest = rest - part
        back_ref[:, width:] = value.astype(bf16)


def expert_pass(own, x, packet, router, weight_in, weight_out, after):
    slots, width = x.shape
    hidden = weight_in.shape[2]
    step = 512

    def fixed(shape):
        return pl.BlockSpec(shape, lambda index, place: (0, 0))

    saved = pl.BlockSpec((slots, step), lambda index, place: (0, index))
    return pl.pallas_call(
        expert_kernel,
        grid_spec=pltpu.PrefetchScalarGridSpec(
            num_scalar_prefetch=1,
            grid=(hidden // step,),
            in_specs=[
                fixed(x.shape),
                fixed(packet.shape),
                fixed(router.shape),
                pl.BlockSpec((1, width, step), lambda index, place: (0, 0, index)),
                pl.BlockSpec((1, step, width), lambda index, place: (0, index, 0)),
            ]
            + [pl.BlockSpec(memory_space=pl.ANY)] * len(after),
            out_specs=(fixed(packet.shape), fixed(x.shape), saved, saved, fixed(x.shape)),
            scratch_shapes=[
                pltpu.VMEM((slots, width), f32),
                pltpu.VMEM((slots, width), f32),
            ],
        ),
        out_shape=(
            jax.ShapeDtypeStruct(packet.shape, bf16),
            jax.ShapeDtypeStruct(x.shape, bf16),
            pltpu.HBM((slots, hidden), bf16),
            pltpu.HBM((slots, hidden), bf16),
            jax.ShapeDtypeStruct(x.shape, bf16),
        ),
        compiler_params=pltpu.CompilerParams(vmem_limit_bytes=44 * 2**20),
        cost_estimate=pl.CostEstimate(
            flops=8 * slots * width * hidden,
            bytes_accessed=16 * 2**20,
            transcendentals=slots * hidden,
        ),
        name="expert_pass",
    )(own, x, packet, router, weight_in, weight_out, *after)


def expert_product_kernel(
    x_ref, up_ref, active_ref, hidden_ref, in_grad, out_grad, x_turned
):
    @pl.when(pl.program_id(0) == 0)
    def _():
        x_turned[...] = x_ref[...].T

    in_grad[...] = nn(x_turned[...], hidden_ref[...]).astype(bf16)
    out_grad[...] = nn(active_ref[...].T, up_ref[...]).astype(bf16)


def expert_products(x, up, active, grad_hidden):
    slots, width = x.shape
    hidden = active.shape[1]
    step = 512
    fixed = pl.BlockSpec((slots, width), lambda index: (0, 0))
    saved = pl.BlockSpec((slots, step), lambda index: (0, index))
    return pl.pallas_call(
        expert_product_kernel,
        grid=(hidden // step,),
        in_specs=[fixed, fixed, saved, saved],
        out_specs=(
            pl.BlockSpec((width, step), lambda index: (0, index)),
            pl.BlockSpec((step, width), lambda index: (index, 0)),
        ),
        out_shape=(pltpu.HBM((width, hidden), bf16), pltpu.HBM((hidden, width), bf16)),
        scratch_shapes=[pltpu.VMEM((width, slots), bf16)],
        compiler_params=pltpu.CompilerParams(vmem_limit_bytes=44 * 2**20),
        cost_estimate=pl.CostEstimate(
            flops=4 * slots * width * hidden, bytes_accessed=16 * 2**20, transcendentals=0
        ),
        name="expert_products",
    )(x, up, kept_far(active), kept_far(grad_hidden))


def join_kernel(section, mine_ref, other_ref, *rest):
    out_ref = rest[-1]

    @pl.when(pl.program_id(0) == section[0])
    def _():
        out_ref[...] = mine_ref[...].astype(f32)

    @pl.when(pl.program_id(0) != section[0])
    def _():
        out_ref[...] = other_ref[...].astype(f32)


def held_step(which, step, wanted, steps):
    return jnp.where(which == wanted, step, jnp.where(which > wanted, steps - 1, 0))


def join_halves(section, mine, other, axis, after):
    rows, width = mine.shape
    steps = 3
    block = (rows // steps, width)

    def mine_map(which, step, place):
        return (held_step(which, step, place[0], steps), 0)

    def other_map(which, step, place):
        return (held_step(which, step, 1 - place[0], steps), 0)

    def out_map(which, step, place):
        return (which * steps + step, 0) if axis == 0 else (step, which)

    return pl.pallas_call(
        join_kernel,
        grid_spec=pltpu.PrefetchScalarGridSpec(
            num_scalar_prefetch=1,
            grid=(2, steps),
            in_specs=[pl.BlockSpec(block, mine_map), pl.BlockSpec(block, other_map)]
            + [pl.BlockSpec(memory_space=pl.ANY)] * len(after),
            out_specs=pl.BlockSpec(block, out_map),
        ),
        out_shape=pltpu.HBM((2 * rows, width) if axis == 0 else (rows, 2 * width), f32),
        compiler_params=pltpu.CompilerParams(vmem_limit_bytes=44 * 2**20),
        cost_estimate=pl.CostEstimate(
            flops=0, bytes_accessed=12 * rows * width, transcendentals=0
        ),
        name="join_halves",
    )(section, mine, other, *after)


def block_kernel(counts, section, *refs):
    refs = list(refs)
    sources = [[refs.pop(0) for _ in range(count)] for count in counts]
    own_small, other_small, qkv_out, proj_out, router_out, gains_out = refs
    own = pl.program_id(0) == section[0]
    cut = qkv_out.shape[1]

    def emit_small(part):
        value = part[:, part.shape[1] - EXTRA :].astype(f32)
        router_out[...] = value[:, : router_out.shape[1]]
        gains_out[...] = value[:, 128:].T[:16]

    @pl.when(own)
    def _():
        emit_small(own_small)

    @pl.when(jnp.logical_not(own))
    def _():
        emit_small(other_small)

    def emit(parts):
        start = 0
        for part in parts:
            size = min(part.shape[1], cut + proj_out.shape[1] - start)
            left = max(0, min(size, cut - start))
            if left:
                qkv_out[:, start : start + left] = part[:, :left].astype(f32)
            if left < size:
                proj_out[:, start + left - cut : start + size - cut] = part[:, left:size].astype(f32)
            start += size

    for index, parts in enumerate(sources):
        place, mine = index % 2, index < 2

        @pl.when((own == mine) & (section[0] == place))
        def _():
            emit(parts)


def own_block(section, groups, own_small, other_small, experts):
    half = groups[0][0].shape[0]
    width = 2 * half
    steps = 3
    specs = []
    for index, parts in enumerate(groups):

        def place_map(which, step, section, place=index % 2, mine=index < 2):
            wanted = section[0] if mine else 1 - section[0]
            held = held_step(which, step, wanted, steps)
            return (jnp.where(section[0] == place, held, 0), 0)

        specs += [pl.BlockSpec((half // steps, part.shape[1]), place_map) for part in parts]

    for value, mine in ((own_small, True), (other_small, False)):

        def small_map(which, step, section, mine=mine):
            return (held_step(which, step, section[0] if mine else 1 - section[0], steps), 0)

        specs.append(pl.BlockSpec((half // steps, value.shape[1]), small_map))

    def out_map(which, step, section):
        return (which * steps + step, 0)

    return pl.pallas_call(
        functools.partial(block_kernel, [len(parts) for parts in groups]),
        grid_spec=pltpu.PrefetchScalarGridSpec(
            num_scalar_prefetch=1,
            grid=(2, steps),
            in_specs=specs,
            out_specs=(
                pl.BlockSpec((half // steps, 3 * width), out_map),
                pl.BlockSpec((half // steps, width), out_map),
                pl.BlockSpec((half // steps, experts), out_map),
                pl.BlockSpec(
                    (16, half // steps), lambda which, step, section: (0, which * steps + step)
                ),
            ),
        ),
        out_shape=(
            pltpu.HBM((2 * half, 3 * width), f32),
            pltpu.HBM((2 * half, width), f32),
            jax.ShapeDtypeStruct((2 * half, experts), f32),
            jax.ShapeDtypeStruct((16, 2 * half), f32),
        ),
        compiler_params=pltpu.CompilerParams(vmem_limit_bytes=44 * 2**20),
        cost_estimate=pl.CostEstimate(
            flops=0, bytes_accessed=48 * half * width, transcendentals=0
        ),
        name="own_block",
    )(section, *[part for parts in groups for part in parts], own_small, other_small)


def total_kernel(mine_ref, other_ref, *rest):
    rest[-1][0] = mine_ref[...].astype(f32) + other_ref[...].astype(f32)


def pair_total(mine, other, after):
    rows, width = mine.shape
    steps = 6
    block = pl.BlockSpec((rows // steps, width), lambda step: (step, 0))
    return pl.pallas_call(
        total_kernel,
        grid=(steps,),
        in_specs=[block, block] + [pl.BlockSpec(memory_space=pl.ANY)] * len(after),
        out_specs=pl.BlockSpec((1, rows // steps, width), lambda step: (0, step, 0)),
        out_shape=pltpu.HBM((1, rows, width), f32),
        compiler_params=pltpu.CompilerParams(vmem_limit_bytes=44 * 2**20),
        cost_estimate=pl.CostEstimate(
            flops=rows * width, bytes_accessed=8 * rows * width, transcendentals=0
        ),
        name="pair_total",
    )(mine, other, *after)


def span(axis, start, size):
    multiple = size & -size
    piece = pl.ds(pl.multiple_of(start * size, multiple), size)
    return (piece, slice(None)) if axis == 0 else (slice(None), piece)


def in_blocks(rows, work):
    size = next(size for size in (96, 64, 48, 32, 16) if rows % size == 0)
    if rows == size:
        work(slice(0, rows))
    else:

        @pl.loop(0, rows // size)
        def _(step):
            work(pl.ds(pl.multiple_of(step * size, size), size))


def combine_kernel(plans, extra, marks, *refs):
    count = len(plans)
    sources, outs = refs[: 2 * count], list(refs[2 * count + extra :])
    for index, (now, later) in enumerate(plans):
        stays, got = sources[2 * index : 2 * index + 2]
        rows, width = got.shape
        if now[0] == "gather":
            out = outs.pop(0)
            mine = marks[now[2]]
            for source, place in ((stays, mine), (got, 1 - mine)):
                target = out.at[span(now[1], place, got.shape[now[1]])]

                def move(block, source=source, target=target):
                    target[block, :] = source[block, :]

                in_blocks(rows, move)
        elif later is not None and later[0] == "reduce":
            mine = marks[later[2]]
            for place in (1 - mine, mine):
                out = outs.pop(0)
                window = span(later[1], place, out.shape[later[1]])
                first, second = stays.at[window], got.at[window]

                def add(block, first=first, second=second, out=out):
                    out[block, :] = first[block, :] + second[block, :]

                in_blocks(out.shape[0], add)
        else:
            out = outs.pop(0)

            def add_all(block, stays=stays, got=got, out=out):
                out[block, :] = stays[block, :] + got[block, :]

            in_blocks(rows, add_all)


def combine(marks, plans, pairs, after):
    near = whole_spec()
    shapes = []
    for (now, later), (stays, got) in zip(plans, pairs):
        shape = list(got.shape)
        if now[0] == "gather":
            shape[now[1]] *= 2
            shapes.append(shape)
        elif later is not None and later[0] == "reduce":
            shape[later[1]] //= 2
            shapes += [shape, shape]
        else:
            shapes.append(shape)
    values = [value for pair in pairs for value in pair]
    return pl.pallas_call(
        functools.partial(combine_kernel, plans, len(after)),
        out_shape=[jax.ShapeDtypeStruct(shape, bf16) for shape in shapes],
        in_specs=[pl.BlockSpec(memory_space=pltpu.SMEM)]
        + [near] * len(values)
        + [pl.BlockSpec(memory_space=pl.ANY)] * len(after),
        out_specs=[near] * len(shapes),
        compiler_params=pltpu.CompilerParams(vmem_limit_bytes=8 * 2**20),
        cost_estimate=pl.CostEstimate(flops=0, bytes_accessed=1024, transcendentals=0),
        name="combine",
    )(marks, *values, *after)


def combine_plainly(marks, plans, pairs):
    outs = []
    for (now, later), (stays, got) in zip(plans, pairs):
        if now[0] == "gather":
            outs.append(
                jnp.where(
                    marks[now[2]] == 0,
                    jnp.concatenate([stays, got], axis=now[1]),
                    jnp.concatenate([got, stays], axis=now[1]),
                )
            )
            continue
        total = stays + got
        if later is not None and later[0] == "reduce":
            size = total.shape[later[1]] // 2
            for place in (1 - marks[later[2]], marks[later[2]]):
                outs.append(lax.dynamic_slice_in_dim(total, place * size, size, axis=later[1]))
        else:
            outs.append(total)
    return outs


def flipped(value, axis, bit):
    pairs = [(place, place ^ (1 << bit)) for place in range(lax.axis_size(axis))]
    return lax.ppermute(value, axis, pairs)


class Travel:
    def __init__(self, marks, sends, keeps, orders):
        self.marks = marks
        self.plans = []
        self.aligned = True
        for value, order in zip(sends, orders):
            shape = list(value.shape)
            steps = []
            for bit in order:
                axis = 0 if shape[0] % 32 == 0 or shape[1] % 256 else 1
                if shape[axis] % (32, 256)[axis]:
                    self.aligned = False
                steps.append((axis, bit))
                shape[axis] //= 2
            self.plans.append(
                [("pair", 0, 0)]
                + [("reduce", *step) for step in steps]
                + [("gather", *step) for step in reversed(steps)]
            )
        self.stage = 0
        self.stays = list(keeps)
        self.got = [flipped(value, "section", 0) for value in sends]

    @property
    def done(self):
        return not self.got

    def pending(self):
        plans = []
        for plan in self.plans:
            later = plan[self.stage + 1] if self.stage + 1 < len(plan) else None
            plans.append((plan[self.stage], later))
        return plans, list(zip(self.stays, self.got))

    def accept(self, plans, outs):
        self.stage += 1
        self.stays, self.got = [], []
        for _, later in plans:
            sent = outs.pop(0)
            if later is not None and later[0] == "reduce":
                self.stays.append(outs.pop(0))
            else:
                self.stays.append(sent)
            if later is not None:
                self.got.append(flipped(sent, "wide", later[2]))


def joint_step(travels, after=()):
    travels = [travel for travel in travels if not travel.done]
    pending = [travel.pending() for travel in travels]
    plans = sum((item[0] for item in pending), [])
    pairs = sum((item[1] for item in pending), [])
    if all(travel.aligned for travel in travels):
        outs = list(combine(travels[0].marks, plans, pairs, after))
    else:
        outs = combine_plainly(travels[0].marks, plans, pairs)
    for travel, item in zip(travels, pending):
        travel.accept(item[0], outs)
    return sum((travel.stays for travel in travels), [])


def pad_kernel(section, x_ref, out_ref):
    out_ref[...] = jnp.zeros_like(out_ref)
    out_ref[0, : x_ref.shape[1], :] = x_ref[0]


def padded_images(section, value, images, pad):
    length, width = value.shape[1:]
    out = pl.pallas_call(
        pad_kernel,
        grid_spec=pltpu.PrefetchScalarGridSpec(
            num_scalar_prefetch=1,
            grid=(images,),
            in_specs=[
                pl.BlockSpec(
                    (1, length, width), lambda index, place: (place[0] * images + index, 0, 0)
                )
            ],
            out_specs=pl.BlockSpec((1, pad, width), lambda index, place: (index, 0, 0)),
        ),
        out_shape=jax.ShapeDtypeStruct((images, pad, width), value.dtype),
        compiler_params=pltpu.CompilerParams(vmem_limit_bytes=44 * 2**20),
        cost_estimate=pl.CostEstimate(flops=0, bytes_accessed=4 * value.size, transcendentals=0),
        name="padded_images",
    )(section, value)
    return out.reshape(images * pad, width)


def images_kernel(section, one_ref, two_ref, from_one, from_two, *rest):
    out_ref = rest[-1]
    own = pl.program_id(0) == section[0]
    for place, mine, other in ((0, one_ref, from_one), (1, two_ref, from_two)):
        for source, wanted in ((mine, own), (other, jnp.logical_not(own))):

            @pl.when(wanted & (section[0] == place))
            def _():
                out_ref[0, 0] = source[0, : out_ref.shape[2], :].astype(out_ref.dtype)


def own_images(section, one, two, from_one, from_two, images, length, dtype, after):
    rows, width = one.shape
    pad = rows // images
    sources = [value.reshape(images, pad, width) for value in (one, two, from_one, from_two)]
    specs = []
    for index in range(4):

        def place_map(which, image, section, place=index % 2, mine=index < 2):
            wanted = (section[0] == place) & ((which == section[0]) == mine)
            return (jnp.where(wanted, image, 0), 0, 0)

        specs.append(pl.BlockSpec((1, pad, width), place_map))
    return pl.pallas_call(
        images_kernel,
        grid_spec=pltpu.PrefetchScalarGridSpec(
            num_scalar_prefetch=1,
            grid=(2, images),
            in_specs=specs + [pl.BlockSpec(memory_space=pl.ANY)] * len(after),
            out_specs=pl.BlockSpec(
                (1, 1, length, width),
                lambda which, image, section: (0, which * images + image, 0, 0),
            ),
        ),
        out_shape=pltpu.HBM((1, 2 * images, length, width), dtype),
        compiler_params=pltpu.CompilerParams(vmem_limit_bytes=44 * 2**20),
        cost_estimate=pl.CostEstimate(flops=0, bytes_accessed=12 * one.size, transcendentals=0),
        name="own_images",
    )(section, *sources, *after)


def norm_stats(stream):
    mean_value = jnp.mean(stream, axis=-1, keepdims=True)
    centered = stream - mean_value
    variance = jnp.mean(centered * centered, axis=-1, keepdims=True)
    return centered * lax.rsqrt(variance + norm_epsilon)


def slot_plan(ids, rank, capacity):
    before = rank[None, :] < rank[:, None]
    first, second = ids[:, 0], ids[:, 1]
    same_first = (first[:, None] == first[None, :]) & before
    same_second = (second[:, None] == second[None, :]) & before
    crossed = second[:, None] == first[None, :]
    place_first = jnp.sum(same_first.astype(jnp.int32), axis=1)
    place_second = jnp.sum(same_second.astype(jnp.int32) + crossed.astype(jnp.int32), axis=1)
    slot_first = jnp.where(place_first < capacity, first * capacity + place_first, -1)
    slot_second = jnp.where(place_second < capacity, second * capacity + place_second, -1)
    return (jnp.where(first >= 0, slot_first, -1), jnp.where(second >= 0, slot_second, -1))


def body(
    patches,
    out_cotangent,
    attn_gain,
    qkv_weight,
    proj_weight,
    ffn_gain,
    mlp_in,
    mlp_out,
    router_weight,
    expert_in,
    expert_out,
    expert_ids,
    priority,
):
    expert_count = lax.axis_size("wide")
    sections = lax.axis_size("section")
    section = lax.axis_index("section")
    own_expert = lax.axis_index("wide")
    is_first = section == 0
    images = patches.shape[0] // sections
    length, width = patches.shape[1:]
    pad = -(-length // STEP) * STEP
    rows = images * pad
    capacity = max(2, images * length // expert_count)
    slots = expert_count * capacity
    levels = expert_count.bit_length() - 1
    assert 1 << levels == expert_count
    place = section[None]
    marks = (own_expert >> jnp.arange(levels, dtype=jnp.int32)) & 1
    bits = list(range(levels))
    third = max(1, levels // 3)
    groups = [bits[:third], bits[third : 2 * third], bits[2 * third : -1]]
    across_x = groups[0] + groups[1] + groups[2] + bits[-1:]
    across_y = groups[1] + groups[2] + groups[0] + bits[-1:]
    across_z = groups[2] + groups[0] + groups[1] + bits[-1:]

    def swap(value):
        return flipped(value, "section", 0)

    def exchange(value):
        return lax.all_to_all(value, "wide", split_axis=0, concat_axis=0, tiled=True)

    def across(value):
        shape = (expert_count, capacity, value.shape[1])
        return exchange(value.reshape(shape)).reshape(value.shape)

    other_qkv, other_proj = swap(qkv_weight[0]), swap(proj_weight[0])
    gains = jnp.concatenate([attn_gain, ffn_gain], axis=0)
    other_gains = swap(gains)
    gains_one = jnp.where(is_first, gains, other_gains)
    gains_two = jnp.where(is_first, other_gains, gains)
    weights = (qkv_weight[0], other_qkv, proj_weight[0], other_proj)
    which_one = jnp.stack([(section == 0).astype(jnp.int32), section])
    which_two = jnp.stack([(section == 1).astype(jnp.int32), section])

    ids = lax.dynamic_slice_in_dim(expert_ids, section * images, images)
    ids = jnp.pad(ids, ((0, 0), (0, pad - length), (0, 0)), constant_values=-1).reshape(rows, 2)
    rank = lax.dynamic_slice_in_dim(priority, section, 1).reshape(images, length)
    rank = jnp.pad(rank, ((0, 0), (0, pad - length))).reshape(rows)
    slot_first, slot_second = slot_plan(ids, rank, capacity)
    slot_range = jnp.arange(slots, dtype=jnp.int32)
    pick_first = slot_first[:, None] == slot_range[None, :]
    pick_second = slot_second[:, None] == slot_range[None, :]
    pick_any = (pick_first | pick_second).astype(bf16)
    kept_first = (slot_first >= 0).astype(f32)[:, None]
    kept_second = (slot_second >= 0).astype(f32)[:, None]
    rival = jnp.sum(
        jnp.where(pick_first, ids[:, 1:], 0) + jnp.where(pick_second, ids[:, :1], 0), axis=0
    )
    cotangent = padded_images(place, out_cotangent, images, pad)
    packet = jnp.concatenate(
        [
            tn(pick_any, cotangent).astype(bf16),
            jnp.broadcast_to(rival.astype(bf16)[:, None], (slots, PAIR)),
        ],
        axis=1,
    )

    stream_one = padded_images(place, patches, images, pad)
    mixed_one, packed_one, mix_one, normed_one = attention_forward(
        which_one, stream_one, weights, gains_one[:1], gains_one[1:], images, length
    )
    arrived_packet = across(packet)
    active_first = jax.nn.gelu(nn(normed_one, mlp_in)).astype(bf16)
    first_low = (mixed_one + nn(active_first, mlp_out)).astype(bf16)

    mixed_two, packed_two, mix_two, normed_two = attention_forward(
        which_two, first_low, weights, gains_two[:1], gains_two[1:], images, length
    )
    leaving = tn(pick_any, normed_two).astype(bf16)
    arrived = across(leaving)
    active_one, slope_one = mlp_refresh(normed_one, mlp_in, (leaving,))
    back, result, active, grad_hidden, grad_rows = expert_pass(
        own_expert[None],
        arrived,
        arrived_packet,
        router_weight,
        expert_in,
        expert_out,
        (kept_far(active_one), kept_far(slope_one)),
    )
    grad_expert_in, grad_expert_out = expert_products(arrived, grad_rows, active, grad_hidden)
    back = across(back)
    result, back, _ = lax.optimization_barrier((result, back, grad_expert_out[:16, :128]))
    returned = across(result)
    other_expert_in, other_expert_out = swap(grad_expert_in), swap(grad_expert_out)

    from_low_one = lax.ppermute(first_low, "section", [(1, 0)])
    expert_range = jnp.arange(expert_count, dtype=jnp.int32)
    logits = nn(normed_two, router_weight)
    one_hot = (ids[:, :, None] == expert_range[None, None, :]).astype(f32)
    chosen = jnp.sum(one_hot * logits[:, None, :], axis=-1)
    gates = jax.nn.softmax(chosen, axis=-1)
    low_first, low_second = pick_first.astype(bf16), pick_second.astype(bf16)
    grad_gates = jnp.concatenate(
        [
            jnp.sum(nn(low, back[:, width:]), axis=-1, keepdims=True)
            for low in (low_first, low_second)
        ],
        axis=1,
    )
    grad_chosen = gates * (grad_gates - jnp.sum(gates * grad_gates, axis=-1, keepdims=True))
    grad_logits = jnp.sum(one_hot * grad_chosen[:, :, None], axis=1).astype(bf16)
    grad_router = tn(normed_two, grad_logits)
    grad_normed_two = nn(pick_any, back[:, :width]) + nt(grad_logits, router_weight)
    second_low = (
        mixed_two
        + kept_first * gates[:, :1] * nn(low_first, returned)
        + kept_second * gates[:, 1:] * nn(low_second, returned)
    ).astype(bf16)
    grad_first, small_two, *pieces = attention_backward(
        which_two,
        first_low,
        mixed_two,
        cotangent,
        grad_normed_two,
        packed_two,
        mix_two,
        weights,
        gains_two[:1],
        gains_two[1:],
        images,
        length,
        1,
        bf16,
    )
    two = Travel(marks, pieces[:1], pieces[1:], [across_x])
    grad_normed_one, in_send, in_keep, out_send, out_keep = mlp_backward(
        place,
        normed_one,
        grad_first,
        mlp_in,
        mlp_out,
        active_one,
        slope_one,
        after=(kept_far(other_expert_in), kept_far(other_expert_out), from_low_one, returned),
    )
    mlp_first = Travel(marks, [in_send], [in_keep], [across_z])
    mlp_second = Travel(marks, [out_send], [out_keep], [across_y])
    early = [two, mlp_first, mlp_second]
    from_low_two = lax.ppermute(second_low, "section", [(0, 1)])
    from_grad_two = lax.ppermute(grad_first, "section", [(0, 1)])
    grad_one, small_one, *pieces = attention_backward(
        which_one,
        stream_one,
        mixed_one,
        grad_first,
        grad_normed_one,
        packed_one,
        mix_one,
        weights,
        gains_one[:1],
        gains_one[1:],
        images,
        length,
        2,
        f32,
        small=(grad_router, small_two),
        after=joint_step(early, after=[second_low]),
    )
    one = Travel(marks, pieces[:2], pieces[2:], [across_x, across_y])
    last = joint_step(early, after=[from_low_two, from_grad_two])

    def settled(value):
        return lax.optimization_barrier(jnp.transpose(value[0], (1, 0, 2)))

    activations = settled(
        own_images(
            place, first_low, second_low, from_low_one, from_low_two, images, length, bf16, last
        )
    )
    last = joint_step(early + [one], after=[kept_far(activations)])
    expert_in_sum = pair_total(grad_expert_in, other_expert_in, tuple(last))
    last = joint_step(early + [one], after=[kept_far(expert_in_sum)])
    expert_out_sum = pair_total(grad_expert_out, other_expert_out, tuple(last))
    last = joint_step(early + [one], after=[kept_far(expert_out_sum)])
    while not two.done:
        last = joint_step(early + [one], after=last)

    other_in, other_out = swap(mlp_first.stays[0]), swap(mlp_second.stays[0])
    late_grad, *last = lax.optimization_barrier((grad_one, *last))
    from_grad_one = lax.ppermute(late_grad, "section", [(1, 0)])
    last = joint_step([one], after=(other_in, other_out, from_grad_one))
    late_two, *last = lax.optimization_barrier((two.stays[0], *last))
    from_two = [lax.ppermute(late_two, "section", [(0, 1)])]
    mlp_in_sum = join_halves(place, mlp_first.stays[0], other_in, 0, tuple(last))
    mlp_out_sum = join_halves(
        place, mlp_second.stays[0], other_out, 1, (kept_far(mlp_in_sum),)
    )
    input_grads = settled(
        own_images(
            place,
            grad_one,
            grad_first,
            from_grad_one,
            from_grad_two,
            images,
            length,
            f32,
            (kept_far(mlp_out_sum),),
        )
    )
    last = [kept_far(input_grads)]
    while not one.done:
        last = joint_step([one], after=last)
    from_one = [lax.ppermute(one.stays[0], "section", [(1, 0)]), swap(one.stays[1])]
    qkv_grad, proj_grad, sum_router, gain_sums = own_block(
        place,
        (one.stays, two.stays, from_one, from_two),
        one.stays[1],
        from_one[1],
        expert_count,
    )
    small_block = lax.dynamic_slice_in_dim(gain_sums, 8 * section, 8)
    return (
        jnp.transpose(activations, (1, 0, 2))[None],
        jnp.transpose(input_grads, (1, 0, 2))[None],
        small_block[:1],
        qkv_grad[None],
        proj_grad[None],
        small_block[1:2],
        mlp_in_sum,
        mlp_out_sum,
        sum_router,
        expert_in_sum,
        expert_out_sum,
    )


def solution(mesh):
    in_specs = (
        P("wide", None, None),
        P("wide", None, None),
        P("section", None),
        P("section", None, None),
        P("section", None, None),
        P("section", None),
        P(),
        P(),
        P(),
        P("wide", None, None),
        P("wide", None, None),
        P("wide", None, None),
        P("wide", None),
    )
    out_specs = (
        P("section", "wide", None, None),
        P("section", "wide", None, None),
        P("section", None),
        P("section", None, None),
        P("section", None, None),
        P("section", None),
        P(),
        P(),
        P(),
        P("wide", None, None),
        P("wide", None, None),
    )
    return jax.shard_map(body, mesh=mesh, in_specs=in_specs, out_specs=out_specs, check_vma=False)
```
